32 devices in a mesh: span: 4 (over z), wall: 4 (over y, core), stream: 2 (over x).
Axes of the slice: x: 2, y: 2, z: 4, core: 2. Of those that a mesh axis runs over, the one named last changes fastest.
Arguments:
- fields: float32 [4, 16, 64, 512], P(None, 'stream', 'wall', 'span'), may hold values from -67.5 to 67.5, as said below
Outputs:
- clark_model: float32 [3, 16, 64, 512], P(None, 'stream', 'wall', 'span')
- similar_model: float32 [3, 16, 64, 512], P(None, 'stream', 'wall', 'span')
- clark_corr: float32 [3, 64], P(None, 'wall')
- similar_corr: float32 [3, 64], P(None, 'wall')
The draws below stay inside these ranges and needn't reach their ends.
Inputs may be any that keep to these rules, and one draw needn't show every extreme that they name: The fields are rough from cell to cell.
All inputs are finite; a program needn't handle non-finite values.
Results may differ from the reference program's by a relative error of at most 0.00024.
Values sent between devices are 32-bit elements; how exact they have to be, the bound alone decides.
No kernel may reach another device: no remote copies, remote signals or barrier semaphores. Data moves between devices by JAX's collectives and lax.ppermute only.
A program may use at most 64 MiB of HBM per device.

```python
import math
import jax
import jax.numpy as jnp
from jax import lax

NS = 16
NW = 64
NP = 512


def draw_fields(key, part):
    first_key, second_key = jax.random.split(key)
    shape = (4, NS, NW, NP)
    spanwise = jnp.arange(NP, dtype=jnp.float32)
    base = jnp.clip(jax.random.normal(first_key, shape, jnp.float32), -5.0, 5.0)
    rough = jax.random.uniform(second_key, shape, jnp.float32, 0.5, 1.5)
    ramp = 1.0 + 2.0 * spanwise / max(NP - 1, 1)
    return 3.0 * base * rough * ramp[None, None, None, :]


def setup_inputs(seed: int = 0) -> dict:
    keys = jax.random.split(jax.random.key(seed), 2)
    return {
        "fields": draw_fields(jax.random.fold_in(keys[1], 71), 0),
    }


raw_taps = [math.exp(-(k - 8) ** 2 / 18.0) for k in range(17)]
filter_taps = [value / sum(raw_taps) for value in raw_taps]
clark_coef = 9.0
small_eps = 1e-06

def smooth(padded, direction, length):
    result = filter_taps[0] * lax.slice_in_dim(padded, 0, length, axis=direction)
    for k in range(1, 17):
        result = result + filter_taps[k] * lax.slice_in_dim(padded, k, k + length, axis=direction)
    return result

def filter_one(field):
    padded = jnp.pad(field, ((0, 0), (0, 0), (8, 8)), mode='wrap')
    field = smooth(padded, 2, NP)
    padded = jnp.pad(field, ((0, 0), (8, 8), (0, 0)))
    field = smooth(padded, 1, NW)
    padded = jnp.pad(field, ((8, 8), (0, 0), (0, 0)))
    return smooth(padded, 0, NS)

def with_products(quad):
    return jnp.concatenate([quad, quad[:3] * quad[3:4]], axis=0)

def filter_all(quad):
    return lax.map(filter_one, with_products(quad))

def clark_flux(means):
    padded = jnp.pad(means, ((0, 0), (0, 0), (0, 0), (1, 1)), mode='wrap')
    along_span = (padded[..., 2:] - padded[..., :-2]) * 0.5
    padded = jnp.pad(means, ((0, 0), (0, 0), (1, 1), (0, 0)))
    along_wall = (padded[:, :, 2:, :] - padded[:, :, :-2, :]) * 0.5
    padded = jnp.pad(means, ((0, 0), (1, 1), (0, 0), (0, 0)))
    along_stream = (padded[:, 2:] - padded[:, :-2]) * 0.5
    total = along_span[:3] * along_span[3:4] + along_wall[:3] * along_wall[3:4]
    total = total + along_stream[:3] * along_stream[3:4]
    return clark_coef * total

def reference(fields):
    first = filter_all(fields)
    means = first[:4]
    exact = first[4:] - means[:3] * means[3:4]
    second = filter_all(means)
    similar = second[4:] - second[:3] * second[3:4]
    clark = clark_flux(means)
    plane_cells = float(NS * NP)
    cross_c = lax.optimization_barrier(jnp.sum(exact * clark, axis=(1, 3))) / plane_cells
    cross_s = lax.optimization_barrier(jnp.sum(exact * similar, axis=(1, 3))) / plane_cells
    power_e = lax.optimization_barrier(jnp.sum(exact * exact, axis=(1, 3))) / plane_cells
    power_c = lax.optimization_barrier(jnp.sum(clark * clark, axis=(1, 3))) / plane_cells
    power_s = lax.optimization_barrier(jnp.sum(similar * similar, axis=(1, 3))) / plane_cells
    clark_corr = cross_c / jnp.sqrt((power_e + small_eps) * (power_c + small_eps))
    similar_corr = cross_s / jnp.sqrt((power_e + small_eps) * (power_s + small_eps))
    clark_model = clark / jnp.sqrt(power_c + small_eps)[:, None, :, None]
    similar_model = similar / jnp.sqrt(power_s + small_eps)[:, None, :, None]
    return (clark_model, similar_model, clark_corr, similar_corr)
```

```python
import functools
import math

import jax
import jax.numpy as jnp
import ml_dtypes
import numpy as np
from jax import lax
from jax.experimental import pallas as pl
from jax.experimental.pallas import tpu as pltpu
from jax.sharding import PartitionSpec as P

raw_taps = [math.exp(-((k - 8) ** 2) / 18.0) for k in range(17)]
filter_taps = [value / sum(raw_taps) for value in raw_taps]
clark_coef = 9.0
small_eps = 1e-06

reach = 8
rim = 2 * reach


def split_constant(matrix):
    high = matrix.astype(ml_dtypes.bfloat16)
    low = (matrix - high.astype(np.float64)).astype(ml_dtypes.bfloat16)
    return high, low


def band(outs, ins, offset):
    matrix = np.zeros((outs, ins))
    for o in range(outs):
        for i in range(ins):
            k = i - o - offset + reach
            if 0 <= k <= 2 * reach:
                matrix[o, i] = filter_taps[k]
    return matrix


def plane_constants(layers, rows):
    stream = band(layers, layers, 0)
    wall = band(rows, 2 * rows, reach)
    blocks = [np.kron(stream, wall[:, :rows]), np.kron(stream, wall[:, rows:])]
    return split_constant(np.concatenate(blocks, axis=1))


def span_constants(width):
    everything = band(width + 2 * rim, width + 2 * rim, 0)
    weights = np.zeros((4, 2 * width, 2 * width))
    for f in range(4):
        place = np.full(width + 2 * rim, -1)
        for c in range(rim):
            place[c] = width + 64 + f * rim + c
            place[rim + width + c] = width + f * rim + c
        place[rim : rim + width] = np.arange(width)
        swapped = np.where(place >= width, place - width, place + width)
        weights[f][np.ix_(place, swapped)] = everything.T
    high, low = split_constant(weights)
    low = np.concatenate([low[..., width:], low[..., :width]], axis=2)
    return np.concatenate([high, low], axis=2)


def halves(value):
    high = value.astype(jnp.bfloat16)
    return high, (value - high.astype(jnp.float32)).astype(jnp.bfloat16)


def dot(a, b):
    return lax.dot_general(a, b, (((1,), (0,)), ((), ())), preferred_element_type=jnp.float32)


def lane_index(shape):
    return lax.broadcasted_iota(jnp.int32, shape, len(shape) - 1)


def edge_kernel(own, edges):
    _, layers, rows, width = own.shape
    lane = lane_index((layers * rows, width))
    total = jnp.zeros((layers * rows, width), jnp.float32)
    for f in range(4):
        cells = own[f].reshape(layers * rows, width)
        first = pltpu.roll(cells, f * rim, 1) if f else cells
        total = jnp.where((lane >= f * rim) & (lane < (f + 1) * rim), first, total)
        last = pltpu.roll(cells, (64 + f * rim + rim) % width, 1) if (f + 1) * rim != 64 else cells
        start = 64 + f * rim
        total = jnp.where((lane >= start) & (lane < start + rim), last, total)
    edges[...] = total.reshape(layers, rows, width)


def spread_temperature(strip):
    width = strip.shape[1]
    field = lax.rem(lane_index(strip.shape), 64) // rim
    result = strip
    for f in range(3):
        moved = pltpu.roll(strip, width - (3 - f) * rim, 1)
        result = jnp.where(field == f, moved, result)
    return result


def flux_kernel(
    walls, own, part, a_own, b_own, a_part, b_part, s_own, s_part, a_strip, b_strip,
    plane_h, plane_l, span_w, clark_ref, similar_ref, sums_ref,
    raw, in_h, in_l, prod_h, prod_l, mean, mid_h, mid_l,
):
    _, layers, rows, width = own.shape
    both = 2 * layers
    cells = both * rows
    here = layers * rows
    me_s = lax.axis_index("stream")
    me_w = lax.axis_index("wall")
    odd = lax.rem(me_w, 2)
    mine = pl.multiple_of(me_s * layers, layers)
    other = pl.multiple_of((1 - me_s) * layers, layers)
    row_a = pl.multiple_of((1 - odd) * (2 * rows), rows)
    row_b = pl.multiple_of(odd * (2 * rows), rows)
    at_end = (me_w == 0) | (me_w == walls - 1)
    keep_b = jnp.where(at_end, 0.0, 1.0).astype(jnp.float32)

    for where, blocks in ((mine, (own, a_own, b_own)), (other, (part, a_part, b_part))):
        raw[:4, pl.ds(where, layers), rows : 2 * rows, :] = blocks[0][...]
        raw[:4, pl.ds(where, layers), pl.ds(row_a, rows), :] = blocks[1][...]
        raw[:4, pl.ds(where, layers), pl.ds(row_b, rows), :] = blocks[2][...] * keep_b
    for k, where, block in ((0, mine, s_own), (1, other, s_part)):
        raw[4, pl.ds(where, layers), rows : 2 * rows, :] = block[...]
        raw[4, pl.ds(where, layers), pl.ds(row_a, rows), :] = a_strip[k]
        raw[4, pl.ds(where, layers), pl.ds(row_b, rows), :] = b_strip[k] * keep_b

    for block in range(3):
        for t in range(5):
            value = raw[t, :, block * rows : (block + 1) * rows, :].reshape(cells, width)
            high, low = halves(value)
            in_h[block * cells : (block + 1) * cells, t * width : (t + 1) * width] = high
            in_l[block * cells : (block + 1) * cells, t * width : (t + 1) * width] = low

    for t in range(4):
        mean[t, 0] = jnp.zeros((2 * rows, width), jnp.float32)
        mean[t, both + 1] = jnp.zeros((2 * rows, width), jnp.float32)
    for half in range(2):
        part_h = in_h[half * cells : (half + 2) * cells, :]
        part_l = in_l[half * cells : (half + 2) * cells, :]
        planes = dot(plane_h[...], part_h) + dot(plane_l[...], part_h) + dot(plane_h[...], part_l)
        row = lax.rem(lax.broadcasted_iota(jnp.int32, planes.shape, 0), rows)
        if half == 0:
            inside = (me_w > 0) | (row >= reach)
        else:
            inside = (me_w < walls - 1) | (row < rows - reach)
        planes = jnp.where(inside, planes, 0.0)
        high, low = halves(planes)
        strip = jnp.zeros((cells, width), jnp.float32)
        for f in range(4):
            lhs_h = jnp.concatenate([high[:, f * width : (f + 1) * width], high[:, 4 * width :]], axis=1)
            lhs_l = jnp.concatenate([low[:, f * width : (f + 1) * width], low[:, 4 * width :]], axis=1)
            one = dot(lhs_h, span_w[f])
            two = dot(lhs_l, span_w[f, :, : 2 * width])
            value = one[:, width : 2 * width] + one[:, 2 * width : 3 * width] + two[:, width:]
            strip = strip + one[:, :width] + one[:, 3 * width :] + two[:, :width]
            mean[f, 1 : both + 1, half * rows : (half + 1) * rows, :] = value.reshape(both, rows, width)
        mean[4, 1 : both + 1, half * rows : (half + 1) * rows, :] = strip.reshape(both, rows, width)

    own_rows = pl.ds(pl.multiple_of(me_s * here, here), here)

    def filtered(high, low, tiles):
        lhs_h = plane_h[own_rows, :]
        planes = dot(lhs_h, high[...]) + dot(plane_l[own_rows, :], high[...]) + dot(lhs_h, low[...])
        high, low = halves(planes)
        results = []
        for t, s, f in tiles:
            pick_h = jnp.concatenate([high[:, t * width : (t + 1) * width], high[:, s * width : (s + 1) * width]], axis=1)
            pick_l = jnp.concatenate([low[:, t * width : (t + 1) * width], low[:, s * width : (s + 1) * width]], axis=1)
            one = dot(pick_h, span_w[f, :, width : 3 * width])
            two = dot(pick_l, span_w[f, :, width : 2 * width])
            results.append((one[:, :width] + one[:, width:] + two).reshape(layers, rows, width))
        return results

    for half in range(2):
        span = slice(reach + half * rows, reach + (half + 1) * rows)
        down = slice(half * cells, (half + 1) * cells)
        temperature = raw[3, :, span, :].reshape(cells, width)
        strip = raw[4, :, span, :].reshape(cells, width)
        factors = [(raw[i, :, span, :].reshape(cells, width), temperature) for i in range(3)]
        factors.append((strip, spread_temperature(strip)))
        for t, (left, right) in enumerate(factors):
            high, low = halves(left * right)
            prod_h[down, t * width : (t + 1) * width] = high
            prod_l[down, t * width : (t + 1) * width] = low
    flux = filtered(prod_h, prod_l, [(i, 3, i) for i in range(3)])

    for half in range(2):
        span = slice(half * rows, (half + 1) * rows)
        down = slice(half * cells, (half + 1) * cells)
        tiles = [mean[t, 1 : both + 1, span, :].reshape(cells, width) for t in range(5)]
        tiles += [tiles[i] * tiles[3] for i in range(3)]
        tiles.append(tiles[4] * spread_temperature(tiles[4]))
        for t, value in enumerate(tiles):
            high, low = halves(value)
            mid_h[down, t * width : (t + 1) * width] = high
            mid_l[down, t * width : (t + 1) * width] = low
    second = filtered(mid_h, mid_l, [(f, 4, f) for f in range(4)] + [(5 + i, 8, i) for i in range(3)])

    lane = lane_index((layers, rows, width))
    mid = slice(reach, reach + rows)
    centre, along_span, along_wall, along_stream = [], [], [], []
    strip = mean[4, pl.ds(mine + 1, layers), mid, :]
    for f in range(4):
        here_f = mean[f, pl.ds(mine + 1, layers), mid, :]
        centre.append(here_f)
        after = pltpu.roll(here_f, width - 1, 2)
        after = jnp.where(lane == width - 1, pltpu.roll(strip, (width - 1 - f * rim) % width, 2), after)
        before = pltpu.roll(here_f, 1, 2)
        before = jnp.where(lane == 0, pltpu.roll(strip, (width - (64 + f * rim + rim - 1)) % width, 2), before)
        along_span.append((after - before) * 0.5)
        below = mean[f, pl.ds(mine + 1, layers), reach + 1 : reach + rows + 1, :]
        above = mean[f, pl.ds(mine + 1, layers), reach - 1 : reach + rows - 1, :]
        along_wall.append((below - above) * 0.5)
        ahead = mean[f, pl.ds(mine + 2, layers), mid, :]
        behind = mean[f, pl.ds(mine, layers), mid, :]
        along_stream.append((ahead - behind) * 0.5)

    lane = lane_index((rows, width))
    table = jnp.zeros((rows, width), jnp.float32)
    for i in range(3):
        exact = flux[i] - centre[i] * centre[3]
        similar = second[4 + i] - second[i] * second[3]
        total = along_span[i] * along_span[3] + along_wall[i] * along_wall[3]
        clark = clark_coef * (total + along_stream[i] * along_stream[3])
        clark_ref[i] = clark
        similar_ref[i] = similar
        terms = (exact * clark, exact * similar, exact * exact, clark * clark, similar * similar)
        for q, term in enumerate(terms):
            value = jnp.sum(jnp.sum(term, axis=0), axis=1, keepdims=True)
            table = jnp.where(lane == 3 * q + i, value, table)
    sums_ref[...] = table


def finish_kernel(plane_cells, *refs):
    sums = refs[:-6]
    clark, similar, clark_model, similar_model, clark_corr, similar_corr = refs[-6:]
    rows, width = sums[0].shape
    table = sums[0][...]
    for more in sums[1:]:
        table = table + more[...]
    table = table / plane_cells
    lane = lane_index((rows, width))
    corr = jnp.zeros((rows, width), jnp.float32)
    for i in range(3):
        cross_c, cross_s, power_e, power_c, power_s = (
            table[:, 3 * q + i : 3 * q + i + 1] for q in range(5)
        )
        clark_model[i] = clark[i] / jnp.sqrt(power_c + small_eps)[None]
        similar_model[i] = similar[i] / jnp.sqrt(power_s + small_eps)[None]
        value = cross_c / jnp.sqrt((power_e + small_eps) * (power_c + small_eps))
        corr = jnp.where(lane == i, value, corr)
        value = cross_s / jnp.sqrt((power_e + small_eps) * (power_s + small_eps))
        corr = jnp.where(lane == 8 + i, value, corr)
    square = jnp.concatenate([corr, jnp.zeros((width - rows, width), jnp.float32)], axis=0)
    turned = square.T
    clark_corr[...] = turned[:3, :rows]
    similar_corr[...] = turned[8:11, :rows]


def vmem(count):
    return [pl.BlockSpec(memory_space=pltpu.VMEM)] * count


def shards(fields):
    _, layers, rows, width = fields.shape
    spans = lax.axis_size("span")
    walls = lax.axis_size("wall")
    streams = lax.axis_size("stream")
    cells = 2 * layers * rows

    def swap(value):
        return lax.ppermute(value, "stream", [(0, 1), (1, 0)])

    def pair_a(value):
        return lax.ppermute(value, "wall", [(w, w ^ 1) for w in range(walls)])

    def pair_b(value):
        return lax.ppermute(
            value, "wall", [(w, min(max(((w + 1) ^ 1) - 1, 0), walls - 1)) for w in range(walls)]
        )

    edges = pl.pallas_call(
        edge_kernel,
        out_shape=jax.ShapeDtypeStruct((layers, rows, width), jnp.float32),
        in_specs=vmem(1),
        out_specs=vmem(1)[0],
        name="edges",
    )(fields)
    before = lax.ppermute(edges, "span", [(p, (p + 1) % spans) for p in range(spans)])
    after = lax.ppermute(edges, "span", [(p, (p - 1) % spans) for p in range(spans)])
    part = swap(fields)
    a_own, b_own = pair_a(fields), pair_b(fields)
    a_part, b_part = pair_a(part), pair_b(part)
    s_own = jnp.where(lane_index(edges.shape) < width // 2, after, before)
    s_part = swap(s_own)
    strips = jnp.stack([s_own, s_part])
    a_strip, b_strip = pair_a(strips), pair_b(strips)

    plane_h, plane_l = plane_constants(2 * layers, rows)
    span_w = span_constants(width)
    block = jax.ShapeDtypeStruct((3, layers, rows, width), jnp.float32)
    clark, similar, sums = pl.pallas_call(
        functools.partial(flux_kernel, walls),
        out_shape=(block, block, jax.ShapeDtypeStruct((rows, width), jnp.float32)),
        in_specs=vmem(13),
        out_specs=tuple(vmem(3)),
        scratch_shapes=[
            pltpu.VMEM((5, 2 * layers, 3 * rows, width), jnp.float32),
            pltpu.VMEM((3 * cells, 5 * width), jnp.bfloat16),
            pltpu.VMEM((3 * cells, 5 * width), jnp.bfloat16),
            pltpu.VMEM((2 * cells, 4 * width), jnp.bfloat16),
            pltpu.VMEM((2 * cells, 4 * width), jnp.bfloat16),
            pltpu.VMEM((5, 2 * layers + 2, 2 * rows, width), jnp.float32),
            pltpu.VMEM((2 * cells, 9 * width), jnp.bfloat16),
            pltpu.VMEM((2 * cells, 9 * width), jnp.bfloat16),
        ],
        compiler_params=pltpu.CompilerParams(vmem_limit_bytes=40 * 1024 * 1024),
        name="flux",
    )(
        fields, part, a_own, b_own, a_part, b_part, s_own, s_part, a_strip, b_strip,
        jnp.asarray(plane_h), jnp.asarray(plane_l), jnp.asarray(span_w),
    )

    group = spans * streams
    tables = [sums]
    for step in range(1, group):
        tables.append(
            lax.ppermute(sums, ("span", "stream"), [(g, (g + step) % group) for g in range(group)])
        )
    corr = jax.ShapeDtypeStruct((3, rows), jnp.float32)
    return pl.pallas_call(
        functools.partial(finish_kernel, float(layers * width * group)),
        out_shape=(block, block, corr, corr),
        in_specs=vmem(group + 2),
        out_specs=tuple(vmem(4)),
        name="finish",
    )(*tables, clark, similar)


def solution(mesh):
    return jax.shard_map(
        shards,
        mesh=mesh,
        in_specs=(P(None, "stream", "wall", "span"),),
        out_specs=(
            P(None, "stream", "wall", "span"),
            P(None, "stream", "wall", "span"),
            P(None, "wall"),
            P(None, "wall"),
        ),
        check_vma=False,
    )
```

```python
import functools
import math

import jax
import jax.numpy as jnp
import ml_dtypes
import numpy as np
from jax import lax
from jax.experimental import pallas as pl
from jax.experimental.pallas import tpu as pltpu
from jax.sharding import PartitionSpec as P

raw_taps = [math.exp(-((k - 8) ** 2) / 18.0) for k in range(17)]
filter_taps = [value / sum(raw_taps) for value in raw_taps]
clark_coef = 9.0
small_eps = 1e-06

reach = 8
rim = 2 * reach


def split_constant(matrix):
    high = matrix.astype(ml_dtypes.bfloat16)
    low = (matrix - high.astype(np.float64)).astype(ml_dtypes.bfloat16)
    return high, low


def band(outs, ins, offset):
    matrix = np.zeros((outs, ins))
    for o in range(outs):
        for i in range(ins):
            k = i - o - offset + reach
            if 0 <= k <= 2 * reach:
                matrix[o, i] = filter_taps[k]
    return matrix


def plane_constants(layers, rows):
    stream = band(layers, layers, 0)
    wall = band(rows, 2 * rows, reach)
    blocks = [np.kron(stream, wall[:, :rows]), np.kron(stream, wall[:, rows:])]
    return split_constant(np.concatenate(blocks, axis=1))


def span_constants(width):
    everything = band(width + 2 * rim, width + 2 * rim, 0)
    weights = np.zeros((4, 2 * width, 2 * width))
    for f in range(4):
        place = np.full(width + 2 * rim, -1)
        for c in range(rim):
            place[c] = width + 64 + f * rim + c
            place[rim + width + c] = width + f * rim + c
        place[rim : rim + width] = np.arange(width)
        swapped = np.where(place >= width, place - width, place + width)
        weights[f][np.ix_(place, swapped)] = everything.T
    high, low = split_constant(weights)
    low = np.concatenate([low[..., width:], low[..., :width]], axis=2)
    return np.concatenate([high, low], axis=2)


def halves(value):
    high = value.astype(jnp.bfloat16)
    return high, (value - high.astype(jnp.float32)).astype(jnp.bfloat16)


def dot(a, b):
    return lax.dot_general(a, b, (((1,), (0,)), ((), ())), preferred_element_type=jnp.float32)


def lane_index(shape):
    return lax.broadcasted_iota(jnp.int32, shape, len(shape) - 1)


def edge_kernel(own, edges):
    _, layers, rows, width = own.shape
    lane = lane_index((layers * rows, width))
    total = jnp.zeros((layers * rows, width), jnp.float32)
    for f in range(4):
        cells = own[f].reshape(layers * rows, width)
        first = pltpu.roll(cells, f * rim, 1) if f else cells
        total = jnp.where((lane >= f * rim) & (lane < (f + 1) * rim), first, total)
        last = pltpu.roll(cells, (64 + f * rim + rim) % width, 1) if (f + 1) * rim != 64 else cells
        start = 64 + f * rim
        total = jnp.where((lane >= start) & (lane < start + rim), last, total)
    edges[...] = total.reshape(layers, rows, width)


def spread_temperature(strip):
    width = strip.shape[1]
    field = lax.rem(lane_index(strip.shape), 64) // rim
    result = strip
    for f in range(3):
        moved = pltpu.roll(strip, width - (3 - f) * rim, 1)
        result = jnp.where(field == f, moved, result)
    return result


def flux_kernel(
    walls, own, part, a_own, b_own, a_part, b_part, s_own, s_part, a_strip, b_strip,
    plane_h, plane_l, span_w, clark_ref, similar_ref, sums_ref,
    raw, in_h, in_l, prod_h, prod_l, mean, mid_h, mid_l,
):
    _, layers, rows, width = own.shape
    both = 2 * layers
    cells = both * rows
    here = layers * rows
    me_s = lax.axis_index("stream")
    me_w = lax.axis_index("wall")
    odd = lax.rem(me_w, 2)
    mine = pl.multiple_of(me_s * layers, layers)
    other = pl.multiple_of((1 - me_s) * layers, layers)
    row_a = pl.multiple_of((1 - odd) * (2 * rows), rows)
    row_b = pl.multiple_of(odd * (2 * rows), rows)
    at_end = (me_w == 0) | (me_w == walls - 1)
    keep_b = jnp.where(at_end, 0.0, 1.0).astype(jnp.float32)

    for where, blocks in ((mine, (own, a_own, b_own)), (other, (part, a_part, b_part))):
        raw[:4, pl.ds(where, layers), rows : 2 * rows, :] = blocks[0][...]
        raw[:4, pl.ds(where, layers), pl.ds(row_a, rows), :] = blocks[1][...]
        raw[:4, pl.ds(where, layers), pl.ds(row_b, rows), :] = blocks[2][...] * keep_b
    for k, where, block in ((0, mine, s_own), (1, other, s_part)):
        raw[4, pl.ds(where, layers), rows : 2 * rows, :] = block[...]
        raw[4, pl.ds(where, layers), pl.ds(row_a, rows), :] = a_strip[k]
        raw[4, pl.ds(where, layers), pl.ds(row_b, rows), :] = b_strip[k] * keep_b

    for block in range(3):
        for t in range(5):
            value = raw[t, :, block * rows : (block + 1) * rows, :].reshape(cells, width)
            high, low = halves(value)
            in_h[block * cells : (block + 1) * cells, t * width : (t + 1) * width] = high
            in_l[block * cells : (block + 1) * cells, t * width : (t + 1) * width] = low

    for t in range(4):
        mean[t, 0] = jnp.zeros((2 * rows, width), jnp.float32)
        mean[t, both + 1] = jnp.zeros((2 * rows, width), jnp.float32)
    for half in range(2):
        part_h = in_h[half * cells : (half + 2) * cells, :]
        part_l = in_l[half * cells : (half + 2) * cells, :]
        planes = dot(plane_h[...], part_h) + dot(plane_l[...], part_h) + dot(plane_h[...], part_l)
        row = lax.rem(lax.broadcasted_iota(jnp.int32, planes.shape, 0), rows)
        if half == 0:
            inside = (me_w > 0) | (row >= reach)
        else:
            inside = (me_w < walls - 1) | (row < rows - reach)
        planes = jnp.where(inside, planes, 0.0)
        high, low = halves(planes)
        strip = jnp.zeros((cells, width), jnp.float32)
        for f in range(4):
            lhs_h = jnp.concatenate([high[:, f * width : (f + 1) * width], high[:, 4 * width :]], axis=1)
            lhs_l = jnp.concatenate([low[:, f * width : (f + 1) * width], low[:, 4 * width :]], axis=1)
            one = dot(lhs_h, span_w[f])
            two = dot(lhs_l, span_w[f, :, : 2 * width])
            value = one[:, width : 2 * width] + one[:, 2 * width : 3 * width] + two[:, width:]
            strip = strip + one[:, :width] + one[:, 3 * width :] + two[:, :width]
            mean[f, 1 : both + 1, half * rows : (half + 1) * rows, :] = value.reshape(both, rows, width)
        mean[4, 1 : both + 1, half * rows : (half + 1) * rows, :] = strip.reshape(both, rows, width)

    own_rows = pl.ds(pl.multiple_of(me_s * here, here), here)

    def filtered(high, low, tiles):
        lhs_h = plane_h[own_rows, :]
        planes = dot(lhs_h, high[...]) + dot(plane_l[own_rows, :], high[...]) + dot(lhs_h, low[...])
        high, low = halves(planes)
        results = []
        for t, s, f in tiles:
            pick_h = jnp.concatenate([high[:, t * width : (t + 1) * width], high[:, s * width : (s + 1) * width]], axis=1)
            pick_l = jnp.concatenate([low[:, t * width : (t + 1) * width], low[:, s * width : (s + 1) * width]], axis=1)
            one = dot(pick_h, span_w[f, :, width : 3 * width])
            two = dot(pick_l, span_w[f, :, width : 2 * width])
            results.append((one[:, :width] + one[:, width:] + two).reshape(layers, rows, width))
        return results

    for half in range(2):
        span = slice(reach + half * rows, reach + (half + 1) * rows)
        down = slice(half * cells, (half + 1) * cells)
        temperature = raw[3, :, span, :].reshape(cells, width)
        strip = raw[4, :, span, :].reshape(cells, width)
        factors = [(raw[i, :, span, :].reshape(cells, width), temperature) for i in range(3)]
        factors.append((strip, spread_temperature(strip)))
        for t, (left, right) in enumerate(factors):
            high, low = halves(left * right)
            prod_h[down, t * width : (t + 1) * width] = high
            prod_l[down, t * width : (t + 1) * width] = low
    flux = filtered(prod_h, prod_l, [(i, 3, i) for i in range(3)])

    for half in range(2):
        span = slice(half * rows, (half + 1) * rows)
        down = slice(half * cells, (half + 1) * cells)
        tiles = [mean[t, 1 : both + 1, span, :].reshape(cells, width) for t in range(5)]
        tiles += [tiles[i] * tiles[3] for i in range(3)]
        tiles.append(tiles[4] * spread_temperature(tiles[4]))
        for t, value in enumerate(tiles):
            high, low = halves(value)
            mid_h[down, t * width : (t + 1) * width] = high
            mid_l[down, t * width : (t + 1) * width] = low
    second = filtered(mid_h, mid_l, [(f, 4, f) for f in range(4)] + [(5 + i, 8, i) for i in range(3)])

    lane = lane_index((layers, rows, width))
    mid = slice(reach, reach + rows)
    centre, along_span, along_wall, along_stream = [], [], [], []
    strip = mean[4, pl.ds(mine + 1, layers), mid, :]
    for f in range(4):
        here_f = mean[f, pl.ds(mine + 1, layers), mid, :]
        centre.append(here_f)
        after = pltpu.roll(here_f, width - 1, 2)
        after = jnp.where(lane == width - 1, pltpu.roll(strip, (width - 1 - f * rim) % width, 2), after)
        before = pltpu.roll(here_f, 1, 2)
        before = jnp.where(lane == 0, pltpu.roll(strip, (width - (64 + f * rim + rim - 1)) % width, 2), before)
        along_span.append((after - before) * 0.5)
        below = mean[f, pl.ds(mine + 1, layers), reach + 1 : reach + rows + 1, :]
        above = mean[f, pl.ds(mine + 1, layers), reach - 1 : reach + rows - 1, :]
        along_wall.append((below - above) * 0.5)
        ahead = mean[f, pl.ds(mine + 2, layers), mid, :]
        behind = mean[f, pl.ds(mine, layers), mid, :]
        along_stream.append((ahead - behind) * 0.5)

    lane = lane_index((rows, width))
    table = jnp.zeros((rows, width), jnp.float32)
    for i in range(3):
        exact = flux[i] - centre[i] * centre[3]
        similar = second[4 + i] - second[i] * second[3]
        total = along_span[i] * along_span[3] + along_wall[i] * along_wall[3]
        clark = clark_coef * (total + along_stream[i] * along_stream[3])
        clark_ref[i] = clark
        similar_ref[i] = similar
        terms = (exact * clark, exact * similar, exact * exact, clark * clark, similar * similar)
        for q, term in enumerate(terms):
            value = jnp.sum(jnp.sum(term, axis=0), axis=1, keepdims=True)
            table = jnp.where(lane == 3 * q + i, value, table)
    sums_ref[...] = table


def finish_kernel(
    plane_cells, sums, clark, similar, clark_model, similar_model, clark_corr, similar_corr
):
    rows, width = sums.shape
    table = sums[...] / plane_cells
    lane = lane_index((rows, width))
    corr = jnp.zeros((rows, width), jnp.float32)
    for i in range(3):
        cross_c, cross_s, power_e, power_c, power_s = (
            table[:, 3 * q + i : 3 * q + i + 1] for q in range(5)
        )
        clark_model[i] = clark[i] / jnp.sqrt(power_c + small_eps)[None]
        similar_model[i] = similar[i] / jnp.sqrt(power_s + small_eps)[None]
        value = cross_c / jnp.sqrt((power_e + small_eps) * (power_c + small_eps))
        corr = jnp.where(lane == i, value, corr)
        value = cross_s / jnp.sqrt((power_e + small_eps) * (power_s + small_eps))
        corr = jnp.where(lane == 8 + i, value, corr)
    square = jnp.concatenate([corr, jnp.zeros((width - rows, width), jnp.float32)], axis=0)
    turned = square.T
    clark_corr[...] = turned[:3, :rows]
    similar_corr[...] = turned[8:11, :rows]


def vmem(count):
    return [pl.BlockSpec(memory_space=pltpu.VMEM)] * count


def shards(fields):
    _, layers, rows, width = fields.shape
    spans = lax.axis_size("span")
    walls = lax.axis_size("wall")
    streams = lax.axis_size("stream")
    cells = 2 * layers * rows

    def swap(value):
        return lax.ppermute(value, "stream", [(0, 1), (1, 0)])

    def pair_a(value):
        return lax.ppermute(value, "wall", [(w, w ^ 1) for w in range(walls)])

    def pair_b(value):
        return lax.ppermute(
            value, "wall", [(w, min(max(((w + 1) ^ 1) - 1, 0), walls - 1)) for w in range(walls)]
        )

    edges = pl.pallas_call(
        edge_kernel,
        out_shape=jax.ShapeDtypeStruct((layers, rows, width), jnp.float32),
        in_specs=vmem(1),
        out_specs=vmem(1)[0],
        compiler_params=pltpu.CompilerParams(vmem_limit_bytes=4 * 1024 * 1024),
        name="edges",
    )(fields)
    before = lax.ppermute(edges, "span", [(p, (p + 1) % spans) for p in range(spans)])
    after = lax.ppermute(edges, "span", [(p, (p - 1) % spans) for p in range(spans)])
    part = swap(fields)
    a_own, b_own = pair_a(fields), pair_b(fields)
    a_part, b_part = pair_a(part), pair_b(part)
    s_own = jnp.where(lane_index(edges.shape) < width // 2, after, before)
    s_part = swap(s_own)
    strips = jnp.stack([s_own, s_part])
    a_strip, b_strip = pair_a(strips), pair_b(strips)

    plane_h, plane_l = plane_constants(2 * layers, rows)
    span_w = span_constants(width)
    block = jax.ShapeDtypeStruct((3, layers, rows, width), jnp.float32)
    clark, similar, sums = pl.pallas_call(
        functools.partial(flux_kernel, walls),
        out_shape=(block, block, jax.ShapeDtypeStruct((rows, width), jnp.float32)),
        in_specs=vmem(13),
        out_specs=tuple(vmem(3)),
        scratch_shapes=[
            pltpu.VMEM((5, 2 * layers, 3 * rows, width), jnp.float32),
            pltpu.VMEM((3 * cells, 5 * width), jnp.bfloat16),
            pltpu.VMEM((3 * cells, 5 * width), jnp.bfloat16),
            pltpu.VMEM((2 * cells, 4 * width), jnp.bfloat16),
            pltpu.VMEM((2 * cells, 4 * width), jnp.bfloat16),
            pltpu.VMEM((5, 2 * layers + 2, 2 * rows, width), jnp.float32),
            pltpu.VMEM((2 * cells, 9 * width), jnp.bfloat16),
            pltpu.VMEM((2 * cells, 9 * width), jnp.bfloat16),
        ],
        compiler_params=pltpu.CompilerParams(vmem_limit_bytes=40 * 1024 * 1024),
        name="flux",
    )(
        fields, part, a_own, b_own, a_part, b_part, s_own, s_part, a_strip, b_strip,
        jnp.asarray(plane_h), jnp.asarray(plane_l), jnp.asarray(span_w),
    )

    group = spans * streams
    step = 1
    while step < group:
        pairs = [(g, g ^ step) for g in range(group)]
        sums = sums + lax.ppermute(sums, ("span", "stream"), pairs)
        step *= 2
    corr = jax.ShapeDtypeStruct((3, rows), jnp.float32)
    return pl.pallas_call(
        functools.partial(finish_kernel, float(layers * width * group)),
        out_shape=(block, block, corr, corr),
        in_specs=vmem(3),
        out_specs=tuple(vmem(4)),
        compiler_params=pltpu.CompilerParams(vmem_limit_bytes=4 * 1024 * 1024),
        name="finish",
    )(sums, clark, similar)


def solution(mesh):
    return jax.shard_map(
        shards,
        mesh=mesh,
        in_specs=(P(None, "stream", "wall", "span"),),
        out_specs=(
            P(None, "stream", "wall", "span"),
            P(None, "stream", "wall", "span"),
            P(None, "wall"),
            P(None, "wall"),
        ),
        check_vma=False,
    )
```

```python
import functools
import math

import jax
import jax.numpy as jnp
import ml_dtypes
import numpy as np
from jax import lax
from jax.experimental import pallas as pl
from jax.experimental.pallas import tpu as pltpu
from jax.sharding import PartitionSpec as P

raw_taps = [math.exp(-((k - 8) ** 2) / 18.0) for k in range(17)]
filter_taps = [value / sum(raw_taps) for value in raw_taps]
clark_coef = 9.0
small_eps = 1e-06

reach = 8
rim = 2 * reach


def split_constant(matrix):
    high = matrix.astype(ml_dtypes.bfloat16)
    low = (matrix - high.astype(np.float64)).astype(ml_dtypes.bfloat16)
    return high, low


def band(outs, ins, offset):
    matrix = np.zeros((outs, ins))
    for o in range(outs):
        for i in range(ins):
            k = i - o - offset + reach
            if 0 <= k <= 2 * reach:
                matrix[o, i] = filter_taps[k]
    return matrix


def plane_constants(layers, rows):
    stream = band(layers, layers, 0)
    wall = band(rows, 2 * rows, reach)
    blocks = [np.kron(stream, wall[:, :rows]), np.kron(stream, wall[:, rows:])]
    return split_constant(np.concatenate(blocks, axis=1))


def span_constants(width):
    everything = band(width + 2 * rim, width + 2 * rim, 0)
    weights = np.zeros((4, 2 * width, 2 * width))
    for f in range(4):
        place = np.full(width + 2 * rim, -1)
        for c in range(rim):
            place[c] = width + 64 + f * rim + c
            place[rim + width + c] = width + f * rim + c
        place[rim : rim + width] = np.arange(width)
        swapped = np.where(place >= width, place - width, place + width)
        weights[f][np.ix_(place, swapped)] = everything.T
    high, low = split_constant(weights)
    low = np.concatenate([low[..., width:], low[..., :width]], axis=2)
    return np.concatenate([high, low], axis=2)


def halves(value):
    high = value.astype(jnp.bfloat16)
    return high, (value - high.astype(jnp.float32)).astype(jnp.bfloat16)


def dot(a, b):
    return lax.dot_general(a, b, (((1,), (0,)), ((), ())), preferred_element_type=jnp.float32)


def lane_index(shape):
    return lax.broadcasted_iota(jnp.int32, shape, len(shape) - 1)


def edge_kernel(own, edges):
    _, layers, rows, width = own.shape
    lane = lane_index((layers * rows, width))
    total = jnp.zeros((layers * rows, width), jnp.float32)
    for f in range(4):
        cells = own[f].reshape(layers * rows, width)
        first = pltpu.roll(cells, f * rim, 1) if f else cells
        total = jnp.where((lane >= f * rim) & (lane < (f + 1) * rim), first, total)
        last = pltpu.roll(cells, (64 + f * rim + rim) % width, 1) if (f + 1) * rim != 64 else cells
        start = 64 + f * rim
        total = jnp.where((lane >= start) & (lane < start + rim), last, total)
    edges[...] = total.reshape(layers, rows, width)


def spread_temperature(strip):
    width = strip.shape[1]
    field = lax.rem(lane_index(strip.shape), 64) // rim
    result = strip
    for f in range(3):
        moved = pltpu.roll(strip, width - (3 - f) * rim, 1)
        result = jnp.where(field == f, moved, result)
    return result


def flux_kernel(
    walls, own, part, a_own, b_own, a_part, b_part, s_own, s_part, a_strip, b_strip,
    plane_h, plane_l, span_w, clark_ref, similar_ref, sums_ref,
    raw, in_h, in_l, prod_h, prod_l, mean, mid_h, mid_l,
):
    _, layers, rows, width = own.shape
    both = 2 * layers
    cells = both * rows
    here = layers * rows
    me_s = lax.axis_index("stream")
    me_w = lax.axis_index("wall")
    odd = lax.rem(me_w, 2)
    mine = pl.multiple_of(me_s * layers, layers)
    other = pl.multiple_of((1 - me_s) * layers, layers)
    row_a = pl.multiple_of((1 - odd) * (2 * rows), rows)
    row_b = pl.multiple_of(odd * (2 * rows), rows)
    at_end = (me_w == 0) | (me_w == walls - 1)
    keep_b = jnp.where(at_end, 0.0, 1.0).astype(jnp.float32)

    for where, blocks in ((mine, (own, a_own, b_own)), (other, (part, a_part, b_part))):
        raw[:4, pl.ds(where, layers), rows : 2 * rows, :] = blocks[0][...]
        raw[:4, pl.ds(where, layers), pl.ds(row_a, rows), :] = blocks[1][...]
        raw[:4, pl.ds(where, layers), pl.ds(row_b, rows), :] = blocks[2][...] * keep_b
    for k, where, block in ((0, mine, s_own), (1, other, s_part)):
        raw[4, pl.ds(where, layers), rows : 2 * rows, :] = block[...]
        raw[4, pl.ds(where, layers), pl.ds(row_a, rows), :] = a_strip[k]
        raw[4, pl.ds(where, layers), pl.ds(row_b, rows), :] = b_strip[k] * keep_b

    for block in range(3):
        for t in range(5):
            value = raw[t, :, block * rows : (block + 1) * rows, :].reshape(cells, width)
            high, low = halves(value)
            in_h[block * cells : (block + 1) * cells, t * width : (t + 1) * width] = high
            in_l[block * cells : (block + 1) * cells, t * width : (t + 1) * width] = low

    for t in range(4):
        mean[t, 0] = jnp.zeros((2 * rows, width), jnp.float32)
        mean[t, both + 1] = jnp.zeros((2 * rows, width), jnp.float32)
    for half in range(2):
        part_h = in_h[half * cells : (half + 2) * cells, :]
        part_l = in_l[half * cells : (half + 2) * cells, :]
        planes = dot(plane_h[...], part_h) + dot(plane_l[...], part_h) + dot(plane_h[...], part_l)
        row = lax.rem(lax.broadcasted_iota(jnp.int32, planes.shape, 0), rows)
        if half == 0:
            inside = (me_w > 0) | (row >= reach)
        else:
            inside = (me_w < walls - 1) | (row < rows - reach)
        planes = jnp.where(inside, planes, 0.0)
        high, low = halves(planes)
        strip = jnp.zeros((cells, width), jnp.float32)
        for f in range(4):
            lhs_h = jnp.concatenate([high[:, f * width : (f + 1) * width], high[:, 4 * width :]], axis=1)
            lhs_l = jnp.concatenate([low[:, f * width : (f + 1) * width], low[:, 4 * width :]], axis=1)
            one = dot(lhs_h, span_w[f])
            two = dot(lhs_l, span_w[f, :, : 2 * width])
            value = one[:, width : 2 * width] + one[:, 2 * width : 3 * width] + two[:, width:]
            strip = strip + one[:, :width] + one[:, 3 * width :] + two[:, :width]
            mean[f, 1 : both + 1, half * rows : (half + 1) * rows, :] = value.reshape(both, rows, width)
        mean[4, 1 : both + 1, half * rows : (half + 1) * rows, :] = strip.reshape(both, rows, width)

    own_rows = pl.ds(pl.multiple_of(me_s * here, here), here)

    def filtered(high, low, tiles):
        lhs_h = plane_h[own_rows, :]
        planes = dot(lhs_h, high[...]) + dot(plane_l[own_rows, :], high[...]) + dot(lhs_h, low[...])
        high, low = halves(planes)
        results = []
        for t, s, f in tiles:
            pick_h = jnp.concatenate([high[:, t * width : (t + 1) * width], high[:, s * width : (s + 1) * width]], axis=1)
            pick_l = jnp.concatenate([low[:, t * width : (t + 1) * width], low[:, s * width : (s + 1) * width]], axis=1)
            one = dot(pick_h, span_w[f, :, width : 3 * width])
            two = dot(pick_l, span_w[f, :, width : 2 * width])
            results.append((one[:, :width] + one[:, width:] + two).reshape(layers, rows, width))
        return results

    for half in range(2):
        span = slice(reach + half * rows, reach + (half + 1) * rows)
        down = slice(half * cells, (half + 1) * cells)
        temperature = raw[3, :, span, :].reshape(cells, width)
        strip = raw[4, :, span, :].reshape(cells, width)
        factors = [(raw[i, :, span, :].reshape(cells, width), temperature) for i in range(3)]
        factors.append((strip, spread_temperature(strip)))
        for t, (left, right) in enumerate(factors):
            high, low = halves(left * right)
            prod_h[down, t * width : (t + 1) * width] = high
            prod_l[down, t * width : (t + 1) * width] = low
    flux = filtered(prod_h, prod_l, [(i, 3, i) for i in range(3)])

    for half in range(2):
        span = slice(half * rows, (half + 1) * rows)
        down = slice(half * cells, (half + 1) * cells)
        tiles = [mean[t, 1 : both + 1, span, :].reshape(cells, width) for t in range(5)]
        tiles += [tiles[i] * tiles[3] for i in range(3)]
        tiles.append(tiles[4] * spread_temperature(tiles[4]))
        for t, value in enumerate(tiles):
            high, low = halves(value)
            mid_h[down, t * width : (t + 1) * width] = high
            mid_l[down, t * width : (t + 1) * width] = low
    second = filtered(mid_h, mid_l, [(f, 4, f) for f in range(4)] + [(5 + i, 8, i) for i in range(3)])

    lane = lane_index((layers, rows, width))
    mid = slice(reach, reach + rows)
    centre, along_span, along_wall, along_stream = [], [], [], []
    strip = mean[4, pl.ds(mine + 1, layers), mid, :]
    for f in range(4):
        here_f = mean[f, pl.ds(mine + 1, layers), mid, :]
        centre.append(here_f)
        after = pltpu.roll(here_f, width - 1, 2)
        after = jnp.where(lane == width - 1, pltpu.roll(strip, (width - 1 - f * rim) % width, 2), after)
        before = pltpu.roll(here_f, 1, 2)
        before = jnp.where(lane == 0, pltpu.roll(strip, (width - (64 + f * rim + rim - 1)) % width, 2), before)
        along_span.append((after - before) * 0.5)
        below = mean[f, pl.ds(mine + 1, layers), reach + 1 : reach + rows + 1, :]
        above = mean[f, pl.ds(mine + 1, layers), reach - 1 : reach + rows - 1, :]
        along_wall.append((below - above) * 0.5)
        ahead = mean[f, pl.ds(mine + 2, layers), mid, :]
        behind = mean[f, pl.ds(mine, layers), mid, :]
        along_stream.append((ahead - behind) * 0.5)

    lane = lane_index((rows, width))
    table = jnp.zeros((rows, width), jnp.float32)
    for i in range(3):
        exact = flux[i] - centre[i] * centre[3]
        similar = second[4 + i] - second[i] * second[3]
        total = along_span[i] * along_span[3] + along_wall[i] * along_wall[3]
        clark = clark_coef * (total + along_stream[i] * along_stream[3])
        clark_ref[i] = clark
        similar_ref[i] = similar
        terms = (exact * clark, exact * similar, exact * exact, clark * clark, similar * similar)
        for q, term in enumerate(terms):
            value = jnp.sum(jnp.sum(term, axis=0), axis=1, keepdims=True)
            table = jnp.where(lane == 3 * q + i, value, table)
    sums_ref[...] = table


def finish_kernel(
    plane_cells, sums, clark, similar, clark_model, similar_model, clark_corr, similar_corr
):
    _, rows, width = sums.shape
    table = jnp.sum(sums[...], axis=0) / plane_cells
    lane = lane_index((rows, width))
    corr = jnp.zeros((rows, width), jnp.float32)
    for i in range(3):
        cross_c, cross_s, power_e, power_c, power_s = (
            table[:, 3 * q + i : 3 * q + i + 1] for q in range(5)
        )
        clark_model[i] = clark[i] / jnp.sqrt(power_c + small_eps)[None]
        similar_model[i] = similar[i] / jnp.sqrt(power_s + small_eps)[None]
        value = cross_c / jnp.sqrt((power_e + small_eps) * (power_c + small_eps))
        corr = jnp.where(lane == i, value, corr)
        value = cross_s / jnp.sqrt((power_e + small_eps) * (power_s + small_eps))
        corr = jnp.where(lane == 8 + i, value, corr)
    square = jnp.concatenate([corr, jnp.zeros((width - rows, width), jnp.float32)], axis=0)
    turned = square.T
    clark_corr[...] = turned[:3, :rows]
    similar_corr[...] = turned[8:11, :rows]


def vmem(count):
    return [pl.BlockSpec(memory_space=pltpu.VMEM)] * count


def shards(fields):
    _, layers, rows, width = fields.shape
    spans = lax.axis_size("span")
    walls = lax.axis_size("wall")
    streams = lax.axis_size("stream")
    cells = 2 * layers * rows

    def swap(value):
        return lax.ppermute(value, "stream", [(0, 1), (1, 0)])

    def pair_a(value):
        return lax.ppermute(value, "wall", [(w, w ^ 1) for w in range(walls)])

    def pair_b(value):
        return lax.ppermute(
            value, "wall", [(w, min(max(((w + 1) ^ 1) - 1, 0), walls - 1)) for w in range(walls)]
        )

    edges = pl.pallas_call(
        edge_kernel,
        out_shape=jax.ShapeDtypeStruct((layers, rows, width), jnp.float32),
        in_specs=vmem(1),
        out_specs=vmem(1)[0],
        compiler_params=pltpu.CompilerParams(vmem_limit_bytes=4 * 1024 * 1024),
        name="edges",
    )(fields)
    before = lax.ppermute(edges, "span", [(p, (p + 1) % spans) for p in range(spans)])
    after = lax.ppermute(edges, "span", [(p, (p - 1) % spans) for p in range(spans)])
    part = swap(fields)
    a_own, b_own = pair_a(fields), pair_b(fields)
    a_part, b_part = pair_a(part), pair_b(part)
    s_own = jnp.where(lane_index(edges.shape) < width // 2, after, before)
    s_part = swap(s_own)
    strips = jnp.stack([s_own, s_part])
    a_strip, b_strip = pair_a(strips), pair_b(strips)

    plane_h, plane_l = plane_constants(2 * layers, rows)
    span_w = span_constants(width)
    block = jax.ShapeDtypeStruct((3, layers, rows, width), jnp.float32)
    clark, similar, sums = pl.pallas_call(
        functools.partial(flux_kernel, walls),
        out_shape=(block, block, jax.ShapeDtypeStruct((rows, width), jnp.float32)),
        in_specs=vmem(13),
        out_specs=tuple(vmem(3)),
        scratch_shapes=[
            pltpu.VMEM((5, 2 * layers, 3 * rows, width), jnp.float32),
            pltpu.VMEM((3 * cells, 5 * width), jnp.bfloat16),
            pltpu.VMEM((3 * cells, 5 * width), jnp.bfloat16),
            pltpu.VMEM((2 * cells, 4 * width), jnp.bfloat16),
            pltpu.VMEM((2 * cells, 4 * width), jnp.bfloat16),
            pltpu.VMEM((5, 2 * layers + 2, 2 * rows, width), jnp.float32),
            pltpu.VMEM((2 * cells, 9 * width), jnp.bfloat16),
            pltpu.VMEM((2 * cells, 9 * width), jnp.bfloat16),
        ],
        compiler_params=pltpu.CompilerParams(vmem_limit_bytes=40 * 1024 * 1024),
        name="flux",
    )(
        fields, part, a_own, b_own, a_part, b_part, s_own, s_part, a_strip, b_strip,
        jnp.asarray(plane_h), jnp.asarray(plane_l), jnp.asarray(span_w),
    )

    group = spans * streams
    tables = jnp.broadcast_to(sums[None], (group, rows, width))
    tables = lax.all_to_all(tables, ("span", "stream"), 0, 0)
    corr = jax.ShapeDtypeStruct((3, rows), jnp.float32)
    return pl.pallas_call(
        functools.partial(finish_kernel, float(layers * width * group)),
        out_shape=(block, block, corr, corr),
        in_specs=vmem(3),
        out_specs=tuple(vmem(4)),
        compiler_params=pltpu.CompilerParams(vmem_limit_bytes=4 * 1024 * 1024),
        name="finish",
    )(tables, clark, similar)


def solution(mesh):
    return jax.shard_map(
        shards,
        mesh=mesh,
        in_specs=(P(None, "stream", "wall", "span"),),
        out_specs=(
            P(None, "stream", "wall", "span"),
            P(None, "stream", "wall", "span"),
            P(None, "wall"),
            P(None, "wall"),
        ),
        check_vma=False,
    )
```

```python
import functools
import math

import jax
import jax.numpy as jnp
import ml_dtypes
import numpy as np
from jax import lax
from jax.experimental import pallas as pl
from jax.experimental.pallas import tpu as pltpu
from jax.sharding import PartitionSpec as P

raw_taps = [math.exp(-((k - 8) ** 2) / 18.0) for k in range(17)]
filter_taps = [value / sum(raw_taps) for value in raw_taps]
clark_coef = 9.0
small_eps = 1e-06

reach = 8
rim = 2 * reach


def split_constant(matrix):
    high = matrix.astype(ml_dtypes.bfloat16)
    low = (matrix - high.astype(np.float64)).astype(ml_dtypes.bfloat16)
    return high, low


def band(outs, ins, offset):
    matrix = np.zeros((outs, ins))
    for o in range(outs):
        for i in range(ins):
            k = i - o - offset + reach
            if 0 <= k <= 2 * reach:
                matrix[o, i] = filter_taps[k]
    return matrix


def plane_constants(layers, rows):
    stream = band(layers, layers, 0)
    wall = band(rows, 2 * rows, reach)
    blocks = [np.kron(stream, wall[:, :rows]), np.kron(stream, wall[:, rows:])]
    return split_constant(np.concatenate(blocks, axis=1))


def span_constants(width):
    everything = band(width + 2 * rim, width + 2 * rim, 0)
    weights = np.zeros((4, 2 * width, 2 * width))
    for f in range(4):
        place = np.full(width + 2 * rim, -1)
        for c in range(rim):
            place[c] = width + 64 + f * rim + c
            place[rim + width + c] = width + f * rim + c
        place[rim : rim + width] = np.arange(width)
        swapped = np.where(place >= width, place - width, place + width)
        weights[f][np.ix_(place, swapped)] = everything.T
    high, low = split_constant(weights)
    low = np.concatenate([low[..., width:], low[..., :width]], axis=2)
    return np.concatenate([high, low], axis=2)


def halves(value):
    high = value.astype(jnp.bfloat16)
    return high, (value - high.astype(jnp.float32)).astype(jnp.bfloat16)


def dot(a, b):
    return lax.dot_general(a, b, (((1,), (0,)), ((), ())), preferred_element_type=jnp.float32)


def lane_index(shape):
    return lax.broadcasted_iota(jnp.int32, shape, len(shape) - 1)


def edge_kernel(own, edges):
    _, layers, rows, width = own.shape
    lane = lane_index((layers * rows, width))
    total = jnp.zeros((layers * rows, width), jnp.float32)
    for f in range(4):
        cells = own[f].reshape(layers * rows, width)
        first = pltpu.roll(cells, f * rim, 1) if f else cells
        total = jnp.where((lane >= f * rim) & (lane < (f + 1) * rim), first, total)
        last = pltpu.roll(cells, (64 + f * rim + rim) % width, 1) if (f + 1) * rim != 64 else cells
        start = 64 + f * rim
        total = jnp.where((lane >= start) & (lane < start + rim), last, total)
    edges[...] = total.reshape(layers, rows, width)


def spread_temperature(strip):
    width = strip.shape[1]
    field = lax.rem(lane_index(strip.shape), 64) // rim
    result = strip
    for f in range(3):
        moved = pltpu.roll(strip, width - (3 - f) * rim, 1)
        result = jnp.where(field == f, moved, result)
    return result


def flux_kernel(
    walls, blocks, strips, plane_h, plane_l, span_w, clark_ref, similar_ref, sums_ref,
    raw, in_h, in_l, prod_h, prod_l, mean, mid_h, mid_l,
):
    _, _, layers, rows, width = blocks.shape
    both = 2 * layers
    cells = both * rows
    here = layers * rows
    me_s = lax.axis_index("stream")
    me_w = lax.axis_index("wall")
    mine = pl.multiple_of(me_s * layers, layers)

    for block in range(3):
        wall = me_w + block - 1
        keep = jnp.where((wall >= 0) & (wall < walls), 1.0, 0.0).astype(jnp.float32)
        wall = jnp.clip(wall, 0, walls - 1)
        for k in range(2):
            down = slice(block * rows, (block + 1) * rows)
            along = slice(k * layers, (k + 1) * layers)
            raw[:4, along, down, :] = blocks[2 * wall + k] * keep
            raw[4, along, down, :] = strips[2 * wall + k] * keep

    for block in range(3):
        for t in range(5):
            value = raw[t, :, block * rows : (block + 1) * rows, :].reshape(cells, width)
            high, low = halves(value)
            in_h[block * cells : (block + 1) * cells, t * width : (t + 1) * width] = high
            in_l[block * cells : (block + 1) * cells, t * width : (t + 1) * width] = low

    for t in range(4):
        mean[t, 0] = jnp.zeros((2 * rows, width), jnp.float32)
        mean[t, both + 1] = jnp.zeros((2 * rows, width), jnp.float32)
    for half in range(2):
        part_h = in_h[half * cells : (half + 2) * cells, :]
        part_l = in_l[half * cells : (half + 2) * cells, :]
        planes = dot(plane_h[...], part_h) + dot(plane_l[...], part_h) + dot(plane_h[...], part_l)
        row = lax.rem(lax.broadcasted_iota(jnp.int32, planes.shape, 0), rows)
        if half == 0:
            inside = (me_w > 0) | (row >= reach)
        else:
            inside = (me_w < walls - 1) | (row < rows - reach)
        planes = jnp.where(inside, planes, 0.0)
        high, low = halves(planes)
        strip = jnp.zeros((cells, width), jnp.float32)
        for f in range(4):
            lhs_h = jnp.concatenate([high[:, f * width : (f + 1) * width], high[:, 4 * width :]], axis=1)
            lhs_l = jnp.concatenate([low[:, f * width : (f + 1) * width], low[:, 4 * width :]], axis=1)
            one = dot(lhs_h, span_w[f])
            two = dot(lhs_l, span_w[f, :, : 2 * width])
            value = one[:, width : 2 * width] + one[:, 2 * width : 3 * width] + two[:, width:]
            strip = strip + one[:, :width] + one[:, 3 * width :] + two[:, :width]
            mean[f, 1 : both + 1, half * rows : (half + 1) * rows, :] = value.reshape(both, rows, width)
        mean[4, 1 : both + 1, half * rows : (half + 1) * rows, :] = strip.reshape(both, rows, width)

    own_rows = pl.ds(pl.multiple_of(me_s * here, here), here)

    def filtered(high, low, tiles):
        lhs_h = plane_h[own_rows, :]
        planes = dot(lhs_h, high[...]) + dot(plane_l[own_rows, :], high[...]) + dot(lhs_h, low[...])
        high, low = halves(planes)
        results = []
        for t, s, f in tiles:
            pick_h = jnp.concatenate([high[:, t * width : (t + 1) * width], high[:, s * width : (s + 1) * width]], axis=1)
            pick_l = jnp.concatenate([low[:, t * width : (t + 1) * width], low[:, s * width : (s + 1) * width]], axis=1)
            one = dot(pick_h, span_w[f, :, width : 3 * width])
            two = dot(pick_l, span_w[f, :, width : 2 * width])
            results.append((one[:, :width] + one[:, width:] + two).reshape(layers, rows, width))
        return results

    for half in range(2):
        span = slice(reach + half * rows, reach + (half + 1) * rows)
        down = slice(half * cells, (half + 1) * cells)
        temperature = raw[3, :, span, :].reshape(cells, width)
        strip = raw[4, :, span, :].reshape(cells, width)
        factors = [(raw[i, :, span, :].reshape(cells, width), temperature) for i in range(3)]
        factors.append((strip, spread_temperature(strip)))
        for t, (left, right) in enumerate(factors):
            high, low = halves(left * right)
            prod_h[down, t * width : (t + 1) * width] = high
            prod_l[down, t * width : (t + 1) * width] = low
    flux = filtered(prod_h, prod_l, [(i, 3, i) for i in range(3)])

    for half in range(2):
        span = slice(half * rows, (half + 1) * rows)
        down = slice(half * cells, (half + 1) * cells)
        tiles = [mean[t, 1 : both + 1, span, :].reshape(cells, width) for t in range(5)]
        tiles += [tiles[i] * tiles[3] for i in range(3)]
        tiles.append(tiles[4] * spread_temperature(tiles[4]))
        for t, value in enumerate(tiles):
            high, low = halves(value)
            mid_h[down, t * width : (t + 1) * width] = high
            mid_l[down, t * width : (t + 1) * width] = low
    second = filtered(mid_h, mid_l, [(f, 4, f) for f in range(4)] + [(5 + i, 8, i) for i in range(3)])

    lane = lane_index((layers, rows, width))
    mid = slice(reach, reach + rows)
    centre, along_span, along_wall, along_stream = [], [], [], []
    strip = mean[4, pl.ds(mine + 1, layers), mid, :]
    for f in range(4):
        here_f = mean[f, pl.ds(mine + 1, layers), mid, :]
        centre.append(here_f)
        after = pltpu.roll(here_f, width - 1, 2)
        after = jnp.where(lane == width - 1, pltpu.roll(strip, (width - 1 - f * rim) % width, 2), after)
        before = pltpu.roll(here_f, 1, 2)
        before = jnp.where(lane == 0, pltpu.roll(strip, (width - (64 + f * rim + rim - 1)) % width, 2), before)
        along_span.append((after - before) * 0.5)
        below = mean[f, pl.ds(mine + 1, layers), reach + 1 : reach + rows + 1, :]
        above = mean[f, pl.ds(mine + 1, layers), reach - 1 : reach + rows - 1, :]
        along_wall.append((below - above) * 0.5)
        ahead = mean[f, pl.ds(mine + 2, layers), mid, :]
        behind = mean[f, pl.ds(mine, layers), mid, :]
        along_stream.append((ahead - behind) * 0.5)

    lane = lane_index((rows, width))
    table = jnp.zeros((rows, width), jnp.float32)
    for i in range(3):
        exact = flux[i] - centre[i] * centre[3]
        similar = second[4 + i] - second[i] * second[3]
        total = along_span[i] * along_span[3] + along_wall[i] * along_wall[3]
        clark = clark_coef * (total + along_stream[i] * along_stream[3])
        clark_ref[i] = clark
        similar_ref[i] = similar
        terms = (exact * clark, exact * similar, exact * exact, clark * clark, similar * similar)
        for q, term in enumerate(terms):
            value = jnp.sum(jnp.sum(term, axis=0), axis=1, keepdims=True)
            table = jnp.where(lane == 3 * q + i, value, table)
    sums_ref[...] = table


def finish_kernel(
    plane_cells, sums, clark, similar, clark_model, similar_model, clark_corr, similar_corr
):
    _, rows, width = sums.shape
    table = jnp.sum(sums[...], axis=0) / plane_cells
    lane = lane_index((rows, width))
    corr = jnp.zeros((rows, width), jnp.float32)
    for i in range(3):
        cross_c, cross_s, power_e, power_c, power_s = (
            table[:, 3 * q + i : 3 * q + i + 1] for q in range(5)
        )
        clark_model[i] = clark[i] / jnp.sqrt(power_c + small_eps)[None]
        similar_model[i] = similar[i] / jnp.sqrt(power_s + small_eps)[None]
        value = cross_c / jnp.sqrt((power_e + small_eps) * (power_c + small_eps))
        corr = jnp.where(lane == i, value, corr)
        value = cross_s / jnp.sqrt((power_e + small_eps) * (power_s + small_eps))
        corr = jnp.where(lane == 8 + i, value, corr)
    square = jnp.concatenate([corr, jnp.zeros((width - rows, width), jnp.float32)], axis=0)
    turned = square.T
    clark_corr[...] = turned[:3, :rows]
    similar_corr[...] = turned[8:11, :rows]


def vmem(count):
    return [pl.BlockSpec(memory_space=pltpu.VMEM)] * count


def shards(fields):
    _, layers, rows, width = fields.shape
    spans = lax.axis_size("span")
    walls = lax.axis_size("wall")
    streams = lax.axis_size("stream")
    cells = 2 * layers * rows

    edges = pl.pallas_call(
        edge_kernel,
        out_shape=jax.ShapeDtypeStruct((layers, rows, width), jnp.float32),
        in_specs=vmem(1),
        out_specs=vmem(1)[0],
        compiler_params=pltpu.CompilerParams(vmem_limit_bytes=4 * 1024 * 1024),
        name="edges",
    )(fields)
    before = lax.ppermute(edges, "span", [(p, (p + 1) % spans) for p in range(spans)])
    after = lax.ppermute(edges, "span", [(p, (p - 1) % spans) for p in range(spans)])
    blocks = lax.all_gather(fields, ("wall", "stream"))
    s_own = jnp.where(lane_index(edges.shape) < width // 2, after, before)
    strips = lax.all_gather(s_own, ("wall", "stream"))

    plane_h, plane_l = plane_constants(2 * layers, rows)
    span_w = span_constants(width)
    block = jax.ShapeDtypeStruct((3, layers, rows, width), jnp.float32)
    clark, similar, sums = pl.pallas_call(
        functools.partial(flux_kernel, walls),
        out_shape=(block, block, jax.ShapeDtypeStruct((rows, width), jnp.float32)),
        in_specs=vmem(5),
        out_specs=tuple(vmem(3)),
        scratch_shapes=[
            pltpu.VMEM((5, 2 * layers, 3 * rows, width), jnp.float32),
            pltpu.VMEM((3 * cells, 5 * width), jnp.bfloat16),
            pltpu.VMEM((3 * cells, 5 * width), jnp.bfloat16),
            pltpu.VMEM((2 * cells, 4 * width), jnp.bfloat16),
            pltpu.VMEM((2 * cells, 4 * width), jnp.bfloat16),
            pltpu.VMEM((5, 2 * layers + 2, 2 * rows, width), jnp.float32),
            pltpu.VMEM((2 * cells, 9 * width), jnp.bfloat16),
            pltpu.VMEM((2 * cells, 9 * width), jnp.bfloat16),
        ],
        compiler_params=pltpu.CompilerParams(vmem_limit_bytes=40 * 1024 * 1024),
        name="flux",
    )(
        blocks, strips,
        jnp.asarray(plane_h), jnp.asarray(plane_l), jnp.asarray(span_w),
    )

    group = spans * streams
    tables = jnp.broadcast_to(sums[None], (group, rows, width))
    tables = lax.all_to_all(tables, ("span", "stream"), 0, 0)
    corr = jax.ShapeDtypeStruct((3, rows), jnp.float32)
    return pl.pallas_call(
        functools.partial(finish_kernel, float(layers * width * group)),
        out_shape=(block, block, corr, corr),
        in_specs=vmem(3),
        out_specs=tuple(vmem(4)),
        compiler_params=pltpu.CompilerParams(vmem_limit_bytes=4 * 1024 * 1024),
        name="finish",
    )(tables, clark, similar)


def solution(mesh):
    return jax.shard_map(
        shards,
        mesh=mesh,
        in_specs=(P(None, "stream", "wall", "span"),),
        out_specs=(
            P(None, "stream", "wall", "span"),
            P(None, "stream", "wall", "span"),
            P(None, "wall"),
            P(None, "wall"),
        ),
        check_vma=False,
    )
```

```python
import functools
import math

import jax
import jax.numpy as jnp
import ml_dtypes
import numpy as np
from jax import lax
from jax.experimental import pallas as pl
from jax.experimental.pallas import tpu as pltpu
from jax.sharding import PartitionSpec as P

raw_taps = [math.exp(-((k - 8) ** 2) / 18.0) for k in range(17)]
filter_taps = [value / sum(raw_taps) for value in raw_taps]
clark_coef = 9.0
small_eps = 1e-06

reach = 8
rim = 2 * reach


def split_constant(matrix):
    high = matrix.astype(ml_dtypes.bfloat16)
    low = (matrix - high.astype(np.float64)).astype(ml_dtypes.bfloat16)
    return high, low


def band(outs, ins, offset):
    matrix = np.zeros((outs, ins))
    for o in range(outs):
        for i in range(ins):
            k = i - o - offset + reach
            if 0 <= k <= 2 * reach:
                matrix[o, i] = filter_taps[k]
    return matrix


def plane_constants(layers, rows):
    stream = band(layers, layers, 0)
    wall = band(rows, 2 * rows, reach)
    blocks = [np.kron(stream, wall[:, :rows]), np.kron(stream, wall[:, rows:])]
    return split_constant(np.concatenate(blocks, axis=1))


def span_constants(width):
    circle = np.zeros((width, width))
    for o in range(width):
        for k in range(2 * reach + 1):
            circle[(o + k - reach) % width, o] = filter_taps[k]
    high, low = split_constant(circle)
    return np.block([[high, low], [high, np.zeros_like(low)]])


def halves(value):
    high = value.astype(jnp.bfloat16)
    return high, (value - high.astype(jnp.float32)).astype(jnp.bfloat16)


def dot(a, b):
    return lax.dot_general(a, b, (((1,), (0,)), ((), ())), preferred_element_type=jnp.float32)


def lane_index(shape):
    return lax.broadcasted_iota(jnp.int32, shape, len(shape) - 1)


def edge_kernel(own, to_partner_side, to_own_side):
    _, layers, rows, width = own.shape
    half = layers // 2
    lane = lane_index((half, rows, width))
    me_s = lax.axis_index("stream")
    sides = []
    for start in (0, width - rim):
        total = jnp.zeros((half, rows, width), jnp.float32)
        for k in range(2):
            for f in range(4):
                place = k * 64 + f * rim
                cells = pltpu.roll(own[f, k * half : (k + 1) * half], (place - start) % width, 2)
                total = jnp.where(lane // rim == place // rim, cells, total)
        sides.append(total)
    to_partner_side[...] = jnp.where(me_s == 0, sides[0], sides[1])
    to_own_side[...] = jnp.where(me_s == 0, sides[1], sides[0])


def merge_kernel(own, part, own_strip, part_strip, merged):
    _, layers, rows, width = own.shape
    half = layers // 2
    me_s = lax.axis_index("stream")
    start = jnp.where(me_s == 0, width - rim, 0)
    lane = lane_index((half, rows, width))
    beyond = lane // rim == start // rim
    for where, block, strip in ((me_s, own, own_strip), (1 - me_s, part, part_strip)):
        packed = strip[...]
        for k in range(2):
            for f in range(4):
                place = k * 64 + f * rim
                cells = pltpu.roll(packed, lax.rem(start - place + 2 * width, width), 2)
                layer = where * layers + k * half
                merged[f, pl.ds(layer, half)] = jnp.where(beyond, cells, block[f, k * half : (k + 1) * half])


def flux_kernel(
    walls, mid, a_block, b_block, plane_h, plane_l, span_w, keep_ref, send_ref, sums_ref,
    raw, in_h, in_l, prod_h, prod_l, mean, mid_h, mid_l, clark_all, similar_all,
):
    _, both, rows, width = mid.shape
    layers = both // 2
    cells = both * rows
    me_s = lax.axis_index("stream")
    me_w = lax.axis_index("wall")
    odd = lax.rem(me_w, 2)
    row_a = pl.multiple_of((1 - odd) * (2 * rows), rows)
    row_b = pl.multiple_of(odd * (2 * rows), rows)
    at_end = (me_w == 0) | (me_w == walls - 1)
    keep_b = jnp.where(at_end, 0.0, 1.0).astype(jnp.float32)

    raw[:, :, rows : 2 * rows, :] = mid[...]
    raw[:, :, pl.ds(row_a, rows), :] = a_block[...]
    raw[:, :, pl.ds(row_b, rows), :] = b_block[...] * keep_b

    def column(t):
        return slice(t * width, (t + 1) * width)

    for block in range(3):
        down = slice(block * cells, (block + 1) * cells)
        for t in range(4):
            value = raw[t, :, block * rows : (block + 1) * rows, :].reshape(cells, width)
            in_h[down, column(t)], in_l[down, column(t)] = halves(value)

    def planes_of(high, low):
        return dot(plane_h[...], high) + dot(plane_l[...], high) + dot(plane_h[...], low)

    def along_span_of(planes):
        high, low = halves(planes)
        tiles = planes.shape[1] // width
        parts = [jnp.concatenate([high[:, column(t)], low[:, column(t)]], axis=1) for t in range(tiles)]
        result = dot(jnp.concatenate(parts, axis=0), span_w[...])
        result = result[:, :width] + result[:, width:]
        return [result[t * cells : (t + 1) * cells].reshape(both, rows, width) for t in range(tiles)]

    for t in range(4):
        mean[t, 0] = jnp.zeros((2 * rows, width), jnp.float32)
        mean[t, both + 1] = jnp.zeros((2 * rows, width), jnp.float32)
    for half in range(2):
        span = slice(half * cells, (half + 2) * cells)
        planes = planes_of(in_h[span, :], in_l[span, :])
        row = lax.rem(lax.broadcasted_iota(jnp.int32, planes.shape, 0), rows)
        if half == 0:
            inside = (me_w > 0) | (row >= reach)
        else:
            inside = (me_w < walls - 1) | (row < rows - reach)
        planes = jnp.where(inside, planes, 0.0)
        for t, value in enumerate(along_span_of(planes)):
            mean[t, 1 : both + 1, half * rows : (half + 1) * rows, :] = value

    for half in range(2):
        span = slice(reach + half * rows, reach + (half + 1) * rows)
        down = slice(half * cells, (half + 1) * cells)
        temperature = raw[3, :, span, :].reshape(cells, width)
        for t in range(3):
            value = raw[t, :, span, :].reshape(cells, width) * temperature
            prod_h[down, column(t)], prod_l[down, column(t)] = halves(value)
    flux = along_span_of(planes_of(prod_h[...], prod_l[...]))

    for half in range(2):
        span = slice(half * rows, (half + 1) * rows)
        down = slice(half * cells, (half + 1) * cells)
        tiles = [mean[t, 1 : both + 1, span, :].reshape(cells, width) for t in range(4)]
        tiles += [tiles[i] * tiles[3] for i in range(3)]
        for t, value in enumerate(tiles):
            mid_h[down, column(t)], mid_l[down, column(t)] = halves(value)
    second = along_span_of(planes_of(mid_h[...], mid_l[...]))

    mid_rows = slice(reach, reach + rows)
    centre, along_span, along_wall, along_stream = [], [], [], []
    for f in range(4):
        here = mean[f, 1 : both + 1, mid_rows, :]
        centre.append(here)
        along_span.append((pltpu.roll(here, width - 1, 2) - pltpu.roll(here, 1, 2)) * 0.5)
        below = mean[f, 1 : both + 1, reach + 1 : reach + rows + 1, :]
        above = mean[f, 1 : both + 1, reach - 1 : reach + rows - 1, :]
        along_wall.append((below - above) * 0.5)
        along_stream.append((mean[f, 2 : both + 2, mid_rows, :] - mean[f, :both, mid_rows, :]) * 0.5)

    lane = lane_index((rows, width))
    useful = lane // (width // 2) == me_s
    table = jnp.zeros((rows, width), jnp.float32)
    for i in range(3):
        exact = flux[i] - centre[i] * centre[3]
        similar = second[4 + i] - second[i] * second[3]
        total = along_span[i] * along_span[3] + along_wall[i] * along_wall[3]
        clark = clark_coef * (total + along_stream[i] * along_stream[3])
        clark_all[i] = clark
        similar_all[i] = similar
        terms = (exact * clark, exact * similar, exact * exact, clark * clark, similar * similar)
        for q, term in enumerate(terms):
            value = jnp.where(useful, jnp.sum(term, axis=0), 0.0)
            table = jnp.where(lane == 3 * q + i, jnp.sum(value, axis=1, keepdims=True), table)
    sums_ref[...] = table

    first = lane_index((layers, rows, width)) < width // 2
    for i in range(3):
        keep_ref[i] = clark_all[i, pl.ds(me_s * layers, layers)]
        keep_ref[3 + i] = similar_all[i, pl.ds(me_s * layers, layers)]
        clark = clark_all[i, pl.ds((1 - me_s) * layers, layers)]
        similar = similar_all[i, pl.ds((1 - me_s) * layers, layers)]
        turn = me_s == 0
        clark = jnp.where(turn, clark, pltpu.roll(clark, width // 2, 2))
        similar = jnp.where(turn, pltpu.roll(similar, width // 2, 2), similar)
        send_ref[i] = jnp.where(first, clark, similar)


def finish_kernel(plane_cells, spans, *refs):
    tables = refs[:spans]
    keep, come, clark_model, similar_model, clark_corr, similar_corr, ordered = refs[spans:]
    _, layers, rows, width = keep.shape
    me_s = lax.axis_index("stream")
    me_p = lax.axis_index("span")
    for step, one in enumerate(tables):
        ordered[lax.rem(me_p - step + spans, spans)] = one[...]
    table = jnp.sum(ordered[...], axis=0) / plane_cells
    lane = lane_index((rows, width))
    useful = lane // (width // 2) == me_s
    corr = jnp.zeros((rows, width), jnp.float32)
    for i in range(3):
        cross_c, cross_s, power_e, power_c, power_s = (
            table[:, 3 * q + i : 3 * q + i + 1] for q in range(5)
        )
        packed = come[i]
        turned = pltpu.roll(packed, width // 2, 2)
        clark = jnp.where(useful[None], keep[i], jnp.where(me_s == 0, turned, packed))
        similar = jnp.where(useful[None], keep[3 + i], jnp.where(me_s == 0, packed, turned))
        clark_model[i] = clark / jnp.sqrt(power_c + small_eps)[None]
        similar_model[i] = similar / jnp.sqrt(power_s + small_eps)[None]
        value = cross_c / jnp.sqrt((power_e + small_eps) * (power_c + small_eps))
        corr = jnp.where(lane == i, value, corr)
        value = cross_s / jnp.sqrt((power_e + small_eps) * (power_s + small_eps))
        corr = jnp.where(lane == 8 + i, value, corr)
    square = jnp.concatenate([corr, jnp.zeros((width - rows, width), jnp.float32)], axis=0)
    turned = square.T
    clark_corr[...] = turned[:3, :rows]
    similar_corr[...] = turned[8:11, :rows]


def call(kernel, name, ins, outs, scratch=(), mib=4):
    return pl.pallas_call(
        kernel,
        out_shape=tuple(jax.ShapeDtypeStruct(shape, jnp.float32) for shape in outs),
        in_specs=[pl.BlockSpec(memory_space=pltpu.VMEM)] * len(ins),
        out_specs=tuple(pl.BlockSpec(memory_space=pltpu.VMEM) for _ in outs),
        scratch_shapes=[pltpu.VMEM(shape, dtype) for shape, dtype in scratch],
        compiler_params=pltpu.CompilerParams(vmem_limit_bytes=mib * 1024 * 1024),
        name=name,
    )(*ins)


def shards(fields):
    _, layers, rows, width = fields.shape
    spans = lax.axis_size("span")
    walls = lax.axis_size("wall")
    streams = lax.axis_size("stream")
    both = streams * layers
    cells = both * rows

    def swap(value):
        return lax.ppermute(value, "stream", [(0, 1), (1, 0)])

    def pair_a(value):
        return lax.ppermute(value, "wall", [(w, w ^ 1) for w in range(walls)])

    def pair_b(value):
        return lax.ppermute(
            value, "wall", [(w, min(max(((w + 1) ^ 1) - 1, 0), walls - 1)) for w in range(walls)]
        )

    def place(p, s):
        return (p % spans) * streams + s

    to_other, to_same = [], []
    for p in range(spans):
        to_other += [(place(p, 0), place(p - 1, 1)), (place(p, 1), place(p + 1, 0))]
        to_same += [(place(p, 1), place(p - 1, 1)), (place(p, 0), place(p + 1, 0))]

    strip = (layers // 2, rows, width)
    first, second = call(edge_kernel, "edges", (fields,), (strip, strip))
    part = swap(fields)
    part_strip = lax.ppermute(first, ("span", "stream"), to_other)
    own_strip = lax.ppermute(second, ("span", "stream"), to_same)
    (mid,) = call(merge_kernel, "merge", (fields, part, own_strip, part_strip), ((4, both, rows, width),))
    b_block, a_block = pair_b(mid), pair_a(mid)

    plane_h, plane_l = plane_constants(both, rows)
    single, brief = jnp.float32, jnp.bfloat16
    keep, send, sums = call(
        functools.partial(flux_kernel, walls),
        "flux",
        (mid, a_block, b_block, jnp.asarray(plane_h), jnp.asarray(plane_l), jnp.asarray(span_constants(width))),
        ((6, layers, rows, width), (3, layers, rows, width), (rows, width)),
        [
            ((4, both, 3 * rows, width), single),
            ((3 * cells, 4 * width), brief),
            ((3 * cells, 4 * width), brief),
            ((2 * cells, 3 * width), brief),
            ((2 * cells, 3 * width), brief),
            ((4, both + 2, 2 * rows, width), single),
            ((2 * cells, 7 * width), brief),
            ((2 * cells, 7 * width), brief),
            ((3, both, rows, width), single),
            ((3, both, rows, width), single),
        ],
        mib=32,
    )

    sums = sums + swap(sums)
    come = swap(send)
    tables = [sums]
    for step in range(1, spans):
        tables.append(lax.ppermute(sums, "span", [(p, (p + step) % spans) for p in range(spans)]))
    block, corr = (3, layers, rows, width), (3, rows)
    return call(
        functools.partial(finish_kernel, float(layers * width * spans * streams), spans),
        "finish",
        (*tables, keep, come),
        (block, block, corr, corr),
        [((spans, rows, width), single)],
    )


def solution(mesh):
    return jax.shard_map(
        shards,
        mesh=mesh,
        in_specs=(P(None, "stream", "wall", "span"),),
        out_specs=(
            P(None, "stream", "wall", "span"),
            P(None, "stream", "wall", "span"),
            P(None, "wall"),
            P(None, "wall"),
        ),
        check_vma=False,
    )
```

```python
import functools
import math

import jax
import jax.numpy as jnp
import ml_dtypes
import numpy as np
from jax import lax
from jax.experimental import pallas as pl
from jax.experimental.pallas import tpu as pltpu
from jax.sharding import PartitionSpec as P

raw_taps = [math.exp(-((k - 8) ** 2) / 18.0) for k in range(17)]
filter_taps = [value / sum(raw_taps) for value in raw_taps]
clark_coef = 9.0
small_eps = 1e-06

reach = 8
rim = 2 * reach


def split_constant(matrix):
    high = matrix.astype(ml_dtypes.bfloat16)
    low = (matrix - high.astype(np.float64)).astype(ml_dtypes.bfloat16)
    return high, low


def band(outs, ins, offset):
    matrix = np.zeros((outs, ins))
    for o in range(outs):
        for i in range(ins):
            k = i - o - offset + reach
            if 0 <= k <= 2 * reach:
                matrix[o, i] = filter_taps[k]
    return matrix


def plane_constants(layers, rows):
    stream = band(layers, layers, 0)
    wall = band(rows, 2 * rows, reach)
    blocks = [np.kron(stream, wall[:, :rows]), np.kron(stream, wall[:, rows:])]
    return split_constant(np.concatenate(blocks, axis=1))


def span_constants(width):
    circle = np.zeros((width, width))
    for o in range(width):
        for k in range(2 * reach + 1):
            circle[(o + k - reach) % width, o] = filter_taps[k]
    high, low = split_constant(circle)
    return np.block([[high, low], [high, np.zeros_like(low)]])


def halves(value):
    high = value.astype(jnp.bfloat16)
    return high, (value - high.astype(jnp.float32)).astype(jnp.bfloat16)


def dot(a, b):
    return lax.dot_general(a, b, (((1,), (0,)), ((), ())), preferred_element_type=jnp.float32)


def lane_index(shape):
    return lax.broadcasted_iota(jnp.int32, shape, len(shape) - 1)


def edge_kernel(own, to_partner_side, to_own_side):
    _, layers, rows, width = own.shape
    half = layers // 2
    lane = lane_index((half, rows, width))
    me_s = lax.axis_index("stream")
    sides = []
    for start in (0, width - rim):
        total = jnp.zeros((half, rows, width), jnp.float32)
        for k in range(2):
            for f in range(4):
                place = k * 64 + f * rim
                cells = pltpu.roll(own[f, k * half : (k + 1) * half], (place - start) % width, 2)
                total = jnp.where(lane // rim == place // rim, cells, total)
        sides.append(total)
    to_partner_side[...] = jnp.where(me_s == 0, sides[0], sides[1])
    to_own_side[...] = jnp.where(me_s == 0, sides[1], sides[0])


def unpack(packed, block, start):
    _, layers, rows, width = block.shape
    half = layers // 2
    beyond = lane_index((half, rows, width)) // rim == start // rim
    for f in range(4):
        for k in range(2):
            place = k * 64 + f * rim
            cells = pltpu.roll(packed, lax.rem(start - place + 2 * width, width), 2)
            yield f, k, jnp.where(beyond, cells, block[f, k * half : (k + 1) * half])


def merge_kernel(own, part, own_strip, part_strip, merged, rest):
    _, layers, rows, width = own.shape
    half = layers // 2
    me_s = lax.axis_index("stream")
    start = jnp.where(me_s == 0, width - rim, 0)
    for f, k, cells in unpack(own_strip[...], own, start):
        merged[f, pl.ds(me_s * layers + k * half, half)] = cells
    for f, k, cells in unpack(part_strip[...], part, start):
        merged[f, pl.ds((1 - me_s) * layers + k * half, half)] = cells
        rest[f * layers + k * half : f * layers + (k + 1) * half] = cells
    rest[4 * layers :] = own_strip[...]


def flux_kernel(
    walls, mid, a_block, b_own, b_rest, plane_h, plane_l, span_w, keep_ref, send_ref, sums_ref,
    raw, in_h, in_l, prod_h, prod_l, mean, mid_h, mid_l, clark_all, similar_all,
):
    _, both, rows, width = mid.shape
    layers = both // 2
    cells = both * rows
    me_s = lax.axis_index("stream")
    me_w = lax.axis_index("wall")
    odd = lax.rem(me_w, 2)
    row_a = pl.multiple_of((1 - odd) * (2 * rows), rows)
    row_b = pl.multiple_of(odd * (2 * rows), rows)
    at_end = (me_w == 0) | (me_w == walls - 1)
    keep_b = jnp.where(at_end, 0.0, 1.0).astype(jnp.float32)

    raw[:, :, rows : 2 * rows, :] = mid[...]
    raw[:, :, pl.ds(row_a, rows), :] = a_block[...]
    start = jnp.where(me_s == 0, width - rim, 0)
    for f, k, value in unpack(b_rest[4 * layers :], b_own, start):
        along = pl.ds(me_s * layers + k * (layers // 2), layers // 2)
        raw[f, along, pl.ds(row_b, rows), :] = value * keep_b
    for f in range(4):
        value = b_rest[f * layers : (f + 1) * layers]
        raw[f, pl.ds((1 - me_s) * layers, layers), pl.ds(row_b, rows), :] = value * keep_b

    def column(t):
        return slice(t * width, (t + 1) * width)

    for block in range(3):
        down = slice(block * cells, (block + 1) * cells)
        for t in range(4):
            value = raw[t, :, block * rows : (block + 1) * rows, :].reshape(cells, width)
            in_h[down, column(t)], in_l[down, column(t)] = halves(value)

    def planes_of(high, low):
        return dot(plane_h[...], high) + dot(plane_l[...], high) + dot(plane_h[...], low)

    def along_span_of(planes):
        high, low = halves(planes)
        tiles = planes.shape[1] // width
        parts = [jnp.concatenate([high[:, column(t)], low[:, column(t)]], axis=1) for t in range(tiles)]
        result = dot(jnp.concatenate(parts, axis=0), span_w[...])
        result = result[:, :width] + result[:, width:]
        return [result[t * cells : (t + 1) * cells].reshape(both, rows, width) for t in range(tiles)]

    for t in range(4):
        mean[t, 0] = jnp.zeros((2 * rows, width), jnp.float32)
        mean[t, both + 1] = jnp.zeros((2 * rows, width), jnp.float32)
    for half in range(2):
        span = slice(half * cells, (half + 2) * cells)
        planes = planes_of(in_h[span, :], in_l[span, :])
        row = lax.rem(lax.broadcasted_iota(jnp.int32, planes.shape, 0), rows)
        if half == 0:
            inside = (me_w > 0) | (row >= reach)
        else:
            inside = (me_w < walls - 1) | (row < rows - reach)
        planes = jnp.where(inside, planes, 0.0)
        for t, value in enumerate(along_span_of(planes)):
            mean[t, 1 : both + 1, half * rows : (half + 1) * rows, :] = value

    for half in range(2):
        span = slice(reach + half * rows, reach + (half + 1) * rows)
        down = slice(half * cells, (half + 1) * cells)
        temperature = raw[3, :, span, :].reshape(cells, width)
        for t in range(3):
            value = raw[t, :, span, :].reshape(cells, width) * temperature
            prod_h[down, column(t)], prod_l[down, column(t)] = halves(value)
    flux = along_span_of(planes_of(prod_h[...], prod_l[...]))

    for half in range(2):
        span = slice(half * rows, (half + 1) * rows)
        down = slice(half * cells, (half + 1) * cells)
        tiles = [mean[t, 1 : both + 1, span, :].reshape(cells, width) for t in range(4)]
        tiles += [tiles[i] * tiles[3] for i in range(3)]
        for t, value in enumerate(tiles):
            mid_h[down, column(t)], mid_l[down, column(t)] = halves(value)
    second = along_span_of(planes_of(mid_h[...], mid_l[...]))

    mid_rows = slice(reach, reach + rows)
    centre, along_span, along_wall, along_stream = [], [], [], []
    for f in range(4):
        here = mean[f, 1 : both + 1, mid_rows, :]
        centre.append(here)
        along_span.append((pltpu.roll(here, width - 1, 2) - pltpu.roll(here, 1, 2)) * 0.5)
        below = mean[f, 1 : both + 1, reach + 1 : reach + rows + 1, :]
        above = mean[f, 1 : both + 1, reach - 1 : reach + rows - 1, :]
        along_wall.append((below - above) * 0.5)
        along_stream.append((mean[f, 2 : both + 2, mid_rows, :] - mean[f, :both, mid_rows, :]) * 0.5)

    lane = lane_index((rows, width))
    useful = lane // (width // 2) == me_s
    table = jnp.zeros((rows, width), jnp.float32)
    for i in range(3):
        exact = flux[i] - centre[i] * centre[3]
        similar = second[4 + i] - second[i] * second[3]
        total = along_span[i] * along_span[3] + along_wall[i] * along_wall[3]
        clark = clark_coef * (total + along_stream[i] * along_stream[3])
        clark_all[i] = clark
        similar_all[i] = similar
        terms = (exact * clark, exact * similar, exact * exact, clark * clark, similar * similar)
        for q, term in enumerate(terms):
            value = jnp.where(useful, jnp.sum(term, axis=0), 0.0)
            table = jnp.where(lane == 3 * q + i, jnp.sum(value, axis=1, keepdims=True), table)
    sums_ref[...] = table

    first = lane_index((layers, rows, width)) < width // 2
    for i in range(3):
        keep_ref[i] = clark_all[i, pl.ds(me_s * layers, layers)]
        keep_ref[3 + i] = similar_all[i, pl.ds(me_s * layers, layers)]
        clark = clark_all[i, pl.ds((1 - me_s) * layers, layers)]
        similar = similar_all[i, pl.ds((1 - me_s) * layers, layers)]
        turn = me_s == 0
        clark = jnp.where(turn, clark, pltpu.roll(clark, width // 2, 2))
        similar = jnp.where(turn, pltpu.roll(similar, width // 2, 2), similar)
        send_ref[i] = jnp.where(first, clark, similar)


def finish_kernel(
    plane_cells, tables, keep, come, clark_model, similar_model, clark_corr, similar_corr
):
    _, layers, rows, width = keep.shape
    me_s = lax.axis_index("stream")
    table = jnp.sum(tables[...], axis=0) / plane_cells
    lane = lane_index((rows, width))
    useful = lane // (width // 2) == me_s
    corr = jnp.zeros((rows, width), jnp.float32)
    for i in range(3):
        cross_c, cross_s, power_e, power_c, power_s = (
            table[:, 3 * q + i : 3 * q + i + 1] for q in range(5)
        )
        packed = come[i]
        turned = pltpu.roll(packed, width // 2, 2)
        clark = jnp.where(useful[None], keep[i], jnp.where(me_s == 0, turned, packed))
        similar = jnp.where(useful[None], keep[3 + i], jnp.where(me_s == 0, packed, turned))
        clark_model[i] = clark / jnp.sqrt(power_c + small_eps)[None]
        similar_model[i] = similar / jnp.sqrt(power_s + small_eps)[None]
        value = cross_c / jnp.sqrt((power_e + small_eps) * (power_c + small_eps))
        corr = jnp.where(lane == i, value, corr)
        value = cross_s / jnp.sqrt((power_e + small_eps) * (power_s + small_eps))
        corr = jnp.where(lane == 8 + i, value, corr)
    square = jnp.concatenate([corr, jnp.zeros((width - rows, width), jnp.float32)], axis=0)
    turned = square.T
    clark_corr[...] = turned[:3, :rows]
    similar_corr[...] = turned[8:11, :rows]


def call(kernel, name, ins, outs, scratch=(), mib=4):
    return pl.pallas_call(
        kernel,
        out_shape=tuple(jax.ShapeDtypeStruct(shape, jnp.float32) for shape in outs),
        in_specs=[pl.BlockSpec(memory_space=pltpu.VMEM)] * len(ins),
        out_specs=tuple(pl.BlockSpec(memory_space=pltpu.VMEM) for _ in outs),
        scratch_shapes=[pltpu.VMEM(shape, dtype) for shape, dtype in scratch],
        compiler_params=pltpu.CompilerParams(vmem_limit_bytes=mib * 1024 * 1024),
        name=name,
    )(*ins)


def shards(fields):
    _, layers, rows, width = fields.shape
    spans = lax.axis_size("span")
    walls = lax.axis_size("wall")
    streams = lax.axis_size("stream")
    both = streams * layers
    cells = both * rows

    def swap(value):
        return lax.ppermute(value, "stream", [(0, 1), (1, 0)])

    def pair_a(value):
        return lax.ppermute(value, "wall", [(w, w ^ 1) for w in range(walls)])

    def pair_b(value):
        return lax.ppermute(
            value, "wall", [(w, min(max(((w + 1) ^ 1) - 1, 0), walls - 1)) for w in range(walls)]
        )

    def place(p, s):
        return (p % spans) * streams + s

    to_other, to_same = [], []
    for p in range(spans):
        to_other += [(place(p, 0), place(p - 1, 1)), (place(p, 1), place(p + 1, 0))]
        to_same += [(place(p, 1), place(p - 1, 1)), (place(p, 0), place(p + 1, 0))]

    strip = (layers // 2, rows, width)
    first, second = call(edge_kernel, "edges", (fields,), (strip, strip))
    part = swap(fields)
    part_strip = lax.ppermute(first, ("span", "stream"), to_other)
    own_strip = lax.ppermute(second, ("span", "stream"), to_same)
    part, b_own = lax.optimization_barrier((part, pair_b(fields)))
    mid, rest = call(
        merge_kernel,
        "merge",
        (fields, part, own_strip, part_strip),
        ((4, both, rows, width), (4 * layers + layers // 2, rows, width)),
    )
    b_rest, a_block = pair_b(rest), pair_a(mid)

    plane_h, plane_l = plane_constants(both, rows)
    single, brief = jnp.float32, jnp.bfloat16
    keep, send, sums = call(
        functools.partial(flux_kernel, walls),
        "flux",
        (mid, a_block, b_own, b_rest, jnp.asarray(plane_h), jnp.asarray(plane_l), jnp.asarray(span_constants(width))),
        ((6, layers, rows, width), (3, layers, rows, width), (rows, width)),
        [
            ((4, both, 3 * rows, width), single),
            ((3 * cells, 4 * width), brief),
            ((3 * cells, 4 * width), brief),
            ((2 * cells, 3 * width), brief),
            ((2 * cells, 3 * width), brief),
            ((4, both + 2, 2 * rows, width), single),
            ((2 * cells, 7 * width), brief),
            ((2 * cells, 7 * width), brief),
            ((3, both, rows, width), single),
            ((3, both, rows, width), single),
        ],
        mib=32,
    )

    other, send = lax.optimization_barrier((swap(sums), send))
    come = swap(send)
    tables = jnp.broadcast_to((sums + other)[None], (spans, rows, width))
    tables = lax.all_to_all(tables, "span", 0, 0)
    block, corr = (3, layers, rows, width), (3, rows)
    return call(
        functools.partial(finish_kernel, float(layers * width * spans * streams)),
        "finish",
        (tables, keep, come),
        (block, block, corr, corr),
    )


def solution(mesh):
    return jax.shard_map(
        shards,
        mesh=mesh,
        in_specs=(P(None, "stream", "wall", "span"),),
        out_specs=(
            P(None, "stream", "wall", "span"),
            P(None, "stream", "wall", "span"),
            P(None, "wall"),
            P(None, "wall"),
        ),
        check_vma=False,
    )
```

```python
import functools
import math

import jax
import jax.numpy as jnp
import ml_dtypes
import numpy as np
from jax import lax
from jax.experimental import pallas as pl
from jax.experimental.pallas import tpu as pltpu
from jax.sharding import PartitionSpec as P

raw_taps = [math.exp(-((k - 8) ** 2) / 18.0) for k in range(17)]
filter_taps = [value / sum(raw_taps) for value in raw_taps]
clark_coef = 9.0
small_eps = 1e-06

reach = 8
rim = 2 * reach


def split_constant(matrix):
    high = matrix.astype(ml_dtypes.bfloat16)
    low = (matrix - high.astype(np.float64)).astype(ml_dtypes.bfloat16)
    return high, low


def band(outs, ins, offset):
    matrix = np.zeros((outs, ins))
    for o in range(outs):
        for i in range(ins):
            k = i - o - offset + reach
            if 0 <= k <= 2 * reach:
                matrix[o, i] = filter_taps[k]
    return matrix


def plane_constants(layers, rows):
    stream = band(layers, layers, 0)
    wall = band(rows, 2 * rows, reach)
    blocks = [np.kron(stream, wall[:, :rows]), np.kron(stream, wall[:, rows:])]
    return split_constant(np.concatenate(blocks, axis=1))


def span_constants(width):
    circle = np.zeros((width, width))
    for o in range(width):
        for k in range(2 * reach + 1):
            circle[(o + k - reach) % width, o] = filter_taps[k]
    high, low = split_constant(circle)
    return np.block([[high, low], [high, np.zeros_like(low)]])


def halves(value):
    high = value.astype(jnp.bfloat16)
    return high, (value - high.astype(jnp.float32)).astype(jnp.bfloat16)


def dot(a, b):
    return lax.dot_general(a, b, (((1,), (0,)), ((), ())), preferred_element_type=jnp.float32)


def lane_index(shape):
    return lax.broadcasted_iota(jnp.int32, shape, len(shape) - 1)


def unit_index(shape):
    return lane_index(shape) // rim


def pack_halves(block, half):
    width = block.shape[-1]
    in_place = lane_index(block.shape[1:]) // (width // 2) == half
    for pair in range(2):
        moved = pltpu.roll(block[2 * pair + 1], width // 2, 2)
        yield pair, jnp.where(in_place, block[2 * pair], moved)


def pack_strip(block, unit):
    _, layers, rows, width = block.shape
    half = layers // 2
    units = unit_index((half, rows, width))
    total = jnp.zeros((half, rows, width), jnp.float32)
    for k in range(2):
        for f in range(4):
            step = 2 * f + k
            cells = block[f, k * half : (k + 1) * half]
            cells = pltpu.roll(cells, step * rim, 2) if step else cells
            total = jnp.where(units == lax.rem(unit + step, width // rim), cells, total)
    return total


def strip_tile(inner, outer, me_s):
    width = inner.shape[-1]
    is_outer = lax.rem(unit_index(inner.shape), 2) == 1 - me_s
    for k in range(2):
        shift = (width - k * rim) % width
        pieces = [pltpu.roll(strip, shift, 2) if k else strip for strip in (inner, outer)]
        yield k, jnp.where(is_outer, pieces[1], pieces[0])


def pack_kernel(own, to_partner, to_other, to_same):
    _, layers, _, _ = own.shape
    me_s = lax.axis_index("stream")
    for pair, tile in pack_halves(own, 1 - me_s):
        to_partner[pair * layers : (pair + 1) * layers] = tile
    to_partner[2 * layers :] = pack_strip(own, 3 + me_s)
    to_other[...] = pack_strip(own, 7 * me_s)
    to_same[...] = pack_strip(own, 7 * (1 - me_s))


def merge_kernel(own, part, own_strip, part_strip, packed):
    _, layers, rows, width = own.shape
    half = layers // 2
    me_s = lax.axis_index("stream")
    mine, other = me_s * layers, (1 - me_s) * layers
    for pair, tile in pack_halves(own, me_s):
        packed[pair, pl.ds(mine, layers)] = tile
        packed[pair, pl.ds(other, layers)] = part[pair * layers : (pair + 1) * layers]
    for k, tile in strip_tile(pack_strip(own, 4 - me_s), own_strip[...], me_s):
        packed[2, pl.ds(mine + k * half, half)] = tile
    for k, tile in strip_tile(part[2 * layers :], part_strip[...], me_s):
        packed[2, pl.ds(other + k * half, half)] = tile


def unpack(packed, me_s):
    width = packed.shape[-1]
    unit = unit_index(packed.shape[1:])
    first = 4 * (1 - me_s)
    in_strip = (unit == first) | (unit == first + 3)
    for f in range(4):
        cells = packed[f // 2]
        cells = pltpu.roll(cells, width // 2, 2) if f % 2 else cells
        strip = packed[2]
        strip = pltpu.roll(strip, width - 2 * f * rim, 2) if f else strip
        yield f, jnp.where(in_strip, strip, cells)


def flux_kernel(
    walls, mid, a_block, b_block, weights, keep_ref, send_ref, sums_ref,
    raw, in_h, in_l, prod_h, prod_l, mean, mid_h, mid_l, clark_all, similar_all,
):
    _, both, rows, width = mid.shape
    layers = both // 2
    cells = both * rows
    plane_h = weights.at[:cells]
    plane_l = weights.at[cells : 2 * cells]
    span_w = weights.at[2 * cells :, : 2 * width]
    me_s = lax.axis_index("stream")
    me_w = lax.axis_index("wall")
    odd = lax.rem(me_w, 2)
    row_a = pl.multiple_of((1 - odd) * (2 * rows), rows)
    row_b = pl.multiple_of(odd * (2 * rows), rows)
    at_end = (me_w == 0) | (me_w == walls - 1)
    keep_b = jnp.where(at_end, 0.0, 1.0).astype(jnp.float32)

    for f, value in unpack(mid, me_s):
        raw[f, :, rows : 2 * rows, :] = value
    for f, value in unpack(a_block, me_s):
        raw[f, :, pl.ds(row_a, rows), :] = value
    for f, value in unpack(b_block, me_s):
        raw[f, :, pl.ds(row_b, rows), :] = value * keep_b

    def column(t):
        return slice(t * width, (t + 1) * width)

    for block in range(3):
        down = slice(block * cells, (block + 1) * cells)
        for t in range(4):
            value = raw[t, :, block * rows : (block + 1) * rows, :].reshape(cells, width)
            in_h[down, column(t)], in_l[down, column(t)] = halves(value)

    def planes_of(high, low):
        return dot(plane_h[...], high) + dot(plane_l[...], high) + dot(plane_h[...], low)

    def along_span_of(planes):
        high, low = halves(planes)
        tiles = planes.shape[1] // width
        parts = [jnp.concatenate([high[:, column(t)], low[:, column(t)]], axis=1) for t in range(tiles)]
        result = dot(jnp.concatenate(parts, axis=0), span_w[...])
        result = result[:, :width] + result[:, width:]
        return [result[t * cells : (t + 1) * cells].reshape(both, rows, width) for t in range(tiles)]

    for t in range(4):
        mean[t, 0] = jnp.zeros((2 * rows, width), jnp.float32)
        mean[t, both + 1] = jnp.zeros((2 * rows, width), jnp.float32)
    for half in range(2):
        span = slice(half * cells, (half + 2) * cells)
        planes = planes_of(in_h[span, :], in_l[span, :])
        row = lax.rem(lax.broadcasted_iota(jnp.int32, planes.shape, 0), rows)
        if half == 0:
            inside = (me_w > 0) | (row >= reach)
        else:
            inside = (me_w < walls - 1) | (row < rows - reach)
        planes = jnp.where(inside, planes, 0.0)
        for t, value in enumerate(along_span_of(planes)):
            mean[t, 1 : both + 1, half * rows : (half + 1) * rows, :] = value

    for half in range(2):
        span = slice(reach + half * rows, reach + (half + 1) * rows)
        down = slice(half * cells, (half + 1) * cells)
        temperature = raw[3, :, span, :].reshape(cells, width)
        for t in range(3):
            value = raw[t, :, span, :].reshape(cells, width) * temperature
            prod_h[down, column(t)], prod_l[down, column(t)] = halves(value)
    flux = along_span_of(planes_of(prod_h[...], prod_l[...]))

    for half in range(2):
        span = slice(half * rows, (half + 1) * rows)
        down = slice(half * cells, (half + 1) * cells)
        tiles = [mean[t, 1 : both + 1, span, :].reshape(cells, width) for t in range(4)]
        tiles += [tiles[i] * tiles[3] for i in range(3)]
        for t, value in enumerate(tiles):
            mid_h[down, column(t)], mid_l[down, column(t)] = halves(value)
    second = along_span_of(planes_of(mid_h[...], mid_l[...]))

    mid_rows = slice(reach, reach + rows)
    centre, along_span, along_wall, along_stream = [], [], [], []
    for f in range(4):
        here = mean[f, 1 : both + 1, mid_rows, :]
        centre.append(here)
        along_span.append((pltpu.roll(here, width - 1, 2) - pltpu.roll(here, 1, 2)) * 0.5)
        below = mean[f, 1 : both + 1, reach + 1 : reach + rows + 1, :]
        above = mean[f, 1 : both + 1, reach - 1 : reach + rows - 1, :]
        along_wall.append((below - above) * 0.5)
        along_stream.append((mean[f, 2 : both + 2, mid_rows, :] - mean[f, :both, mid_rows, :]) * 0.5)

    lane = lane_index((rows, width))
    useful = lane // (width // 2) == me_s
    table = jnp.zeros((rows, width), jnp.float32)
    for i in range(3):
        exact = flux[i] - centre[i] * centre[3]
        similar = second[4 + i] - second[i] * second[3]
        total = along_span[i] * along_span[3] + along_wall[i] * along_wall[3]
        clark = clark_coef * (total + along_stream[i] * along_stream[3])
        clark_all[i] = clark
        similar_all[i] = similar
        terms = (exact * clark, exact * similar, exact * exact, clark * clark, similar * similar)
        for q, term in enumerate(terms):
            value = jnp.where(useful, jnp.sum(term, axis=0), 0.0)
            table = jnp.where(lane == 3 * q + i, jnp.sum(value, axis=1, keepdims=True), table)
    sums_ref[...] = table

    first = lane_index((layers, rows, width)) < width // 2
    for i in range(3):
        keep_ref[i] = clark_all[i, pl.ds(me_s * layers, layers)]
        keep_ref[3 + i] = similar_all[i, pl.ds(me_s * layers, layers)]
        clark = clark_all[i, pl.ds((1 - me_s) * layers, layers)]
        similar = similar_all[i, pl.ds((1 - me_s) * layers, layers)]
        turn = me_s == 0
        clark = jnp.where(turn, clark, pltpu.roll(clark, width // 2, 2))
        similar = jnp.where(turn, pltpu.roll(similar, width // 2, 2), similar)
        send_ref[i] = jnp.where(first, clark, similar)


def finish_kernel(
    plane_cells, tables, keep, come, clark_model, similar_model, clark_corr, similar_corr
):
    _, layers, rows, width = keep.shape
    me_s = lax.axis_index("stream")
    table = jnp.sum(tables[...], axis=0) / plane_cells
    lane = lane_index((rows, width))
    useful = lane // (width // 2) == me_s
    corr = jnp.zeros((rows, width), jnp.float32)
    for i in range(3):
        cross_c, cross_s, power_e, power_c, power_s = (
            table[:, 3 * q + i : 3 * q + i + 1] for q in range(5)
        )
        packed = come[i]
        turned = pltpu.roll(packed, width // 2, 2)
        clark = jnp.where(useful[None], keep[i], jnp.where(me_s == 0, turned, packed))
        similar = jnp.where(useful[None], keep[3 + i], jnp.where(me_s == 0, packed, turned))
        clark_model[i] = clark / jnp.sqrt(power_c + small_eps)[None]
        similar_model[i] = similar / jnp.sqrt(power_s + small_eps)[None]
        value = cross_c / jnp.sqrt((power_e + small_eps) * (power_c + small_eps))
        corr = jnp.where(lane == i, value, corr)
        value = cross_s / jnp.sqrt((power_e + small_eps) * (power_s + small_eps))
        corr = jnp.where(lane == 8 + i, value, corr)
    square = jnp.concatenate([corr, jnp.zeros((width - rows, width), jnp.float32)], axis=0)
    turned = square.T
    clark_corr[...] = turned[:3, :rows]
    similar_corr[...] = turned[8:11, :rows]


def call(kernel, name, ins, outs, scratch=(), mib=4):
    return pl.pallas_call(
        kernel,
        out_shape=tuple(jax.ShapeDtypeStruct(shape, jnp.float32) for shape in outs),
        in_specs=[pl.BlockSpec(memory_space=pltpu.VMEM)] * len(ins),
        out_specs=tuple(pl.BlockSpec(memory_space=pltpu.VMEM) for _ in outs),
        scratch_shapes=[pltpu.VMEM(shape, dtype) for shape, dtype in scratch],
        compiler_params=pltpu.CompilerParams(vmem_limit_bytes=mib * 1024 * 1024),
        name=name,
    )(*ins)


def shards(fields):
    _, layers, rows, width = fields.shape
    spans = lax.axis_size("span")
    walls = lax.axis_size("wall")
    streams = lax.axis_size("stream")
    both = streams * layers
    cells = both * rows

    def swap(value):
        return lax.ppermute(value, "stream", [(0, 1), (1, 0)])

    def pair_a(value):
        return lax.ppermute(value, "wall", [(w, w ^ 1) for w in range(walls)])

    def pair_b(value):
        return lax.ppermute(
            value, "wall", [(w, min(max(((w + 1) ^ 1) - 1, 0), walls - 1)) for w in range(walls)]
        )

    def place(p, s):
        return (p % spans) * streams + s

    to_other, to_same = [], []
    for p in range(spans):
        to_other += [(place(p, 0), place(p - 1, 1)), (place(p, 1), place(p + 1, 0))]
        to_same += [(place(p, 1), place(p - 1, 1)), (place(p, 0), place(p + 1, 0))]

    strip = (layers // 2, rows, width)
    to_partner, first, second = call(
        pack_kernel, "pack", (fields,), ((2 * layers + layers // 2, rows, width), strip, strip)
    )
    part = swap(to_partner)
    part_strip = lax.ppermute(first, ("span", "stream"), to_other)
    own_strip = lax.ppermute(second, ("span", "stream"), to_same)
    (mid,) = call(merge_kernel, "merge", (fields, part, own_strip, part_strip), ((3, both, rows, width),))
    b_block, a_block = pair_b(mid), pair_a(mid)

    weights = np.zeros((2 * cells + 2 * width, 2 * cells), ml_dtypes.bfloat16)
    weights[:cells], weights[cells : 2 * cells] = plane_constants(both, rows)
    weights[2 * cells :, : 2 * width] = span_constants(width)
    single, brief = jnp.float32, jnp.bfloat16
    keep, send, sums = call(
        functools.partial(flux_kernel, walls),
        "flux",
        (mid, a_block, b_block, jnp.asarray(weights)),
        ((6, layers, rows, width), (3, layers, rows, width), (rows, width)),
        [
            ((4, both, 3 * rows, width), single),
            ((3 * cells, 4 * width), brief),
            ((3 * cells, 4 * width), brief),
            ((2 * cells, 3 * width), brief),
            ((2 * cells, 3 * width), brief),
            ((4, both + 2, 2 * rows, width), single),
            ((2 * cells, 7 * width), brief),
            ((2 * cells, 7 * width), brief),
            ((3, both, rows, width), single),
            ((3, both, rows, width), single),
        ],
        mib=32,
    )

    come = swap(send)
    group = spans * streams
    tables = lax.all_to_all(
        jnp.broadcast_to(sums[None], (group, rows, width)), ("span", "stream"), 0, 0
    )
    block, corr = (3, layers, rows, width), (3, rows)
    return call(
        functools.partial(finish_kernel, float(layers * width * group)),
        "finish",
        (tables, keep, come),
        (block, block, corr, corr),
    )


def solution(mesh):
    return jax.shard_map(
        shards,
        mesh=mesh,
        in_specs=(P(None, "stream", "wall", "span"),),
        out_specs=(
            P(None, "stream", "wall", "span"),
            P(None, "stream", "wall", "span"),
            P(None, "wall"),
            P(None, "wall"),
        ),
        check_vma=False,
    )
```

```python
import functools
import math

import jax
import jax.numpy as jnp
import ml_dtypes
import numpy as np
from jax import lax
from jax.experimental import pallas as pl
from jax.experimental.pallas import tpu as pltpu
from jax.sharding import PartitionSpec as P

raw_taps = [math.exp(-((k - 8) ** 2) / 18.0) for k in range(17)]
filter_taps = [value / sum(raw_taps) for value in raw_taps]
clark_coef = 9.0
small_eps = 1e-06

reach = 8
rim = 2 * reach


def split_constant(matrix):
    high = matrix.astype(ml_dtypes.bfloat16)
    low = (matrix - high.astype(np.float64)).astype(ml_dtypes.bfloat16)
    return high, low


def band(outs, ins, offset):
    matrix = np.zeros((outs, ins))
    for o in range(outs):
        for i in range(ins):
            k = i - o - offset + reach
            if 0 <= k <= 2 * reach:
                matrix[o, i] = filter_taps[k]
    return matrix


def plane_constants(layers, rows):
    stream = band(layers, layers, 0)
    wall = band(rows, 2 * rows, reach)
    blocks = [np.kron(stream, wall[:, :rows]), np.kron(stream, wall[:, rows:])]
    return split_constant(np.concatenate(blocks, axis=1))


def span_constants(width):
    circle = np.zeros((width, width))
    for o in range(width):
        for k in range(2 * reach + 1):
            circle[(o + k - reach) % width, o] = filter_taps[k]
    high, low = split_constant(circle)
    return np.block([[high, low], [high, np.zeros_like(low)]])


def halves(value):
    high = value.astype(jnp.bfloat16)
    return high, (value - high.astype(jnp.float32)).astype(jnp.bfloat16)


def dot(a, b):
    return lax.dot_general(a, b, (((1,), (0,)), ((), ())), preferred_element_type=jnp.float32)


def lane_index(shape):
    return lax.broadcasted_iota(jnp.int32, shape, len(shape) - 1)


def unit_index(shape):
    return lane_index(shape) // rim


def pack_halves(block, half):
    width = block.shape[-1]
    in_place = lane_index(block.shape[1:]) // (width // 2) == half
    for pair in range(2):
        moved = pltpu.roll(block[2 * pair + 1], width // 2, 2)
        yield pair, jnp.where(in_place, block[2 * pair], moved)


def pack_strip(block, unit):
    _, layers, rows, width = block.shape
    half = layers // 2
    units = unit_index((half, rows, width))
    total = jnp.zeros((half, rows, width), jnp.float32)
    for k in range(2):
        for f in range(4):
            step = 2 * f + k
            cells = block[f, k * half : (k + 1) * half]
            cells = pltpu.roll(cells, step * rim, 2) if step else cells
            total = jnp.where(units == lax.rem(unit + step, width // rim), cells, total)
    return total


def strip_tile(inner, outer, me_s):
    width = inner.shape[-1]
    is_outer = lax.rem(unit_index(inner.shape), 2) == 1 - me_s
    for k in range(2):
        shift = (width - k * rim) % width
        pieces = [pltpu.roll(strip, shift, 2) if k else strip for strip in (inner, outer)]
        yield k, jnp.where(is_outer, pieces[1], pieces[0])


def pack_kernel(own, to_partner, to_other, to_same):
    _, layers, _, _ = own.shape
    me_s = lax.axis_index("stream")
    for pair, tile in pack_halves(own, 1 - me_s):
        to_partner[pair * layers : (pair + 1) * layers] = tile
    to_partner[2 * layers :] = pack_strip(own, 3 + me_s)
    to_other[...] = pack_strip(own, 7 * me_s)
    to_same[...] = pack_strip(own, 7 * (1 - me_s))


def main_kernel(own, part, main):
    _, layers, _, _ = own.shape
    me_s = lax.axis_index("stream")
    for pair, tile in pack_halves(own, me_s):
        main[pair, pl.ds(me_s * layers, layers)] = tile
        main[pair, pl.ds((1 - me_s) * layers, layers)] = part[pair * layers : (pair + 1) * layers]


def rim_kernel(own, part, own_strip, part_strip, strips):
    _, layers, _, _ = own.shape
    half = layers // 2
    me_s = lax.axis_index("stream")
    for k, tile in strip_tile(pack_strip(own, 4 - me_s), own_strip[...], me_s):
        strips[pl.ds(me_s * layers + k * half, half)] = tile
    for k, tile in strip_tile(part[2 * layers :], part_strip[...], me_s):
        strips[pl.ds((1 - me_s) * layers + k * half, half)] = tile


def unpack(main, strips, me_s):
    width = strips.shape[-1]
    unit = unit_index(strips.shape)
    first = 4 * (1 - me_s)
    in_strip = (unit == first) | (unit == first + 3)
    for f in range(4):
        cells = main[f // 2]
        cells = pltpu.roll(cells, width // 2, 2) if f % 2 else cells
        strip = strips[...]
        strip = pltpu.roll(strip, width - 2 * f * rim, 2) if f else strip
        yield f, jnp.where(in_strip, strip, cells)


def flux_kernel(
    walls, main, a_main, b_main, strips, a_strips, b_strips, weights, keep_ref, send_ref, sums_ref,
    raw, in_h, in_l, prod_h, prod_l, mean, mid_h, mid_l, clark_all, similar_all,
):
    _, layers, rows, width = keep_ref.shape
    both = 2 * layers
    cells = both * rows
    plane_h = weights.at[:cells]
    plane_l = weights.at[cells : 2 * cells]
    span_w = weights.at[2 * cells :, : 2 * width]
    me_s = lax.axis_index("stream")
    me_w = lax.axis_index("wall")
    odd = lax.rem(me_w, 2)
    row_a = pl.multiple_of((1 - odd) * (2 * rows), rows)
    row_b = pl.multiple_of(odd * (2 * rows), rows)
    at_end = (me_w == 0) | (me_w == walls - 1)
    keep_b = jnp.where(at_end, 0.0, 1.0).astype(jnp.float32)

    for f, value in unpack(main, strips, me_s):
        raw[f, :, rows : 2 * rows, :] = value
    for f, value in unpack(a_main, a_strips, me_s):
        raw[f, :, pl.ds(row_a, rows), :] = value
    for f, value in unpack(b_main, b_strips, me_s):
        raw[f, :, pl.ds(row_b, rows), :] = value * keep_b

    def column(t):
        return slice(t * width, (t + 1) * width)

    for block in range(3):
        down = slice(block * cells, (block + 1) * cells)
        for t in range(4):
            value = raw[t, :, block * rows : (block + 1) * rows, :].reshape(cells, width)
            in_h[down, column(t)], in_l[down, column(t)] = halves(value)

    def planes_of(high, low):
        return dot(plane_h[...], high) + dot(plane_l[...], high) + dot(plane_h[...], low)

    def along_span_of(planes):
        high, low = halves(planes)
        tiles = planes.shape[1] // width
        parts = [jnp.concatenate([high[:, column(t)], low[:, column(t)]], axis=1) for t in range(tiles)]
        result = dot(jnp.concatenate(parts, axis=0), span_w[...])
        result = result[:, :width] + result[:, width:]
        return [result[t * cells : (t + 1) * cells].reshape(both, rows, width) for t in range(tiles)]

    for t in range(4):
        mean[t, 0] = jnp.zeros((2 * rows, width), jnp.float32)
        mean[t, both + 1] = jnp.zeros((2 * rows, width), jnp.float32)
    for half in range(2):
        span = slice(half * cells, (half + 2) * cells)
        planes = planes_of(in_h[span, :], in_l[span, :])
        row = lax.rem(lax.broadcasted_iota(jnp.int32, planes.shape, 0), rows)
        if half == 0:
            inside = (me_w > 0) | (row >= reach)
        else:
            inside = (me_w < walls - 1) | (row < rows - reach)
        planes = jnp.where(inside, planes, 0.0)
        for t, value in enumerate(along_span_of(planes)):
            mean[t, 1 : both + 1, half * rows : (half + 1) * rows, :] = value

    for half in range(2):
        span = slice(reach + half * rows, reach + (half + 1) * rows)
        down = slice(half * cells, (half + 1) * cells)
        temperature = raw[3, :, span, :].reshape(cells, width)
        for t in range(3):
            value = raw[t, :, span, :].reshape(cells, width) * temperature
            prod_h[down, column(t)], prod_l[down, column(t)] = halves(value)
    flux = along_span_of(planes_of(prod_h[...], prod_l[...]))

    for half in range(2):
        span = slice(half * rows, (half + 1) * rows)
        down = slice(half * cells, (half + 1) * cells)
        tiles = [mean[t, 1 : both + 1, span, :].reshape(cells, width) for t in range(4)]
        tiles += [tiles[i] * tiles[3] for i in range(3)]
        for t, value in enumerate(tiles):
            mid_h[down, column(t)], mid_l[down, column(t)] = halves(value)
    second = along_span_of(planes_of(mid_h[...], mid_l[...]))

    mid_rows = slice(reach, reach + rows)
    centre, along_span, along_wall, along_stream = [], [], [], []
    for f in range(4):
        here = mean[f, 1 : both + 1, mid_rows, :]
        centre.append(here)
        along_span.append((pltpu.roll(here, width - 1, 2) - pltpu.roll(here, 1, 2)) * 0.5)
        below = mean[f, 1 : both + 1, reach + 1 : reach + rows + 1, :]
        above = mean[f, 1 : both + 1, reach - 1 : reach + rows - 1, :]
        along_wall.append((below - above) * 0.5)
        along_stream.append((mean[f, 2 : both + 2, mid_rows, :] - mean[f, :both, mid_rows, :]) * 0.5)

    lane = lane_index((rows, width))
    useful = lane // (width // 2) == me_s
    table = jnp.zeros((rows, width), jnp.float32)
    for i in range(3):
        exact = flux[i] - centre[i] * centre[3]
        similar = second[4 + i] - second[i] * second[3]
        total = along_span[i] * along_span[3] + along_wall[i] * along_wall[3]
        clark = clark_coef * (total + along_stream[i] * along_stream[3])
        clark_all[i] = clark
        similar_all[i] = similar
        terms = (exact * clark, exact * similar, exact * exact, clark * clark, similar * similar)
        for q, term in enumerate(terms):
            value = jnp.where(useful, jnp.sum(term, axis=0), 0.0)
            table = jnp.where(lane == 3 * q + i, jnp.sum(value, axis=1, keepdims=True), table)
    sums_ref[...] = table

    first = lane_index((layers, rows, width)) < width // 2
    for i in range(3):
        keep_ref[i] = clark_all[i, pl.ds(me_s * layers, layers)]
        keep_ref[3 + i] = similar_all[i, pl.ds(me_s * layers, layers)]
        clark = clark_all[i, pl.ds((1 - me_s) * layers, layers)]
        similar = similar_all[i, pl.ds((1 - me_s) * layers, layers)]
        turn = me_s == 0
        clark = jnp.where(turn, clark, pltpu.roll(clark, width // 2, 2))
        similar = jnp.where(turn, pltpu.roll(similar, width // 2, 2), similar)
        send_ref[i] = jnp.where(first, clark, similar)


def finish_kernel(
    plane_cells, tables, keep, come, clark_model, similar_model, clark_corr, similar_corr
):
    _, layers, rows, width = keep.shape
    me_s = lax.axis_index("stream")
    table = jnp.sum(tables[...], axis=0) / plane_cells
    lane = lane_index((rows, width))
    useful = lane // (width // 2) == me_s
    corr = jnp.zeros((rows, width), jnp.float32)
    for i in range(3):
        cross_c, cross_s, power_e, power_c, power_s = (
            table[:, 3 * q + i : 3 * q + i + 1] for q in range(5)
        )
        packed = come[i]
        turned = pltpu.roll(packed, width // 2, 2)
        clark = jnp.where(useful[None], keep[i], jnp.where(me_s == 0, turned, packed))
        similar = jnp.where(useful[None], keep[3 + i], jnp.where(me_s == 0, packed, turned))
        clark_model[i] = clark / jnp.sqrt(power_c + small_eps)[None]
        similar_model[i] = similar / jnp.sqrt(power_s + small_eps)[None]
        value = cross_c / jnp.sqrt((power_e + small_eps) * (power_c + small_eps))
        corr = jnp.where(lane == i, value, corr)
        value = cross_s / jnp.sqrt((power_e + small_eps) * (power_s + small_eps))
        corr = jnp.where(lane == 8 + i, value, corr)
    square = jnp.concatenate([corr, jnp.zeros((width - rows, width), jnp.float32)], axis=0)
    turned = square.T
    clark_corr[...] = turned[:3, :rows]
    similar_corr[...] = turned[8:11, :rows]


def call(kernel, name, ins, outs, scratch=(), mib=4, hint=None):
    cost = hint and pl.CostEstimate(flops=hint, bytes_accessed=hint // 100, transcendentals=0)
    return pl.pallas_call(
        kernel,
        out_shape=tuple(jax.ShapeDtypeStruct(shape, jnp.float32) for shape in outs),
        in_specs=[pl.BlockSpec(memory_space=pltpu.VMEM)] * len(ins),
        out_specs=tuple(pl.BlockSpec(memory_space=pltpu.VMEM) for _ in outs),
        scratch_shapes=[pltpu.VMEM(shape, dtype) for shape, dtype in scratch],
        compiler_params=pltpu.CompilerParams(vmem_limit_bytes=mib * 1024 * 1024),
        cost_estimate=cost,
        name=name,
    )(*ins)


def shards(fields):
    _, layers, rows, width = fields.shape
    spans = lax.axis_size("span")
    walls = lax.axis_size("wall")
    streams = lax.axis_size("stream")
    both = streams * layers
    cells = both * rows

    def swap(value):
        return lax.ppermute(value, "stream", [(0, 1), (1, 0)])

    def pair_a(value):
        return lax.ppermute(value, "wall", [(w, w ^ 1) for w in range(walls)])

    def pair_b(value):
        return lax.ppermute(
            value, "wall", [(w, min(max(((w + 1) ^ 1) - 1, 0), walls - 1)) for w in range(walls)]
        )

    def place(p, s):
        return (p % spans) * streams + s

    to_other, to_same = [], []
    for p in range(spans):
        to_other += [(place(p, 0), place(p - 1, 1)), (place(p, 1), place(p + 1, 0))]
        to_same += [(place(p, 1), place(p - 1, 1)), (place(p, 0), place(p + 1, 0))]

    strip = (layers // 2, rows, width)
    to_partner, first, second = call(
        pack_kernel, "pack", (fields,), ((2 * layers + layers // 2, rows, width), strip, strip)
    )
    part = swap(to_partner)
    part_strip = lax.ppermute(first, ("span", "stream"), to_other)
    own_strip = lax.ppermute(second, ("span", "stream"), to_same)
    (main,) = call(main_kernel, "main", (fields, part), ((2, both, rows, width),))
    b_main, a_main = pair_b(main), pair_a(main)
    (strips,) = call(rim_kernel, "strips", (fields, part, own_strip, part_strip), ((both, rows, width),), hint=2**35)
    b_strips, a_strips = pair_b(strips), pair_a(strips)

    weights = np.zeros((2 * cells + 2 * width, 2 * cells), ml_dtypes.bfloat16)
    weights[:cells], weights[cells : 2 * cells] = plane_constants(both, rows)
    weights[2 * cells :, : 2 * width] = span_constants(width)
    single, brief = jnp.float32, jnp.bfloat16
    keep, send, sums = call(
        functools.partial(flux_kernel, walls),
        "flux",
        (main, a_main, b_main, strips, a_strips, b_strips, jnp.asarray(weights)),
        ((6, layers, rows, width), (3, layers, rows, width), (rows, width)),
        [
            ((4, both, 3 * rows, width), single),
            ((3 * cells, 4 * width), brief),
            ((3 * cells, 4 * width), brief),
            ((2 * cells, 3 * width), brief),
            ((2 * cells, 3 * width), brief),
            ((4, both + 2, 2 * rows, width), single),
            ((2 * cells, 7 * width), brief),
            ((2 * cells, 7 * width), brief),
            ((3, both, rows, width), single),
            ((3, both, rows, width), single),
        ],
        mib=32,
    )

    come = swap(send)
    group = spans * streams
    tables = lax.all_to_all(
        jnp.broadcast_to(sums[None], (group, rows, width)), ("span", "stream"), 0, 0
    )
    block, corr = (3, layers, rows, width), (3, rows)
    return call(
        functools.partial(finish_kernel, float(layers * width * group)),
        "finish",
        (tables, keep, come),
        (block, block, corr, corr),
    )


def solution(mesh):
    return jax.shard_map(
        shards,
        mesh=mesh,
        in_specs=(P(None, "stream", "wall", "span"),),
        out_specs=(
            P(None, "stream", "wall", "span"),
            P(None, "stream", "wall", "span"),
            P(None, "wall"),
            P(None, "wall"),
        ),
        check_vma=False,
    )
```

```python
import functools
import math

import jax
import jax.numpy as jnp
import ml_dtypes
import numpy as np
from jax import lax
from jax.experimental import pallas as pl
from jax.experimental.pallas import tpu as pltpu
from jax.sharding import PartitionSpec as P

raw_taps = [math.exp(-((k - 8) ** 2) / 18.0) for k in range(17)]
filter_taps = [value / sum(raw_taps) for value in raw_taps]
clark_coef = 9.0
small_eps = 1e-06

reach = 8
rim = 2 * reach


def split_constant(matrix):
    high = matrix.astype(ml_dtypes.bfloat16)
    low = (matrix - high.astype(np.float64)).astype(ml_dtypes.bfloat16)
    return high, low


def band(outs, ins, offset):
    matrix = np.zeros((outs, ins))
    for o in range(outs):
        for i in range(ins):
            k = i - o - offset + reach
            if 0 <= k <= 2 * reach:
                matrix[o, i] = filter_taps[k]
    return matrix


def plane_constants(layers, rows):
    stream = band(layers, layers, 0)
    wall = band(rows, 2 * rows, reach)
    blocks = [np.kron(stream, wall[:, :rows]), np.kron(stream, wall[:, rows:])]
    return split_constant(np.concatenate(blocks, axis=1))


def span_constants(width):
    circle = np.zeros((width, width))
    for o in range(width):
        for k in range(2 * reach + 1):
            circle[(o + k - reach) % width, o] = filter_taps[k]
    high, low = split_constant(circle)
    return np.block([[high, low], [high, np.zeros_like(low)]])


def halves(value):
    high = value.astype(jnp.bfloat16)
    return high, (value - high.astype(jnp.float32)).astype(jnp.bfloat16)


def dot(a, b):
    return lax.dot_general(a, b, (((1,), (0,)), ((), ())), preferred_element_type=jnp.float32)


def lane_index(shape):
    return lax.broadcasted_iota(jnp.int32, shape, len(shape) - 1)


def unit_index(shape):
    return lane_index(shape) // rim


def pack_halves(block, half):
    width = block.shape[-1]
    in_place = lane_index(block.shape[1:]) // (width // 2) == half
    for pair in range(2):
        moved = pltpu.roll(block[2 * pair + 1], width // 2, 2)
        yield pair, jnp.where(in_place, block[2 * pair], moved)


def pack_strip(block, unit):
    _, layers, rows, width = block.shape
    half = layers // 2
    units = unit_index((half, rows, width))
    total = jnp.zeros((half, rows, width), jnp.float32)
    for k in range(2):
        for f in range(4):
            step = 2 * f + k
            cells = block[f, k * half : (k + 1) * half]
            cells = pltpu.roll(cells, step * rim, 2) if step else cells
            total = jnp.where(units == lax.rem(unit + step, width // rim), cells, total)
    return total


def strip_tile(inner, outer, me_s):
    width = inner.shape[-1]
    is_outer = lax.rem(unit_index(inner.shape), 2) == 1 - me_s
    for k in range(2):
        shift = (width - k * rim) % width
        pieces = [pltpu.roll(strip, shift, 2) if k else strip for strip in (inner, outer)]
        yield k, jnp.where(is_outer, pieces[1], pieces[0])


def pack_kernel(own, to_partner, to_other, to_same):
    _, layers, _, _ = own.shape
    me_s = lax.axis_index("stream")
    for pair, tile in pack_halves(own, 1 - me_s):
        to_partner[pair * layers : (pair + 1) * layers] = tile
    to_partner[2 * layers :] = pack_strip(own, 3 + me_s)
    to_other[...] = pack_strip(own, 7 * me_s)
    to_same[...] = pack_strip(own, 7 * (1 - me_s))


def main_kernel(own, part, main):
    _, layers, _, _ = own.shape
    me_s = lax.axis_index("stream")
    for pair, tile in pack_halves(own, me_s):
        main[pair, pl.ds(me_s * layers, layers)] = tile
        main[pair, pl.ds((1 - me_s) * layers, layers)] = part[pair * layers : (pair + 1) * layers]


def rim_kernel(own, part, own_strip, part_strip, strips):
    _, layers, _, _ = own.shape
    half = layers // 2
    me_s = lax.axis_index("stream")
    for k, tile in strip_tile(pack_strip(own, 4 - me_s), own_strip[...], me_s):
        strips[pl.ds(me_s * layers + k * half, half)] = tile
    for k, tile in strip_tile(part[2 * layers :], part_strip[...], me_s):
        strips[pl.ds((1 - me_s) * layers + k * half, half)] = tile


def unpack(main, strips, me_s):
    width = strips.shape[-1]
    unit = unit_index(strips.shape)
    first = 4 * (1 - me_s)
    in_strip = (unit == first) | (unit == first + 3)
    for f in range(4):
        cells = main[f // 2]
        cells = pltpu.roll(cells, width // 2, 2) if f % 2 else cells
        strip = strips[...]
        strip = pltpu.roll(strip, width - 2 * f * rim, 2) if f else strip
        yield f, jnp.where(in_strip, strip, cells)


def flux_kernel(
    walls, main, a_main, b_main, strips, a_strips, b_strips, weights, keep_ref, send_ref, sums_ref,
    raw, in_h, in_l, prod_h, prod_l, mean, mid_h, mid_l, clark_all, similar_all,
):
    _, layers, rows, width = keep_ref.shape
    both = 2 * layers
    cells = both * rows
    plane_h = weights.at[:cells]
    plane_l = weights.at[cells : 2 * cells]
    span_w = weights.at[2 * cells :, : 2 * width]
    me_s = lax.axis_index("stream")
    me_w = lax.axis_index("wall")
    odd = lax.rem(me_w, 2)
    row_a = pl.multiple_of((1 - odd) * (2 * rows), rows)
    row_b = pl.multiple_of(odd * (2 * rows), rows)
    at_end = (me_w == 0) | (me_w == walls - 1)
    keep_b = jnp.where(at_end, 0.0, 1.0).astype(jnp.float32)

    for f, value in unpack(main, strips, me_s):
        raw[f, :, rows : 2 * rows, :] = value
    for f, value in unpack(a_main, a_strips, me_s):
        raw[f, :, pl.ds(row_a, rows), :] = value
    for f, value in unpack(b_main, b_strips, me_s):
        raw[f, :, pl.ds(row_b, rows), :] = value * keep_b

    def column(t):
        return slice(t * width, (t + 1) * width)

    for block in range(3):
        down = slice(block * cells, (block + 1) * cells)
        for t in range(4):
            value = raw[t, :, block * rows : (block + 1) * rows, :].reshape(cells, width)
            in_h[down, column(t)], in_l[down, column(t)] = halves(value)

    def planes_of(high, low):
        return dot(plane_h[...], high) + dot(plane_l[...], high) + dot(plane_h[...], low)

    def along_span_of(planes):
        high, low = halves(planes)
        tiles = planes.shape[1] // width
        parts = [jnp.concatenate([high[:, column(t)], low[:, column(t)]], axis=1) for t in range(tiles)]
        result = dot(jnp.concatenate(parts, axis=0), span_w[...])
        result = result[:, :width] + result[:, width:]
        return [result[t * cells : (t + 1) * cells].reshape(both, rows, width) for t in range(tiles)]

    for t in range(4):
        mean[t, 0] = jnp.zeros((2 * rows, width), jnp.float32)
        mean[t, both + 1] = jnp.zeros((2 * rows, width), jnp.float32)
    for half in range(2):
        span = slice(half * cells, (half + 2) * cells)
        planes = planes_of(in_h[span, :], in_l[span, :])
        row = lax.rem(lax.broadcasted_iota(jnp.int32, planes.shape, 0), rows)
        if half == 0:
            inside = (me_w > 0) | (row >= reach)
        else:
            inside = (me_w < walls - 1) | (row < rows - reach)
        planes = jnp.where(inside, planes, 0.0)
        for t, value in enumerate(along_span_of(planes)):
            mean[t, 1 : both + 1, half * rows : (half + 1) * rows, :] = value

    for half in range(2):
        span = slice(reach + half * rows, reach + (half + 1) * rows)
        down = slice(half * cells, (half + 1) * cells)
        temperature = raw[3, :, span, :].reshape(cells, width)
        for t in range(3):
            value = raw[t, :, span, :].reshape(cells, width) * temperature
            prod_h[down, column(t)], prod_l[down, column(t)] = halves(value)
    flux = along_span_of(planes_of(prod_h[...], prod_l[...]))

    for half in range(2):
        span = slice(half * rows, (half + 1) * rows)
        down = slice(half * cells, (half + 1) * cells)
        tiles = [mean[t, 1 : both + 1, span, :].reshape(cells, width) for t in range(4)]
        tiles += [tiles[i] * tiles[3] for i in range(3)]
        for t, value in enumerate(tiles):
            mid_h[down, column(t)], mid_l[down, column(t)] = halves(value)
    second = along_span_of(planes_of(mid_h[...], mid_l[...]))

    mid_rows = slice(reach, reach + rows)
    centre, along_span, along_wall, along_stream = [], [], [], []
    for f in range(4):
        here = mean[f, 1 : both + 1, mid_rows, :]
        centre.append(here)
        along_span.append((pltpu.roll(here, width - 1, 2) - pltpu.roll(here, 1, 2)) * 0.5)
        below = mean[f, 1 : both + 1, reach + 1 : reach + rows + 1, :]
        above = mean[f, 1 : both + 1, reach - 1 : reach + rows - 1, :]
        along_wall.append((below - above) * 0.5)
        along_stream.append((mean[f, 2 : both + 2, mid_rows, :] - mean[f, :both, mid_rows, :]) * 0.5)

    lane = lane_index((rows, width))
    useful = lane // (width // 2) == me_s
    table = jnp.zeros((rows, width), jnp.float32)
    for i in range(3):
        exact = flux[i] - centre[i] * centre[3]
        similar = second[4 + i] - second[i] * second[3]
        total = along_span[i] * along_span[3] + along_wall[i] * along_wall[3]
        clark = clark_coef * (total + along_stream[i] * along_stream[3])
        clark_all[i] = clark
        similar_all[i] = similar
        terms = (exact * clark, exact * similar, exact * exact, clark * clark, similar * similar)
        for q, term in enumerate(terms):
            value = jnp.where(useful, jnp.sum(term, axis=0), 0.0)
            table = jnp.where(lane == 3 * q + i, jnp.sum(value, axis=1, keepdims=True), table)
    sums_ref[...] = table

    first = lane_index((layers, rows, width)) < width // 2
    for i in range(3):
        keep_ref[i] = clark_all[i, pl.ds(me_s * layers, layers)]
        keep_ref[3 + i] = similar_all[i, pl.ds(me_s * layers, layers)]
        clark = clark_all[i, pl.ds((1 - me_s) * layers, layers)]
        similar = similar_all[i, pl.ds((1 - me_s) * layers, layers)]
        turn = me_s == 0
        clark = jnp.where(turn, clark, pltpu.roll(clark, width // 2, 2))
        similar = jnp.where(turn, pltpu.roll(similar, width // 2, 2), similar)
        send_ref[i] = jnp.where(first, clark, similar)


def finish_kernel(
    plane_cells, sums, keep, come, clark_model, similar_model, clark_corr, similar_corr
):
    _, layers, rows, width = keep.shape
    me_s = lax.axis_index("stream")
    table = sums[...] / plane_cells
    lane = lane_index((rows, width))
    useful = lane // (width // 2) == me_s
    corr = jnp.zeros((rows, width), jnp.float32)
    for i in range(3):
        cross_c, cross_s, power_e, power_c, power_s = (
            table[:, 3 * q + i : 3 * q + i + 1] for q in range(5)
        )
        packed = come[i]
        turned = pltpu.roll(packed, width // 2, 2)
        clark = jnp.where(useful[None], keep[i], jnp.where(me_s == 0, turned, packed))
        similar = jnp.where(useful[None], keep[3 + i], jnp.where(me_s == 0, packed, turned))
        clark_model[i] = clark / jnp.sqrt(power_c + small_eps)[None]
        similar_model[i] = similar / jnp.sqrt(power_s + small_eps)[None]
        value = cross_c / jnp.sqrt((power_e + small_eps) * (power_c + small_eps))
        corr = jnp.where(lane == i, value, corr)
        value = cross_s / jnp.sqrt((power_e + small_eps) * (power_s + small_eps))
        corr = jnp.where(lane == 8 + i, value, corr)
    square = jnp.concatenate([corr, jnp.zeros((width - rows, width), jnp.float32)], axis=0)
    turned = square.T
    clark_corr[...] = turned[:3, :rows]
    similar_corr[...] = turned[8:11, :rows]


def call(kernel, name, ins, outs, scratch=(), mib=4, hint=None):
    cost = hint and pl.CostEstimate(flops=hint, bytes_accessed=hint // 100, transcendentals=0)
    return pl.pallas_call(
        kernel,
        out_shape=tuple(jax.ShapeDtypeStruct(shape, jnp.float32) for shape in outs),
        in_specs=[pl.BlockSpec(memory_space=pltpu.VMEM)] * len(ins),
        out_specs=tuple(pl.BlockSpec(memory_space=pltpu.VMEM) for _ in outs),
        scratch_shapes=[pltpu.VMEM(shape, dtype) for shape, dtype in scratch],
        compiler_params=pltpu.CompilerParams(vmem_limit_bytes=mib * 1024 * 1024),
        cost_estimate=cost,
        name=name,
    )(*ins)


def shards(fields):
    _, layers, rows, width = fields.shape
    spans = lax.axis_size("span")
    walls = lax.axis_size("wall")
    streams = lax.axis_size("stream")
    both = streams * layers
    cells = both * rows

    def swap(value):
        return lax.ppermute(value, "stream", [(0, 1), (1, 0)])

    def pair_a(value):
        return lax.ppermute(value, "wall", [(w, w ^ 1) for w in range(walls)])

    def pair_b(value):
        return lax.ppermute(
            value, "wall", [(w, min(max(((w + 1) ^ 1) - 1, 0), walls - 1)) for w in range(walls)]
        )

    def place(p, s):
        return (p % spans) * streams + s

    to_other, to_same = [], []
    for p in range(spans):
        to_other += [(place(p, 0), place(p - 1, 1)), (place(p, 1), place(p + 1, 0))]
        to_same += [(place(p, 1), place(p - 1, 1)), (place(p, 0), place(p + 1, 0))]

    strip = (layers // 2, rows, width)
    to_partner, first, second = call(
        pack_kernel, "pack", (fields,), ((2 * layers + layers // 2, rows, width), strip, strip)
    )
    part = swap(to_partner)
    part_strip = lax.ppermute(first, ("span", "stream"), to_other)
    own_strip = lax.ppermute(second, ("span", "stream"), to_same)
    (main,) = call(main_kernel, "main", (fields, part), ((2, both, rows, width),))
    b_main, a_main = pair_b(main), pair_a(main)
    (strips,) = call(rim_kernel, "strips", (fields, part, own_strip, part_strip), ((both, rows, width),), hint=2**35)
    b_strips, a_strips = pair_b(strips), pair_a(strips)

    weights = np.zeros((2 * cells + 2 * width, 2 * cells), ml_dtypes.bfloat16)
    weights[:cells], weights[cells : 2 * cells] = plane_constants(both, rows)
    weights[2 * cells :, : 2 * width] = span_constants(width)
    single, brief = jnp.float32, jnp.bfloat16
    keep, send, sums = call(
        functools.partial(flux_kernel, walls),
        "flux",
        (main, a_main, b_main, strips, a_strips, b_strips, jnp.asarray(weights)),
        ((6, layers, rows, width), (3, layers, rows, width), (rows, width)),
        [
            ((4, both, 3 * rows, width), single),
            ((3 * cells, 4 * width), brief),
            ((3 * cells, 4 * width), brief),
            ((2 * cells, 3 * width), brief),
            ((2 * cells, 3 * width), brief),
            ((4, both + 2, 2 * rows, width), single),
            ((2 * cells, 7 * width), brief),
            ((2 * cells, 7 * width), brief),
            ((3, both, rows, width), single),
            ((3, both, rows, width), single),
        ],
        mib=32,
    )

    group = spans * streams

    def exchange(value, step):
        return lax.ppermute(value, ("span", "stream"), [(g, g ^ step) for g in range(group)])

    sums = (sums + exchange(sums, 1)) + (exchange(sums, 2) + exchange(sums, 3))
    sums, send = lax.optimization_barrier((sums, send))
    come = swap(send)
    step = 4
    while step < group:
        sums = sums + exchange(sums, step)
        step *= 2
    block, corr = (3, layers, rows, width), (3, rows)
    return call(
        functools.partial(finish_kernel, float(layers * width * group)),
        "finish",
        (sums, keep, come),
        (block, block, corr, corr),
    )


def solution(mesh):
    return jax.shard_map(
        shards,
        mesh=mesh,
        in_specs=(P(None, "stream", "wall", "span"),),
        out_specs=(
            P(None, "stream", "wall", "span"),
            P(None, "stream", "wall", "span"),
            P(None, "wall"),
            P(None, "wall"),
        ),
        check_vma=False,
    )
```

```python
import functools
import math

import jax
import jax.numpy as jnp
import ml_dtypes
import numpy as np
from jax import lax
from jax.experimental import pallas as pl
from jax.experimental.pallas import tpu as pltpu
from jax.sharding import PartitionSpec as P

raw_taps = [math.exp(-((k - 8) ** 2) / 18.0) for k in range(17)]
filter_taps = [value / sum(raw_taps) for value in raw_taps]
clark_coef = 9.0
small_eps = 1e-06

reach = 8
rim = 2 * reach


def split_constant(matrix):
    high = matrix.astype(ml_dtypes.bfloat16)
    low = (matrix - high.astype(np.float64)).astype(ml_dtypes.bfloat16)
    return high, low


def band(outs, ins, offset):
    matrix = np.zeros((outs, ins))
    for o in range(outs):
        for i in range(ins):
            k = i - o - offset + reach
            if 0 <= k <= 2 * reach:
                matrix[o, i] = filter_taps[k]
    return matrix


def plane_constants(layers, rows):
    stream = band(layers, layers, 0)
    wall = band(rows, 2 * rows, reach)
    near = np.arange(reach, reach + rows)
    far = np.setdiff1d(np.arange(2 * rows), near)
    parts = [np.arange(rows), np.arange(rows, 2 * rows), near, far]
    blocks = [np.kron(stream, wall[:, part]) for part in parts]
    return split_constant(np.concatenate(blocks, axis=1))


def span_constants(width):
    circle = np.zeros((width, width))
    for o in range(width):
        for k in range(2 * reach + 1):
            circle[(o + k - reach) % width, o] = filter_taps[k]
    high, low = split_constant(circle)
    return np.block([[high, low], [high, np.zeros_like(low)]])


def halves(value):
    high = value.astype(jnp.bfloat16)
    return high, (value - high.astype(jnp.float32)).astype(jnp.bfloat16)


def dot(a, b):
    return lax.dot_general(a, b, (((1,), (0,)), ((), ())), preferred_element_type=jnp.float32)


def lane_index(shape):
    return lax.broadcasted_iota(jnp.int32, shape, len(shape) - 1)


def unit_index(shape):
    return lane_index(shape) // rim


def pack_halves(block, half):
    width = block.shape[-1]
    in_place = lane_index(block.shape[1:]) // (width // 2) == half
    for pair in range(2):
        moved = pltpu.roll(block[2 * pair + 1], width // 2, 2)
        yield pair, jnp.where(in_place, block[2 * pair], moved)


def pack_strip(block, unit):
    _, layers, rows, width = block.shape
    half = layers // 2
    units = unit_index((half, rows, width))
    total = jnp.zeros((half, rows, width), jnp.float32)
    for k in range(2):
        for f in range(4):
            step = 2 * f + k
            cells = block[f, k * half : (k + 1) * half]
            cells = pltpu.roll(cells, step * rim, 2) if step else cells
            total = jnp.where(units == lax.rem(unit + step, width // rim), cells, total)
    return total


def strip_tile(inner, outer, me_s):
    width = inner.shape[-1]
    is_outer = lax.rem(unit_index(inner.shape), 2) == 1 - me_s
    for k in range(2):
        shift = (width - k * rim) % width
        pieces = [pltpu.roll(strip, shift, 2) if k else strip for strip in (inner, outer)]
        yield k, jnp.where(is_outer, pieces[1], pieces[0])


def pack_kernel(own, to_partner, to_other, to_same):
    _, layers, _, _ = own.shape
    me_s = lax.axis_index("stream")
    for pair, tile in pack_halves(own, 1 - me_s):
        to_partner[pair * layers : (pair + 1) * layers] = tile
    to_partner[2 * layers :] = pack_strip(own, 3 + me_s)
    to_other[...] = pack_strip(own, 7 * me_s)
    to_same[...] = pack_strip(own, 7 * (1 - me_s))


def main_kernel(own, part, main):
    _, layers, _, _ = own.shape
    me_s = lax.axis_index("stream")
    for pair, tile in pack_halves(own, me_s):
        main[pair, pl.ds(me_s * layers, layers)] = tile
        main[pair, pl.ds((1 - me_s) * layers, layers)] = part[pair * layers : (pair + 1) * layers]


def rim_kernel(own, part, own_strip, part_strip, strips):
    _, layers, _, _ = own.shape
    half = layers // 2
    me_s = lax.axis_index("stream")
    for k, tile in strip_tile(pack_strip(own, 4 - me_s), own_strip[...], me_s):
        strips[pl.ds(me_s * layers + k * half, half)] = tile
    for k, tile in strip_tile(part[2 * layers :], part_strip[...], me_s):
        strips[pl.ds((1 - me_s) * layers + k * half, half)] = tile


def unpack(main, strips, me_s):
    width = strips.shape[-1]
    unit = unit_index(strips.shape)
    first = 4 * (1 - me_s)
    in_strip = (unit == first) | (unit == first + 3)
    for f in range(4):
        cells = main[f // 2]
        cells = pltpu.roll(cells, width // 2, 2) if f % 2 else cells
        strip = strips[...]
        strip = pltpu.roll(strip, width - 2 * f * rim, 2) if f else strip
        yield f, jnp.where(in_strip, strip, cells)


def column(t, width=128):
    return slice(t * width, (t + 1) * width)


def planes_of(weights, part, high, low):
    cells = weights.shape[1] // 4
    plane_h = weights[:cells, part.start * cells : part.stop * cells]
    plane_l = weights[cells : 2 * cells, part.start * cells : part.stop * cells]
    return dot(plane_h, high) + dot(plane_l, high) + dot(plane_h, low)


def centre_kernel(main, strips, weights, centre, upper, lower, products, in_h, in_l, prod_h, prod_l):
    _, both, rows, width = main.shape
    cells = both * rows
    me_s = lax.axis_index("stream")
    for f, value in unpack(main, strips, me_s):
        centre[f] = value
        in_h[:, column(f)], in_l[:, column(f)] = halves(value.reshape(cells, width))
    for i in range(3):
        value = (centre[i] * centre[3]).reshape(cells, width)
        prod_h[:, column(i)], prod_l[:, column(i)] = halves(value)
    upper[...] = planes_of(weights, slice(1, 2), in_h[...], in_l[...])
    lower[...] = planes_of(weights, slice(0, 1), in_h[...], in_l[...])
    products[...] = planes_of(weights, slice(2, 3), prod_h[...], prod_l[...])


def flux_kernel(
    walls, a_main, b_main, a_strips, b_strips, centre_raw, upper, lower, products, weights,
    keep_ref, send_ref, sums_ref,
    raw, in_h, in_l, prod_h, prod_l, mean, mid_h, mid_l, clark_all, similar_all,
):
    _, layers, rows, width = keep_ref.shape
    both = 2 * layers
    cells = both * rows
    span_w = weights.at[2 * cells :, : 2 * width]
    me_s = lax.axis_index("stream")
    me_w = lax.axis_index("wall")
    odd = lax.rem(me_w, 2)
    at_end = (me_w == 0) | (me_w == walls - 1)
    keep_b = jnp.where(at_end, 0.0, 1.0).astype(jnp.float32)

    for f, value in unpack(a_main, a_strips, me_s):
        raw[1 - odd, f] = value
    for f, value in unpack(b_main, b_strips, me_s):
        raw[odd, f] = value * keep_b

    def along_span_of(planes):
        high, low = halves(planes)
        tiles = planes.shape[1] // width
        parts = [jnp.concatenate([high[:, column(t)], low[:, column(t)]], axis=1) for t in range(tiles)]
        result = dot(jnp.concatenate(parts, axis=0), span_w[...])
        result = result[:, :width] + result[:, width:]
        return [result[t * cells : (t + 1) * cells].reshape(both, rows, width) for t in range(tiles)]

    for t in range(4):
        mean[t, 0] = jnp.zeros((2 * rows, width), jnp.float32)
        mean[t, both + 1] = jnp.zeros((2 * rows, width), jnp.float32)
    for half, partial in enumerate((upper, lower)):
        for f in range(4):
            in_h[:, column(f)], in_l[:, column(f)] = halves(raw[half, f].reshape(cells, width))
        planes = partial[...] + planes_of(weights, slice(half, half + 1), in_h[...], in_l[...])
        row = lax.rem(lax.broadcasted_iota(jnp.int32, planes.shape, 0), rows)
        if half == 0:
            inside = (me_w > 0) | (row >= reach)
        else:
            inside = (me_w < walls - 1) | (row < rows - reach)
        planes = jnp.where(inside, planes, 0.0)
        for t, value in enumerate(along_span_of(planes)):
            mean[t, 1 : both + 1, half * rows : (half + 1) * rows, :] = value

    def around(f):
        return jnp.concatenate([raw[0, f, :, rows - reach :, :], raw[1, f, :, :reach, :]], axis=1)

    temperature = around(3)
    for i in range(3):
        value = (around(i) * temperature).reshape(cells, width)
        prod_h[:, column(i)], prod_l[:, column(i)] = halves(value)
    flux = along_span_of(products[...] + planes_of(weights, slice(3, 4), prod_h[...], prod_l[...]))

    for half in range(2):
        span = slice(half * rows, (half + 1) * rows)
        down = slice(half * cells, (half + 1) * cells)
        tiles = [mean[t, 1 : both + 1, span, :].reshape(cells, width) for t in range(4)]
        tiles += [tiles[i] * tiles[3] for i in range(3)]
        for t, value in enumerate(tiles):
            mid_h[down, column(t)], mid_l[down, column(t)] = halves(value)
    second = along_span_of(planes_of(weights, slice(0, 2), mid_h[...], mid_l[...]))

    mid_rows = slice(reach, reach + rows)
    centre, along_span, along_wall, along_stream = [], [], [], []
    for f in range(4):
        here = mean[f, 1 : both + 1, mid_rows, :]
        centre.append(here)
        along_span.append((pltpu.roll(here, width - 1, 2) - pltpu.roll(here, 1, 2)) * 0.5)
        below = mean[f, 1 : both + 1, reach + 1 : reach + rows + 1, :]
        above = mean[f, 1 : both + 1, reach - 1 : reach + rows - 1, :]
        along_wall.append((below - above) * 0.5)
        along_stream.append((mean[f, 2 : both + 2, mid_rows, :] - mean[f, :both, mid_rows, :]) * 0.5)

    lane = lane_index((rows, width))
    useful = lane // (width // 2) == me_s
    table = jnp.zeros((rows, width), jnp.float32)
    for i in range(3):
        exact = flux[i] - centre[i] * centre[3]
        similar = second[4 + i] - second[i] * second[3]
        total = along_span[i] * along_span[3] + along_wall[i] * along_wall[3]
        clark = clark_coef * (total + along_stream[i] * along_stream[3])
        clark_all[i] = clark
        similar_all[i] = similar
        terms = (exact * clark, exact * similar, exact * exact, clark * clark, similar * similar)
        for q, term in enumerate(terms):
            value = jnp.where(useful, jnp.sum(term, axis=0), 0.0)
            table = jnp.where(lane == 3 * q + i, jnp.sum(value, axis=1, keepdims=True), table)
    sums_ref[...] = table

    first = lane_index((layers, rows, width)) < width // 2
    for i in range(3):
        keep_ref[i] = clark_all[i, pl.ds(me_s * layers, layers)]
        keep_ref[3 + i] = similar_all[i, pl.ds(me_s * layers, layers)]
        clark = clark_all[i, pl.ds((1 - me_s) * layers, layers)]
        similar = similar_all[i, pl.ds((1 - me_s) * layers, layers)]
        turn = me_s == 0
        clark = jnp.where(turn, clark, pltpu.roll(clark, width // 2, 2))
        similar = jnp.where(turn, pltpu.roll(similar, width // 2, 2), similar)
        send_ref[i] = jnp.where(first, clark, similar)


def finish_kernel(
    plane_cells, sums, keep, come, clark_model, similar_model, clark_corr, similar_corr
):
    _, layers, rows, width = keep.shape
    me_s = lax.axis_index("stream")
    table = sums[...] / plane_cells
    lane = lane_index((rows, width))
    useful = lane // (width // 2) == me_s
    corr = jnp.zeros((rows, width), jnp.float32)
    for i in range(3):
        cross_c, cross_s, power_e, power_c, power_s = (
            table[:, 3 * q + i : 3 * q + i + 1] for q in range(5)
        )
        packed = come[i]
        turned = pltpu.roll(packed, width // 2, 2)
        clark = jnp.where(useful[None], keep[i], jnp.where(me_s == 0, turned, packed))
        similar = jnp.where(useful[None], keep[3 + i], jnp.where(me_s == 0, packed, turned))
        clark_model[i] = clark / jnp.sqrt(power_c + small_eps)[None]
        similar_model[i] = similar / jnp.sqrt(power_s + small_eps)[None]
        value = cross_c / jnp.sqrt((power_e + small_eps) * (power_c + small_eps))
        corr = jnp.where(lane == i, value, corr)
        value = cross_s / jnp.sqrt((power_e + small_eps) * (power_s + small_eps))
        corr = jnp.where(lane == 8 + i, value, corr)
    square = jnp.concatenate([corr, jnp.zeros((width - rows, width), jnp.float32)], axis=0)
    turned = square.T
    clark_corr[...] = turned[:3, :rows]
    similar_corr[...] = turned[8:11, :rows]


def call(kernel, name, ins, outs, scratch=(), mib=4, hint=None):
    cost = hint and pl.CostEstimate(flops=hint, bytes_accessed=hint // 100, transcendentals=0)
    return pl.pallas_call(
        kernel,
        out_shape=tuple(jax.ShapeDtypeStruct(shape, jnp.float32) for shape in outs),
        in_specs=[pl.BlockSpec(memory_space=pltpu.VMEM)] * len(ins),
        out_specs=tuple(pl.BlockSpec(memory_space=pltpu.VMEM) for _ in outs),
        scratch_shapes=[pltpu.VMEM(shape, dtype) for shape, dtype in scratch],
        compiler_params=pltpu.CompilerParams(vmem_limit_bytes=mib * 1024 * 1024),
        cost_estimate=cost,
        name=name,
    )(*ins)


def shards(fields):
    _, layers, rows, width = fields.shape
    spans = lax.axis_size("span")
    walls = lax.axis_size("wall")
    streams = lax.axis_size("stream")
    both = streams * layers
    cells = both * rows

    def swap(value):
        return lax.ppermute(value, "stream", [(0, 1), (1, 0)])

    def pair_a(value):
        return lax.ppermute(value, "wall", [(w, w ^ 1) for w in range(walls)])

    def pair_b(value):
        return lax.ppermute(
            value, "wall", [(w, min(max(((w + 1) ^ 1) - 1, 0), walls - 1)) for w in range(walls)]
        )

    def place(p, s):
        return (p % spans) * streams + s

    to_other, to_same = [], []
    for p in range(spans):
        to_other += [(place(p, 0), place(p - 1, 1)), (place(p, 1), place(p + 1, 0))]
        to_same += [(place(p, 1), place(p - 1, 1)), (place(p, 0), place(p + 1, 0))]

    strip = (layers // 2, rows, width)
    to_partner, first, second = call(
        pack_kernel, "pack", (fields,), ((2 * layers + layers // 2, rows, width), strip, strip)
    )
    part = swap(to_partner)
    part_strip = lax.ppermute(first, ("span", "stream"), to_other)
    own_strip = lax.ppermute(second, ("span", "stream"), to_same)
    (main,) = call(main_kernel, "main", (fields, part), ((2, both, rows, width),))
    b_main, a_main = pair_b(main), pair_a(main)
    (strips,) = call(rim_kernel, "strips", (fields, part, own_strip, part_strip), ((both, rows, width),), hint=2**35)
    b_strips, a_strips = pair_b(strips), pair_a(strips)

    matrices = np.zeros((2 * cells + 2 * width, 4 * cells), ml_dtypes.bfloat16)
    matrices[:cells], matrices[cells : 2 * cells] = plane_constants(both, rows)
    matrices[2 * cells :, : 2 * width] = span_constants(width)
    weights = jnp.asarray(matrices)
    single, brief = jnp.float32, jnp.bfloat16
    partial = call(
        centre_kernel,
        "centre",
        (main, strips, weights),
        ((4, both, rows, width), (cells, 4 * width), (cells, 4 * width), (cells, 3 * width)),
        [
            ((cells, 4 * width), brief),
            ((cells, 4 * width), brief),
            ((cells, 3 * width), brief),
            ((cells, 3 * width), brief),
        ],
        mib=16,
        hint=2**31,
    )
    keep, send, sums = call(
        functools.partial(flux_kernel, walls),
        "flux",
        (a_main, b_main, a_strips, b_strips, *partial, weights),
        ((6, layers, rows, width), (3, layers, rows, width), (rows, width)),
        [
            ((2, 4, both, rows, width), single),
            ((cells, 4 * width), brief),
            ((cells, 4 * width), brief),
            ((cells, 3 * width), brief),
            ((cells, 3 * width), brief),
            ((4, both + 2, 2 * rows, width), single),
            ((2 * cells, 7 * width), brief),
            ((2 * cells, 7 * width), brief),
            ((3, both, rows, width), single),
            ((3, both, rows, width), single),
        ],
        mib=24,
    )

    come = swap(send)

    def from_span(value, step):
        return lax.ppermute(value, "span", [(p, p ^ step) for p in range(spans)])

    step = 1
    while step < spans:
        if 2 * step < spans:
            far = from_span(sums, 3 * step) + from_span(sums, 2 * step)
            sums = (sums + from_span(sums, step)) + far
        else:
            sums = sums + from_span(sums, step)
        step *= 4
    sums = sums + swap(sums)
    block, corr = (3, layers, rows, width), (3, rows)
    return call(
        functools.partial(finish_kernel, float(layers * width * spans * streams)),
        "finish",
        (sums, keep, come),
        (block, block, corr, corr),
    )


def solution(mesh):
    return jax.shard_map(
        shards,
        mesh=mesh,
        in_specs=(P(None, "stream", "wall", "span"),),
        out_specs=(
            P(None, "stream", "wall", "span"),
            P(None, "stream", "wall", "span"),
            P(None, "wall"),
            P(None, "wall"),
        ),
        check_vma=False,
    )
```

```python
import functools
import math

import jax
import jax.numpy as jnp
import ml_dtypes
import numpy as np
from jax import lax
from jax.experimental import pallas as pl
from jax.experimental.pallas import tpu as pltpu
from jax.sharding import PartitionSpec as P

raw_taps = [math.exp(-((k - 8) ** 2) / 18.0) for k in range(17)]
filter_taps = [value / sum(raw_taps) for value in raw_taps]
clark_coef = 9.0
small_eps = 1e-06

reach = 8
rim = 2 * reach


def split_constant(matrix):
    high = matrix.astype(ml_dtypes.bfloat16)
    low = (matrix - high.astype(np.float64)).astype(ml_dtypes.bfloat16)
    return high, low


def band(outs, ins, offset):
    matrix = np.zeros((outs, ins))
    for o in range(outs):
        for i in range(ins):
            k = i - o - offset + reach
            if 0 <= k <= 2 * reach:
                matrix[o, i] = filter_taps[k]
    return matrix


def plane_constants(layers, rows):
    stream = band(layers, layers, 0)
    wall = band(rows, 2 * rows, reach)
    near = np.arange(reach, reach + rows)
    far = np.setdiff1d(np.arange(2 * rows), near)
    parts = [np.arange(rows), np.arange(rows, 2 * rows), near, far]
    blocks = [np.kron(stream, wall[:, part]) for part in parts]
    return split_constant(np.concatenate(blocks, axis=1))


def span_constants(width):
    circle = np.zeros((width, width))
    for o in range(width):
        for k in range(2 * reach + 1):
            circle[(o + k - reach) % width, o] = filter_taps[k]
    high, low = split_constant(circle)
    return np.block([[high, low], [high, np.zeros_like(low)]])


def halves(value):
    high = value.astype(jnp.bfloat16)
    return high, (value - high.astype(jnp.float32)).astype(jnp.bfloat16)


def dot(a, b):
    return lax.dot_general(a, b, (((1,), (0,)), ((), ())), preferred_element_type=jnp.float32)


def lane_index(shape):
    return lax.broadcasted_iota(jnp.int32, shape, len(shape) - 1)


def unit_index(shape):
    return lane_index(shape) // rim


def pack_halves(block, half):
    width = block.shape[-1]
    in_place = lane_index(block.shape[1:]) // (width // 2) == half
    for pair in range(2):
        moved = pltpu.roll(block[2 * pair + 1], width // 2, 2)
        yield pair, jnp.where(in_place, block[2 * pair], moved)


def pack_strip(block, unit):
    _, layers, rows, width = block.shape
    half = layers // 2
    units = unit_index((half, rows, width))
    total = jnp.zeros((half, rows, width), jnp.float32)
    for k in range(2):
        for f in range(4):
            step = 2 * f + k
            cells = block[f, k * half : (k + 1) * half]
            cells = pltpu.roll(cells, step * rim, 2) if step else cells
            total = jnp.where(units == lax.rem(unit + step, width // rim), cells, total)
    return total


def strip_tile(inner, outer, me_s):
    width = inner.shape[-1]
    is_outer = lax.rem(unit_index(inner.shape), 2) == 1 - me_s
    for k in range(2):
        shift = (width - k * rim) % width
        pieces = [pltpu.roll(strip, shift, 2) if k else strip for strip in (inner, outer)]
        yield k, jnp.where(is_outer, pieces[1], pieces[0])


def pack_kernel(own, to_partner, to_other, to_same):
    _, layers, _, _ = own.shape
    me_s = lax.axis_index("stream")
    for pair, tile in pack_halves(own, 1 - me_s):
        to_partner[pair * layers : (pair + 1) * layers] = tile
    to_partner[2 * layers :] = pack_strip(own, 3 + me_s)
    to_other[...] = pack_strip(own, 7 * me_s)
    to_same[...] = pack_strip(own, 7 * (1 - me_s))


def main_kernel(own, part, packed):
    _, layers, _, _ = own.shape
    both = 2 * layers
    half = layers // 2
    me_s = lax.axis_index("stream")
    mine, other = me_s * layers, (1 - me_s) * layers
    for pair, tile in pack_halves(own, me_s):
        packed[pl.ds(pair * both + mine, layers)] = tile
        packed[pl.ds(pair * both + other, layers)] = part[pair * layers : (pair + 1) * layers]
    packed[pl.ds(2 * both + me_s * half, half)] = pack_strip(own, 4 - me_s)
    packed[pl.ds(2 * both + (1 - me_s) * half, half)] = part[2 * layers :]


def outer_kernel(own_strip, part_strip, outer):
    half = own_strip.shape[0]
    me_s = lax.axis_index("stream")
    outer[pl.ds(me_s * half, half)] = own_strip[...]
    outer[pl.ds((1 - me_s) * half, half)] = part_strip[...]


def unpack(packed, outer, me_s):
    layers, rows, width = outer.shape
    both = 2 * layers
    half = layers // 2
    unit = unit_index((half, rows, width))
    first = 4 * (1 - me_s)
    in_strip = (unit == first) | (unit == first + 3)
    for s in range(2):
        inner = packed[2 * both + s * half : 2 * both + (s + 1) * half]
        for k, strip in strip_tile(inner, outer[s * half : (s + 1) * half], me_s):
            layer = s * layers + k * half
            for f in range(4):
                start = f // 2 * both + layer
                cells = packed[start : start + half]
                cells = pltpu.roll(cells, width // 2, 2) if f % 2 else cells
                moved = pltpu.roll(strip, width - 2 * f * rim, 2) if f else strip
                yield f, slice(layer, layer + half), jnp.where(in_strip, moved, cells)


def column(t, width=128):
    return slice(t * width, (t + 1) * width)


def planes_of(weights, part, high, low):
    cells = weights.shape[1] // 4
    if part is None:
        along = slice(0, 2 * cells)
    else:
        along = pl.ds(part * cells if isinstance(part, int) else pl.multiple_of(part * cells, cells), cells)
    plane_h, plane_l = weights[:cells, along], weights[cells : 2 * cells, along]
    return dot(plane_h, high) + dot(plane_l, high) + dot(plane_h, low)


def bring(packed, outer, raw, high, low, keep=None):
    rows, width = packed.shape[1:]
    for f, along, value in unpack(packed, outer, lax.axis_index("stream")):
        value = value if keep is None else value * keep
        raw[f, along] = value
        down = slice(along.start * rows, along.stop * rows)
        high[down, column(f)], low[down, column(f)] = halves(value.reshape(-1, width))


def centre_kernel(main, outer, weights, upper, lower, products, centre, in_h, in_l, prod_h, prod_l):
    cells, width = in_h.shape[0], main.shape[-1]
    bring(main, outer, centre, in_h, in_l)
    for i in range(3):
        value = (centre[i] * centre[3]).reshape(cells, width)
        prod_h[:, column(i)], prod_l[:, column(i)] = halves(value)
    upper[...] = planes_of(weights, 1, in_h[...], in_l[...])
    lower[...] = planes_of(weights, 0, in_h[...], in_l[...])
    products[...] = planes_of(weights, 2, prod_h[...], prod_l[...])


def mate_kernel(main, outer, upper, lower, weights, raw, partial, in_h, in_l):
    odd = lax.rem(lax.axis_index("wall"), 2)
    bring(main, outer, raw, in_h, in_l)
    base = jnp.where(odd == 1, upper[...], lower[...])
    partial[...] = base + planes_of(weights, 1 - odd, in_h[...], in_l[...])


def flux_kernel(
    walls, b_main, b_outer, a_raw, a_partial, upper, lower, products, weights,
    keep_ref, send_ref, sums_ref,
    raw, in_h, in_l, prod_h, prod_l, mean, mid_h, mid_l, clark_all, similar_all,
):
    _, layers, rows, width = keep_ref.shape
    both = 2 * layers
    cells = both * rows
    span_w = weights.at[2 * cells :, : 2 * width]
    me_s = lax.axis_index("stream")
    me_w = lax.axis_index("wall")
    odd = lax.rem(me_w, 2)
    at_end = (me_w == 0) | (me_w == walls - 1)
    keep_b = jnp.where(at_end, 0.0, 1.0).astype(jnp.float32)

    bring(b_main, b_outer, raw, in_h, in_l, keep_b)

    def along_span_of(planes):
        high, low = halves(planes)
        tiles = planes.shape[1] // width
        parts = [jnp.concatenate([high[:, column(t)], low[:, column(t)]], axis=1) for t in range(tiles)]
        result = dot(jnp.concatenate(parts, axis=0), span_w[...])
        result = result[:, :width] + result[:, width:]
        return [result[t * cells : (t + 1) * cells].reshape(both, rows, width) for t in range(tiles)]

    for t in range(4):
        mean[t, 0] = jnp.zeros((2 * rows, width), jnp.float32)
        mean[t, both + 1] = jnp.zeros((2 * rows, width), jnp.float32)
    from_b = planes_of(weights, odd, in_h[...], in_l[...])
    from_b += jnp.where(odd == 0, upper[...], lower[...])
    from_a = a_partial[...]
    for half in range(2):
        planes = jnp.where(odd == half, from_b, from_a)
        row = lax.rem(lax.broadcasted_iota(jnp.int32, planes.shape, 0), rows)
        if half == 0:
            inside = (me_w > 0) | (row >= reach)
        else:
            inside = (me_w < walls - 1) | (row < rows - reach)
        planes = jnp.where(inside, planes, 0.0)
        for t, value in enumerate(along_span_of(planes)):
            mean[t, 1 : both + 1, half * rows : (half + 1) * rows, :] = value

    def around(f):
        above = jnp.where(odd == 0, raw[f, :, rows - reach :, :], a_raw[f, :, rows - reach :, :])
        below = jnp.where(odd == 1, raw[f, :, :reach, :], a_raw[f, :, :reach, :])
        return jnp.concatenate([above, below], axis=1)

    temperature = around(3)
    for i in range(3):
        value = (around(i) * temperature).reshape(cells, width)
        prod_h[:, column(i)], prod_l[:, column(i)] = halves(value)
    flux = along_span_of(products[...] + planes_of(weights, 3, prod_h[...], prod_l[...]))

    for half in range(2):
        span = slice(half * rows, (half + 1) * rows)
        down = slice(half * cells, (half + 1) * cells)
        tiles = [mean[t, 1 : both + 1, span, :].reshape(cells, width) for t in range(4)]
        tiles += [tiles[i] * tiles[3] for i in range(3)]
        for t, value in enumerate(tiles):
            mid_h[down, column(t)], mid_l[down, column(t)] = halves(value)
    second = along_span_of(planes_of(weights, None, mid_h[...], mid_l[...]))

    mid_rows = slice(reach, reach + rows)
    centre, along_span, along_wall, along_stream = [], [], [], []
    for f in range(4):
        here = mean[f, 1 : both + 1, mid_rows, :]
        centre.append(here)
        along_span.append((pltpu.roll(here, width - 1, 2) - pltpu.roll(here, 1, 2)) * 0.5)
        below = mean[f, 1 : both + 1, reach + 1 : reach + rows + 1, :]
        above = mean[f, 1 : both + 1, reach - 1 : reach + rows - 1, :]
        along_wall.append((below - above) * 0.5)
        along_stream.append((mean[f, 2 : both + 2, mid_rows, :] - mean[f, :both, mid_rows, :]) * 0.5)

    lane = lane_index((rows, width))
    useful = lane // (width // 2) == me_s
    table = jnp.zeros((rows, width), jnp.float32)
    for i in range(3):
        exact = flux[i] - centre[i] * centre[3]
        similar = second[4 + i] - second[i] * second[3]
        total = along_span[i] * along_span[3] + along_wall[i] * along_wall[3]
        clark = clark_coef * (total + along_stream[i] * along_stream[3])
        clark_all[i] = clark
        similar_all[i] = similar
        terms = (exact * clark, exact * similar, exact * exact, clark * clark, similar * similar)
        for q, term in enumerate(terms):
            value = jnp.where(useful, jnp.sum(term, axis=0), 0.0)
            table = jnp.where(lane == 3 * q + i, jnp.sum(value, axis=1, keepdims=True), table)
    sums_ref[...] = table

    first = lane_index((layers, rows, width)) < width // 2
    for i in range(3):
        keep_ref[i] = clark_all[i, pl.ds(me_s * layers, layers)]
        keep_ref[3 + i] = similar_all[i, pl.ds(me_s * layers, layers)]
        clark = clark_all[i, pl.ds((1 - me_s) * layers, layers)]
        similar = similar_all[i, pl.ds((1 - me_s) * layers, layers)]
        turn = me_s == 0
        clark = jnp.where(turn, clark, pltpu.roll(clark, width // 2, 2))
        similar = jnp.where(turn, pltpu.roll(similar, width // 2, 2), similar)
        send_ref[i] = jnp.where(first, clark, similar)


def finish_kernel(
    plane_cells, sums, keep, come, clark_model, similar_model, clark_corr, similar_corr
):
    _, layers, rows, width = keep.shape
    me_s = lax.axis_index("stream")
    table = sums[...] / plane_cells
    lane = lane_index((rows, width))
    useful = lane // (width // 2) == me_s
    corr = jnp.zeros((rows, width), jnp.float32)
    for i in range(3):
        cross_c, cross_s, power_e, power_c, power_s = (
            table[:, 3 * q + i : 3 * q + i + 1] for q in range(5)
        )
        packed = come[i]
        turned = pltpu.roll(packed, width // 2, 2)
        clark = jnp.where(useful[None], keep[i], jnp.where(me_s == 0, turned, packed))
        similar = jnp.where(useful[None], keep[3 + i], jnp.where(me_s == 0, packed, turned))
        clark_model[i] = clark / jnp.sqrt(power_c + small_eps)[None]
        similar_model[i] = similar / jnp.sqrt(power_s + small_eps)[None]
        value = cross_c / jnp.sqrt((power_e + small_eps) * (power_c + small_eps))
        corr = jnp.where(lane == i, value, corr)
        value = cross_s / jnp.sqrt((power_e + small_eps) * (power_s + small_eps))
        corr = jnp.where(lane == 8 + i, value, corr)
    square = jnp.concatenate([corr, jnp.zeros((width - rows, width), jnp.float32)], axis=0)
    turned = square.T
    clark_corr[...] = turned[:3, :rows]
    similar_corr[...] = turned[8:11, :rows]


def call(kernel, name, ins, outs, scratch=(), mib=4, hint=None):
    cost = hint and pl.CostEstimate(flops=hint, bytes_accessed=0, transcendentals=0)
    return pl.pallas_call(
        kernel,
        out_shape=tuple(jax.ShapeDtypeStruct(shape, jnp.float32) for shape in outs),
        in_specs=[pl.BlockSpec(memory_space=pltpu.VMEM)] * len(ins),
        out_specs=tuple(pl.BlockSpec(memory_space=pltpu.VMEM) for _ in outs),
        scratch_shapes=[pltpu.VMEM(shape, dtype) for shape, dtype in scratch],
        compiler_params=pltpu.CompilerParams(vmem_limit_bytes=mib * 1024 * 1024),
        cost_estimate=cost,
        name=name,
    )(*ins)


def shards(fields):
    _, layers, rows, width = fields.shape
    spans = lax.axis_size("span")
    walls = lax.axis_size("wall")
    streams = lax.axis_size("stream")
    both = streams * layers
    cells = both * rows

    def swap(value):
        return lax.ppermute(value, "stream", [(0, 1), (1, 0)])

    def pair_a(value):
        return lax.ppermute(value, "wall", [(w, w ^ 1) for w in range(walls)])

    def pair_b(value):
        return lax.ppermute(
            value, "wall", [(w, min(max(((w + 1) ^ 1) - 1, 0), walls - 1)) for w in range(walls)]
        )

    def place(p, s):
        return (p % spans) * streams + s

    to_other, to_same = [], []
    for p in range(spans):
        to_other += [(place(p, 0), place(p - 1, 1)), (place(p, 1), place(p + 1, 0))]
        to_same += [(place(p, 1), place(p - 1, 1)), (place(p, 0), place(p + 1, 0))]

    strip = (layers // 2, rows, width)
    to_partner, first, second = call(
        pack_kernel, "pack", (fields,), ((2 * layers + layers // 2, rows, width), strip, strip)
    )
    part = swap(to_partner)
    part_strip = lax.ppermute(first, ("span", "stream"), to_other)
    own_strip = lax.ppermute(second, ("span", "stream"), to_same)
    (main,) = call(main_kernel, "main", (fields, part), ((2 * both + layers, rows, width),))
    b_main, a_main = pair_b(main), pair_a(main)
    (outer,) = call(outer_kernel, "outer", (own_strip, part_strip), ((layers, rows, width),), hint=2**35)
    b_outer, a_outer = pair_b(outer), pair_a(outer)

    matrices = np.zeros((2 * cells + 2 * width, 4 * cells), ml_dtypes.bfloat16)
    matrices[:cells], matrices[cells : 2 * cells] = plane_constants(both, rows)
    matrices[2 * cells :, : 2 * width] = span_constants(width)
    weights = jnp.asarray(matrices)
    single, brief = jnp.float32, jnp.bfloat16
    block = (4, both, rows, width)
    pieces = [((cells, 4 * width), brief), ((cells, 4 * width), brief)]
    upper, lower, products = call(
        centre_kernel,
        "centre",
        (main, outer, weights),
        ((cells, 4 * width), (cells, 4 * width), (cells, 3 * width)),
        [(block, single), *pieces, ((cells, 3 * width), brief), ((cells, 3 * width), brief)],
        mib=16,
        hint=2**29,
    )
    a_raw, a_partial = call(
        mate_kernel,
        "mate",
        (a_main, a_outer, upper, lower, weights),
        (block, (cells, 4 * width)),
        pieces,
        mib=16,
        hint=2**29,
    )
    keep, send, sums = call(
        functools.partial(flux_kernel, walls),
        "flux",
        (b_main, b_outer, a_raw, a_partial, upper, lower, products, weights),
        ((6, layers, rows, width), (3, layers, rows, width), (rows, width)),
        [
            (block, single),
            ((cells, 4 * width), brief),
            ((cells, 4 * width), brief),
            ((cells, 3 * width), brief),
            ((cells, 3 * width), brief),
            ((4, both + 2, 2 * rows, width), single),
            ((2 * cells, 7 * width), brief),
            ((2 * cells, 7 * width), brief),
            ((3, both, rows, width), single),
            ((3, both, rows, width), single),
        ],
        mib=24,
    )

    come = swap(send)

    def from_span(value, step):
        return lax.ppermute(value, "span", [(p, p ^ step) for p in range(spans)])

    step = 1
    while step < spans:
        near = from_span(sums, step)
        if 2 * step < spans:
            far = [from_span(sums, 2 * step), from_span(sums, 3 * step)]
            near, far, come = lax.optimization_barrier((near, far, come))
            sums = (sums + near) + (far[0] + far[1])
        else:
            sums = sums + near
        step *= 4
    sums = sums + swap(sums)
    block, corr = (3, layers, rows, width), (3, rows)
    return call(
        functools.partial(finish_kernel, float(layers * width * spans * streams)),
        "finish",
        (sums, keep, come),
        (block, block, corr, corr),
    )


def solution(mesh):
    return jax.shard_map(
        shards,
        mesh=mesh,
        in_specs=(P(None, "stream", "wall", "span"),),
        out_specs=(
            P(None, "stream", "wall", "span"),
            P(None, "stream", "wall", "span"),
            P(None, "wall"),
            P(None, "wall"),
        ),
        check_vma=False,
    )
```

```python
import functools
import math

import jax
import jax.numpy as jnp
import ml_dtypes
import numpy as np
from jax import lax
from jax.experimental import pallas as pl
from jax.experimental.pallas import tpu as pltpu
from jax.sharding import PartitionSpec as P

raw_taps = [math.exp(-((k - 8) ** 2) / 18.0) for k in range(17)]
filter_taps = [value / sum(raw_taps) for value in raw_taps]
clark_coef = 9.0
small_eps = 1e-06

reach = 8
rim = 2 * reach


def split_constant(matrix):
    high = matrix.astype(ml_dtypes.bfloat16)
    low = (matrix - high.astype(np.float64)).astype(ml_dtypes.bfloat16)
    return high, low


def band(outs, ins, offset):
    matrix = np.zeros((outs, ins))
    for o in range(outs):
        for i in range(ins):
            k = i - o - offset + reach
            if 0 <= k <= 2 * reach:
                matrix[o, i] = filter_taps[k]
    return matrix


def plane_constants(layers, rows):
    stream = band(layers, layers, 0)
    wall = band(rows, 2 * rows, reach)
    near = np.arange(reach, reach + rows)
    far = np.setdiff1d(np.arange(2 * rows), near)
    parts = [np.arange(rows), np.arange(rows, 2 * rows), near, far]
    blocks = [np.kron(stream, wall[:, part]) for part in parts]
    return split_constant(np.concatenate(blocks, axis=1))


def span_constants(width):
    circle = np.zeros((width, width))
    for o in range(width):
        for k in range(2 * reach + 1):
            circle[(o + k - reach) % width, o] = filter_taps[k]
    high, low = split_constant(circle)
    return np.block([[high, low], [high, np.zeros_like(low)]])


def halves(value):
    high = value.astype(jnp.bfloat16)
    return high, (value - high.astype(jnp.float32)).astype(jnp.bfloat16)


def dot(a, b):
    return lax.dot_general(a, b, (((1,), (0,)), ((), ())), preferred_element_type=jnp.float32)


def lane_index(shape):
    return lax.broadcasted_iota(jnp.int32, shape, len(shape) - 1)


def unit_index(shape):
    return lane_index(shape) // rim


def pack_halves(block, half):
    width = block.shape[-1]
    in_place = lane_index(block.shape[1:]) // (width // 2) == half
    for pair in range(2):
        moved = pltpu.roll(block[2 * pair + 1], width // 2, 2)
        yield pair, jnp.where(in_place, block[2 * pair], moved)


def pack_strip(block, unit):
    _, layers, rows, width = block.shape
    half = layers // 2
    units = unit_index((half, rows, width))
    total = jnp.zeros((half, rows, width), jnp.float32)
    for k in range(2):
        for f in range(4):
            step = 2 * f + k
            cells = block[f, k * half : (k + 1) * half]
            cells = pltpu.roll(cells, step * rim, 2) if step else cells
            total = jnp.where(units == lax.rem(unit + step, width // rim), cells, total)
    return total


def strip_tile(inner, outer, me_s):
    width = inner.shape[-1]
    is_outer = lax.rem(unit_index(inner.shape), 2) == 1 - me_s
    for k in range(2):
        shift = (width - k * rim) % width
        pieces = [pltpu.roll(strip, shift, 2) if k else strip for strip in (inner, outer)]
        yield k, jnp.where(is_outer, pieces[1], pieces[0])


def pack_kernel(own, to_partner, to_mine, to_other, to_same):
    _, layers, _, _ = own.shape
    me_s = lax.axis_index("stream")
    for message, half in ((to_partner, 1 - me_s), (to_mine, me_s)):
        for pair, tile in pack_halves(own, half):
            message[pair * layers : (pair + 1) * layers] = tile
        message[2 * layers :] = pack_strip(own, 4 - half)
    to_other[...] = pack_strip(own, 7 * me_s)
    to_same[...] = pack_strip(own, 7 * (1 - me_s))


def outer_kernel(own_strip, part_strip, outer):
    half = own_strip.shape[0]
    outer[:half] = own_strip[...]
    outer[half:] = part_strip[...]


def unpack(mine, part, outer, me_s):
    layers, rows, width = outer.shape
    half = layers // 2
    unit = unit_index((half, rows, width))
    first = 4 * (1 - me_s)
    in_strip = (unit == first) | (unit == first + 3)
    for which, packed in enumerate((mine, part)):
        far = outer[which * half : (which + 1) * half]
        for k, strip in strip_tile(packed[2 * layers :], far, me_s):
            layer = (me_s if which == 0 else 1 - me_s) * layers + k * half
            for f in range(4):
                start = f // 2 * layers + k * half
                cells = packed[start : start + half]
                cells = pltpu.roll(cells, width // 2, 2) if f % 2 else cells
                moved = pltpu.roll(strip, width - 2 * f * rim, 2) if f else strip
                yield f, layer, jnp.where(in_strip, moved, cells)


def column(t, width=128):
    return slice(t * width, (t + 1) * width)


def planes_of(weights, part, high, low):
    cells = weights.shape[1] // 4
    if part is None:
        along = slice(0, 2 * cells)
    else:
        along = pl.ds(part * cells if isinstance(part, int) else pl.multiple_of(part * cells, cells), cells)
    plane_h, plane_l = weights[:cells, along], weights[cells : 2 * cells, along]
    return dot(plane_h, high) + dot(plane_l, high) + dot(plane_h, low)


def bring(mine, part, outer, raw, high, low, keep=None):
    rows, width = outer.shape[1:]
    for f, layer, value in unpack(mine, part, outer, lax.axis_index("stream")):
        count = value.shape[0]
        value = value if keep is None else value * keep
        raw[f, pl.ds(layer, count)] = value
        down = pl.ds(pl.multiple_of(layer * rows, count * rows), count * rows)
        high[down, column(f)], low[down, column(f)] = halves(value.reshape(-1, width))


def centre_kernel(
    mine, part, outer, weights, upper, lower, products, centre, in_h, in_l, prod_h, prod_l
):
    cells, width = in_h.shape[0], outer.shape[-1]
    bring(mine, part, outer, centre, in_h, in_l)
    for i in range(3):
        value = (centre[i] * centre[3]).reshape(cells, width)
        prod_h[:, column(i)], prod_l[:, column(i)] = halves(value)
    upper[...] = planes_of(weights, 1, in_h[...], in_l[...])
    lower[...] = planes_of(weights, 0, in_h[...], in_l[...])
    products[...] = planes_of(weights, 2, prod_h[...], prod_l[...])


def mate_kernel(mine, part, outer, upper, lower, weights, raw, partial, in_h, in_l):
    odd = lax.rem(lax.axis_index("wall"), 2)
    bring(mine, part, outer, raw, in_h, in_l)
    base = jnp.where(odd == 1, upper[...], lower[...])
    partial[...] = base + planes_of(weights, 1 - odd, in_h[...], in_l[...])


def flux_kernel(
    walls, b_mine, b_part, b_outer, a_raw, a_partial, upper, lower, products, weights,
    keep_ref, send_ref, sums_ref,
    raw, in_h, in_l, prod_h, prod_l, mean, mid_h, mid_l, clark_all, similar_all,
):
    _, layers, rows, width = keep_ref.shape
    both = 2 * layers
    cells = both * rows
    span_w = weights.at[2 * cells :, : 2 * width]
    me_s = lax.axis_index("stream")
    me_w = lax.axis_index("wall")
    odd = lax.rem(me_w, 2)
    at_end = (me_w == 0) | (me_w == walls - 1)
    keep_b = jnp.where(at_end, 0.0, 1.0).astype(jnp.float32)

    bring(b_mine, b_part, b_outer, raw, in_h, in_l, keep_b)

    def along_span_of(planes):
        high, low = halves(planes)
        tiles = planes.shape[1] // width
        parts = [jnp.concatenate([high[:, column(t)], low[:, column(t)]], axis=1) for t in range(tiles)]
        result = dot(jnp.concatenate(parts, axis=0), span_w[...])
        result = result[:, :width] + result[:, width:]
        return [result[t * cells : (t + 1) * cells].reshape(both, rows, width) for t in range(tiles)]

    for t in range(4):
        mean[t, 0] = jnp.zeros((2 * rows, width), jnp.float32)
        mean[t, both + 1] = jnp.zeros((2 * rows, width), jnp.float32)
    from_b = planes_of(weights, odd, in_h[...], in_l[...])
    from_b += jnp.where(odd == 0, upper[...], lower[...])
    from_a = a_partial[...]
    for half in range(2):
        planes = jnp.where(odd == half, from_b, from_a)
        row = lax.rem(lax.broadcasted_iota(jnp.int32, planes.shape, 0), rows)
        if half == 0:
            inside = (me_w > 0) | (row >= reach)
        else:
            inside = (me_w < walls - 1) | (row < rows - reach)
        planes = jnp.where(inside, planes, 0.0)
        for t, value in enumerate(along_span_of(planes)):
            mean[t, 1 : both + 1, half * rows : (half + 1) * rows, :] = value

    def around(f):
        above = jnp.where(odd == 0, raw[f, :, rows - reach :, :], a_raw[f, :, rows - reach :, :])
        below = jnp.where(odd == 1, raw[f, :, :reach, :], a_raw[f, :, :reach, :])
        return jnp.concatenate([above, below], axis=1)

    temperature = around(3)
    for i in range(3):
        value = (around(i) * temperature).reshape(cells, width)
        prod_h[:, column(i)], prod_l[:, column(i)] = halves(value)
    flux = along_span_of(products[...] + planes_of(weights, 3, prod_h[...], prod_l[...]))

    for half in range(2):
        span = slice(half * rows, (half + 1) * rows)
        down = slice(half * cells, (half + 1) * cells)
        tiles = [mean[t, 1 : both + 1, span, :].reshape(cells, width) for t in range(4)]
        tiles += [tiles[i] * tiles[3] for i in range(3)]
        for t, value in enumerate(tiles):
            mid_h[down, column(t)], mid_l[down, column(t)] = halves(value)
    second = along_span_of(planes_of(weights, None, mid_h[...], mid_l[...]))

    mid_rows = slice(reach, reach + rows)
    centre, along_span, along_wall, along_stream = [], [], [], []
    for f in range(4):
        here = mean[f, 1 : both + 1, mid_rows, :]
        centre.append(here)
        along_span.append((pltpu.roll(here, width - 1, 2) - pltpu.roll(here, 1, 2)) * 0.5)
        below = mean[f, 1 : both + 1, reach + 1 : reach + rows + 1, :]
        above = mean[f, 1 : both + 1, reach - 1 : reach + rows - 1, :]
        along_wall.append((below - above) * 0.5)
        along_stream.append((mean[f, 2 : both + 2, mid_rows, :] - mean[f, :both, mid_rows, :]) * 0.5)

    lane = lane_index((rows, width))
    useful = lane // (width // 2) == me_s
    table = jnp.zeros((rows, width), jnp.float32)
    for i in range(3):
        exact = flux[i] - centre[i] * centre[3]
        similar = second[4 + i] - second[i] * second[3]
        total = along_span[i] * along_span[3] + along_wall[i] * along_wall[3]
        clark = clark_coef * (total + along_stream[i] * along_stream[3])
        clark_all[i] = clark
        similar_all[i] = similar
        terms = (exact * clark, exact * similar, exact * exact, clark * clark, similar * similar)
        for q, term in enumerate(terms):
            value = jnp.where(useful, jnp.sum(term, axis=0), 0.0)
            table = jnp.where(lane == 3 * q + i, jnp.sum(value, axis=1, keepdims=True), table)
    sums_ref[...] = table

    first = lane_index((layers, rows, width)) < width // 2
    for i in range(3):
        keep_ref[i] = clark_all[i, pl.ds(me_s * layers, layers)]
        keep_ref[3 + i] = similar_all[i, pl.ds(me_s * layers, layers)]
        clark = clark_all[i, pl.ds((1 - me_s) * layers, layers)]
        similar = similar_all[i, pl.ds((1 - me_s) * layers, layers)]
        turn = me_s == 0
        clark = jnp.where(turn, clark, pltpu.roll(clark, width // 2, 2))
        similar = jnp.where(turn, pltpu.roll(similar, width // 2, 2), similar)
        send_ref[i] = jnp.where(first, clark, similar)


def finish_kernel(
    plane_cells, sums, keep, come, clark_model, similar_model, clark_corr, similar_corr
):
    _, layers, rows, width = keep.shape
    me_s = lax.axis_index("stream")
    table = sums[...] / plane_cells
    lane = lane_index((rows, width))
    useful = lane // (width // 2) == me_s
    corr = jnp.zeros((rows, width), jnp.float32)
    for i in range(3):
        cross_c, cross_s, power_e, power_c, power_s = (
            table[:, 3 * q + i : 3 * q + i + 1] for q in range(5)
        )
        packed = come[i]
        turned = pltpu.roll(packed, width // 2, 2)
        clark = jnp.where(useful[None], keep[i], jnp.where(me_s == 0, turned, packed))
        similar = jnp.where(useful[None], keep[3 + i], jnp.where(me_s == 0, packed, turned))
        clark_model[i] = clark / jnp.sqrt(power_c + small_eps)[None]
        similar_model[i] = similar / jnp.sqrt(power_s + small_eps)[None]
        value = cross_c / jnp.sqrt((power_e + small_eps) * (power_c + small_eps))
        corr = jnp.where(lane == i, value, corr)
        value = cross_s / jnp.sqrt((power_e + small_eps) * (power_s + small_eps))
        corr = jnp.where(lane == 8 + i, value, corr)
    square = jnp.concatenate([corr, jnp.zeros((width - rows, width), jnp.float32)], axis=0)
    turned = square.T
    clark_corr[...] = turned[:3, :rows]
    similar_corr[...] = turned[8:11, :rows]


def call(kernel, name, ins, outs, scratch=(), mib=4, hint=None):
    cost = hint and pl.CostEstimate(flops=hint, bytes_accessed=0, transcendentals=0)
    return pl.pallas_call(
        kernel,
        out_shape=tuple(jax.ShapeDtypeStruct(shape, jnp.float32) for shape in outs),
        in_specs=[pl.BlockSpec(memory_space=pltpu.VMEM)] * len(ins),
        out_specs=tuple(pl.BlockSpec(memory_space=pltpu.VMEM) for _ in outs),
        scratch_shapes=[pltpu.VMEM(shape, dtype) for shape, dtype in scratch],
        compiler_params=pltpu.CompilerParams(vmem_limit_bytes=mib * 1024 * 1024),
        cost_estimate=cost,
        name=name,
    )(*ins)


def shards(fields):
    _, layers, rows, width = fields.shape
    spans = lax.axis_size("span")
    walls = lax.axis_size("wall")
    streams = lax.axis_size("stream")
    both = streams * layers
    cells = both * rows

    def swap(value):
        return lax.ppermute(value, "stream", [(0, 1), (1, 0)])

    def pair_a(value):
        return lax.ppermute(value, "wall", [(w, w ^ 1) for w in range(walls)])

    def pair_b(value):
        return lax.ppermute(
            value, "wall", [(w, min(max(((w + 1) ^ 1) - 1, 0), walls - 1)) for w in range(walls)]
        )

    def place(p, s):
        return (p % spans) * streams + s

    to_other, to_same = [], []
    for p in range(spans):
        to_other += [(place(p, 0), place(p - 1, 1)), (place(p, 1), place(p + 1, 0))]
        to_same += [(place(p, 1), place(p - 1, 1)), (place(p, 0), place(p + 1, 0))]

    message, strip = (2 * layers + layers // 2, rows, width), (layers // 2, rows, width)
    to_partner, mine, first, second = call(
        pack_kernel, "pack", (fields,), (message, message, strip, strip)
    )
    part = swap(to_partner)
    part_strip = lax.ppermute(first, ("span", "stream"), to_other)
    own_strip = lax.ppermute(second, ("span", "stream"), to_same)
    part, b_mine, a_mine = lax.optimization_barrier((part, pair_b(mine), pair_a(mine)))
    b_part, a_part = pair_b(part), pair_a(part)
    (outer,) = call(outer_kernel, "outer", (own_strip, part_strip), ((layers, rows, width),), hint=2**35)
    b_outer, a_outer = pair_b(outer), pair_a(outer)

    matrices = np.zeros((2 * cells + 2 * width, 4 * cells), ml_dtypes.bfloat16)
    matrices[:cells], matrices[cells : 2 * cells] = plane_constants(both, rows)
    matrices[2 * cells :, : 2 * width] = span_constants(width)
    weights = jnp.asarray(matrices)
    single, brief = jnp.float32, jnp.bfloat16
    block = (4, both, rows, width)
    pieces = [((cells, 4 * width), brief), ((cells, 4 * width), brief)]
    upper, lower, products = call(
        centre_kernel,
        "centre",
        (mine, part, outer, weights),
        ((cells, 4 * width), (cells, 4 * width), (cells, 3 * width)),
        [(block, single), *pieces, ((cells, 3 * width), brief), ((cells, 3 * width), brief)],
        mib=16,
        hint=2**29,
    )
    a_raw, a_partial = call(
        mate_kernel,
        "mate",
        (a_mine, a_part, a_outer, upper, lower, weights),
        (block, (cells, 4 * width)),
        pieces,
        mib=16,
        hint=2**29,
    )
    keep, send, sums = call(
        functools.partial(flux_kernel, walls),
        "flux",
        (b_mine, b_part, b_outer, a_raw, a_partial, upper, lower, products, weights),
        ((6, layers, rows, width), (3, layers, rows, width), (rows, width)),
        [
            (block, single),
            ((cells, 4 * width), brief),
            ((cells, 4 * width), brief),
            ((cells, 3 * width), brief),
            ((cells, 3 * width), brief),
            ((4, both + 2, 2 * rows, width), single),
            ((2 * cells, 7 * width), brief),
            ((2 * cells, 7 * width), brief),
            ((3, both, rows, width), single),
            ((3, both, rows, width), single),
        ],
        mib=24,
    )

    come = swap(send)

    def from_span(value, step):
        return lax.ppermute(value, "span", [(p, p ^ step) for p in range(spans)])

    step = 1
    while step < spans:
        if 2 * step < spans:
            far = from_span(sums, 3 * step) + from_span(sums, 2 * step)
            sums = (sums + from_span(sums, step)) + far
        else:
            sums = sums + from_span(sums, step)
        step *= 4
    sums = sums + swap(sums)
    block, corr = (3, layers, rows, width), (3, rows)
    return call(
        functools.partial(finish_kernel, float(layers * width * spans * streams)),
        "finish",
        (sums, keep, come),
        (block, block, corr, corr),
    )


def solution(mesh):
    return jax.shard_map(
        shards,
        mesh=mesh,
        in_specs=(P(None, "stream", "wall", "span"),),
        out_specs=(
            P(None, "stream", "wall", "span"),
            P(None, "stream", "wall", "span"),
            P(None, "wall"),
            P(None, "wall"),
        ),
        check_vma=False,
    )
```

```python
import functools
import math

import jax
import jax.numpy as jnp
import ml_dtypes
import numpy as np
from jax import lax
from jax.experimental import pallas as pl
from jax.experimental.pallas import tpu as pltpu
from jax.sharding import PartitionSpec as P

raw_taps = [math.exp(-((k - 8) ** 2) / 18.0) for k in range(17)]
filter_taps = [value / sum(raw_taps) for value in raw_taps]
clark_coef = 9.0
small_eps = 1e-06

reach = 8
rim = 2 * reach


def split_constant(matrix):
    high = matrix.astype(ml_dtypes.bfloat16)
    low = (matrix - high.astype(np.float64)).astype(ml_dtypes.bfloat16)
    return high, low


def band(outs, ins, offset):
    matrix = np.zeros((outs, ins))
    for o in range(outs):
        for i in range(ins):
            k = i - o - offset + reach
            if 0 <= k <= 2 * reach:
                matrix[o, i] = filter_taps[k]
    return matrix


def plane_constants(layers, rows):
    stream = band(layers, layers, 0)
    wall = band(rows, 2 * rows, reach)
    near = np.arange(reach, reach + rows)
    far = np.setdiff1d(np.arange(2 * rows), near)
    parts = [np.arange(rows), np.arange(rows, 2 * rows), near, far]
    blocks = [np.kron(stream, wall[:, part]) for part in parts]
    return split_constant(np.concatenate(blocks, axis=1))


def span_constants(width):
    circle = np.zeros((width, width))
    for o in range(width):
        for k in range(2 * reach + 1):
            circle[(o + k - reach) % width, o] = filter_taps[k]
    high, low = split_constant(circle)
    return np.block([[high, low], [high, np.zeros_like(low)]])


def halves(value):
    high = value.astype(jnp.bfloat16)
    return high, (value - high.astype(jnp.float32)).astype(jnp.bfloat16)


def dot(a, b):
    return lax.dot_general(a, b, (((1,), (0,)), ((), ())), preferred_element_type=jnp.float32)


def lane_index(shape):
    return lax.broadcasted_iota(jnp.int32, shape, len(shape) - 1)


def unit_index(shape):
    return lane_index(shape) // rim


def pack_halves(block, half):
    width = block.shape[-1]
    in_place = lane_index(block.shape[1:]) // (width // 2) == half
    for pair in range(2):
        moved = pltpu.roll(block[2 * pair + 1], width // 2, 2)
        yield pair, jnp.where(in_place, block[2 * pair], moved)


def pack_strip(block, unit):
    _, layers, rows, width = block.shape
    half = layers // 2
    units = unit_index((half, rows, width))
    total = jnp.zeros((half, rows, width), jnp.float32)
    for k in range(2):
        for f in range(4):
            step = 2 * f + k
            cells = block[f, k * half : (k + 1) * half]
            cells = pltpu.roll(cells, step * rim, 2) if step else cells
            total = jnp.where(units == lax.rem(unit + step, width // rim), cells, total)
    return total


def strip_tile(inner, outer, me_s):
    width = inner.shape[-1]
    is_outer = lax.rem(unit_index(inner.shape), 2) == 1 - me_s
    for k in range(2):
        shift = (width - k * rim) % width
        pieces = [pltpu.roll(strip, shift, 2) if k else strip for strip in (inner, outer)]
        yield k, jnp.where(is_outer, pieces[1], pieces[0])


def pack_kernel(own, to_partner, tiles, to_other, to_same):
    _, layers, _, _ = own.shape
    me_s = lax.axis_index("stream")
    for message, half in ((to_partner, 1 - me_s), (tiles, me_s)):
        for pair, tile in pack_halves(own, half):
            message[pair * layers : (pair + 1) * layers] = tile
    to_partner[2 * layers :] = pack_strip(own, 3 + me_s)
    to_other[...] = pack_strip(own, 7 * me_s)
    to_same[...] = pack_strip(own, 7 * (1 - me_s))


def join_kernel(own, tiles, part, own_strip, part_strip, whole, rest):
    count, half = tiles.shape[0], own_strip.shape[0]
    inner = pack_strip(own, 4 - lax.axis_index("stream"))
    whole[:count] = tiles[...]
    for message, start in ((whole, count), (rest, 0)):
        start += count + half
        message[start - count - half : start] = part[...]
        message[start : start + half] = inner
        message[start + half : start + 2 * half] = own_strip[...]
        message[start + 2 * half :] = part_strip[...]


def unpack(tiles, rest, me_s):
    count, rows, width = tiles.shape
    layers, half = count // 2, count // 4
    unit = unit_index((half, rows, width))
    first = 4 * (1 - me_s)
    in_strip = (unit == first) | (unit == first + 3)
    strips = [rest[count + i * half : count + (i + 1) * half] for i in range(4)]
    for which, packed, near, far in ((0, tiles, strips[1], strips[2]), (1, rest, strips[0], strips[3])):
        for k, strip in strip_tile(near, far, me_s):
            layer = (me_s if which == 0 else 1 - me_s) * layers + k * half
            for f in range(4):
                start = f // 2 * layers + k * half
                cells = packed[start : start + half]
                cells = pltpu.roll(cells, width // 2, 2) if f % 2 else cells
                moved = pltpu.roll(strip, width - 2 * f * rim, 2) if f else strip
                yield f, layer, jnp.where(in_strip, moved, cells)


def column(t, width=128):
    return slice(t * width, (t + 1) * width)


def planes_of(weights, part, high, low):
    cells = weights.shape[1] // 4
    if part is None:
        along = slice(0, 2 * cells)
    else:
        along = pl.ds(part * cells if isinstance(part, int) else pl.multiple_of(part * cells, cells), cells)
    plane_h, plane_l = weights[:cells, along], weights[cells : 2 * cells, along]
    return dot(plane_h, high) + dot(plane_l, high) + dot(plane_h, low)


def bring(tiles, rest, raw, high, low, keep=None):
    rows, width = tiles.shape[1:]
    for f, layer, value in unpack(tiles, rest, lax.axis_index("stream")):
        count = value.shape[0]
        value = value if keep is None else value * keep
        raw[f, pl.ds(layer, count)] = value
        down = pl.ds(pl.multiple_of(layer * rows, count * rows), count * rows)
        high[down, column(f)], low[down, column(f)] = halves(value.reshape(-1, width))


def centre_kernel(
    tiles, rest, weights, upper, lower, products, centre, in_h, in_l, prod_h, prod_l
):
    cells, width = in_h.shape[0], tiles.shape[-1]
    bring(tiles, rest, centre, in_h, in_l)
    for i in range(3):
        value = (centre[i] * centre[3]).reshape(cells, width)
        prod_h[:, column(i)], prod_l[:, column(i)] = halves(value)
    upper[...] = planes_of(weights, 1, in_h[...], in_l[...])
    lower[...] = planes_of(weights, 0, in_h[...], in_l[...])
    products[...] = planes_of(weights, 2, prod_h[...], prod_l[...])


def mate_kernel(whole, upper, lower, weights, raw, partial, in_h, in_l):
    odd = lax.rem(lax.axis_index("wall"), 2)
    count = raw.shape[1]
    bring(whole.at[:count], whole.at[count:], raw, in_h, in_l)
    base = jnp.where(odd == 1, upper[...], lower[...])
    partial[...] = base + planes_of(weights, 1 - odd, in_h[...], in_l[...])


def flux_kernel(
    walls, b_tiles, b_rest, a_raw, a_partial, upper, lower, products, weights,
    keep_ref, send_ref, sums_ref,
    raw, in_h, in_l, prod_h, prod_l, mean, mid_h, mid_l, clark_all, similar_all,
):
    _, layers, rows, width = keep_ref.shape
    both = 2 * layers
    cells = both * rows
    span_w = weights.at[2 * cells :, : 2 * width]
    me_s = lax.axis_index("stream")
    me_w = lax.axis_index("wall")
    odd = lax.rem(me_w, 2)
    at_end = (me_w == 0) | (me_w == walls - 1)
    keep_b = jnp.where(at_end, 0.0, 1.0).astype(jnp.float32)

    bring(b_tiles, b_rest, raw, in_h, in_l, keep_b)

    def along_span_of(planes):
        high, low = halves(planes)
        tiles = planes.shape[1] // width
        parts = [jnp.concatenate([high[:, column(t)], low[:, column(t)]], axis=1) for t in range(tiles)]
        result = dot(jnp.concatenate(parts, axis=0), span_w[...])
        result = result[:, :width] + result[:, width:]
        return [result[t * cells : (t + 1) * cells].reshape(both, rows, width) for t in range(tiles)]

    for t in range(4):
        mean[t, 0] = jnp.zeros((2 * rows, width), jnp.float32)
        mean[t, both + 1] = jnp.zeros((2 * rows, width), jnp.float32)
    from_b = planes_of(weights, odd, in_h[...], in_l[...])
    from_b += jnp.where(odd == 0, upper[...], lower[...])
    from_a = a_partial[...]
    for half in range(2):
        planes = jnp.where(odd == half, from_b, from_a)
        row = lax.rem(lax.broadcasted_iota(jnp.int32, planes.shape, 0), rows)
        if half == 0:
            inside = (me_w > 0) | (row >= reach)
        else:
            inside = (me_w < walls - 1) | (row < rows - reach)
        planes = jnp.where(inside, planes, 0.0)
        for t, value in enumerate(along_span_of(planes)):
            mean[t, 1 : both + 1, half * rows : (half + 1) * rows, :] = value

    def around(f):
        above = jnp.where(odd == 0, raw[f, :, rows - reach :, :], a_raw[f, :, rows - reach :, :])
        below = jnp.where(odd == 1, raw[f, :, :reach, :], a_raw[f, :, :reach, :])
        return jnp.concatenate([above, below], axis=1)

    temperature = around(3)
    for i in range(3):
        value = (around(i) * temperature).reshape(cells, width)
        prod_h[:, column(i)], prod_l[:, column(i)] = halves(value)
    flux = along_span_of(products[...] + planes_of(weights, 3, prod_h[...], prod_l[...]))

    for half in range(2):
        span = slice(half * rows, (half + 1) * rows)
        down = slice(half * cells, (half + 1) * cells)
        tiles = [mean[t, 1 : both + 1, span, :].reshape(cells, width) for t in range(4)]
        tiles += [tiles[i] * tiles[3] for i in range(3)]
        for t, value in enumerate(tiles):
            mid_h[down, column(t)], mid_l[down, column(t)] = halves(value)
    second = along_span_of(planes_of(weights, None, mid_h[...], mid_l[...]))

    mid_rows = slice(reach, reach + rows)
    centre, along_span, along_wall, along_stream = [], [], [], []
    for f in range(4):
        here = mean[f, 1 : both + 1, mid_rows, :]
        centre.append(here)
        along_span.append((pltpu.roll(here, width - 1, 2) - pltpu.roll(here, 1, 2)) * 0.5)
        below = mean[f, 1 : both + 1, reach + 1 : reach + rows + 1, :]
        above = mean[f, 1 : both + 1, reach - 1 : reach + rows - 1, :]
        along_wall.append((below - above) * 0.5)
        along_stream.append((mean[f, 2 : both + 2, mid_rows, :] - mean[f, :both, mid_rows, :]) * 0.5)

    lane = lane_index((rows, width))
    useful = lane // (width // 2) == me_s
    table = jnp.zeros((rows, width), jnp.float32)
    for i in range(3):
        exact = flux[i] - centre[i] * centre[3]
        similar = second[4 + i] - second[i] * second[3]
        total = along_span[i] * along_span[3] + along_wall[i] * along_wall[3]
        clark = clark_coef * (total + along_stream[i] * along_stream[3])
        clark_all[i] = clark
        similar_all[i] = similar
        terms = (exact * clark, exact * similar, exact * exact, clark * clark, similar * similar)
        for q, term in enumerate(terms):
            value = jnp.where(useful, jnp.sum(term, axis=0), 0.0)
            table = jnp.where(lane == 3 * q + i, jnp.sum(value, axis=1, keepdims=True), table)
    sums_ref[...] = table

    first = lane_index((layers, rows, width)) < width // 2
    for i in range(3):
        keep_ref[i] = clark_all[i, pl.ds(me_s * layers, layers)]
        keep_ref[3 + i] = similar_all[i, pl.ds(me_s * layers, layers)]
        clark = clark_all[i, pl.ds((1 - me_s) * layers, layers)]
        similar = similar_all[i, pl.ds((1 - me_s) * layers, layers)]
        turn = me_s == 0
        clark = jnp.where(turn, clark, pltpu.roll(clark, width // 2, 2))
        similar = jnp.where(turn, pltpu.roll(similar, width // 2, 2), similar)
        send_ref[i] = jnp.where(first, clark, similar)


def finish_kernel(
    plane_cells, sums, keep, come, clark_model, similar_model, clark_corr, similar_corr
):
    _, layers, rows, width = keep.shape
    me_s = lax.axis_index("stream")
    table = sums[...] / plane_cells
    lane = lane_index((rows, width))
    useful = lane // (width // 2) == me_s
    corr = jnp.zeros((rows, width), jnp.float32)
    for i in range(3):
        cross_c, cross_s, power_e, power_c, power_s = (
            table[:, 3 * q + i : 3 * q + i + 1] for q in range(5)
        )
        packed = come[i]
        turned = pltpu.roll(packed, width // 2, 2)
        clark = jnp.where(useful[None], keep[i], jnp.where(me_s == 0, turned, packed))
        similar = jnp.where(useful[None], keep[3 + i], jnp.where(me_s == 0, packed, turned))
        clark_model[i] = clark / jnp.sqrt(power_c + small_eps)[None]
        similar_model[i] = similar / jnp.sqrt(power_s + small_eps)[None]
        value = cross_c / jnp.sqrt((power_e + small_eps) * (power_c + small_eps))
        corr = jnp.where(lane == i, value, corr)
        value = cross_s / jnp.sqrt((power_e + small_eps) * (power_s + small_eps))
        corr = jnp.where(lane == 8 + i, value, corr)
    square = jnp.concatenate([corr, jnp.zeros((width - rows, width), jnp.float32)], axis=0)
    turned = square.T
    clark_corr[...] = turned[:3, :rows]
    similar_corr[...] = turned[8:11, :rows]


def call(kernel, name, ins, outs, scratch=(), mib=4, hint=None):
    cost = hint and pl.CostEstimate(flops=hint, bytes_accessed=0, transcendentals=0)
    return pl.pallas_call(
        kernel,
        out_shape=tuple(jax.ShapeDtypeStruct(shape, jnp.float32) for shape in outs),
        in_specs=[pl.BlockSpec(memory_space=pltpu.VMEM)] * len(ins),
        out_specs=tuple(pl.BlockSpec(memory_space=pltpu.VMEM) for _ in outs),
        scratch_shapes=[pltpu.VMEM(shape, dtype) for shape, dtype in scratch],
        compiler_params=pltpu.CompilerParams(vmem_limit_bytes=mib * 1024 * 1024),
        cost_estimate=cost,
        name=name,
    )(*ins)


def shards(fields):
    _, layers, rows, width = fields.shape
    spans = lax.axis_size("span")
    walls = lax.axis_size("wall")
    streams = lax.axis_size("stream")
    both = streams * layers
    cells = both * rows

    def swap(value):
        return lax.ppermute(value, "stream", [(0, 1), (1, 0)])

    def pair_a(value):
        return lax.ppermute(value, "wall", [(w, w ^ 1) for w in range(walls)])

    def pair_b(value):
        return lax.ppermute(
            value, "wall", [(w, min(max(((w + 1) ^ 1) - 1, 0), walls - 1)) for w in range(walls)]
        )

    def place(p, s):
        return (p % spans) * streams + s

    to_other, to_same = [], []
    for p in range(spans):
        to_other += [(place(p, 0), place(p - 1, 1)), (place(p, 1), place(p + 1, 0))]
        to_same += [(place(p, 1), place(p - 1, 1)), (place(p, 0), place(p + 1, 0))]

    message, strip = (both + layers // 2, rows, width), (layers // 2, rows, width)
    to_partner, own_tiles, first, second = call(
        pack_kernel, "pack", (fields,), (message, (both, rows, width), strip, strip)
    )
    part = swap(to_partner)
    part_strip = lax.ppermute(first, ("span", "stream"), to_other)
    own_strip = lax.ppermute(second, ("span", "stream"), to_same)
    tiles, b_tiles = lax.optimization_barrier((own_tiles, pair_b(own_tiles)))
    whole, rest = call(
        join_kernel,
        "join",
        (fields, own_tiles, part, own_strip, part_strip),
        ((2 * both + 2 * layers, rows, width), (both + 2 * layers, rows, width)),
        hint=2**35,
    )
    b_rest, a_whole = pair_b(rest), pair_a(whole)

    matrices = np.zeros((2 * cells + 2 * width, 4 * cells), ml_dtypes.bfloat16)
    matrices[:cells], matrices[cells : 2 * cells] = plane_constants(both, rows)
    matrices[2 * cells :, : 2 * width] = span_constants(width)
    weights = jnp.asarray(matrices)
    single, brief = jnp.float32, jnp.bfloat16
    block = (4, both, rows, width)
    pieces = [((cells, 4 * width), brief), ((cells, 4 * width), brief)]
    upper, lower, products = call(
        centre_kernel,
        "centre",
        (tiles, rest, weights),
        ((cells, 4 * width), (cells, 4 * width), (cells, 3 * width)),
        [(block, single), *pieces, ((cells, 3 * width), brief), ((cells, 3 * width), brief)],
        mib=16,
        hint=2**35,
    )
    a_raw, a_partial = call(
        mate_kernel,
        "mate",
        (a_whole, upper, lower, weights),
        (block, (cells, 4 * width)),
        pieces,
        mib=16,
        hint=2**29,
    )
    keep, send, sums = call(
        functools.partial(flux_kernel, walls),
        "flux",
        (b_tiles, b_rest, a_raw, a_partial, upper, lower, products, weights),
        ((6, layers, rows, width), (3, layers, rows, width), (rows, width)),
        [
            (block, single),
            ((cells, 4 * width), brief),
            ((cells, 4 * width), brief),
            ((cells, 3 * width), brief),
            ((cells, 3 * width), brief),
            ((4, both + 2, 2 * rows, width), single),
            ((2 * cells, 7 * width), brief),
            ((2 * cells, 7 * width), brief),
            ((3, both, rows, width), single),
            ((3, both, rows, width), single),
        ],
        mib=24,
    )

    come = swap(send)

    def from_span(value, step):
        return lax.ppermute(value, "span", [(p, p ^ step) for p in range(spans)])

    step = 1
    while step < spans:
        if 2 * step < spans:
            far = from_span(sums, 3 * step) + from_span(sums, 2 * step)
            sums = (sums + from_span(sums, step)) + far
        else:
            sums = sums + from_span(sums, step)
        step *= 4
    sums = sums + swap(sums)
    block, corr = (3, layers, rows, width), (3, rows)
    return call(
        functools.partial(finish_kernel, float(layers * width * spans * streams)),
        "finish",
        (sums, keep, come),
        (block, block, corr, corr),
    )


def solution(mesh):
    return jax.shard_map(
        shards,
        mesh=mesh,
        in_specs=(P(None, "stream", "wall", "span"),),
        out_specs=(
            P(None, "stream", "wall", "span"),
            P(None, "stream", "wall", "span"),
            P(None, "wall"),
            P(None, "wall"),
        ),
        check_vma=False,
    )
```

```python
import functools
import math

import jax
import jax.numpy as jnp
import ml_dtypes
import numpy as np
from jax import lax
from jax.experimental import pallas as pl
from jax.experimental.pallas import tpu as pltpu
from jax.sharding import PartitionSpec as P

raw_taps = [math.exp(-((k - 8) ** 2) / 18.0) for k in range(17)]
filter_taps = [value / sum(raw_taps) for value in raw_taps]
clark_coef = 9.0
small_eps = 1e-06

reach = 8
rim = 2 * reach


def split_constant(matrix):
    high = matrix.astype(ml_dtypes.bfloat16)
    low = (matrix - high.astype(np.float64)).astype(ml_dtypes.bfloat16)
    return high, low


def band(outs, ins, offset):
    matrix = np.zeros((outs, ins))
    for o in range(outs):
        for i in range(ins):
            k = i - o - offset + reach
            if 0 <= k <= 2 * reach:
                matrix[o, i] = filter_taps[k]
    return matrix


def plane_constants(layers, rows):
    stream = band(layers, layers, 0)
    wall = band(rows, 2 * rows, reach)
    near = np.arange(reach, reach + rows)
    far = np.setdiff1d(np.arange(2 * rows), near)
    parts = [np.arange(rows), np.arange(rows, 2 * rows), near, far]
    blocks = [np.kron(stream, wall[:, part]) for part in parts]
    return split_constant(np.concatenate(blocks, axis=1))


def span_constants(width):
    circle = np.zeros((width, width))
    for o in range(width):
        for k in range(2 * reach + 1):
            circle[(o + k - reach) % width, o] = filter_taps[k]
    high, low = split_constant(circle)
    return np.block([[high, low], [high, np.zeros_like(low)]])


def halves(value):
    high = value.astype(jnp.bfloat16)
    return high, (value - high.astype(jnp.float32)).astype(jnp.bfloat16)


def dot(a, b):
    return lax.dot_general(a, b, (((1,), (0,)), ((), ())), preferred_element_type=jnp.float32)


def lane_index(shape):
    return lax.broadcasted_iota(jnp.int32, shape, len(shape) - 1)


def unit_index(shape):
    return lane_index(shape) // rim


def pack_halves(block, half):
    width = block.shape[-1]
    in_place = lane_index(block.shape[1:]) // (width // 2) == half
    for pair in range(2):
        moved = pltpu.roll(block[2 * pair + 1], width // 2, 2)
        yield pair, jnp.where(in_place, block[2 * pair], moved)


def pack_strip(block, unit):
    _, layers, rows, width = block.shape
    half = layers // 2
    units = unit_index((half, rows, width))
    total = jnp.zeros((half, rows, width), jnp.float32)
    for k in range(2):
        for f in range(4):
            step = 2 * f + k
            cells = block[f, k * half : (k + 1) * half]
            cells = pltpu.roll(cells, step * rim, 2) if step else cells
            total = jnp.where(units == lax.rem(unit + step, width // rim), cells, total)
    return total


def strip_tile(inner, outer, me_s):
    width = inner.shape[-1]
    is_outer = lax.rem(unit_index(inner.shape), 2) == 1 - me_s
    for k in range(2):
        shift = (width - k * rim) % width
        pieces = [pltpu.roll(strip, shift, 2) if k else strip for strip in (inner, outer)]
        yield k, jnp.where(is_outer, pieces[1], pieces[0])


def pack_kernel(own, to_partner, to_other, to_same):
    _, layers, _, _ = own.shape
    me_s = lax.axis_index("stream")
    for pair, tile in pack_halves(own, 1 - me_s):
        to_partner[pair * layers : (pair + 1) * layers] = tile
    to_partner[2 * layers :] = pack_strip(own, 3 + me_s)
    to_other[...] = pack_strip(own, 7 * me_s)
    to_same[...] = pack_strip(own, 7 * (1 - me_s))


def main_kernel(own, part, packed):
    _, layers, _, _ = own.shape
    both = 2 * layers
    half = layers // 2
    me_s = lax.axis_index("stream")
    mine, other = me_s * layers, (1 - me_s) * layers
    for pair, tile in pack_halves(own, me_s):
        packed[pl.ds(pair * both + mine, layers)] = tile
        packed[pl.ds(pair * both + other, layers)] = part[pair * layers : (pair + 1) * layers]
    packed[pl.ds(2 * both + me_s * half, half)] = pack_strip(own, 4 - me_s)
    packed[pl.ds(2 * both + (1 - me_s) * half, half)] = part[2 * layers :]


def outer_kernel(own_strip, part_strip, outer):
    half = own_strip.shape[0]
    me_s = lax.axis_index("stream")
    outer[pl.ds(me_s * half, half)] = own_strip[...]
    outer[pl.ds((1 - me_s) * half, half)] = part_strip[...]


def unpack(packed, outer, me_s):
    layers, rows, width = outer.shape
    both = 2 * layers
    half = layers // 2
    unit = unit_index((half, rows, width))
    first = 4 * (1 - me_s)
    in_strip = (unit == first) | (unit == first + 3)
    for s in range(2):
        inner = packed[2 * both + s * half : 2 * both + (s + 1) * half]
        for k, strip in strip_tile(inner, outer[s * half : (s + 1) * half], me_s):
            layer = s * layers + k * half
            for f in range(4):
                start = f // 2 * both + layer
                cells = packed[start : start + half]
                cells = pltpu.roll(cells, width // 2, 2) if f % 2 else cells
                moved = pltpu.roll(strip, width - 2 * f * rim, 2) if f else strip
                yield f, slice(layer, layer + half), jnp.where(in_strip, moved, cells)


def column(t, width=128):
    return slice(t * width, (t + 1) * width)


def planes_of(weights, part, high, low):
    cells = weights.shape[1] // 4
    along = pl.ds(part * cells if isinstance(part, int) else pl.multiple_of(part * cells, cells), cells)
    plane_h, plane_l = weights[:cells, along], weights[cells : 2 * cells, along]
    return dot(plane_h, high) + dot(plane_l, high) + dot(plane_h, low)


def bring(packed, outer, raw, high, low, keep=None):
    rows, width = packed.shape[1:]
    for f, along, value in unpack(packed, outer, lax.axis_index("stream")):
        value = value if keep is None else value * keep
        raw[f, along] = value
        down = slice(along.start * rows, along.stop * rows)
        high[down, column(f)], low[down, column(f)] = halves(value.reshape(-1, width))


def centre_kernel(main, outer, weights, upper, lower, products, centre, in_h, in_l, prod_h, prod_l):
    cells, width = in_h.shape[0], main.shape[-1]
    bring(main, outer, centre, in_h, in_l)
    for i in range(3):
        value = (centre[i] * centre[3]).reshape(cells, width)
        prod_h[:, column(i)], prod_l[:, column(i)] = halves(value)
    upper[...] = planes_of(weights, 1, in_h[...], in_l[...])
    lower[...] = planes_of(weights, 0, in_h[...], in_l[...])
    products[...] = planes_of(weights, 2, prod_h[...], prod_l[...])


def span_pass(weights, planes, both):
    cells = planes.shape[0]
    rows = cells // both
    width = 128
    span_w = weights[2 * cells :, : 2 * width]
    high, low = halves(planes)
    tiles = planes.shape[1] // width
    parts = [jnp.concatenate([high[:, column(t)], low[:, column(t)]], axis=1) for t in range(tiles)]
    result = dot(jnp.concatenate(parts, axis=0), span_w)
    result = result[:, :width] + result[:, width:]
    return [result[t * cells : (t + 1) * cells].reshape(both, rows, width) for t in range(tiles)]


def second_input(means, high, low):
    tiles = means + [means[i] * means[3] for i in range(3)]
    for t, value in enumerate(tiles):
        high[:, column(t)], low[:, column(t)] = halves(value.reshape(-1, value.shape[-1]))


def mate_kernel(
    main, outer, upper, lower, weights, raw, mean, second, in_h, in_l, mid_h, mid_l
):
    both = raw.shape[1]
    odd = lax.rem(lax.axis_index("wall"), 2)
    bring(main, outer, raw, in_h, in_l)
    planes = jnp.where(odd == 1, upper[...], lower[...])
    planes = planes + planes_of(weights, 1 - odd, in_h[...], in_l[...])
    means = span_pass(weights, planes, both)
    for t, value in enumerate(means):
        mean[t] = value
    second_input(means, mid_h, mid_l)
    second[...] = planes_of(weights, 1 - odd, mid_h[...], mid_l[...])


def flux_kernel(
    walls, b_main, b_outer, a_raw, a_mean, a_second, upper, lower, products, weights,
    keep_ref, send_ref, sums_ref,
    raw, in_h, in_l, prod_h, prod_l, mean, mid_h, mid_l, clark_all, similar_all,
):
    _, layers, rows, width = keep_ref.shape
    both = 2 * layers
    cells = both * rows
    me_s = lax.axis_index("stream")
    me_w = lax.axis_index("wall")
    odd = lax.rem(me_w, 2)
    at_end = (me_w == 0) | (me_w == walls - 1)
    keep_b = jnp.where(at_end, 0.0, 1.0).astype(jnp.float32)

    bring(b_main, b_outer, raw, in_h, in_l, keep_b)

    for t in range(4):
        mean[t, 0] = jnp.zeros((2 * rows, width), jnp.float32)
        mean[t, both + 1] = jnp.zeros((2 * rows, width), jnp.float32)
    planes = jnp.where(odd == 0, upper[...], lower[...])
    planes = planes + planes_of(weights, odd, in_h[...], in_l[...])
    row = lax.rem(lax.broadcasted_iota(jnp.int32, planes.shape, 0), rows)
    inside = (row < reach) == (odd == 1)
    planes = jnp.where(jnp.logical_or(inside, jnp.logical_not(at_end)), planes, 0.0)
    means = span_pass(weights, planes, both)
    rows_b = pl.ds(pl.multiple_of(odd * rows, rows), rows)
    rows_a = pl.ds(pl.multiple_of((1 - odd) * rows, rows), rows)
    for t, value in enumerate(means):
        mean[t, 1 : both + 1, rows_b, :] = value
        mean[t, 1 : both + 1, rows_a, :] = a_mean[t]
    second_input(means, mid_h, mid_l)
    second = span_pass(weights, a_second[...] + planes_of(weights, odd, mid_h[...], mid_l[...]), both)

    def around(f):
        above = jnp.where(odd == 0, raw[f, :, rows - reach :, :], a_raw[f, :, rows - reach :, :])
        below = jnp.where(odd == 1, raw[f, :, :reach, :], a_raw[f, :, :reach, :])
        return jnp.concatenate([above, below], axis=1)

    temperature = around(3)
    for i in range(3):
        value = (around(i) * temperature).reshape(cells, width)
        prod_h[:, column(i)], prod_l[:, column(i)] = halves(value)
    flux = span_pass(weights, products[...] + planes_of(weights, 3, prod_h[...], prod_l[...]), both)

    mid_rows = slice(reach, reach + rows)
    centre, along_span, along_wall, along_stream = [], [], [], []
    for f in range(4):
        here = mean[f, 1 : both + 1, mid_rows, :]
        centre.append(here)
        along_span.append((pltpu.roll(here, width - 1, 2) - pltpu.roll(here, 1, 2)) * 0.5)
        below = mean[f, 1 : both + 1, reach + 1 : reach + rows + 1, :]
        above = mean[f, 1 : both + 1, reach - 1 : reach + rows - 1, :]
        along_wall.append((below - above) * 0.5)
        along_stream.append((mean[f, 2 : both + 2, mid_rows, :] - mean[f, :both, mid_rows, :]) * 0.5)

    lane = lane_index((rows, width))
    useful = lane // (width // 2) == me_s
    table = jnp.zeros((rows, width), jnp.float32)
    for i in range(3):
        exact = flux[i] - centre[i] * centre[3]
        similar = second[4 + i] - second[i] * second[3]
        total = along_span[i] * along_span[3] + along_wall[i] * along_wall[3]
        clark = clark_coef * (total + along_stream[i] * along_stream[3])
        clark_all[i] = clark
        similar_all[i] = similar
        terms = (exact * clark, exact * similar, exact * exact, clark * clark, similar * similar)
        for q, term in enumerate(terms):
            value = jnp.where(useful, jnp.sum(term, axis=0), 0.0)
            table = jnp.where(lane == 3 * q + i, jnp.sum(value, axis=1, keepdims=True), table)
    sums_ref[...] = table

    first = lane_index((layers, rows, width)) < width // 2
    for i in range(3):
        keep_ref[i] = clark_all[i, pl.ds(me_s * layers, layers)]
        keep_ref[3 + i] = similar_all[i, pl.ds(me_s * layers, layers)]
        clark = clark_all[i, pl.ds((1 - me_s) * layers, layers)]
        similar = similar_all[i, pl.ds((1 - me_s) * layers, layers)]
        turn = me_s == 0
        clark = jnp.where(turn, clark, pltpu.roll(clark, width // 2, 2))
        similar = jnp.where(turn, pltpu.roll(similar, width // 2, 2), similar)
        send_ref[i] = jnp.where(first, clark, similar)


def finish_kernel(
    plane_cells, sums, keep, come, clark_model, similar_model, clark_corr, similar_corr
):
    _, layers, rows, width = keep.shape
    me_s = lax.axis_index("stream")
    table = sums[...] / plane_cells
    lane = lane_index((rows, width))
    useful = lane // (width // 2) == me_s
    corr = jnp.zeros((rows, width), jnp.float32)
    for i in range(3):
        cross_c, cross_s, power_e, power_c, power_s = (
            table[:, 3 * q + i : 3 * q + i + 1] for q in range(5)
        )
        packed = come[i]
        turned = pltpu.roll(packed, width // 2, 2)
        clark = jnp.where(useful[None], keep[i], jnp.where(me_s == 0, turned, packed))
        similar = jnp.where(useful[None], keep[3 + i], jnp.where(me_s == 0, packed, turned))
        clark_model[i] = clark / jnp.sqrt(power_c + small_eps)[None]
        similar_model[i] = similar / jnp.sqrt(power_s + small_eps)[None]
        value = cross_c / jnp.sqrt((power_e + small_eps) * (power_c + small_eps))
        corr = jnp.where(lane == i, value, corr)
        value = cross_s / jnp.sqrt((power_e + small_eps) * (power_s + small_eps))
        corr = jnp.where(lane == 8 + i, value, corr)
    square = jnp.concatenate([corr, jnp.zeros((width - rows, width), jnp.float32)], axis=0)
    turned = square.T
    clark_corr[...] = turned[:3, :rows]
    similar_corr[...] = turned[8:11, :rows]


def call(kernel, name, ins, outs, scratch=(), mib=4, hint=None):
    cost = hint and pl.CostEstimate(flops=hint, bytes_accessed=0, transcendentals=0)
    return pl.pallas_call(
        kernel,
        out_shape=tuple(jax.ShapeDtypeStruct(shape, jnp.float32) for shape in outs),
        in_specs=[pl.BlockSpec(memory_space=pltpu.VMEM)] * len(ins),
        out_specs=tuple(pl.BlockSpec(memory_space=pltpu.VMEM) for _ in outs),
        scratch_shapes=[pltpu.VMEM(shape, dtype) for shape, dtype in scratch],
        compiler_params=pltpu.CompilerParams(vmem_limit_bytes=mib * 1024 * 1024),
        cost_estimate=cost,
        name=name,
    )(*ins)


def shards(fields):
    _, layers, rows, width = fields.shape
    spans = lax.axis_size("span")
    walls = lax.axis_size("wall")
    streams = lax.axis_size("stream")
    both = streams * layers
    cells = both * rows

    def swap(value):
        return lax.ppermute(value, "stream", [(0, 1), (1, 0)])

    def pair_a(value):
        return lax.ppermute(value, "wall", [(w, w ^ 1) for w in range(walls)])

    def pair_b(value):
        return lax.ppermute(
            value, "wall", [(w, min(max(((w + 1) ^ 1) - 1, 0), walls - 1)) for w in range(walls)]
        )

    def place(p, s):
        return (p % spans) * streams + s

    to_other, to_same = [], []
    for p in range(spans):
        to_other += [(place(p, 0), place(p - 1, 1)), (place(p, 1), place(p + 1, 0))]
        to_same += [(place(p, 1), place(p - 1, 1)), (place(p, 0), place(p + 1, 0))]

    strip = (layers // 2, rows, width)
    to_partner, first, second = call(
        pack_kernel, "pack", (fields,), ((2 * layers + layers // 2, rows, width), strip, strip)
    )
    part = swap(to_partner)
    part_strip = lax.ppermute(first, ("span", "stream"), to_other)
    own_strip = lax.ppermute(second, ("span", "stream"), to_same)
    (main,) = call(main_kernel, "main", (fields, part), ((2 * both + layers, rows, width),))
    a_main, b_main = pair_a(main), pair_b(main)
    (outer,) = call(outer_kernel, "outer", (own_strip, part_strip), ((layers, rows, width),), hint=2**35)
    a_outer, b_outer = pair_a(outer), pair_b(outer)

    matrices = np.zeros((2 * cells + 2 * width, 4 * cells), ml_dtypes.bfloat16)
    matrices[:cells], matrices[cells : 2 * cells] = plane_constants(both, rows)
    matrices[2 * cells :, : 2 * width] = span_constants(width)
    weights = jnp.asarray(matrices)
    single, brief = jnp.float32, jnp.bfloat16
    block = (4, both, rows, width)
    pieces = [((cells, 4 * width), brief), ((cells, 4 * width), brief)]
    upper, lower, products = call(
        centre_kernel,
        "centre",
        (main, outer, weights),
        ((cells, 4 * width), (cells, 4 * width), (cells, 3 * width)),
        [(block, single), *pieces, ((cells, 3 * width), brief), ((cells, 3 * width), brief)],
        mib=16,
        hint=2**29,
    )
    a_raw, a_mean, a_second = call(
        mate_kernel,
        "mate",
        (a_main, a_outer, upper, lower, weights),
        (block, block, (cells, 7 * width)),
        [*pieces, ((cells, 7 * width), brief), ((cells, 7 * width), brief)],
        mib=16,
        hint=2**29,
    )
    keep, send, sums = call(
        functools.partial(flux_kernel, walls),
        "flux",
        (b_main, b_outer, a_raw, a_mean, a_second, upper, lower, products, weights),
        ((6, layers, rows, width), (3, layers, rows, width), (rows, width)),
        [
            (block, single),
            ((cells, 4 * width), brief),
            ((cells, 4 * width), brief),
            ((cells, 3 * width), brief),
            ((cells, 3 * width), brief),
            ((4, both + 2, 2 * rows, width), single),
            ((cells, 7 * width), brief),
            ((cells, 7 * width), brief),
            ((3, both, rows, width), single),
            ((3, both, rows, width), single),
        ],
        mib=24,
    )

    come = swap(send)

    def from_span(value, step):
        return lax.ppermute(value, "span", [(p, p ^ step) for p in range(spans)])

    step = 1
    while step < spans:
        if 2 * step < spans:
            far = from_span(sums, 3 * step) + from_span(sums, 2 * step)
            sums = (sums + from_span(sums, step)) + far
        else:
            sums = sums + from_span(sums, step)
        step *= 4
    sums = sums + swap(sums)
    block, corr = (3, layers, rows, width), (3, rows)
    return call(
        functools.partial(finish_kernel, float(layers * width * spans * streams)),
        "finish",
        (sums, keep, come),
        (block, block, corr, corr),
    )


def solution(mesh):
    return jax.shard_map(
        shards,
        mesh=mesh,
        in_specs=(P(None, "stream", "wall", "span"),),
        out_specs=(
            P(None, "stream", "wall", "span"),
            P(None, "stream", "wall", "span"),
            P(None, "wall"),
            P(None, "wall"),
        ),
        check_vma=False,
    )
```

```python
import functools
import math

import jax
import jax.numpy as jnp
import ml_dtypes
import numpy as np
from jax import lax
from jax.experimental import pallas as pl
from jax.experimental.pallas import tpu as pltpu
from jax.sharding import PartitionSpec as P

raw_taps = [math.exp(-((k - 8) ** 2) / 18.0) for k in range(17)]
filter_taps = [value / sum(raw_taps) for value in raw_taps]
clark_coef = 9.0
small_eps = 1e-06

reach = 8
rim = 2 * reach


def split_constant(matrix):
    high = matrix.astype(ml_dtypes.bfloat16)
    low = (matrix - high.astype(np.float64)).astype(ml_dtypes.bfloat16)
    return high, low


def band(outs, ins, offset):
    matrix = np.zeros((outs, ins))
    for o in range(outs):
        for i in range(ins):
            k = i - o - offset + reach
            if 0 <= k <= 2 * reach:
                matrix[o, i] = filter_taps[k]
    return matrix


def plane_constants(layers, rows):
    stream = band(layers, layers, 0)
    wall = band(rows, 2 * rows, reach)
    near = np.arange(reach, reach + rows)
    far = np.setdiff1d(np.arange(2 * rows), near)
    parts = [np.arange(rows), np.arange(rows, 2 * rows), near, far]
    blocks = [np.kron(stream, wall[:, part]) for part in parts]
    return split_constant(np.concatenate(blocks, axis=1))


def span_constants(width):
    circle = np.zeros((width, width))
    for o in range(width):
        for k in range(2 * reach + 1):
            circle[(o + k - reach) % width, o] = filter_taps[k]
    high, low = split_constant(circle)
    return np.block([[high, low], [high, np.zeros_like(low)]])


def halves(value):
    high = value.astype(jnp.bfloat16)
    return high, (value - high.astype(jnp.float32)).astype(jnp.bfloat16)


def dot(a, b):
    return lax.dot_general(a, b, (((1,), (0,)), ((), ())), preferred_element_type=jnp.float32)


def lane_index(shape):
    return lax.broadcasted_iota(jnp.int32, shape, len(shape) - 1)


def unit_index(shape):
    return lane_index(shape) // rim


def pack_halves(block, half):
    width = block.shape[-1]
    in_place = lane_index(block.shape[1:]) // (width // 2) == half
    for pair in range(2):
        moved = pltpu.roll(block[2 * pair + 1], width // 2, 2)
        yield pair, jnp.where(in_place, block[2 * pair], moved)


def pack_strip(block, unit):
    _, layers, rows, width = block.shape
    half = layers // 2
    units = unit_index((half, rows, width))
    total = jnp.zeros((half, rows, width), jnp.float32)
    for k in range(2):
        for f in range(4):
            step = 2 * f + k
            cells = block[f, k * half : (k + 1) * half]
            cells = pltpu.roll(cells, step * rim, 2) if step else cells
            total = jnp.where(units == lax.rem(unit + step, width // rim), cells, total)
    return total


def strip_tile(inner, outer, me_s):
    width = inner.shape[-1]
    is_outer = lax.rem(unit_index(inner.shape), 2) == 1 - me_s
    for k in range(2):
        shift = (width - k * rim) % width
        pieces = [pltpu.roll(strip, shift, 2) if k else strip for strip in (inner, outer)]
        yield k, jnp.where(is_outer, pieces[1], pieces[0])


def pack_kernel(own, to_partner, to_mine, to_other, to_same):
    _, layers, _, _ = own.shape
    me_s = lax.axis_index("stream")
    for message, half in ((to_partner, 1 - me_s), (to_mine, me_s)):
        for pair, tile in pack_halves(own, half):
            message[pair * layers : (pair + 1) * layers] = tile
        message[2 * layers :] = pack_strip(own, 4 - half)
    to_other[...] = pack_strip(own, 7 * me_s)
    to_same[...] = pack_strip(own, 7 * (1 - me_s))


def outer_kernel(own_strip, part_strip, outer):
    half = own_strip.shape[0]
    outer[:half] = own_strip[...]
    outer[half:] = part_strip[...]


def join_kernel(mine, part, whole):
    count = mine.shape[0]
    whole[:count] = mine[...]
    whole[count:] = part[...]


def unpack(mine, part, outer, me_s):
    layers, rows, width = outer.shape
    half = layers // 2
    unit = unit_index((half, rows, width))
    first = 4 * (1 - me_s)
    in_strip = (unit == first) | (unit == first + 3)
    for which, packed in enumerate((mine, part)):
        far = outer[which * half : (which + 1) * half]
        for k, strip in strip_tile(packed[2 * layers :], far, me_s):
            layer = (me_s if which == 0 else 1 - me_s) * layers + k * half
            for f in range(4):
                start = f // 2 * layers + k * half
                cells = packed[start : start + half]
                cells = pltpu.roll(cells, width // 2, 2) if f % 2 else cells
                moved = pltpu.roll(strip, width - 2 * f * rim, 2) if f else strip
                yield f, layer, jnp.where(in_strip, moved, cells)


def column(t, width=128):
    return slice(t * width, (t + 1) * width)


def planes_of(weights, part, high, low):
    cells = weights.shape[1] // 4
    along = pl.ds(part * cells if isinstance(part, int) else pl.multiple_of(part * cells, cells), cells)
    plane_h, plane_l = weights[:cells, along], weights[cells : 2 * cells, along]
    return dot(plane_h, high) + dot(plane_l, high) + dot(plane_h, low)


def bring(mine, part, outer, raw, high, low, keep=None):
    rows, width = outer.shape[1:]
    for f, layer, value in unpack(mine, part, outer, lax.axis_index("stream")):
        count = value.shape[0]
        value = value if keep is None else value * keep
        raw[f, pl.ds(layer, count)] = value
        down = pl.ds(pl.multiple_of(layer * rows, count * rows), count * rows)
        high[down, column(f)], low[down, column(f)] = halves(value.reshape(-1, width))


def centre_kernel(mine, part, outer, weights, upper, lower, products, centre, in_h, in_l, prod_h, prod_l):
    cells, width = in_h.shape[0], outer.shape[-1]
    bring(mine, part, outer, centre, in_h, in_l)
    for i in range(3):
        value = (centre[i] * centre[3]).reshape(cells, width)
        prod_h[:, column(i)], prod_l[:, column(i)] = halves(value)
    upper[...] = planes_of(weights, 1, in_h[...], in_l[...])
    lower[...] = planes_of(weights, 0, in_h[...], in_l[...])
    products[...] = planes_of(weights, 2, prod_h[...], prod_l[...])


def span_pass(weights, planes, both):
    cells = planes.shape[0]
    rows = cells // both
    width = 128
    span_w = weights[2 * cells :, : 2 * width]
    high, low = halves(planes)
    tiles = planes.shape[1] // width
    parts = [jnp.concatenate([high[:, column(t)], low[:, column(t)]], axis=1) for t in range(tiles)]
    result = dot(jnp.concatenate(parts, axis=0), span_w)
    result = result[:, :width] + result[:, width:]
    return [result[t * cells : (t + 1) * cells].reshape(both, rows, width) for t in range(tiles)]


def second_input(means, high, low):
    tiles = means + [means[i] * means[3] for i in range(3)]
    for t, value in enumerate(tiles):
        high[:, column(t)], low[:, column(t)] = halves(value.reshape(-1, value.shape[-1]))


def mate_kernel(
    whole, outer, upper, lower, weights, raw, mean, second, in_h, in_l, mid_h, mid_l
):
    both = raw.shape[1]
    odd = lax.rem(lax.axis_index("wall"), 2)
    count = whole.shape[0] // 2
    bring(whole.at[:count], whole.at[count:], outer, raw, in_h, in_l)
    planes = jnp.where(odd == 1, upper[...], lower[...])
    planes = planes + planes_of(weights, 1 - odd, in_h[...], in_l[...])
    means = span_pass(weights, planes, both)
    for t, value in enumerate(means):
        mean[t] = value
    second_input(means, mid_h, mid_l)
    second[...] = planes_of(weights, 1 - odd, mid_h[...], mid_l[...])


def flux_kernel(
    walls, b_mine, b_part, b_outer, a_raw, a_mean, a_second, upper, lower, products, weights,
    keep_ref, send_ref, sums_ref,
    raw, in_h, in_l, prod_h, prod_l, mean, mid_h, mid_l, clark_all, similar_all,
):
    _, layers, rows, width = keep_ref.shape
    both = 2 * layers
    cells = both * rows
    me_s = lax.axis_index("stream")
    me_w = lax.axis_index("wall")
    odd = lax.rem(me_w, 2)
    at_end = (me_w == 0) | (me_w == walls - 1)
    keep_b = jnp.where(at_end, 0.0, 1.0).astype(jnp.float32)

    bring(b_mine, b_part, b_outer, raw, in_h, in_l, keep_b)

    for t in range(4):
        mean[t, 0] = jnp.zeros((2 * rows, width), jnp.float32)
        mean[t, both + 1] = jnp.zeros((2 * rows, width), jnp.float32)
    planes = jnp.where(odd == 0, upper[...], lower[...])
    planes = planes + planes_of(weights, odd, in_h[...], in_l[...])
    row = lax.rem(lax.broadcasted_iota(jnp.int32, planes.shape, 0), rows)
    inside = (row < reach) == (odd == 1)
    planes = jnp.where(jnp.logical_or(inside, jnp.logical_not(at_end)), planes, 0.0)
    means = span_pass(weights, planes, both)
    rows_b = pl.ds(pl.multiple_of(odd * rows, rows), rows)
    rows_a = pl.ds(pl.multiple_of((1 - odd) * rows, rows), rows)
    for t, value in enumerate(means):
        mean[t, 1 : both + 1, rows_b, :] = value
        mean[t, 1 : both + 1, rows_a, :] = a_mean[t]
    second_input(means, mid_h, mid_l)
    second = span_pass(weights, a_second[...] + planes_of(weights, odd, mid_h[...], mid_l[...]), both)

    def around(f):
        above = jnp.where(odd == 0, raw[f, :, rows - reach :, :], a_raw[f, :, rows - reach :, :])
        below = jnp.where(odd == 1, raw[f, :, :reach, :], a_raw[f, :, :reach, :])
        return jnp.concatenate([above, below], axis=1)

    temperature = around(3)
    for i in range(3):
        value = (around(i) * temperature).reshape(cells, width)
        prod_h[:, column(i)], prod_l[:, column(i)] = halves(value)
    flux = span_pass(weights, products[...] + planes_of(weights, 3, prod_h[...], prod_l[...]), both)

    mid_rows = slice(reach, reach + rows)
    centre, along_span, along_wall, along_stream = [], [], [], []
    for f in range(4):
        here = mean[f, 1 : both + 1, mid_rows, :]
        centre.append(here)
        along_span.append((pltpu.roll(here, width - 1, 2) - pltpu.roll(here, 1, 2)) * 0.5)
        below = mean[f, 1 : both + 1, reach + 1 : reach + rows + 1, :]
        above = mean[f, 1 : both + 1, reach - 1 : reach + rows - 1, :]
        along_wall.append((below - above) * 0.5)
        along_stream.append((mean[f, 2 : both + 2, mid_rows, :] - mean[f, :both, mid_rows, :]) * 0.5)

    lane = lane_index((rows, width))
    useful = lane // (width // 2) == me_s
    table = jnp.zeros((rows, width), jnp.float32)
    for i in range(3):
        exact = flux[i] - centre[i] * centre[3]
        similar = second[4 + i] - second[i] * second[3]
        total = along_span[i] * along_span[3] + along_wall[i] * along_wall[3]
        clark = clark_coef * (total + along_stream[i] * along_stream[3])
        clark_all[i] = clark
        similar_all[i] = similar
        terms = (exact * clark, exact * similar, exact * exact, clark * clark, similar * similar)
        for q, term in enumerate(terms):
            value = jnp.where(useful, jnp.sum(term, axis=0), 0.0)
            table = jnp.where(lane == 3 * q + i, jnp.sum(value, axis=1, keepdims=True), table)
    sums_ref[...] = table

    first = lane_index((layers, rows, width)) < width // 2
    for i in range(3):
        keep_ref[i] = clark_all[i, pl.ds(me_s * layers, layers)]
        keep_ref[3 + i] = similar_all[i, pl.ds(me_s * layers, layers)]
        clark = clark_all[i, pl.ds((1 - me_s) * layers, layers)]
        similar = similar_all[i, pl.ds((1 - me_s) * layers, layers)]
        turn = me_s == 0
        clark = jnp.where(turn, clark, pltpu.roll(clark, width // 2, 2))
        similar = jnp.where(turn, pltpu.roll(similar, width // 2, 2), similar)
        send_ref[i] = jnp.where(first, clark, similar)


def finish_kernel(
    plane_cells, sums, keep, come, clark_model, similar_model, clark_corr, similar_corr
):
    _, layers, rows, width = keep.shape
    me_s = lax.axis_index("stream")
    table = sums[...] / plane_cells
    lane = lane_index((rows, width))
    useful = lane // (width // 2) == me_s
    corr = jnp.zeros((rows, width), jnp.float32)
    for i in range(3):
        cross_c, cross_s, power_e, power_c, power_s = (
            table[:, 3 * q + i : 3 * q + i + 1] for q in range(5)
        )
        packed = come[i]
        turned = pltpu.roll(packed, width // 2, 2)
        clark = jnp.where(useful[None], keep[i], jnp.where(me_s == 0, turned, packed))
        similar = jnp.where(useful[None], keep[3 + i], jnp.where(me_s == 0, packed, turned))
        clark_model[i] = clark / jnp.sqrt(power_c + small_eps)[None]
        similar_model[i] = similar / jnp.sqrt(power_s + small_eps)[None]
        value = cross_c / jnp.sqrt((power_e + small_eps) * (power_c + small_eps))
        corr = jnp.where(lane == i, value, corr)
        value = cross_s / jnp.sqrt((power_e + small_eps) * (power_s + small_eps))
        corr = jnp.where(lane == 8 + i, value, corr)
    square = jnp.concatenate([corr, jnp.zeros((width - rows, width), jnp.float32)], axis=0)
    turned = square.T
    clark_corr[...] = turned[:3, :rows]
    similar_corr[...] = turned[8:11, :rows]


def call(kernel, name, ins, outs, scratch=(), mib=4, hint=None):
    cost = hint and pl.CostEstimate(flops=hint, bytes_accessed=0, transcendentals=0)
    return pl.pallas_call(
        kernel,
        out_shape=tuple(jax.ShapeDtypeStruct(shape, jnp.float32) for shape in outs),
        in_specs=[pl.BlockSpec(memory_space=pltpu.VMEM)] * len(ins),
        out_specs=tuple(pl.BlockSpec(memory_space=pltpu.VMEM) for _ in outs),
        scratch_shapes=[pltpu.VMEM(shape, dtype) for shape, dtype in scratch],
        compiler_params=pltpu.CompilerParams(vmem_limit_bytes=mib * 1024 * 1024),
        cost_estimate=cost,
        name=name,
    )(*ins)


def shards(fields):
    _, layers, rows, width = fields.shape
    spans = lax.axis_size("span")
    walls = lax.axis_size("wall")
    streams = lax.axis_size("stream")
    both = streams * layers
    cells = both * rows

    def swap(value):
        return lax.ppermute(value, "stream", [(0, 1), (1, 0)])

    def pair_a(value):
        return lax.ppermute(value, "wall", [(w, w ^ 1) for w in range(walls)])

    def pair_b(value):
        return lax.ppermute(
            value, "wall", [(w, min(max(((w + 1) ^ 1) - 1, 0), walls - 1)) for w in range(walls)]
        )

    def place(p, s):
        return (p % spans) * streams + s

    to_other, to_same = [], []
    for p in range(spans):
        to_other += [(place(p, 0), place(p - 1, 1)), (place(p, 1), place(p + 1, 0))]
        to_same += [(place(p, 1), place(p - 1, 1)), (place(p, 0), place(p + 1, 0))]

    message, strip = (2 * layers + layers // 2, rows, width), (layers // 2, rows, width)
    to_partner, mine, first, second = call(
        pack_kernel, "pack", (fields,), (message, message, strip, strip)
    )
    part = swap(to_partner)
    part_strip = lax.ppermute(first, ("span", "stream"), to_other)
    own_strip = lax.ppermute(second, ("span", "stream"), to_same)
    (whole,) = call(join_kernel, "join", (mine, part), ((2 * message[0], rows, width),))
    a_whole, b_part = pair_a(whole), pair_b(part)
    mine_now, b_mine = lax.optimization_barrier((mine, pair_b(mine)))
    (outer,) = call(outer_kernel, "outer", (own_strip, part_strip), ((layers, rows, width),), hint=2**35)
    a_outer, b_outer = pair_a(outer), pair_b(outer)

    matrices = np.zeros((2 * cells + 2 * width, 4 * cells), ml_dtypes.bfloat16)
    matrices[:cells], matrices[cells : 2 * cells] = plane_constants(both, rows)
    matrices[2 * cells :, : 2 * width] = span_constants(width)
    weights = jnp.asarray(matrices)
    single, brief = jnp.float32, jnp.bfloat16
    block = (4, both, rows, width)
    pieces = [((cells, 4 * width), brief), ((cells, 4 * width), brief)]
    upper, lower, products = call(
        centre_kernel,
        "centre",
        (mine_now, part, outer, weights),
        ((cells, 4 * width), (cells, 4 * width), (cells, 3 * width)),
        [(block, single), *pieces, ((cells, 3 * width), brief), ((cells, 3 * width), brief)],
        mib=16,
        hint=2**29,
    )
    a_raw, a_mean, a_second = call(
        mate_kernel,
        "mate",
        (a_whole, a_outer, upper, lower, weights),
        (block, block, (cells, 7 * width)),
        [*pieces, ((cells, 7 * width), brief), ((cells, 7 * width), brief)],
        mib=16,
        hint=2**29,
    )
    keep, send, sums = call(
        functools.partial(flux_kernel, walls),
        "flux",
        (b_mine, b_part, b_outer, a_raw, a_mean, a_second, upper, lower, products, weights),
        ((6, layers, rows, width), (3, layers, rows, width), (rows, width)),
        [
            (block, single),
            ((cells, 4 * width), brief),
            ((cells, 4 * width), brief),
            ((cells, 3 * width), brief),
            ((cells, 3 * width), brief),
            ((4, both + 2, 2 * rows, width), single),
            ((cells, 7 * width), brief),
            ((cells, 7 * width), brief),
            ((3, both, rows, width), single),
            ((3, both, rows, width), single),
        ],
        mib=24,
    )

    come = swap(send)

    def from_span(value, step):
        return lax.ppermute(value, "span", [(p, p ^ step) for p in range(spans)])

    step = 1
    while step < spans:
        if 2 * step < spans:
            far = from_span(sums, 3 * step) + from_span(sums, 2 * step)
            sums = (sums + from_span(sums, step)) + far
        else:
            sums = sums + from_span(sums, step)
        step *= 4
    sums = sums + swap(sums)
    block, corr = (3, layers, rows, width), (3, rows)
    return call(
        functools.partial(finish_kernel, float(layers * width * spans * streams)),
        "finish",
        (sums, keep, come),
        (block, block, corr, corr),
    )


def solution(mesh):
    return jax.shard_map(
        shards,
        mesh=mesh,
        in_specs=(P(None, "stream", "wall", "span"),),
        out_specs=(
            P(None, "stream", "wall", "span"),
            P(None, "stream", "wall", "span"),
            P(None, "wall"),
            P(None, "wall"),
        ),
        check_vma=False,
    )
```

```python
import functools
import math

import jax
import jax.numpy as jnp
import ml_dtypes
import numpy as np
from jax import lax
from jax.experimental import pallas as pl
from jax.experimental.pallas import tpu as pltpu
from jax.sharding import PartitionSpec as P

raw_taps = [math.exp(-((k - 8) ** 2) / 18.0) for k in range(17)]
filter_taps = [value / sum(raw_taps) for value in raw_taps]
clark_coef = 9.0
small_eps = 1e-06

reach = 8
rim = 2 * reach


def split_constant(matrix):
    high = matrix.astype(ml_dtypes.bfloat16)
    low = (matrix - high.astype(np.float64)).astype(ml_dtypes.bfloat16)
    return high, low


def band(outs, ins, offset):
    matrix = np.zeros((outs, ins))
    for o in range(outs):
        for i in range(ins):
            k = i - o - offset + reach
            if 0 <= k <= 2 * reach:
                matrix[o, i] = filter_taps[k]
    return matrix


def plane_constants(layers, rows):
    stream = band(layers, layers, 0)
    wall = band(rows, 2 * rows, reach)
    near = np.arange(reach, reach + rows)
    far = np.setdiff1d(np.arange(2 * rows), near)
    parts = [np.arange(rows), np.arange(rows, 2 * rows), near, far]
    blocks = [np.kron(stream, wall[:, part]) for part in parts]
    return split_constant(np.concatenate(blocks, axis=1))


def span_constants(width):
    circle = np.zeros((width, width))
    for o in range(width):
        for k in range(2 * reach + 1):
            circle[(o + k - reach) % width, o] = filter_taps[k]
    high, low = split_constant(circle)
    return np.block([[high, low], [high, np.zeros_like(low)]])


def halves(value):
    high = value.astype(jnp.bfloat16)
    return high, (value - high.astype(jnp.float32)).astype(jnp.bfloat16)


def dot(a, b):
    return lax.dot_general(a, b, (((1,), (0,)), ((), ())), preferred_element_type=jnp.float32)


def lane_index(shape):
    return lax.broadcasted_iota(jnp.int32, shape, len(shape) - 1)


def unit_index(shape):
    return lane_index(shape) // rim


def pack_halves(block, half):
    width = block.shape[-1]
    in_place = lane_index(block.shape[1:]) // (width // 2) == half
    for pair in range(2):
        moved = pltpu.roll(block[2 * pair + 1], width // 2, 2)
        yield pair, jnp.where(in_place, block[2 * pair], moved)


def pack_strip(block, unit):
    _, layers, rows, width = block.shape
    half = layers // 2
    units = unit_index((half, rows, width))
    total = jnp.zeros((half, rows, width), jnp.float32)
    for k in range(2):
        for f in range(4):
            step = 2 * f + k
            cells = block[f, k * half : (k + 1) * half]
            cells = pltpu.roll(cells, step * rim, 2) if step else cells
            total = jnp.where(units == lax.rem(unit + step, width // rim), cells, total)
    return total


def strip_tile(inner, outer, me_s):
    width = inner.shape[-1]
    is_outer = lax.rem(unit_index(inner.shape), 2) == 1 - me_s
    for k in range(2):
        shift = (width - k * rim) % width
        pieces = [pltpu.roll(strip, shift, 2) if k else strip for strip in (inner, outer)]
        yield k, jnp.where(is_outer, pieces[1], pieces[0])


def pack_kernel(own, to_partner, to_mine, to_other, to_same):
    _, layers, _, _ = own.shape
    me_s = lax.axis_index("stream")
    for message, half in ((to_partner, 1 - me_s), (to_mine, me_s)):
        for pair, tile in pack_halves(own, half):
            message[pair * layers : (pair + 1) * layers] = tile
        message[2 * layers :] = pack_strip(own, 4 - half)
    to_other[...] = pack_strip(own, 7 * me_s)
    to_same[...] = pack_strip(own, 7 * (1 - me_s))


def rest_kernel(part, own_strip, part_strip, rest, outer):
    count, half = part.shape[0], own_strip.shape[0]
    outer[:half] = own_strip[...]
    outer[half:] = part_strip[...]
    rest[:count] = part[...]
    rest[count:] = outer[...]


def join_kernel(mine, part, whole):
    count = mine.shape[0]
    whole[:count] = mine[...]
    whole[count:] = part[...]


def unpack(mine, part, outer, me_s):
    layers, rows, width = outer.shape
    half = layers // 2
    unit = unit_index((half, rows, width))
    first = 4 * (1 - me_s)
    in_strip = (unit == first) | (unit == first + 3)
    for which, packed in enumerate((mine, part)):
        far = outer[which * half : (which + 1) * half]
        for k, strip in strip_tile(packed[2 * layers :], far, me_s):
            layer = (me_s if which == 0 else 1 - me_s) * layers + k * half
            for f in range(4):
                start = f // 2 * layers + k * half
                cells = packed[start : start + half]
                cells = pltpu.roll(cells, width // 2, 2) if f % 2 else cells
                moved = pltpu.roll(strip, width - 2 * f * rim, 2) if f else strip
                yield f, layer, jnp.where(in_strip, moved, cells)


def column(t, width=128):
    return slice(t * width, (t + 1) * width)


def planes_of(weights, part, high, low):
    cells = weights.shape[1] // 4
    along = pl.ds(part * cells if isinstance(part, int) else pl.multiple_of(part * cells, cells), cells)
    plane_h, plane_l = weights[:cells, along], weights[cells : 2 * cells, along]
    return dot(plane_h, high) + dot(plane_l, high) + dot(plane_h, low)


def bring(mine, part, outer, raw, high, low, keep=None):
    rows, width = outer.shape[1:]
    for f, layer, value in unpack(mine, part, outer, lax.axis_index("stream")):
        count = value.shape[0]
        value = value if keep is None else value * keep
        raw[f, pl.ds(layer, count)] = value
        down = pl.ds(pl.multiple_of(layer * rows, count * rows), count * rows)
        high[down, column(f)], low[down, column(f)] = halves(value.reshape(-1, width))


def centre_kernel(mine, part, outer, weights, upper, lower, products, centre, in_h, in_l, prod_h, prod_l):
    cells, width = in_h.shape[0], outer.shape[-1]
    bring(mine, part, outer, centre, in_h, in_l)
    for i in range(3):
        value = (centre[i] * centre[3]).reshape(cells, width)
        prod_h[:, column(i)], prod_l[:, column(i)] = halves(value)
    upper[...] = planes_of(weights, 1, in_h[...], in_l[...])
    lower[...] = planes_of(weights, 0, in_h[...], in_l[...])
    products[...] = planes_of(weights, 2, prod_h[...], prod_l[...])


def span_pass(weights, planes, both):
    cells = planes.shape[0]
    rows = cells // both
    width = 128
    span_w = weights[2 * cells :, : 2 * width]
    high, low = halves(planes)
    tiles = planes.shape[1] // width
    parts = [jnp.concatenate([high[:, column(t)], low[:, column(t)]], axis=1) for t in range(tiles)]
    result = dot(jnp.concatenate(parts, axis=0), span_w)
    result = result[:, :width] + result[:, width:]
    return [result[t * cells : (t + 1) * cells].reshape(both, rows, width) for t in range(tiles)]


def second_input(means, high, low):
    tiles = means + [means[i] * means[3] for i in range(3)]
    for t, value in enumerate(tiles):
        high[:, column(t)], low[:, column(t)] = halves(value.reshape(-1, value.shape[-1]))


def mate_kernel(
    whole, outer, upper, lower, weights, raw, mean, second, in_h, in_l, mid_h, mid_l
):
    both = raw.shape[1]
    odd = lax.rem(lax.axis_index("wall"), 2)
    count = whole.shape[0] // 2
    bring(whole.at[:count], whole.at[count:], outer, raw, in_h, in_l)
    planes = jnp.where(odd == 1, upper[...], lower[...])
    planes = planes + planes_of(weights, 1 - odd, in_h[...], in_l[...])
    means = span_pass(weights, planes, both)
    for t, value in enumerate(means):
        mean[t] = value
    second_input(means, mid_h, mid_l)
    second[...] = planes_of(weights, 1 - odd, mid_h[...], mid_l[...])


def flux_kernel(
    walls, b_mine, b_rest, a_raw, a_mean, a_second, upper, lower, products, weights,
    keep_ref, send_ref, sums_ref,
    raw, in_h, in_l, prod_h, prod_l, mean, mid_h, mid_l, clark_all, similar_all,
):
    _, layers, rows, width = keep_ref.shape
    both = 2 * layers
    cells = both * rows
    me_s = lax.axis_index("stream")
    me_w = lax.axis_index("wall")
    odd = lax.rem(me_w, 2)
    at_end = (me_w == 0) | (me_w == walls - 1)
    keep_b = jnp.where(at_end, 0.0, 1.0).astype(jnp.float32)

    count = b_mine.shape[0]
    bring(b_mine, b_rest.at[:count], b_rest.at[count:], raw, in_h, in_l, keep_b)

    for t in range(4):
        mean[t, 0] = jnp.zeros((2 * rows, width), jnp.float32)
        mean[t, both + 1] = jnp.zeros((2 * rows, width), jnp.float32)
    planes = jnp.where(odd == 0, upper[...], lower[...])
    planes = planes + planes_of(weights, odd, in_h[...], in_l[...])
    row = lax.rem(lax.broadcasted_iota(jnp.int32, planes.shape, 0), rows)
    inside = (row < reach) == (odd == 1)
    planes = jnp.where(jnp.logical_or(inside, jnp.logical_not(at_end)), planes, 0.0)
    means = span_pass(weights, planes, both)
    rows_b = pl.ds(pl.multiple_of(odd * rows, rows), rows)
    rows_a = pl.ds(pl.multiple_of((1 - odd) * rows, rows), rows)
    for t, value in enumerate(means):
        mean[t, 1 : both + 1, rows_b, :] = value
        mean[t, 1 : both + 1, rows_a, :] = a_mean[t]
    second_input(means, mid_h, mid_l)
    second = span_pass(weights, a_second[...] + planes_of(weights, odd, mid_h[...], mid_l[...]), both)

    def around(f):
        above = jnp.where(odd == 0, raw[f, :, rows - reach :, :], a_raw[f, :, rows - reach :, :])
        below = jnp.where(odd == 1, raw[f, :, :reach, :], a_raw[f, :, :reach, :])
        return jnp.concatenate([above, below], axis=1)

    temperature = around(3)
    for i in range(3):
        value = (around(i) * temperature).reshape(cells, width)
        prod_h[:, column(i)], prod_l[:, column(i)] = halves(value)
    flux = span_pass(weights, products[...] + planes_of(weights, 3, prod_h[...], prod_l[...]), both)

    mid_rows = slice(reach, reach + rows)
    centre, along_span, along_wall, along_stream = [], [], [], []
    for f in range(4):
        here = mean[f, 1 : both + 1, mid_rows, :]
        centre.append(here)
        along_span.append((pltpu.roll(here, width - 1, 2) - pltpu.roll(here, 1, 2)) * 0.5)
        below = mean[f, 1 : both + 1, reach + 1 : reach + rows + 1, :]
        above = mean[f, 1 : both + 1, reach - 1 : reach + rows - 1, :]
        along_wall.append((below - above) * 0.5)
        along_stream.append((mean[f, 2 : both + 2, mid_rows, :] - mean[f, :both, mid_rows, :]) * 0.5)

    lane = lane_index((rows, width))
    useful = lane // (width // 2) == me_s
    table = jnp.zeros((rows, width), jnp.float32)
    for i in range(3):
        exact = flux[i] - centre[i] * centre[3]
        similar = second[4 + i] - second[i] * second[3]
        total = along_span[i] * along_span[3] + along_wall[i] * along_wall[3]
        clark = clark_coef * (total + along_stream[i] * along_stream[3])
        clark_all[i] = clark
        similar_all[i] = similar
        terms = (exact * clark, exact * similar, exact * exact, clark * clark, similar * similar)
        for q, term in enumerate(terms):
            value = jnp.where(useful, jnp.sum(term, axis=0), 0.0)
            table = jnp.where(lane == 3 * q + i, jnp.sum(value, axis=1, keepdims=True), table)
    sums_ref[...] = table

    first = lane_index((layers, rows, width)) < width // 2
    for i in range(3):
        keep_ref[i] = clark_all[i, pl.ds(me_s * layers, layers)]
        keep_ref[3 + i] = similar_all[i, pl.ds(me_s * layers, layers)]
        clark = clark_all[i, pl.ds((1 - me_s) * layers, layers)]
        similar = similar_all[i, pl.ds((1 - me_s) * layers, layers)]
        turn = me_s == 0
        clark = jnp.where(turn, clark, pltpu.roll(clark, width // 2, 2))
        similar = jnp.where(turn, pltpu.roll(similar, width // 2, 2), similar)
        send_ref[i] = jnp.where(first, clark, similar)


def finish_kernel(
    plane_cells, sums, keep, come, clark_model, similar_model, clark_corr, similar_corr
):
    _, layers, rows, width = keep.shape
    me_s = lax.axis_index("stream")
    table = sums[...] / plane_cells
    lane = lane_index((rows, width))
    useful = lane // (width // 2) == me_s
    corr = jnp.zeros((rows, width), jnp.float32)
    for i in range(3):
        cross_c, cross_s, power_e, power_c, power_s = (
            table[:, 3 * q + i : 3 * q + i + 1] for q in range(5)
        )
        packed = come[i]
        turned = pltpu.roll(packed, width // 2, 2)
        clark = jnp.where(useful[None], keep[i], jnp.where(me_s == 0, turned, packed))
        similar = jnp.where(useful[None], keep[3 + i], jnp.where(me_s == 0, packed, turned))
        clark_model[i] = clark / jnp.sqrt(power_c + small_eps)[None]
        similar_model[i] = similar / jnp.sqrt(power_s + small_eps)[None]
        value = cross_c / jnp.sqrt((power_e + small_eps) * (power_c + small_eps))
        corr = jnp.where(lane == i, value, corr)
        value = cross_s / jnp.sqrt((power_e + small_eps) * (power_s + small_eps))
        corr = jnp.where(lane == 8 + i, value, corr)
    square = jnp.concatenate([corr, jnp.zeros((width - rows, width), jnp.float32)], axis=0)
    turned = square.T
    clark_corr[...] = turned[:3, :rows]
    similar_corr[...] = turned[8:11, :rows]


def call(kernel, name, ins, outs, scratch=(), mib=4, hint=None):
    cost = hint and pl.CostEstimate(flops=hint, bytes_accessed=0, transcendentals=0)
    return pl.pallas_call(
        kernel,
        out_shape=tuple(jax.ShapeDtypeStruct(shape, jnp.float32) for shape in outs),
        in_specs=[pl.BlockSpec(memory_space=pltpu.VMEM)] * len(ins),
        out_specs=tuple(pl.BlockSpec(memory_space=pltpu.VMEM) for _ in outs),
        scratch_shapes=[pltpu.VMEM(shape, dtype) for shape, dtype in scratch],
        compiler_params=pltpu.CompilerParams(vmem_limit_bytes=mib * 1024 * 1024),
        cost_estimate=cost,
        name=name,
    )(*ins)


def shards(fields):
    _, layers, rows, width = fields.shape
    spans = lax.axis_size("span")
    walls = lax.axis_size("wall")
    streams = lax.axis_size("stream")
    both = streams * layers
    cells = both * rows

    def swap(value):
        return lax.ppermute(value, "stream", [(0, 1), (1, 0)])

    def pair_a(value):
        return lax.ppermute(value, "wall", [(w, w ^ 1) for w in range(walls)])

    def pair_b(value):
        return lax.ppermute(
            value, "wall", [(w, min(max(((w + 1) ^ 1) - 1, 0), walls - 1)) for w in range(walls)]
        )

    def place(p, s):
        return (p % spans) * streams + s

    to_other, to_same = [], []
    for p in range(spans):
        to_other += [(place(p, 0), place(p - 1, 1)), (place(p, 1), place(p + 1, 0))]
        to_same += [(place(p, 1), place(p - 1, 1)), (place(p, 0), place(p + 1, 0))]

    message, strip = (2 * layers + layers // 2, rows, width), (layers // 2, rows, width)
    to_partner, mine, first, second = call(
        pack_kernel, "pack", (fields,), (message, message, strip, strip)
    )
    part = swap(to_partner)
    part_strip = lax.ppermute(first, ("span", "stream"), to_other)
    own_strip = lax.ppermute(second, ("span", "stream"), to_same)
    (whole,) = call(join_kernel, "join", (mine, part), ((2 * message[0], rows, width),))
    a_whole = pair_a(whole)
    mine_now, b_mine = lax.optimization_barrier((mine, pair_b(mine)))
    rest, outer = call(
        rest_kernel,
        "rest",
        (part, own_strip, part_strip),
        ((message[0] + layers, rows, width), (layers, rows, width)),
        hint=2**35,
    )
    b_rest, a_outer = pair_b(rest), pair_a(outer)

    matrices = np.zeros((2 * cells + 2 * width, 4 * cells), ml_dtypes.bfloat16)
    matrices[:cells], matrices[cells : 2 * cells] = plane_constants(both, rows)
    matrices[2 * cells :, : 2 * width] = span_constants(width)
    weights = jnp.asarray(matrices)
    single, brief = jnp.float32, jnp.bfloat16
    block = (4, both, rows, width)
    pieces = [((cells, 4 * width), brief), ((cells, 4 * width), brief)]
    upper, lower, products = call(
        centre_kernel,
        "centre",
        (mine_now, part, outer, weights),
        ((cells, 4 * width), (cells, 4 * width), (cells, 3 * width)),
        [(block, single), *pieces, ((cells, 3 * width), brief), ((cells, 3 * width), brief)],
        mib=16,
        hint=2**29,
    )
    a_raw, a_mean, a_second = call(
        mate_kernel,
        "mate",
        (a_whole, a_outer, upper, lower, weights),
        (block, block, (cells, 7 * width)),
        [*pieces, ((cells, 7 * width), brief), ((cells, 7 * width), brief)],
        mib=16,
        hint=2**29,
    )
    keep, send, sums = call(
        functools.partial(flux_kernel, walls),
        "flux",
        (b_mine, b_rest, a_raw, a_mean, a_second, upper, lower, products, weights),
        ((6, layers, rows, width), (3, layers, rows, width), (rows, width)),
        [
            (block, single),
            ((cells, 4 * width), brief),
            ((cells, 4 * width), brief),
            ((cells, 3 * width), brief),
            ((cells, 3 * width), brief),
            ((4, both + 2, 2 * rows, width), single),
            ((cells, 7 * width), brief),
            ((cells, 7 * width), brief),
            ((3, both, rows, width), single),
            ((3, both, rows, width), single),
        ],
        mib=24,
    )

    come = swap(send)

    def from_span(value, step):
        return lax.ppermute(value, "span", [(p, p ^ step) for p in range(spans)])

    step = 1
    while step < spans:
        if 2 * step < spans:
            far = from_span(sums, 3 * step) + from_span(sums, 2 * step)
            sums = (sums + from_span(sums, step)) + far
        else:
            sums = sums + from_span(sums, step)
        step *= 4
    sums = sums + swap(sums)
    block, corr = (3, layers, rows, width), (3, rows)
    return call(
        functools.partial(finish_kernel, float(layers * width * spans * streams)),
        "finish",
        (sums, keep, come),
        (block, block, corr, corr),
    )


def solution(mesh):
    return jax.shard_map(
        shards,
        mesh=mesh,
        in_specs=(P(None, "stream", "wall", "span"),),
        out_specs=(
            P(None, "stream", "wall", "span"),
            P(None, "stream", "wall", "span"),
            P(None, "wall"),
            P(None, "wall"),
        ),
        check_vma=False,
    )
```

```python
import functools
import math

import jax
import jax.numpy as jnp
import ml_dtypes
import numpy as np
from jax import lax
from jax.experimental import pallas as pl
from jax.experimental.pallas import tpu as pltpu
from jax.sharding import PartitionSpec as P

raw_taps = [math.exp(-((k - 8) ** 2) / 18.0) for k in range(17)]
filter_taps = [value / sum(raw_taps) for value in raw_taps]
clark_coef = 9.0
small_eps = 1e-06

reach = 8
rim = 2 * reach


def split_constant(matrix):
    high = matrix.astype(ml_dtypes.bfloat16)
    low = (matrix - high.astype(np.float64)).astype(ml_dtypes.bfloat16)
    return high, low


def band(outs, ins, offset):
    matrix = np.zeros((outs, ins))
    for o in range(outs):
        for i in range(ins):
            k = i - o - offset + reach
            if 0 <= k <= 2 * reach:
                matrix[o, i] = filter_taps[k]
    return matrix


def plane_constants(layers, rows):
    stream = band(layers, layers, 0)
    wall = band(rows, 2 * rows, reach)
    near = np.arange(reach, reach + rows)
    far = np.setdiff1d(np.arange(2 * rows), near)
    parts = [np.arange(rows), np.arange(rows, 2 * rows), near, far]
    blocks = [np.kron(stream, wall[:, part]) for part in parts]
    return split_constant(np.concatenate(blocks, axis=1))


def span_constants(width):
    circle = np.zeros((width, width))
    for o in range(width):
        for k in range(2 * reach + 1):
            circle[(o + k - reach) % width, o] = filter_taps[k]
    high, low = split_constant(circle)
    return np.block([[high, low], [high, np.zeros_like(low)]])


def halves(value):
    high = value.astype(jnp.bfloat16)
    return high, (value - high.astype(jnp.float32)).astype(jnp.bfloat16)


def dot(a, b):
    return lax.dot_general(a, b, (((1,), (0,)), ((), ())), preferred_element_type=jnp.float32)


def lane_index(shape):
    return lax.broadcasted_iota(jnp.int32, shape, len(shape) - 1)


def unit_index(shape):
    return lane_index(shape) // rim


def pack_halves(block, half):
    width = block.shape[-1]
    in_place = lane_index(block.shape[1:]) // (width // 2) == half
    for pair in range(2):
        moved = pltpu.roll(block[2 * pair + 1], width // 2, 2)
        yield pair, jnp.where(in_place, block[2 * pair], moved)


def pack_strip(block, unit):
    _, layers, rows, width = block.shape
    half = layers // 2
    units = unit_index((half, rows, width))
    total = jnp.zeros((half, rows, width), jnp.float32)
    for k in range(2):
        for f in range(4):
            step = 2 * f + k
            cells = block[f, k * half : (k + 1) * half]
            cells = pltpu.roll(cells, step * rim, 2) if step else cells
            total = jnp.where(units == lax.rem(unit + step, width // rim), cells, total)
    return total


def strip_tile(inner, outer, me_s):
    width = inner.shape[-1]
    is_outer = lax.rem(unit_index(inner.shape), 2) == 1 - me_s
    for k in range(2):
        shift = (width - k * rim) % width
        pieces = [pltpu.roll(strip, shift, 2) if k else strip for strip in (inner, outer)]
        yield k, jnp.where(is_outer, pieces[1], pieces[0])


def pack_kernel(own, to_partner, to_mine, to_other, to_same):
    _, layers, _, _ = own.shape
    me_s = lax.axis_index("stream")
    for message, half in ((to_partner, 1 - me_s), (to_mine, me_s)):
        for pair, tile in pack_halves(own, half):
            message[pair * layers : (pair + 1) * layers] = tile
        message[2 * layers :] = pack_strip(own, 4 - half)
    to_other[...] = pack_strip(own, 7 * me_s)
    to_same[...] = pack_strip(own, 7 * (1 - me_s))


def rest_kernel(part, own_strip, part_strip, rest):
    count, half = part.shape[0], own_strip.shape[0]
    rest[:count] = part[...]
    rest[count : count + half] = own_strip[...]
    rest[count + half :] = part_strip[...]


def unpack(mine, rest, me_s):
    count, rows, width = mine.shape
    layers = rest.shape[0] - count
    half = layers // 2
    unit = unit_index((half, rows, width))
    first = 4 * (1 - me_s)
    in_strip = (unit == first) | (unit == first + 3)
    for which, packed in enumerate((mine, rest)):
        far = rest[count + which * half : count + (which + 1) * half]
        for k, strip in strip_tile(packed[2 * layers : count], far, me_s):
            layer = (me_s if which == 0 else 1 - me_s) * layers + k * half
            for f in range(4):
                start = f // 2 * layers + k * half
                cells = packed[start : start + half]
                cells = pltpu.roll(cells, width // 2, 2) if f % 2 else cells
                moved = pltpu.roll(strip, width - 2 * f * rim, 2) if f else strip
                yield f, layer, jnp.where(in_strip, moved, cells)


def column(t, width=128):
    return slice(t * width, (t + 1) * width)


def planes_of(weights, part, high, low):
    cells = weights.shape[1] // 4
    along = pl.ds(part * cells if isinstance(part, int) else pl.multiple_of(part * cells, cells), cells)
    plane_h, plane_l = weights[:cells, along], weights[cells : 2 * cells, along]
    return dot(plane_h, high) + dot(plane_l, high) + dot(plane_h, low)


def bring(mine, rest, raw, high, low, keep=None):
    rows, width = mine.shape[1:]
    for f, layer, value in unpack(mine, rest, lax.axis_index("stream")):
        count = value.shape[0]
        value = value if keep is None else value * keep
        raw[f, pl.ds(layer, count)] = value
        down = pl.ds(pl.multiple_of(layer * rows, count * rows), count * rows)
        high[down, column(f)], low[down, column(f)] = halves(value.reshape(-1, width))


def centre_kernel(mine, rest, weights, upper, lower, products, centre, in_h, in_l, prod_h, prod_l):
    cells, width = in_h.shape[0], mine.shape[-1]
    bring(mine, rest, centre, in_h, in_l)
    for i in range(3):
        value = (centre[i] * centre[3]).reshape(cells, width)
        prod_h[:, column(i)], prod_l[:, column(i)] = halves(value)
    upper[...] = planes_of(weights, 1, in_h[...], in_l[...])
    lower[...] = planes_of(weights, 0, in_h[...], in_l[...])
    products[...] = planes_of(weights, 2, prod_h[...], prod_l[...])


def span_pass(weights, planes, both):
    cells = planes.shape[0]
    rows = cells // both
    width = 128
    span_w = weights[2 * cells :, : 2 * width]
    high, low = halves(planes)
    tiles = planes.shape[1] // width
    parts = [jnp.concatenate([high[:, column(t)], low[:, column(t)]], axis=1) for t in range(tiles)]
    result = dot(jnp.concatenate(parts, axis=0), span_w)
    result = result[:, :width] + result[:, width:]
    return [result[t * cells : (t + 1) * cells].reshape(both, rows, width) for t in range(tiles)]


def second_input(means, high, low):
    tiles = means + [means[i] * means[3] for i in range(3)]
    for t, value in enumerate(tiles):
        high[:, column(t)], low[:, column(t)] = halves(value.reshape(-1, value.shape[-1]))


def mate_kernel(
    a_mine, a_rest, upper, lower, weights, raw, mean, second, in_h, in_l, mid_h, mid_l
):
    both = raw.shape[1]
    odd = lax.rem(lax.axis_index("wall"), 2)
    bring(a_mine, a_rest, raw, in_h, in_l)
    planes = jnp.where(odd == 1, upper[...], lower[...])
    planes = planes + planes_of(weights, 1 - odd, in_h[...], in_l[...])
    means = span_pass(weights, planes, both)
    for t, value in enumerate(means):
        mean[t] = value
    second_input(means, mid_h, mid_l)
    second[...] = planes_of(weights, 1 - odd, mid_h[...], mid_l[...])


def flux_kernel(
    walls, b_mine, b_rest, a_raw, a_mean, a_second, upper, lower, products, weights,
    keep_ref, send_ref, sums_ref,
    raw, in_h, in_l, prod_h, prod_l, mean, mid_h, mid_l, clark_all, similar_all,
):
    _, layers, rows, width = keep_ref.shape
    both = 2 * layers
    cells = both * rows
    me_s = lax.axis_index("stream")
    me_w = lax.axis_index("wall")
    odd = lax.rem(me_w, 2)
    at_end = (me_w == 0) | (me_w == walls - 1)
    keep_b = jnp.where(at_end, 0.0, 1.0).astype(jnp.float32)

    bring(b_mine, b_rest, raw, in_h, in_l, keep_b)

    for t in range(4):
        mean[t, 0] = jnp.zeros((2 * rows, width), jnp.float32)
        mean[t, both + 1] = jnp.zeros((2 * rows, width), jnp.float32)
    planes = jnp.where(odd == 0, upper[...], lower[...])
    planes = planes + planes_of(weights, odd, in_h[...], in_l[...])
    row = lax.rem(lax.broadcasted_iota(jnp.int32, planes.shape, 0), rows)
    inside = (row < reach) == (odd == 1)
    planes = jnp.where(jnp.logical_or(inside, jnp.logical_not(at_end)), planes, 0.0)
    means = span_pass(weights, planes, both)
    rows_b = pl.ds(pl.multiple_of(odd * rows, rows), rows)
    rows_a = pl.ds(pl.multiple_of((1 - odd) * rows, rows), rows)
    for t, value in enumerate(means):
        mean[t, 1 : both + 1, rows_b, :] = value
        mean[t, 1 : both + 1, rows_a, :] = a_mean[t]
    second_input(means, mid_h, mid_l)
    second = span_pass(weights, a_second[...] + planes_of(weights, odd, mid_h[...], mid_l[...]), both)

    def around(f):
        above = jnp.where(odd == 0, raw[f, :, rows - reach :, :], a_raw[f, :, rows - reach :, :])
        below = jnp.where(odd == 1, raw[f, :, :reach, :], a_raw[f, :, :reach, :])
        return jnp.concatenate([above, below], axis=1)

    temperature = around(3)
    for i in range(3):
        value = (around(i) * temperature).reshape(cells, width)
        prod_h[:, column(i)], prod_l[:, column(i)] = halves(value)
    flux = span_pass(weights, products[...] + planes_of(weights, 3, prod_h[...], prod_l[...]), both)

    mid_rows = slice(reach, reach + rows)
    centre, along_span, along_wall, along_stream = [], [], [], []
    for f in range(4):
        here = mean[f, 1 : both + 1, mid_rows, :]
        centre.append(here)
        along_span.append((pltpu.roll(here, width - 1, 2) - pltpu.roll(here, 1, 2)) * 0.5)
        below = mean[f, 1 : both + 1, reach + 1 : reach + rows + 1, :]
        above = mean[f, 1 : both + 1, reach - 1 : reach + rows - 1, :]
        along_wall.append((below - above) * 0.5)
        along_stream.append((mean[f, 2 : both + 2, mid_rows, :] - mean[f, :both, mid_rows, :]) * 0.5)

    lane = lane_index((rows, width))
    useful = lane // (width // 2) == me_s
    table = jnp.zeros((rows, width), jnp.float32)
    for i in range(3):
        exact = flux[i] - centre[i] * centre[3]
        similar = second[4 + i] - second[i] * second[3]
        total = along_span[i] * along_span[3] + along_wall[i] * along_wall[3]
        clark = clark_coef * (total + along_stream[i] * along_stream[3])
        clark_all[i] = clark
        similar_all[i] = similar
        terms = (exact * clark, exact * similar, exact * exact, clark * clark, similar * similar)
        for q, term in enumerate(terms):
            value = jnp.where(useful, jnp.sum(term, axis=0), 0.0)
            table = jnp.where(lane == 3 * q + i, jnp.sum(value, axis=1, keepdims=True), table)
    sums_ref[...] = table

    first = lane_index((layers, rows, width)) < width // 2
    for i in range(3):
        keep_ref[i] = clark_all[i, pl.ds(me_s * layers, layers)]
        keep_ref[3 + i] = similar_all[i, pl.ds(me_s * layers, layers)]
        clark = clark_all[i, pl.ds((1 - me_s) * layers, layers)]
        similar = similar_all[i, pl.ds((1 - me_s) * layers, layers)]
        turn = me_s == 0
        clark = jnp.where(turn, clark, pltpu.roll(clark, width // 2, 2))
        similar = jnp.where(turn, pltpu.roll(similar, width // 2, 2), similar)
        send_ref[i] = jnp.where(first, clark, similar)


def finish_kernel(
    plane_cells, sums, keep, come, clark_model, similar_model, clark_corr, similar_corr
):
    _, layers, rows, width = keep.shape
    me_s = lax.axis_index("stream")
    table = sums[...] / plane_cells
    lane = lane_index((rows, width))
    useful = lane // (width // 2) == me_s
    corr = jnp.zeros((rows, width), jnp.float32)
    for i in range(3):
        cross_c, cross_s, power_e, power_c, power_s = (
            table[:, 3 * q + i : 3 * q + i + 1] for q in range(5)
        )
        packed = come[i]
        turned = pltpu.roll(packed, width // 2, 2)
        clark = jnp.where(useful[None], keep[i], jnp.where(me_s == 0, turned, packed))
        similar = jnp.where(useful[None], keep[3 + i], jnp.where(me_s == 0, packed, turned))
        clark_model[i] = clark / jnp.sqrt(power_c + small_eps)[None]
        similar_model[i] = similar / jnp.sqrt(power_s + small_eps)[None]
        value = cross_c / jnp.sqrt((power_e + small_eps) * (power_c + small_eps))
        corr = jnp.where(lane == i, value, corr)
        value = cross_s / jnp.sqrt((power_e + small_eps) * (power_s + small_eps))
        corr = jnp.where(lane == 8 + i, value, corr)
    square = jnp.concatenate([corr, jnp.zeros((width - rows, width), jnp.float32)], axis=0)
    turned = square.T
    clark_corr[...] = turned[:3, :rows]
    similar_corr[...] = turned[8:11, :rows]


def call(kernel, name, ins, outs, scratch=(), mib=4, hint=None):
    cost = hint and pl.CostEstimate(flops=hint, bytes_accessed=0, transcendentals=0)
    return pl.pallas_call(
        kernel,
        out_shape=tuple(jax.ShapeDtypeStruct(shape, jnp.float32) for shape in outs),
        in_specs=[pl.BlockSpec(memory_space=pltpu.VMEM)] * len(ins),
        out_specs=tuple(pl.BlockSpec(memory_space=pltpu.VMEM) for _ in outs),
        scratch_shapes=[pltpu.VMEM(shape, dtype) for shape, dtype in scratch],
        compiler_params=pltpu.CompilerParams(vmem_limit_bytes=mib * 1024 * 1024),
        cost_estimate=cost,
        name=name,
    )(*ins)


def shards(fields):
    _, layers, rows, width = fields.shape
    spans = lax.axis_size("span")
    walls = lax.axis_size("wall")
    streams = lax.axis_size("stream")
    both = streams * layers
    cells = both * rows

    def swap(value):
        return lax.ppermute(value, "stream", [(0, 1), (1, 0)])

    def pair_a(value):
        return lax.ppermute(value, "wall", [(w, w ^ 1) for w in range(walls)])

    def pair_b(value):
        return lax.ppermute(
            value, "wall", [(w, min(max(((w + 1) ^ 1) - 1, 0), walls - 1)) for w in range(walls)]
        )

    def place(p, s):
        return (p % spans) * streams + s

    to_other, to_same = [], []
    for p in range(spans):
        to_other += [(place(p, 0), place(p - 1, 1)), (place(p, 1), place(p + 1, 0))]
        to_same += [(place(p, 1), place(p - 1, 1)), (place(p, 0), place(p + 1, 0))]

    message, strip = (2 * layers + layers // 2, rows, width), (layers // 2, rows, width)
    to_partner, mine, first, second = call(
        pack_kernel, "pack", (fields,), (message, message, strip, strip)
    )
    part = swap(to_partner)
    part_strip = lax.ppermute(first, ("span", "stream"), to_other)
    own_strip = lax.ppermute(second, ("span", "stream"), to_same)
    mine_now, b_mine, a_mine = lax.optimization_barrier((mine, pair_b(mine), pair_a(mine)))
    (rest,) = call(
        rest_kernel,
        "rest",
        (part, own_strip, part_strip),
        ((message[0] + layers, rows, width),),
        hint=2**35,
    )
    a_rest, b_rest = pair_a(rest), pair_b(rest)

    matrices = np.zeros((2 * cells + 2 * width, 4 * cells), ml_dtypes.bfloat16)
    matrices[:cells], matrices[cells : 2 * cells] = plane_constants(both, rows)
    matrices[2 * cells :, : 2 * width] = span_constants(width)
    weights = jnp.asarray(matrices)
    single, brief = jnp.float32, jnp.bfloat16
    block = (4, both, rows, width)
    pieces = [((cells, 4 * width), brief), ((cells, 4 * width), brief)]
    upper, lower, products = call(
        centre_kernel,
        "centre",
        (mine_now, rest, weights),
        ((cells, 4 * width), (cells, 4 * width), (cells, 3 * width)),
        [(block, single), *pieces, ((cells, 3 * width), brief), ((cells, 3 * width), brief)],
        mib=16,
        hint=2**31,
    )
    a_raw, a_mean, a_second = call(
        mate_kernel,
        "mate",
        (a_mine, a_rest, upper, lower, weights),
        (block, block, (cells, 7 * width)),
        [*pieces, ((cells, 7 * width), brief), ((cells, 7 * width), brief)],
        mib=16,
        hint=2**29,
    )
    keep, send, sums = call(
        functools.partial(flux_kernel, walls),
        "flux",
        (b_mine, b_rest, a_raw, a_mean, a_second, upper, lower, products, weights),
        ((6, layers, rows, width), (3, layers, rows, width), (rows, width)),
        [
            (block, single),
            ((cells, 4 * width), brief),
            ((cells, 4 * width), brief),
            ((cells, 3 * width), brief),
            ((cells, 3 * width), brief),
            ((4, both + 2, 2 * rows, width), single),
            ((cells, 7 * width), brief),
            ((cells, 7 * width), brief),
            ((3, both, rows, width), single),
            ((3, both, rows, width), single),
        ],
        mib=24,
    )

    come = swap(send)

    def from_span(value, step):
        return lax.ppermute(value, "span", [(p, p ^ step) for p in range(spans)])

    step = 1
    while step < spans:
        if 2 * step < spans:
            far = from_span(sums, 3 * step) + from_span(sums, 2 * step)
            sums = (sums + from_span(sums, step)) + far
        else:
            sums = sums + from_span(sums, step)
        step *= 4
    sums = sums + swap(sums)
    block, corr = (3, layers, rows, width), (3, rows)
    return call(
        functools.partial(finish_kernel, float(layers * width * spans * streams)),
        "finish",
        (sums, keep, come),
        (block, block, corr, corr),
    )


def solution(mesh):
    return jax.shard_map(
        shards,
        mesh=mesh,
        in_specs=(P(None, "stream", "wall", "span"),),
        out_specs=(
            P(None, "stream", "wall", "span"),
            P(None, "stream", "wall", "span"),
            P(None, "wall"),
            P(None, "wall"),
        ),
        check_vma=False,
    )
```

```python
import functools
import math

import jax
import jax.numpy as jnp
import ml_dtypes
import numpy as np
from jax import lax
from jax.experimental import pallas as pl
from jax.experimental.pallas import tpu as pltpu
from jax.sharding import PartitionSpec as P

raw_taps = [math.exp(-((k - 8) ** 2) / 18.0) for k in range(17)]
filter_taps = [value / sum(raw_taps) for value in raw_taps]
clark_coef = 9.0
small_eps = 1e-06

reach = 8
rim = 2 * reach


def split_constant(matrix):
    high = matrix.astype(ml_dtypes.bfloat16)
    low = (matrix - high.astype(np.float64)).astype(ml_dtypes.bfloat16)
    return high, low


def band(outs, ins, offset):
    matrix = np.zeros((outs, ins))
    for o in range(outs):
        for i in range(ins):
            k = i - o - offset + reach
            if 0 <= k <= 2 * reach:
                matrix[o, i] = filter_taps[k]
    return matrix


def plane_constants(layers, rows):
    stream = band(layers, layers, 0)
    wall = band(rows, 2 * rows, reach)
    near = np.arange(reach, reach + rows)
    far = np.setdiff1d(np.arange(2 * rows), near)
    parts = [np.arange(rows), np.arange(rows, 2 * rows), near, far]
    blocks = [np.kron(stream, wall[:, part]) for part in parts]
    return split_constant(np.concatenate(blocks, axis=1))


def span_constants(width):
    circle = np.zeros((width, width))
    for o in range(width):
        for k in range(2 * reach + 1):
            circle[(o + k - reach) % width, o] = filter_taps[k]
    half = width // 2

    def parts(matrix):
        high, low = split_constant(matrix)
        return np.block([[high, low], [high, np.zeros_like(low)]])

    packed = []
    for layers in range(2):
        row = []
        for s in range(2):
            matrix = np.zeros((width, width))
            matrix[:, layers * half : (layers + 1) * half] = circle[:, s * half : (s + 1) * half]
            row.append(parts(matrix))
        packed.append(np.concatenate(row, axis=1))
    return parts(circle), np.concatenate(packed, axis=0)


def halves(value):
    high = value.astype(jnp.bfloat16)
    return high, (value - high.astype(jnp.float32)).astype(jnp.bfloat16)


def dot(a, b):
    return lax.dot_general(a, b, (((1,), (0,)), ((), ())), preferred_element_type=jnp.float32)


def lane_index(shape):
    return lax.broadcasted_iota(jnp.int32, shape, len(shape) - 1)


def unit_index(shape):
    return lane_index(shape) // rim


def pack_halves(block, half):
    width = block.shape[-1]
    in_place = lane_index(block.shape[1:]) // (width // 2) == half
    for pair in range(2):
        moved = pltpu.roll(block[2 * pair + 1], width // 2, 2)
        yield pair, jnp.where(in_place, block[2 * pair], moved)


def pack_strip(block, unit):
    _, layers, rows, width = block.shape
    half = layers // 2
    units = unit_index((half, rows, width))
    total = jnp.zeros((half, rows, width), jnp.float32)
    for k in range(2):
        for f in range(4):
            step = 2 * f + k
            cells = block[f, k * half : (k + 1) * half]
            cells = pltpu.roll(cells, step * rim, 2) if step else cells
            total = jnp.where(units == lax.rem(unit + step, width // rim), cells, total)
    return total


def strip_tile(inner, outer, me_s):
    width = inner.shape[-1]
    is_outer = lax.rem(unit_index(inner.shape), 2) == 1 - me_s
    for k in range(2):
        shift = (width - k * rim) % width
        pieces = [pltpu.roll(strip, shift, 2) if k else strip for strip in (inner, outer)]
        yield k, jnp.where(is_outer, pieces[1], pieces[0])


def pack_kernel(own, to_partner, to_mine, to_other, to_same):
    _, layers, _, _ = own.shape
    me_s = lax.axis_index("stream")
    for message, half in ((to_partner, 1 - me_s), (to_mine, me_s)):
        for pair, tile in pack_halves(own, half):
            message[pair * layers : (pair + 1) * layers] = tile
        message[2 * layers :] = pack_strip(own, 4 - half)
    to_other[...] = pack_strip(own, 7 * me_s)
    to_same[...] = pack_strip(own, 7 * (1 - me_s))


def rest_kernel(part, own_strip, part_strip, rest):
    count, half = part.shape[0], own_strip.shape[0]
    rest[:count] = part[...]
    rest[count : count + half] = own_strip[...]
    rest[count + half :] = part_strip[...]


def unpack(mine, rest, me_s):
    count, rows, width = mine.shape
    layers = rest.shape[0] - count
    half = layers // 2
    unit = unit_index((half, rows, width))
    first = 4 * (1 - me_s)
    in_strip = (unit == first) | (unit == first + 3)
    for which, packed in enumerate((mine, rest)):
        far = rest[count + which * half : count + (which + 1) * half]
        for k, strip in strip_tile(packed[2 * layers : count], far, me_s):
            layer = (me_s if which == 0 else 1 - me_s) * layers + k * half
            for f in range(4):
                start = f // 2 * layers + k * half
                cells = packed[start : start + half]
                cells = pltpu.roll(cells, width // 2, 2) if f % 2 else cells
                moved = pltpu.roll(strip, width - 2 * f * rim, 2) if f else strip
                yield f, layer, jnp.where(in_strip, moved, cells)


def column(t, width=128):
    return slice(t * width, (t + 1) * width)


def planes_of(weights, part, high, low):
    cells = weights.shape[1] // 4
    along = pl.ds(part * cells if isinstance(part, int) else pl.multiple_of(part * cells, cells), cells)
    plane_h, plane_l = weights[:cells, along], weights[cells : 2 * cells, along]
    return dot(plane_h, high) + dot(plane_l, high) + dot(plane_h, low)


def bring(mine, rest, raw, high, low, keep=None):
    rows, width = mine.shape[1:]
    for f, layer, value in unpack(mine, rest, lax.axis_index("stream")):
        count = value.shape[0]
        value = value if keep is None else value * keep
        raw[f, pl.ds(layer, count)] = value
        down = pl.ds(pl.multiple_of(layer * rows, count * rows), count * rows)
        high[down, column(f)], low[down, column(f)] = halves(value.reshape(-1, width))


def centre_kernel(mine, rest, weights, upper, lower, products, centre, in_h, in_l, prod_h, prod_l):
    cells, width = in_h.shape[0], mine.shape[-1]
    bring(mine, rest, centre, in_h, in_l)
    for i in range(3):
        value = (centre[i] * centre[3]).reshape(cells, width)
        prod_h[:, column(i)], prod_l[:, column(i)] = halves(value)
    upper[...] = planes_of(weights, 1, in_h[...], in_l[...])
    lower[...] = planes_of(weights, 0, in_h[...], in_l[...])
    products[...] = planes_of(weights, 2, prod_h[...], prod_l[...])


def span_pass(weights, planes, both):
    cells = planes.shape[0]
    rows = cells // both
    width = 128
    span_w = weights[2 * cells : 2 * cells + 2 * width, : 2 * width]
    high, low = halves(planes)
    tiles = planes.shape[1] // width
    parts = [jnp.concatenate([high[:, column(t)], low[:, column(t)]], axis=1) for t in range(tiles)]
    result = dot(jnp.concatenate(parts, axis=0), span_w)
    result = result[:, :width] + result[:, width:]
    return [result[t * cells : (t + 1) * cells].reshape(both, rows, width) for t in range(tiles)]


def second_input(means, high, low):
    tiles = means + [means[i] * means[3] for i in range(3)]
    for t, value in enumerate(tiles):
        high[:, column(t)], low[:, column(t)] = halves(value.reshape(-1, value.shape[-1]))


def packed_pass(weights, planes):
    cells = planes.shape[0]
    some, width = cells // 2, 128
    me_s = lax.axis_index("stream")
    along = pl.ds(pl.multiple_of((1 + me_s) * 2 * width, 2 * width), 2 * width)
    matrix = weights[2 * cells : 2 * cells + 4 * width, along]
    high, low = halves(planes)
    tiles = planes.shape[1] // width
    parts = [
        jnp.concatenate(
            [high[:some, column(t)], low[:some, column(t)], high[some:, column(t)], low[some:, column(t)]],
            axis=1,
        )
        for t in range(tiles)
    ]
    result = dot(jnp.concatenate(parts, axis=0), matrix)
    result = result[:, :width] + result[:, width:]
    return [result[t * some : (t + 1) * some] for t in range(tiles)]


def pack_layers(own, other, me_s, shift=0):
    width = own.shape[-1]
    in_place = lane_index(own.shape) // (width // 2) == me_s
    own = pltpu.roll(own, shift % width, 2) if shift else own
    return jnp.where(in_place, own, pltpu.roll(other, (shift + width // 2) % width, 2))


def pack_means(mean, means, rows_near):
    for t, value in enumerate(means):
        mean[t] = value
    both = mean.shape[1]
    me_s = lax.axis_index("stream")
    own, other = pl.ds(me_s * (both // 2), both // 2), pl.ds((1 - me_s) * (both // 2), both // 2)
    for t in range(4):
        near = mean[t, own, rows_near, :], mean[t, other, rows_near, :]
        slope = (pack_layers(*near, me_s, -1) - pack_layers(*near, me_s, 1)) * 0.5
        yield t, pack_layers(mean[t, own], mean[t, other], me_s), slope


def mate_kernel(
    a_mine, a_rest, upper, lower, weights, raw, packed, slopes, second, in_h, in_l, mid_h, mid_l, mean
):
    both, rows = raw.shape[1:3]
    odd = lax.rem(lax.axis_index("wall"), 2)
    bring(a_mine, a_rest, raw, in_h, in_l)
    planes = jnp.where(odd == 1, upper[...], lower[...])
    planes = planes + planes_of(weights, 1 - odd, in_h[...], in_l[...])
    means = span_pass(weights, planes, both)
    for t, value, slope in pack_means(mean, means, pl.ds(pl.multiple_of(odd * reach, reach), reach)):
        packed[t] = value
        slopes[t] = slope
    second_input(means, mid_h, mid_l)
    second[...] = planes_of(weights, 1 - odd, mid_h[...], mid_l[...])


def flux_kernel(
    walls, b_mine, b_rest, a_raw, a_packed, a_slopes, a_second, upper, lower, products, weights,
    keep_ref, send_ref, sums_ref,
    raw, in_h, in_l, prod_h, prod_l, mean, mid_h, mid_l, packed, slopes,
):
    _, layers, rows, width = keep_ref.shape
    both = 2 * layers
    cells = both * rows
    me_s = lax.axis_index("stream")
    me_w = lax.axis_index("wall")
    odd = lax.rem(me_w, 2)
    at_end = (me_w == 0) | (me_w == walls - 1)
    keep_b = jnp.where(at_end, 0.0, 1.0).astype(jnp.float32)

    bring(b_mine, b_rest, raw, in_h, in_l, keep_b)

    planes = jnp.where(odd == 0, upper[...], lower[...])
    planes = planes + planes_of(weights, odd, in_h[...], in_l[...])
    row = lax.rem(lax.broadcasted_iota(jnp.int32, planes.shape, 0), rows)
    inside = (row < reach) == (odd == 1)
    planes = jnp.where(jnp.logical_or(inside, jnp.logical_not(at_end)), planes, 0.0)
    means = span_pass(weights, planes, both)
    rows_b = pl.ds(pl.multiple_of(odd * rows, rows), rows)
    rows_a = pl.ds(pl.multiple_of((1 - odd) * rows, rows), rows)
    near_b = pl.ds(pl.multiple_of(odd * reach, reach), reach)
    near_a = pl.ds(pl.multiple_of((1 - odd) * reach, reach), reach)
    for t, value, slope in pack_means(mean, means, near_a):
        packed[t, :, rows_b, :] = value
        packed[t, :, rows_a, :] = a_packed[t]
        slopes[t, :, near_b, :] = slope
        slopes[t, :, near_a, :] = a_slopes[t]
    second_input(means, mid_h, mid_l)
    second = packed_pass(weights, a_second[...] + planes_of(weights, odd, mid_h[...], mid_l[...]))
    second = [value.reshape(layers, rows, width) for value in second]

    def around(f):
        above = jnp.where(odd == 0, raw[f, :, rows - reach :, :], a_raw[f, :, rows - reach :, :])
        below = jnp.where(odd == 1, raw[f, :, :reach, :], a_raw[f, :, :reach, :])
        return jnp.concatenate([above, below], axis=1)

    temperature = around(3)
    for i in range(3):
        value = (around(i) * temperature).reshape(cells, width)
        prod_h[:, column(i)], prod_l[:, column(i)] = halves(value)
    flux = packed_pass(weights, products[...] + planes_of(weights, 3, prod_h[...], prod_l[...]))
    flux = [value.reshape(layers, rows, width) for value in flux]

    mid_rows = slice(reach, reach + rows)
    first = lane_index((1, rows, width)) < width // 2
    centre, along_wall, along_stream = [], [], []
    for f in range(4):
        here = packed[f, :, mid_rows, :]
        centre.append(here)
        below = packed[f, :, reach + 1 : reach + rows + 1, :]
        above = packed[f, :, reach - 1 : reach + rows - 1, :]
        along_wall.append((below - above) * 0.5)
        after = jnp.where(first, pltpu.roll(here[:1], width // 2, 2), 0.0)
        before = jnp.where(first, 0.0, pltpu.roll(here[layers - 1 :], width // 2, 2))
        ahead = jnp.concatenate([here[1:], after], axis=0)
        behind = jnp.concatenate([before, here[: layers - 1]], axis=0)
        along_stream.append((ahead - behind) * 0.5)

    lane = lane_index((rows, width))
    table = jnp.zeros((rows, width), jnp.float32)
    first = lane_index((layers, rows, width)) < width // 2
    in_first = me_s == 1
    for i in range(3):
        exact = flux[i] - centre[i] * centre[3]
        similar = second[4 + i] - second[i] * second[3]
        total = slopes[i] * slopes[3] + along_wall[i] * along_wall[3]
        clark = clark_coef * (total + along_stream[i] * along_stream[3])
        terms = (exact * clark, exact * similar, exact * exact, clark * clark, similar * similar)
        for q, term in enumerate(terms):
            value = jnp.sum(jnp.sum(term, axis=0), axis=1, keepdims=True)
            table = jnp.where(lane == 3 * q + i, value, table)
        keep_ref[i] = clark
        keep_ref[3 + i] = similar
        clark = jnp.where(in_first, clark, pltpu.roll(clark, width // 2, 2))
        similar = jnp.where(in_first, pltpu.roll(similar, width // 2, 2), similar)
        send_ref[i] = jnp.where(first, clark, similar)
    sums_ref[...] = table


def finish_kernel(
    plane_cells, sums, keep, come, clark_model, similar_model, clark_corr, similar_corr
):
    _, layers, rows, width = keep.shape
    me_s = lax.axis_index("stream")
    table = sums[...] / plane_cells
    lane = lane_index((rows, width))
    useful = lane // (width // 2) == me_s
    corr = jnp.zeros((rows, width), jnp.float32)
    for i in range(3):
        cross_c, cross_s, power_e, power_c, power_s = (
            table[:, 3 * q + i : 3 * q + i + 1] for q in range(5)
        )
        packed = come[i]
        turned = pltpu.roll(packed, width // 2, 2)
        clark = jnp.where(useful[None], keep[i], jnp.where(me_s == 0, turned, packed))
        similar = jnp.where(useful[None], keep[3 + i], jnp.where(me_s == 0, packed, turned))
        clark_model[i] = clark / jnp.sqrt(power_c + small_eps)[None]
        similar_model[i] = similar / jnp.sqrt(power_s + small_eps)[None]
        value = cross_c / jnp.sqrt((power_e + small_eps) * (power_c + small_eps))
        corr = jnp.where(lane == i, value, corr)
        value = cross_s / jnp.sqrt((power_e + small_eps) * (power_s + small_eps))
        corr = jnp.where(lane == 8 + i, value, corr)
    square = jnp.concatenate([corr, jnp.zeros((width - rows, width), jnp.float32)], axis=0)
    turned = square.T
    clark_corr[...] = turned[:3, :rows]
    similar_corr[...] = turned[8:11, :rows]


def call(kernel, name, ins, outs, scratch=(), mib=4, hint=None):
    cost = hint and pl.CostEstimate(flops=hint, bytes_accessed=0, transcendentals=0)
    return pl.pallas_call(
        kernel,
        out_shape=tuple(jax.ShapeDtypeStruct(shape, jnp.float32) for shape in outs),
        in_specs=[pl.BlockSpec(memory_space=pltpu.VMEM)] * len(ins),
        out_specs=tuple(pl.BlockSpec(memory_space=pltpu.VMEM) for _ in outs),
        scratch_shapes=[pltpu.VMEM(shape, dtype) for shape, dtype in scratch],
        compiler_params=pltpu.CompilerParams(vmem_limit_bytes=mib * 1024 * 1024),
        cost_estimate=cost,
        name=name,
    )(*ins)


def shards(fields):
    _, layers, rows, width = fields.shape
    spans = lax.axis_size("span")
    walls = lax.axis_size("wall")
    streams = lax.axis_size("stream")
    both = streams * layers
    cells = both * rows

    def swap(value):
        return lax.ppermute(value, "stream", [(0, 1), (1, 0)])

    def pair_a(value):
        return lax.ppermute(value, "wall", [(w, w ^ 1) for w in range(walls)])

    def pair_b(value):
        return lax.ppermute(
            value, "wall", [(w, min(max(((w + 1) ^ 1) - 1, 0), walls - 1)) for w in range(walls)]
        )

    def place(p, s):
        return (p % spans) * streams + s

    to_other, to_same = [], []
    for p in range(spans):
        to_other += [(place(p, 0), place(p - 1, 1)), (place(p, 1), place(p + 1, 0))]
        to_same += [(place(p, 1), place(p - 1, 1)), (place(p, 0), place(p + 1, 0))]

    message, strip = (2 * layers + layers // 2, rows, width), (layers // 2, rows, width)
    to_partner, mine, first, second = call(
        pack_kernel, "pack", (fields,), (message, message, strip, strip)
    )
    part = swap(to_partner)
    part_strip = lax.ppermute(first, ("span", "stream"), to_other)
    own_strip = lax.ppermute(second, ("span", "stream"), to_same)
    mine_now, b_mine, a_mine = lax.optimization_barrier((mine, pair_b(mine), pair_a(mine)))
    (rest,) = call(
        rest_kernel,
        "rest",
        (part, own_strip, part_strip),
        ((message[0] + layers, rows, width),),
        hint=2**35,
    )
    a_rest, b_rest = pair_a(rest), pair_b(rest)

    matrices = np.zeros((2 * cells + 4 * width, 4 * cells), ml_dtypes.bfloat16)
    matrices[:cells], matrices[cells : 2 * cells] = plane_constants(both, rows)
    single_pass, split_pass = span_constants(width)
    matrices[2 * cells : 2 * cells + 2 * width, : 2 * width] = single_pass
    matrices[2 * cells :, 2 * width : 6 * width] = split_pass
    weights = jnp.asarray(matrices)
    single, brief = jnp.float32, jnp.bfloat16
    block = (4, both, rows, width)
    pieces = [((cells, 4 * width), brief), ((cells, 4 * width), brief)]
    upper, lower, products = call(
        centre_kernel,
        "centre",
        (mine_now, rest, weights),
        ((cells, 4 * width), (cells, 4 * width), (cells, 3 * width)),
        [(block, single), *pieces, ((cells, 3 * width), brief), ((cells, 3 * width), brief)],
        mib=16,
        hint=2**31,
    )
    quarter = (4, layers, rows, width)
    a_raw, a_packed, a_slopes, a_second = call(
        mate_kernel,
        "mate",
        (a_mine, a_rest, upper, lower, weights),
        (block, quarter, (4, layers, reach, width), (cells, 7 * width)),
        [*pieces, ((cells, 7 * width), brief), ((cells, 7 * width), brief), (block, single)],
        mib=16,
        hint=2**29,
    )
    keep, send, sums = call(
        functools.partial(flux_kernel, walls),
        "flux",
        (b_mine, b_rest, a_raw, a_packed, a_slopes, a_second, upper, lower, products, weights),
        ((6, layers, rows, width), (3, layers, rows, width), (rows, width)),
        [
            (block, single),
            ((cells, 4 * width), brief),
            ((cells, 4 * width), brief),
            ((cells, 3 * width), brief),
            ((cells, 3 * width), brief),
            (block, single),
            ((cells, 7 * width), brief),
            ((cells, 7 * width), brief),
            ((4, layers, 2 * rows, width), single),
            (quarter, single),
        ],
        mib=24,
    )

    come = swap(send)

    def from_span(value, step):
        return lax.ppermute(value, "span", [(p, p ^ step) for p in range(spans)])

    step = 1
    while step < spans:
        if 2 * step < spans:
            far = from_span(sums, 3 * step) + from_span(sums, 2 * step)
            sums = (sums + from_span(sums, step)) + far
        else:
            sums = sums + from_span(sums, step)
        step *= 4
    sums = sums + swap(sums)
    block, corr = (3, layers, rows, width), (3, rows)
    return call(
        functools.partial(finish_kernel, float(layers * width * spans * streams)),
        "finish",
        (sums, keep, come),
        (block, block, corr, corr),
    )


def solution(mesh):
    return jax.shard_map(
        shards,
        mesh=mesh,
        in_specs=(P(None, "stream", "wall", "span"),),
        out_specs=(
            P(None, "stream", "wall", "span"),
            P(None, "stream", "wall", "span"),
            P(None, "wall"),
            P(None, "wall"),
        ),
        check_vma=False,
    )
```

```python
import functools
import math

import jax
import jax.numpy as jnp
import ml_dtypes
import numpy as np
from jax import lax
from jax.experimental import pallas as pl
from jax.experimental.pallas import tpu as pltpu
from jax.sharding import PartitionSpec as P

raw_taps = [math.exp(-((k - 8) ** 2) / 18.0) for k in range(17)]
filter_taps = [value / sum(raw_taps) for value in raw_taps]
clark_coef = 9.0
small_eps = 1e-06

reach = 8
rim = 2 * reach


def split_constant(matrix):
    high = matrix.astype(ml_dtypes.bfloat16)
    low = (matrix - high.astype(np.float64)).astype(ml_dtypes.bfloat16)
    return high, low


def band(outs, ins, offset):
    matrix = np.zeros((outs, ins))
    for o in range(outs):
        for i in range(ins):
            k = i - o - offset + reach
            if 0 <= k <= 2 * reach:
                matrix[o, i] = filter_taps[k]
    return matrix


def plane_constants(layers, rows):
    stream = band(layers, layers, 0)
    wall = band(rows, 2 * rows, reach)
    near = np.arange(reach, reach + rows)
    far = np.setdiff1d(np.arange(2 * rows), near)
    parts = [np.arange(rows), np.arange(rows, 2 * rows), near, far]
    blocks = [np.kron(stream, wall[:, part]) for part in parts]
    return split_constant(np.concatenate(blocks, axis=1))


def span_constants(width):
    circle = np.zeros((width, width))
    for o in range(width):
        for k in range(2 * reach + 1):
            circle[(o + k - reach) % width, o] = filter_taps[k]
    half = width // 2

    def parts(matrix):
        high, low = split_constant(matrix)
        return np.block([[high, low], [high, np.zeros_like(low)]])

    packed = []
    for layers in range(2):
        row = []
        for s in range(2):
            matrix = np.zeros((width, width))
            matrix[:, layers * half : (layers + 1) * half] = circle[:, s * half : (s + 1) * half]
            row.append(parts(matrix))
        packed.append(np.concatenate(row, axis=1))
    return parts(circle), np.concatenate(packed, axis=0)


def halves(value):
    high = value.astype(jnp.bfloat16)
    return high, (value - high.astype(jnp.float32)).astype(jnp.bfloat16)


def dot(a, b):
    return lax.dot_general(a, b, (((1,), (0,)), ((), ())), preferred_element_type=jnp.float32)


def lane_index(shape):
    return lax.broadcasted_iota(jnp.int32, shape, len(shape) - 1)


def unit_index(shape):
    return lane_index(shape) // rim


def pack_halves(block, half):
    width = block.shape[-1]
    in_place = lane_index(block.shape[1:]) // (width // 2) == half
    for pair in range(2):
        moved = pltpu.roll(block[2 * pair + 1], width // 2, 2)
        yield pair, jnp.where(in_place, block[2 * pair], moved)


def pack_strip(block, unit):
    _, layers, rows, width = block.shape
    half = layers // 2
    units = unit_index((half, rows, width))
    total = jnp.zeros((half, rows, width), jnp.float32)
    for k in range(2):
        for f in range(4):
            step = 2 * f + k
            cells = block[f, k * half : (k + 1) * half]
            cells = pltpu.roll(cells, step * rim, 2) if step else cells
            total = jnp.where(units == lax.rem(unit + step, width // rim), cells, total)
    return total


def strip_tile(inner, outer, me_s):
    width = inner.shape[-1]
    is_outer = lax.rem(unit_index(inner.shape), 2) == 1 - me_s
    for k in range(2):
        shift = (width - k * rim) % width
        pieces = [pltpu.roll(strip, shift, 2) if k else strip for strip in (inner, outer)]
        yield k, jnp.where(is_outer, pieces[1], pieces[0])


def pack_kernel(own, to_partner, to_mine, to_other, to_same):
    _, layers, _, _ = own.shape
    me_s = lax.axis_index("stream")
    for message, half in ((to_partner, 1 - me_s), (to_mine, me_s)):
        for pair, tile in pack_halves(own, half):
            message[pair * layers : (pair + 1) * layers] = tile
        message[2 * layers :] = pack_strip(own, 4 - half)
    to_other[...] = pack_strip(own, 7 * me_s)
    to_same[...] = pack_strip(own, 7 * (1 - me_s))


def rest_kernel(part, own_strip, part_strip, rest):
    count, half = part.shape[0], own_strip.shape[0]
    rest[:count] = part[...]
    rest[count : count + half] = own_strip[...]
    rest[count + half :] = part_strip[...]


def unpack(mine, rest, me_s):
    count, rows, width = mine.shape
    layers = rest.shape[0] - count
    half = layers // 2
    unit = unit_index((half, rows, width))
    first = 4 * (1 - me_s)
    in_strip = (unit == first) | (unit == first + 3)
    for which, packed in enumerate((mine, rest)):
        far = rest[count + which * half : count + (which + 1) * half]
        for k, strip in strip_tile(packed[2 * layers : count], far, me_s):
            layer = (me_s if which == 0 else 1 - me_s) * layers + k * half
            for f in range(4):
                start = f // 2 * layers + k * half
                cells = packed[start : start + half]
                cells = pltpu.roll(cells, width // 2, 2) if f % 2 else cells
                moved = pltpu.roll(strip, width - 2 * f * rim, 2) if f else strip
                yield f, layer, jnp.where(in_strip, moved, cells)


def column(t, width=128):
    return slice(t * width, (t + 1) * width)


def put_parts(parts, down, across, value):
    third = parts.shape[0] // 3
    high, low = halves(value)
    for k, part in enumerate((high, high, low)):
        parts[pl.ds(k * third + down, value.shape[0]), across] = part


def planes_of(planes, part, parts):
    depth = parts.shape[0]
    start = part * depth if isinstance(part, int) else pl.multiple_of(part * depth, depth)
    return dot(planes[:, pl.ds(start, depth)], parts[...])


def bring(mine, rest, raw, parts, keep=None):
    rows, width = mine.shape[1:]
    for f, layer, value in unpack(mine, rest, lax.axis_index("stream")):
        count = value.shape[0]
        value = value if keep is None else value * keep
        raw[f, pl.ds(layer, count)] = value
        down = pl.multiple_of(layer * rows, count * rows)
        put_parts(parts, down, column(f), value.reshape(-1, width))


def centre_kernel(
    mine, rest, planes, upper, lower, products, centre, parts, prod
):
    bring(mine, rest, centre, parts)
    for i in range(3):
        value = centre[i] * centre[3]
        put_parts(prod, 0, column(i), value.reshape(-1, value.shape[-1]))
    upper[...] = planes_of(planes, 1, parts)
    lower[...] = planes_of(planes, 0, parts)
    products[...] = planes_of(planes, 2, prod)


def span_pass(spans, planes, both):
    cells = planes.shape[0]
    rows = cells // both
    width = 128
    span_w = spans[: 2 * width, : 2 * width]
    high, low = halves(planes)
    tiles = planes.shape[1] // width
    parts = [jnp.concatenate([high[:, column(t)], low[:, column(t)]], axis=1) for t in range(tiles)]
    result = dot(jnp.concatenate(parts, axis=0), span_w)
    result = result[:, :width] + result[:, width:]
    return [result[t * cells : (t + 1) * cells].reshape(both, rows, width) for t in range(tiles)]


def second_input(means, parts):
    tiles = means + [means[i] * means[3] for i in range(3)]
    for t, value in enumerate(tiles):
        put_parts(parts, 0, column(t), value.reshape(-1, value.shape[-1]))


def packed_pass(spans, planes):
    cells = planes.shape[0]
    some, width = cells // 2, 128
    me_s = lax.axis_index("stream")
    along = pl.ds(pl.multiple_of((1 + me_s) * 2 * width, 2 * width), 2 * width)
    matrix = spans[:, along]
    high, low = halves(planes)
    tiles = planes.shape[1] // width
    parts = [
        jnp.concatenate(
            [high[:some, column(t)], low[:some, column(t)], high[some:, column(t)], low[some:, column(t)]],
            axis=1,
        )
        for t in range(tiles)
    ]
    result = dot(jnp.concatenate(parts, axis=0), matrix)
    result = result[:, :width] + result[:, width:]
    return [result[t * some : (t + 1) * some] for t in range(tiles)]


def pack_layers(own, other, me_s, shift=0):
    width = own.shape[-1]
    in_place = lane_index(own.shape) // (width // 2) == me_s
    own = pltpu.roll(own, shift % width, 2) if shift else own
    return jnp.where(in_place, own, pltpu.roll(other, (shift + width // 2) % width, 2))


def pack_means(mean, means, rows_near):
    for t, value in enumerate(means):
        mean[t] = value
    both = mean.shape[1]
    me_s = lax.axis_index("stream")
    own, other = pl.ds(me_s * (both // 2), both // 2), pl.ds((1 - me_s) * (both // 2), both // 2)
    for t in range(4):
        near = mean[t, own, rows_near, :], mean[t, other, rows_near, :]
        slope = (pack_layers(*near, me_s, -1) - pack_layers(*near, me_s, 1)) * 0.5
        yield t, pack_layers(mean[t, own], mean[t, other], me_s), slope


def mate_kernel(
    a_mine, a_rest, upper, lower, matrices, spans, raw, packed, slopes, second, parts, mid, mean
):
    both, rows = raw.shape[1:3]
    odd = lax.rem(lax.axis_index("wall"), 2)
    bring(a_mine, a_rest, raw, parts)
    planes = jnp.where(odd == 1, upper[...], lower[...])
    planes = planes + planes_of(matrices, 1 - odd, parts)
    means = span_pass(spans, planes, both)
    for t, value, slope in pack_means(mean, means, pl.ds(pl.multiple_of(odd * reach, reach), reach)):
        packed[t] = value
        slopes[t] = slope
    second_input(means, mid)
    second[...] = planes_of(matrices, 1 - odd, mid)


def flux_kernel(
    walls, b_mine, b_rest, a_raw, a_packed, a_slopes, a_second, upper, lower, products, matrices, spans,
    keep_ref, send_ref, sums_ref,
    raw, parts, prod, mean, mid, packed, slopes,
):
    _, layers, rows, width = keep_ref.shape
    both = 2 * layers
    cells = both * rows
    me_s = lax.axis_index("stream")
    me_w = lax.axis_index("wall")
    odd = lax.rem(me_w, 2)
    at_end = (me_w == 0) | (me_w == walls - 1)
    keep_b = jnp.where(at_end, 0.0, 1.0).astype(jnp.float32)

    bring(b_mine, b_rest, raw, parts, keep_b)

    planes = jnp.where(odd == 0, upper[...], lower[...])
    planes = planes + planes_of(matrices, odd, parts)
    row = lax.rem(lax.broadcasted_iota(jnp.int32, planes.shape, 0), rows)
    inside = (row < reach) == (odd == 1)
    planes = jnp.where(jnp.logical_or(inside, jnp.logical_not(at_end)), planes, 0.0)
    means = span_pass(spans, planes, both)
    rows_b = pl.ds(pl.multiple_of(odd * rows, rows), rows)
    rows_a = pl.ds(pl.multiple_of((1 - odd) * rows, rows), rows)
    near_b = pl.ds(pl.multiple_of(odd * reach, reach), reach)
    near_a = pl.ds(pl.multiple_of((1 - odd) * reach, reach), reach)
    for t, value, slope in pack_means(mean, means, near_a):
        packed[t, :, rows_b, :] = value
        packed[t, :, rows_a, :] = a_packed[t]
        slopes[t, :, near_b, :] = slope
        slopes[t, :, near_a, :] = a_slopes[t]
    second_input(means, mid)
    second = packed_pass(spans, a_second[...] + planes_of(matrices, odd, mid))
    second = [value.reshape(layers, rows, width) for value in second]

    def around(f):
        above = jnp.where(odd == 0, raw[f, :, rows - reach :, :], a_raw[f, :, rows - reach :, :])
        below = jnp.where(odd == 1, raw[f, :, :reach, :], a_raw[f, :, :reach, :])
        return jnp.concatenate([above, below], axis=1)

    temperature = around(3)
    for i in range(3):
        value = (around(i) * temperature).reshape(cells, width)
        put_parts(prod, 0, column(i), value)
    flux = packed_pass(spans, products[...] + planes_of(matrices, 3, prod))
    flux = [value.reshape(layers, rows, width) for value in flux]

    mid_rows = slice(reach, reach + rows)
    first = lane_index((1, rows, width)) < width // 2
    centre, along_wall, along_stream = [], [], []
    for f in range(4):
        here = packed[f, :, mid_rows, :]
        centre.append(here)
        below = packed[f, :, reach + 1 : reach + rows + 1, :]
        above = packed[f, :, reach - 1 : reach + rows - 1, :]
        along_wall.append((below - above) * 0.5)
        after = jnp.where(first, pltpu.roll(here[:1], width // 2, 2), 0.0)
        before = jnp.where(first, 0.0, pltpu.roll(here[layers - 1 :], width // 2, 2))
        ahead = jnp.concatenate([here[1:], after], axis=0)
        behind = jnp.concatenate([before, here[: layers - 1]], axis=0)
        along_stream.append((ahead - behind) * 0.5)

    lane = lane_index((rows, width))
    table = jnp.zeros((rows, width), jnp.float32)
    first = lane_index((layers, rows, width)) < width // 2
    in_first = me_s == 1
    for i in range(3):
        exact = flux[i] - centre[i] * centre[3]
        similar = second[4 + i] - second[i] * second[3]
        total = slopes[i] * slopes[3] + along_wall[i] * along_wall[3]
        clark = clark_coef * (total + along_stream[i] * along_stream[3])
        terms = (exact * clark, exact * similar, exact * exact, clark * clark, similar * similar)
        for q, term in enumerate(terms):
            value = jnp.sum(jnp.sum(term, axis=0), axis=1, keepdims=True)
            table = jnp.where(lane == 3 * q + i, value, table)
        keep_ref[i] = clark
        keep_ref[3 + i] = similar
        clark = jnp.where(in_first, clark, pltpu.roll(clark, width // 2, 2))
        similar = jnp.where(in_first, pltpu.roll(similar, width // 2, 2), similar)
        send_ref[i] = jnp.where(first, clark, similar)
    sums_ref[...] = table


def finish_kernel(
    plane_cells, sums, keep, come, clark_model, similar_model, clark_corr, similar_corr
):
    _, layers, rows, width = keep.shape
    me_s = lax.axis_index("stream")
    table = sums[...] / plane_cells
    lane = lane_index((rows, width))
    useful = lane // (width // 2) == me_s
    corr = jnp.zeros((rows, width), jnp.float32)
    for i in range(3):
        cross_c, cross_s, power_e, power_c, power_s = (
            table[:, 3 * q + i : 3 * q + i + 1] for q in range(5)
        )
        packed = come[i]
        turned = pltpu.roll(packed, width // 2, 2)
        clark = jnp.where(useful[None], keep[i], jnp.where(me_s == 0, turned, packed))
        similar = jnp.where(useful[None], keep[3 + i], jnp.where(me_s == 0, packed, turned))
        clark_model[i] = clark / jnp.sqrt(power_c + small_eps)[None]
        similar_model[i] = similar / jnp.sqrt(power_s + small_eps)[None]
        value = cross_c / jnp.sqrt((power_e + small_eps) * (power_c + small_eps))
        corr = jnp.where(lane == i, value, corr)
        value = cross_s / jnp.sqrt((power_e + small_eps) * (power_s + small_eps))
        corr = jnp.where(lane == 8 + i, value, corr)
    square = jnp.concatenate([corr, jnp.zeros((width - rows, width), jnp.float32)], axis=0)
    turned = square.T
    clark_corr[...] = turned[:3, :rows]
    similar_corr[...] = turned[8:11, :rows]


def call(kernel, name, ins, outs, scratch=(), mib=4, hint=None):
    cost = hint and pl.CostEstimate(flops=hint, bytes_accessed=0, transcendentals=0)
    return pl.pallas_call(
        kernel,
        out_shape=tuple(jax.ShapeDtypeStruct(shape, jnp.float32) for shape in outs),
        in_specs=[pl.BlockSpec(memory_space=pltpu.VMEM)] * len(ins),
        out_specs=tuple(pl.BlockSpec(memory_space=pltpu.VMEM) for _ in outs),
        scratch_shapes=[pltpu.VMEM(shape, dtype) for shape, dtype in scratch],
        compiler_params=pltpu.CompilerParams(vmem_limit_bytes=mib * 1024 * 1024),
        cost_estimate=cost,
        name=name,
    )(*ins)


def shards(fields):
    _, layers, rows, width = fields.shape
    spans = lax.axis_size("span")
    walls = lax.axis_size("wall")
    streams = lax.axis_size("stream")
    both = streams * layers
    cells = both * rows

    def swap(value):
        return lax.ppermute(value, "stream", [(0, 1), (1, 0)])

    def pair_a(value):
        return lax.ppermute(value, "wall", [(w, w ^ 1) for w in range(walls)])

    def pair_b(value):
        return lax.ppermute(
            value, "wall", [(w, min(max(((w + 1) ^ 1) - 1, 0), walls - 1)) for w in range(walls)]
        )

    def place(p, s):
        return (p % spans) * streams + s

    to_other, to_same = [], []
    for p in range(spans):
        to_other += [(place(p, 0), place(p - 1, 1)), (place(p, 1), place(p + 1, 0))]
        to_same += [(place(p, 1), place(p - 1, 1)), (place(p, 0), place(p + 1, 0))]

    message, strip = (2 * layers + layers // 2, rows, width), (layers // 2, rows, width)
    to_partner, mine, first, second = call(
        pack_kernel, "pack", (fields,), (message, message, strip, strip)
    )
    part = swap(to_partner)
    part_strip = lax.ppermute(first, ("span", "stream"), to_other)
    own_strip = lax.ppermute(second, ("span", "stream"), to_same)
    mine_now, b_mine, a_mine = lax.optimization_barrier((mine, pair_b(mine), pair_a(mine)))
    (rest,) = call(
        rest_kernel,
        "rest",
        (part, own_strip, part_strip),
        ((message[0] + layers, rows, width),),
        hint=2**35,
    )
    a_rest, b_rest = pair_a(rest), pair_b(rest)

    high, low = plane_constants(both, rows)
    thirds = [(high[:, k : k + cells], low[:, k : k + cells], high[:, k : k + cells]) for k in range(0, 4 * cells, cells)]
    matrices = jnp.asarray(np.concatenate([part for third in thirds for part in third], axis=1))
    single_pass, split_pass = span_constants(width)
    both_passes = np.zeros((4 * width, 6 * width), ml_dtypes.bfloat16)
    both_passes[: 2 * width, : 2 * width] = single_pass
    both_passes[:, 2 * width :] = split_pass
    passes = jnp.asarray(both_passes)
    single, brief = jnp.float32, jnp.bfloat16
    block, quarter = (4, both, rows, width), (4, layers, rows, width)
    four, three, seven = (((3 * cells, n * width), brief) for n in (4, 3, 7))
    upper, lower, products = call(
        centre_kernel,
        "centre",
        (mine_now, rest, matrices),
        ((cells, 4 * width), (cells, 4 * width), (cells, 3 * width)),
        [(block, single), four, three],
        mib=16,
        hint=2**31,
    )
    a_raw, a_packed, a_slopes, a_second = call(
        mate_kernel,
        "mate",
        (a_mine, a_rest, upper, lower, matrices, passes),
        (block, quarter, (4, layers, reach, width), (cells, 7 * width)),
        [four, seven, (block, single)],
        mib=16,
        hint=2**29,
    )
    keep, send, sums = call(
        functools.partial(flux_kernel, walls),
        "flux",
        (b_mine, b_rest, a_raw, a_packed, a_slopes, a_second, upper, lower, products, matrices, passes),
        ((6, layers, rows, width), (3, layers, rows, width), (rows, width)),
        [
            (block, single),
            four,
            three,
            (block, single),
            seven,
            ((4, layers, 2 * rows, width), single),
            (quarter, single),
        ],
        mib=24,
    )

    come = swap(send)

    def from_span(value, step):
        return lax.ppermute(value, "span", [(p, p ^ step) for p in range(spans)])

    step = 1
    while step < spans:
        if 2 * step < spans:
            far = from_span(sums, 3 * step) + from_span(sums, 2 * step)
            sums = (sums + from_span(sums, step)) + far
        else:
            sums = sums + from_span(sums, step)
        step *= 4
    sums = sums + swap(sums)
    block, corr = (3, layers, rows, width), (3, rows)
    return call(
        functools.partial(finish_kernel, float(layers * width * spans * streams)),
        "finish",
        (sums, keep, come),
        (block, block, corr, corr),
    )


def solution(mesh):
    return jax.shard_map(
        shards,
        mesh=mesh,
        in_specs=(P(None, "stream", "wall", "span"),),
        out_specs=(
            P(None, "stream", "wall", "span"),
            P(None, "stream", "wall", "span"),
            P(None, "wall"),
            P(None, "wall"),
        ),
        check_vma=False,
    )
```

```python
import functools
import math

import jax
import jax.numpy as jnp
import ml_dtypes
import numpy as np
from jax import lax
from jax.experimental import pallas as pl
from jax.experimental.pallas import tpu as pltpu
from jax.sharding import PartitionSpec as P

raw_taps = [math.exp(-((k - 8) ** 2) / 18.0) for k in range(17)]
filter_taps = [value / sum(raw_taps) for value in raw_taps]
clark_coef = 9.0
small_eps = 1e-06

reach = 8
rim = 2 * reach


def split_constant(matrix):
    high = matrix.astype(ml_dtypes.bfloat16)
    low = (matrix - high.astype(np.float64)).astype(ml_dtypes.bfloat16)
    return high, low


def band(outs, ins, offset):
    matrix = np.zeros((outs, ins))
    for o in range(outs):
        for i in range(ins):
            k = i - o - offset + reach
            if 0 <= k <= 2 * reach:
                matrix[o, i] = filter_taps[k]
    return matrix


def plane_constants(layers, rows):
    stream = band(layers, layers, 0)
    wall = band(rows, 2 * rows, reach)
    near = np.arange(reach, reach + rows)
    far = np.setdiff1d(np.arange(2 * rows), near)
    parts = [np.arange(rows), np.arange(rows, 2 * rows), near, far]
    blocks = [np.kron(stream, wall[:, part]) for part in parts]
    return split_constant(np.concatenate(blocks, axis=1))


def span_constants(width):
    circle = np.zeros((width, width))
    for o in range(width):
        for k in range(2 * reach + 1):
            circle[(o + k - reach) % width, o] = filter_taps[k]
    half = width // 2

    def parts(matrix):
        high, low = split_constant(matrix)
        return np.block([[high, low], [high, np.zeros_like(low)]])

    packed = []
    for layers in range(2):
        row = []
        for s in range(2):
            matrix = np.zeros((width, width))
            matrix[:, layers * half : (layers + 1) * half] = circle[:, s * half : (s + 1) * half]
            row.append(parts(matrix))
        packed.append(np.concatenate(row, axis=1))
    return parts(circle), np.concatenate(packed, axis=0)


def halves(value):
    high = value.astype(jnp.bfloat16)
    return high, (value - high.astype(jnp.float32)).astype(jnp.bfloat16)


def dot(a, b):
    return lax.dot_general(a, b, (((1,), (0,)), ((), ())), preferred_element_type=jnp.float32)


def lane_index(shape):
    return lax.broadcasted_iota(jnp.int32, shape, len(shape) - 1)


def unit_index(shape):
    return lane_index(shape) // rim


def pack_halves(block, half):
    width = block.shape[-1]
    in_place = lane_index(block.shape[1:]) // (width // 2) == half
    for pair in range(2):
        moved = pltpu.roll(block[2 * pair + 1], width // 2, 2)
        yield pair, jnp.where(in_place, block[2 * pair], moved)


def pack_strip(block, unit):
    _, layers, rows, width = block.shape
    half = layers // 2
    units = unit_index((half, rows, width))
    total = jnp.zeros((half, rows, width), jnp.float32)
    for k in range(2):
        for f in range(4):
            step = 2 * f + k
            cells = block[f, k * half : (k + 1) * half]
            cells = pltpu.roll(cells, step * rim, 2) if step else cells
            total = jnp.where(units == lax.rem(unit + step, width // rim), cells, total)
    return total


def strip_tile(inner, outer, me_s):
    width = inner.shape[-1]
    is_outer = lax.rem(unit_index(inner.shape), 2) == 1 - me_s
    for k in range(2):
        shift = (width - k * rim) % width
        pieces = [pltpu.roll(strip, shift, 2) if k else strip for strip in (inner, outer)]
        yield k, jnp.where(is_outer, pieces[1], pieces[0])


def pack_kernel(own, to_partner, to_mine, to_other, to_same):
    _, layers, _, _ = own.shape
    me_s = lax.axis_index("stream")
    for message, half in ((to_partner, 1 - me_s), (to_mine, me_s)):
        for pair, tile in pack_halves(own, half):
            message[pair * layers : (pair + 1) * layers] = tile
        message[2 * layers :] = pack_strip(own, 4 - half)
    to_other[...] = pack_strip(own, 7 * me_s)
    to_same[...] = pack_strip(own, 7 * (1 - me_s))


def rest_kernel(part, part_strip, own_strip, rest):
    count, half = part.shape[0], own_strip.shape[0]
    rest[:count] = part[...]
    rest[count : count + half] = own_strip[...]
    rest[count + half :] = part_strip[...]


def unpack(mine, rest, me_s):
    count, rows, width = mine.shape
    layers = rest.shape[0] - count
    half = layers // 2
    unit = unit_index((half, rows, width))
    first = 4 * (1 - me_s)
    in_strip = (unit == first) | (unit == first + 3)
    for which, packed in enumerate((mine, rest)):
        far = rest[count + which * half : count + (which + 1) * half]
        for k, strip in strip_tile(packed[2 * layers : count], far, me_s):
            layer = (me_s if which == 0 else 1 - me_s) * layers + k * half
            for f in range(4):
                start = f // 2 * layers + k * half
                cells = packed[start : start + half]
                cells = pltpu.roll(cells, width // 2, 2) if f % 2 else cells
                moved = pltpu.roll(strip, width - 2 * f * rim, 2) if f else strip
                yield f, layer, jnp.where(in_strip, moved, cells)


def column(t, width=128):
    return slice(t * width, (t + 1) * width)


def put_parts(parts, down, across, value):
    third = parts.shape[0] // 3
    high, low = halves(value)
    for k, part in enumerate((high, high, low)):
        parts[pl.ds(k * third + down, value.shape[0]), across] = part


def planes_of(planes, part, parts):
    depth = parts.shape[0]
    start = part * depth if isinstance(part, int) else pl.multiple_of(part * depth, depth)
    return dot(planes[:, pl.ds(start, depth)], parts[...])


def bring(mine, rest, raw, parts, keep=None):
    rows, width = mine.shape[1:]
    for f, layer, value in unpack(mine, rest, lax.axis_index("stream")):
        count = value.shape[0]
        value = value if keep is None else value * keep
        raw[f, pl.ds(layer, count)] = value
        down = pl.multiple_of(layer * rows, count * rows)
        put_parts(parts, down, column(f), value.reshape(-1, width))


def centre_kernel(
    mine, rest, planes, upper, lower, products, centre, parts, prod
):
    bring(mine, rest, centre, parts)
    for i in range(3):
        value = centre[i] * centre[3]
        put_parts(prod, 0, column(i), value.reshape(-1, value.shape[-1]))
    upper[...] = planes_of(planes, 1, parts)
    lower[...] = planes_of(planes, 0, parts)
    products[...] = planes_of(planes, 2, prod)


def span_pass(spans, planes, both):
    cells = planes.shape[0]
    rows = cells // both
    width = 128
    span_w = spans[: 2 * width, : 2 * width]
    high, low = halves(planes)
    tiles = planes.shape[1] // width
    parts = [jnp.concatenate([high[:, column(t)], low[:, column(t)]], axis=1) for t in range(tiles)]
    result = dot(jnp.concatenate(parts, axis=0), span_w)
    result = result[:, :width] + result[:, width:]
    return [result[t * cells : (t + 1) * cells].reshape(both, rows, width) for t in range(tiles)]


def second_input(means, parts):
    tiles = means + [means[i] * means[3] for i in range(3)]
    for t, value in enumerate(tiles):
        put_parts(parts, 0, column(t), value.reshape(-1, value.shape[-1]))


def packed_pass(spans, planes):
    cells = planes.shape[0]
    some, width = cells // 2, 128
    me_s = lax.axis_index("stream")
    along = pl.ds(pl.multiple_of((1 + me_s) * 2 * width, 2 * width), 2 * width)
    matrix = spans[:, along]
    high, low = halves(planes)
    tiles = planes.shape[1] // width
    parts = [
        jnp.concatenate(
            [high[:some, column(t)], low[:some, column(t)], high[some:, column(t)], low[some:, column(t)]],
            axis=1,
        )
        for t in range(tiles)
    ]
    result = dot(jnp.concatenate(parts, axis=0), matrix)
    result = result[:, :width] + result[:, width:]
    return [result[t * some : (t + 1) * some] for t in range(tiles)]


def pack_layers(own, other, me_s, shift=0):
    width = own.shape[-1]
    in_place = lane_index(own.shape) // (width // 2) == me_s
    own = pltpu.roll(own, shift % width, 2) if shift else own
    return jnp.where(in_place, own, pltpu.roll(other, (shift + width // 2) % width, 2))


def pack_means(mean, means, rows_near):
    for t, value in enumerate(means):
        mean[t] = value
    both = mean.shape[1]
    me_s = lax.axis_index("stream")
    own, other = pl.ds(me_s * (both // 2), both // 2), pl.ds((1 - me_s) * (both // 2), both // 2)
    for t in range(4):
        near = mean[t, own, rows_near, :], mean[t, other, rows_near, :]
        slope = (pack_layers(*near, me_s, -1) - pack_layers(*near, me_s, 1)) * 0.5
        yield t, pack_layers(mean[t, own], mean[t, other], me_s), slope


def mate_kernel(
    a_mine, a_rest, upper, lower, matrices, spans, raw, packed, slopes, second, parts, mid, mean
):
    both, rows = raw.shape[1:3]
    odd = lax.rem(lax.axis_index("wall"), 2)
    bring(a_mine, a_rest, raw, parts)
    planes = jnp.where(odd == 1, upper[...], lower[...])
    planes = planes + planes_of(matrices, 1 - odd, parts)
    means = span_pass(spans, planes, both)
    for t, value, slope in pack_means(mean, means, pl.ds(pl.multiple_of(odd * reach, reach), reach)):
        packed[t] = value
        slopes[t] = slope
    second_input(means, mid)
    second[...] = planes_of(matrices, 1 - odd, mid)


def flux_kernel(
    walls, b_mine, b_rest, a_raw, a_packed, a_slopes, a_second, upper, lower, products, matrices, spans,
    keep_ref, send_ref, sums_ref,
    raw, parts, prod, mean, mid, packed, slopes,
):
    _, layers, rows, width = keep_ref.shape
    both = 2 * layers
    cells = both * rows
    me_s = lax.axis_index("stream")
    me_w = lax.axis_index("wall")
    odd = lax.rem(me_w, 2)
    at_end = (me_w == 0) | (me_w == walls - 1)
    keep_b = jnp.where(at_end, 0.0, 1.0).astype(jnp.float32)

    bring(b_mine, b_rest, raw, parts, keep_b)

    planes = jnp.where(odd == 0, upper[...], lower[...])
    planes = planes + planes_of(matrices, odd, parts)
    row = lax.rem(lax.broadcasted_iota(jnp.int32, planes.shape, 0), rows)
    inside = (row < reach) == (odd == 1)
    planes = jnp.where(jnp.logical_or(inside, jnp.logical_not(at_end)), planes, 0.0)
    means = span_pass(spans, planes, both)
    rows_b = pl.ds(pl.multiple_of(odd * rows, rows), rows)
    rows_a = pl.ds(pl.multiple_of((1 - odd) * rows, rows), rows)
    near_b = pl.ds(pl.multiple_of(odd * reach, reach), reach)
    near_a = pl.ds(pl.multiple_of((1 - odd) * reach, reach), reach)
    for t, value, slope in pack_means(mean, means, near_a):
        packed[t, :, rows_b, :] = value
        packed[t, :, rows_a, :] = a_packed[t]
        slopes[t, :, near_b, :] = slope
        slopes[t, :, near_a, :] = a_slopes[t]
    second_input(means, mid)
    second = packed_pass(spans, a_second[...] + planes_of(matrices, odd, mid))
    second = [value.reshape(layers, rows, width) for value in second]

    def around(f):
        above = jnp.where(odd == 0, raw[f, :, rows - reach :, :], a_raw[f, :, rows - reach :, :])
        below = jnp.where(odd == 1, raw[f, :, :reach, :], a_raw[f, :, :reach, :])
        return jnp.concatenate([above, below], axis=1)

    temperature = around(3)
    for i in range(3):
        value = (around(i) * temperature).reshape(cells, width)
        put_parts(prod, 0, column(i), value)
    flux = packed_pass(spans, products[...] + planes_of(matrices, 3, prod))
    flux = [value.reshape(layers, rows, width) for value in flux]

    mid_rows = slice(reach, reach + rows)
    first = lane_index((1, rows, width)) < width // 2
    centre, along_wall, along_stream = [], [], []
    for f in range(4):
        here = packed[f, :, mid_rows, :]
        centre.append(here)
        below = packed[f, :, reach + 1 : reach + rows + 1, :]
        above = packed[f, :, reach - 1 : reach + rows - 1, :]
        along_wall.append((below - above) * 0.5)
        after = jnp.where(first, pltpu.roll(here[:1], width // 2, 2), 0.0)
        before = jnp.where(first, 0.0, pltpu.roll(here[layers - 1 :], width // 2, 2))
        ahead = jnp.concatenate([here[1:], after], axis=0)
        behind = jnp.concatenate([before, here[: layers - 1]], axis=0)
        along_stream.append((ahead - behind) * 0.5)

    lane = lane_index((rows, width))
    table = jnp.zeros((rows, width), jnp.float32)
    first = lane_index((layers, rows, width)) < width // 2
    in_first = me_s == 1
    for i in range(3):
        exact = flux[i] - centre[i] * centre[3]
        similar = second[4 + i] - second[i] * second[3]
        total = slopes[i] * slopes[3] + along_wall[i] * along_wall[3]
        clark = clark_coef * (total + along_stream[i] * along_stream[3])
        terms = (exact * clark, exact * similar, exact * exact, clark * clark, similar * similar)
        for q, term in enumerate(terms):
            value = jnp.sum(jnp.sum(term, axis=0), axis=1, keepdims=True)
            table = jnp.where(lane == 3 * q + i, value, table)
        keep_ref[i] = clark
        keep_ref[3 + i] = similar
        clark = jnp.where(in_first, clark, pltpu.roll(clark, width // 2, 2))
        similar = jnp.where(in_first, pltpu.roll(similar, width // 2, 2), similar)
        send_ref[i] = jnp.where(first, clark, similar)
    sums_ref[...] = table


def finish_kernel(
    plane_cells, sums, keep, come, clark_model, similar_model, clark_corr, similar_corr
):
    _, layers, rows, width = keep.shape
    me_s = lax.axis_index("stream")
    table = sums[...] / plane_cells
    lane = lane_index((rows, width))
    useful = lane // (width // 2) == me_s
    corr = jnp.zeros((rows, width), jnp.float32)
    for i in range(3):
        cross_c, cross_s, power_e, power_c, power_s = (
            table[:, 3 * q + i : 3 * q + i + 1] for q in range(5)
        )
        packed = come[i]
        turned = pltpu.roll(packed, width // 2, 2)
        clark = jnp.where(useful[None], keep[i], jnp.where(me_s == 0, turned, packed))
        similar = jnp.where(useful[None], keep[3 + i], jnp.where(me_s == 0, packed, turned))
        clark_model[i] = clark / jnp.sqrt(power_c + small_eps)[None]
        similar_model[i] = similar / jnp.sqrt(power_s + small_eps)[None]
        value = cross_c / jnp.sqrt((power_e + small_eps) * (power_c + small_eps))
        corr = jnp.where(lane == i, value, corr)
        value = cross_s / jnp.sqrt((power_e + small_eps) * (power_s + small_eps))
        corr = jnp.where(lane == 8 + i, value, corr)
    square = jnp.concatenate([corr, jnp.zeros((width - rows, width), jnp.float32)], axis=0)
    turned = square.T
    clark_corr[...] = turned[:3, :rows]
    similar_corr[...] = turned[8:11, :rows]


def call(kernel, name, ins, outs, scratch=(), mib=4, hint=None):
    cost = hint and pl.CostEstimate(flops=hint, bytes_accessed=0, transcendentals=0)
    return pl.pallas_call(
        kernel,
        out_shape=tuple(jax.ShapeDtypeStruct(shape, jnp.float32) for shape in outs),
        in_specs=[pl.BlockSpec(memory_space=pltpu.VMEM)] * len(ins),
        out_specs=tuple(pl.BlockSpec(memory_space=pltpu.VMEM) for _ in outs),
        scratch_shapes=[pltpu.VMEM(shape, dtype) for shape, dtype in scratch],
        compiler_params=pltpu.CompilerParams(vmem_limit_bytes=mib * 1024 * 1024),
        cost_estimate=cost,
        name=name,
    )(*ins)


def shards(fields):
    _, layers, rows, width = fields.shape
    spans = lax.axis_size("span")
    walls = lax.axis_size("wall")
    streams = lax.axis_size("stream")
    both = streams * layers
    cells = both * rows

    def swap(value):
        return lax.ppermute(value, "stream", [(0, 1), (1, 0)])

    def pair_a(value):
        return lax.ppermute(value, "wall", [(w, w ^ 1) for w in range(walls)])

    def pair_b(value):
        return lax.ppermute(
            value, "wall", [(w, min(max(((w + 1) ^ 1) - 1, 0), walls - 1)) for w in range(walls)]
        )

    def place(p, s):
        return (p % spans) * streams + s

    to_other, to_same = [], []
    for p in range(spans):
        to_other += [(place(p, 0), place(p - 1, 1)), (place(p, 1), place(p + 1, 0))]
        to_same += [(place(p, 1), place(p - 1, 1)), (place(p, 0), place(p + 1, 0))]

    message, strip = (2 * layers + layers // 2, rows, width), (layers // 2, rows, width)
    to_partner, mine, first, second = call(
        pack_kernel, "pack", (fields,), (message, message, strip, strip)
    )
    part = swap(to_partner)
    part_strip = lax.ppermute(first, ("span", "stream"), to_other)
    own_strip = lax.ppermute(second, ("span", "stream"), to_same)
    mine_now, b_mine, a_mine = lax.optimization_barrier((mine, pair_b(mine), pair_a(mine)))
    (rest,) = call(
        rest_kernel,
        "rest",
        (part, part_strip, own_strip),
        ((message[0] + layers, rows, width),),
        hint=2**35,
    )
    a_rest, b_rest = pair_a(rest), pair_b(rest)

    high, low = plane_constants(both, rows)
    thirds = [(high[:, k : k + cells], low[:, k : k + cells], high[:, k : k + cells]) for k in range(0, 4 * cells, cells)]
    matrices = jnp.asarray(np.concatenate([part for third in thirds for part in third], axis=1))
    single_pass, split_pass = span_constants(width)
    both_passes = np.zeros((4 * width, 6 * width), ml_dtypes.bfloat16)
    both_passes[: 2 * width, : 2 * width] = single_pass
    both_passes[:, 2 * width :] = split_pass
    passes = jnp.asarray(both_passes)
    single, brief = jnp.float32, jnp.bfloat16
    block, quarter = (4, both, rows, width), (4, layers, rows, width)
    four, three, seven = (((3 * cells, n * width), brief) for n in (4, 3, 7))
    upper, lower, products = call(
        centre_kernel,
        "centre",
        (mine_now, rest, matrices),
        ((cells, 4 * width), (cells, 4 * width), (cells, 3 * width)),
        [(block, single), four, three],
        mib=16,
        hint=2**31,
    )
    a_raw, a_packed, a_slopes, a_second = call(
        mate_kernel,
        "mate",
        (a_mine, a_rest, upper, lower, matrices, passes),
        (block, quarter, (4, layers, reach, width), (cells, 7 * width)),
        [four, seven, (block, single)],
        mib=16,
        hint=2**29,
    )
    keep, send, sums = call(
        functools.partial(flux_kernel, walls),
        "flux",
        (b_mine, b_rest, a_raw, a_packed, a_slopes, a_second, upper, lower, products, matrices, passes),
        ((6, layers, rows, width), (3, layers, rows, width), (rows, width)),
        [
            (block, single),
            four,
            three,
            (block, single),
            seven,
            ((4, layers, 2 * rows, width), single),
            (quarter, single),
        ],
        mib=24,
    )

    come = swap(send)

    def from_span(value, step):
        return lax.ppermute(value, "span", [(p, p ^ step) for p in range(spans)])

    step = 1
    while step < spans:
        if 2 * step < spans:
            far = from_span(sums, 2 * step) + from_span(sums, 3 * step)
            sums = (sums + from_span(sums, step)) + far
        else:
            sums = sums + from_span(sums, step)
        step *= 4
    sums = sums + swap(sums)
    block, corr = (3, layers, rows, width), (3, rows)
    return call(
        functools.partial(finish_kernel, float(layers * width * spans * streams)),
        "finish",
        (sums, keep, come),
        (block, block, corr, corr),
    )


def solution(mesh):
    return jax.shard_map(
        shards,
        mesh=mesh,
        in_specs=(P(None, "stream", "wall", "span"),),
        out_specs=(
            P(None, "stream", "wall", "span"),
            P(None, "stream", "wall", "span"),
            P(None, "wall"),
            P(None, "wall"),
        ),
        check_vma=False,
    )
```

```python
import functools
import math

import jax
import jax.numpy as jnp
import ml_dtypes
import numpy as np
from jax import lax
from jax.experimental import pallas as pl
from jax.experimental.pallas import tpu as pltpu
from jax.sharding import PartitionSpec as P

raw_taps = [math.exp(-((k - 8) ** 2) / 18.0) for k in range(17)]
filter_taps = [value / sum(raw_taps) for value in raw_taps]
clark_coef = 9.0
small_eps = 1e-06

reach = 8
rim = 2 * reach


def split_constant(matrix):
    high = matrix.astype(ml_dtypes.bfloat16)
    low = (matrix - high.astype(np.float64)).astype(ml_dtypes.bfloat16)
    return high, low


def band(outs, ins, offset):
    matrix = np.zeros((outs, ins))
    for o in range(outs):
        for i in range(ins):
            k = i - o - offset + reach
            if 0 <= k <= 2 * reach:
                matrix[o, i] = filter_taps[k]
    return matrix


def plane_constants(layers, rows):
    stream = band(layers, layers, 0)
    wall = band(rows, 2 * rows, reach)
    ends = [0, reach, reach + rows, 2 * rows]
    thirds = [np.arange(ends[k], ends[k + 1]) for k in range(3)]
    parts = [np.arange(rows), np.arange(rows, 2 * rows), thirds[1], thirds[0], thirds[2]]
    blocks = [np.kron(stream, wall[:, part]) for part in parts]
    parts = [split_constant(block) for block in blocks]
    return np.concatenate([np.concatenate([high, low, high], axis=1) for high, low in parts], axis=1)


def span_constants(width):
    circle = np.zeros((width, width))
    for o in range(width):
        for k in range(2 * reach + 1):
            circle[(o + k - reach) % width, o] = filter_taps[k]
    half = width // 2

    def parts(matrix):
        high, low = split_constant(matrix)
        return np.block([[high, low], [high, np.zeros_like(low)]])

    packed = []
    for layers in range(2):
        row = []
        for s in range(2):
            matrix = np.zeros((width, width))
            matrix[:, layers * half : (layers + 1) * half] = circle[:, s * half : (s + 1) * half]
            row.append(parts(matrix))
        packed.append(np.concatenate(row, axis=1))
    return parts(circle), np.concatenate(packed, axis=0)


def halves(value):
    high = value.astype(jnp.bfloat16)
    return high, (value - high.astype(jnp.float32)).astype(jnp.bfloat16)


def dot(a, b):
    return lax.dot_general(a, b, (((1,), (0,)), ((), ())), preferred_element_type=jnp.float32)


def lane_index(shape):
    return lax.broadcasted_iota(jnp.int32, shape, len(shape) - 1)


def unit_index(shape):
    return lane_index(shape) // rim


def pack_halves(block, half):
    width = block.shape[-1]
    in_place = lane_index(block.shape[1:]) // (width // 2) == half
    for pair in range(2):
        moved = pltpu.roll(block[2 * pair + 1], width // 2, 2)
        yield pair, jnp.where(in_place, block[2 * pair], moved)


def pack_strip(block, unit):
    _, layers, rows, width = block.shape
    half = layers // 2
    units = unit_index((half, rows, width))
    total = jnp.zeros((half, rows, width), jnp.float32)
    for k in range(2):
        for f in range(4):
            step = 2 * f + k
            cells = block[f, k * half : (k + 1) * half]
            cells = pltpu.roll(cells, step * rim, 2) if step else cells
            total = jnp.where(units == lax.rem(unit + step, width // rim), cells, total)
    return total


def strip_tile(inner, outer, me_s):
    width = inner.shape[-1]
    is_outer = lax.rem(unit_index(inner.shape), 2) == 1 - me_s
    for k in range(2):
        shift = (width - k * rim) % width
        pieces = [pltpu.roll(strip, shift, 2) if k else strip for strip in (inner, outer)]
        yield k, jnp.where(is_outer, pieces[1], pieces[0])


def pack_kernel(own, to_partner, to_mine, to_other, to_same):
    _, layers, _, _ = own.shape
    me_s = lax.axis_index("stream")
    for message, half in ((to_partner, 1 - me_s), (to_mine, me_s)):
        for pair, tile in pack_halves(own, half):
            message[pair * layers : (pair + 1) * layers] = tile
        message[2 * layers :] = pack_strip(own, 4 - half)
    to_other[...] = pack_strip(own, 7 * me_s)
    to_same[...] = pack_strip(own, 7 * (1 - me_s))


def rest_kernel(part, own_strip, part_strip, rest):
    count, half = part.shape[0], own_strip.shape[0]
    rest[:count] = part[...]
    rest[count : count + half] = own_strip[...]
    rest[count + half :] = part_strip[...]


def unpack(mine, rest, me_s):
    count, rows, width = mine.shape
    layers = rest.shape[0] - count
    half = layers // 2
    unit = unit_index((half, rows, width))
    first = 4 * (1 - me_s)
    in_strip = (unit == first) | (unit == first + 3)
    for which, packed in enumerate((mine, rest)):
        far = rest[count + which * half : count + (which + 1) * half]
        for k, strip in strip_tile(packed[2 * layers : count], far, me_s):
            layer = (me_s if which == 0 else 1 - me_s) * layers + k * half
            for f in range(4):
                start = f // 2 * layers + k * half
                cells = packed[start : start + half]
                cells = pltpu.roll(cells, width // 2, 2) if f % 2 else cells
                moved = pltpu.roll(strip, width - 2 * f * rim, 2) if f else strip
                yield f, layer, jnp.where(in_strip, moved, cells)


def column(t, width=128):
    return slice(t * width, (t + 1) * width)


def put_parts(parts, down, across, value):
    third = parts.shape[0] // 3
    high, low = halves(value)
    for k, part in enumerate((high, high, low)):
        parts[pl.ds(k * third + down, value.shape[0]), across] = part


def planes_of(planes, part, parts):
    depth = parts.shape[0]
    start = part * depth if isinstance(part, int) else pl.multiple_of(part * depth, depth)
    return dot(planes[:, pl.ds(start, depth)], parts[...])


def add_products(planes, which, raw, base, parts):
    near = pl.ds(pl.multiple_of((1 - which) * reach, reach), reach)
    temperature = raw[3, :, near, :]
    for i in range(3):
        value = raw[i, :, near, :] * temperature
        put_parts(parts, 0, column(i), value.reshape(-1, value.shape[-1]))
    return base + planes_of(planes, 6 + which, parts)


def bring(mine, rest, raw, parts, keep=None):
    rows, width = mine.shape[1:]
    for f, layer, value in unpack(mine, rest, lax.axis_index("stream")):
        count = value.shape[0]
        value = value if keep is None else value * keep
        raw[f, pl.ds(layer, count)] = value
        down = pl.multiple_of(layer * rows, count * rows)
        put_parts(parts, down, column(f), value.reshape(-1, width))


def centre_kernel(
    mine, rest, planes, upper, lower, products, centre, parts, prod
):
    bring(mine, rest, centre, parts)
    for i in range(3):
        value = centre[i] * centre[3]
        put_parts(prod, 0, column(i), value.reshape(-1, value.shape[-1]))
    upper[...] = planes_of(planes, 1, parts)
    lower[...] = planes_of(planes, 0, parts)
    products[...] = planes_of(planes, 2, prod)


def span_pass(spans, planes, both):
    cells = planes.shape[0]
    rows = cells // both
    width = 128
    span_w = spans[: 2 * width, : 2 * width]
    high, low = halves(planes)
    tiles = planes.shape[1] // width
    parts = [jnp.concatenate([high[:, column(t)], low[:, column(t)]], axis=1) for t in range(tiles)]
    result = dot(jnp.concatenate(parts, axis=0), span_w)
    result = result[:, :width] + result[:, width:]
    return [result[t * cells : (t + 1) * cells].reshape(both, rows, width) for t in range(tiles)]


def second_input(means, parts):
    tiles = means + [means[i] * means[3] for i in range(3)]
    for t, value in enumerate(tiles):
        put_parts(parts, 0, column(t), value.reshape(-1, value.shape[-1]))


def packed_pass(spans, planes):
    cells = planes.shape[0]
    some, width = cells // 2, 128
    me_s = lax.axis_index("stream")
    along = pl.ds(pl.multiple_of((1 + me_s) * 2 * width, 2 * width), 2 * width)
    matrix = spans[:, along]
    high, low = halves(planes)
    tiles = planes.shape[1] // width
    parts = [
        jnp.concatenate(
            [high[:some, column(t)], low[:some, column(t)], high[some:, column(t)], low[some:, column(t)]],
            axis=1,
        )
        for t in range(tiles)
    ]
    result = dot(jnp.concatenate(parts, axis=0), matrix)
    result = result[:, :width] + result[:, width:]
    return [result[t * some : (t + 1) * some] for t in range(tiles)]


def pack_layers(own, other, me_s, shift=0):
    width = own.shape[-1]
    in_place = lane_index(own.shape) // (width // 2) == me_s
    own = pltpu.roll(own, shift % width, 2) if shift else own
    return jnp.where(in_place, own, pltpu.roll(other, (shift + width // 2) % width, 2))


def pack_means(mean, means, rows_near):
    for t, value in enumerate(means):
        mean[t] = value
    both = mean.shape[1]
    me_s = lax.axis_index("stream")
    own, other = pl.ds(me_s * (both // 2), both // 2), pl.ds((1 - me_s) * (both // 2), both // 2)
    for t in range(4):
        near = mean[t, own, rows_near, :], mean[t, other, rows_near, :]
        slope = (pack_layers(*near, me_s, -1) - pack_layers(*near, me_s, 1)) * 0.5
        yield t, pack_layers(mean[t, own], mean[t, other], me_s), slope


def mate_kernel(
    a_mine, a_rest, upper, lower, products, matrices, spans,
    base, packed, slopes, second, products_a, raw, parts, mid, mean, prod,
):
    both, rows = raw.shape[1:3]
    odd = lax.rem(lax.axis_index("wall"), 2)
    bring(a_mine, a_rest, raw, parts)
    planes = jnp.where(odd == 1, upper[...], lower[...])
    planes = planes + planes_of(matrices, 1 - odd, parts)
    means = span_pass(spans, planes, both)
    for t, value, slope in pack_means(mean, means, pl.ds(pl.multiple_of(odd * reach, reach), reach)):
        packed[t] = value
        slopes[t] = slope
    second_input(means, mid)
    second[...] = planes_of(matrices, 1 - odd, mid)
    base[...] = jnp.where(odd == 0, upper[...], lower[...])
    products_a[...] = add_products(matrices, 1 - odd, raw, products[...], prod)


def flux_kernel(
    walls, b_mine, b_rest, base, a_packed, a_slopes, a_second, products, matrices, spans,
    keep_ref, send_ref, sums_ref,
    raw, parts, prod, mean, mid, packed, slopes,
):
    _, layers, rows, width = keep_ref.shape
    both = 2 * layers
    cells = both * rows
    me_s = lax.axis_index("stream")
    me_w = lax.axis_index("wall")
    odd = lax.rem(me_w, 2)
    at_end = (me_w == 0) | (me_w == walls - 1)
    keep_b = jnp.where(at_end, 0.0, 1.0).astype(jnp.float32)

    bring(b_mine, b_rest, raw, parts, keep_b)

    planes = base[...] + planes_of(matrices, odd, parts)
    row = lax.rem(lax.broadcasted_iota(jnp.int32, planes.shape, 0), rows)
    inside = (row < reach) == (odd == 1)
    planes = jnp.where(jnp.logical_or(inside, jnp.logical_not(at_end)), planes, 0.0)
    means = span_pass(spans, planes, both)
    rows_b = pl.ds(pl.multiple_of(odd * rows, rows), rows)
    rows_a = pl.ds(pl.multiple_of((1 - odd) * rows, rows), rows)
    near_b = pl.ds(pl.multiple_of(odd * reach, reach), reach)
    near_a = pl.ds(pl.multiple_of((1 - odd) * reach, reach), reach)
    for t, value, slope in pack_means(mean, means, near_a):
        packed[t, :, rows_b, :] = value
        packed[t, :, rows_a, :] = a_packed[t]
        slopes[t, :, near_b, :] = slope
        slopes[t, :, near_a, :] = a_slopes[t]
    second_input(means, mid)
    second = packed_pass(spans, a_second[...] + planes_of(matrices, odd, mid))
    second = [value.reshape(layers, rows, width) for value in second]

    flux = packed_pass(spans, add_products(matrices, odd, raw, products[...], prod))
    flux = [value.reshape(layers, rows, width) for value in flux]

    mid_rows = slice(reach, reach + rows)
    first = lane_index((1, rows, width)) < width // 2
    centre, along_wall, along_stream = [], [], []
    for f in range(4):
        here = packed[f, :, mid_rows, :]
        centre.append(here)
        below = packed[f, :, reach + 1 : reach + rows + 1, :]
        above = packed[f, :, reach - 1 : reach + rows - 1, :]
        along_wall.append((below - above) * 0.5)
        after = jnp.where(first, pltpu.roll(here[:1], width // 2, 2), 0.0)
        before = jnp.where(first, 0.0, pltpu.roll(here[layers - 1 :], width // 2, 2))
        ahead = jnp.concatenate([here[1:], after], axis=0)
        behind = jnp.concatenate([before, here[: layers - 1]], axis=0)
        along_stream.append((ahead - behind) * 0.5)

    lane = lane_index((rows, width))
    table = jnp.zeros((rows, width), jnp.float32)
    first = lane_index((layers, rows, width)) < width // 2
    in_first = me_s == 1
    for i in range(3):
        exact = flux[i] - centre[i] * centre[3]
        similar = second[4 + i] - second[i] * second[3]
        total = slopes[i] * slopes[3] + along_wall[i] * along_wall[3]
        clark = clark_coef * (total + along_stream[i] * along_stream[3])
        terms = (exact * clark, exact * similar, exact * exact, clark * clark, similar * similar)
        for q, term in enumerate(terms):
            value = jnp.sum(jnp.sum(term, axis=0), axis=1, keepdims=True)
            table = jnp.where(lane == 3 * q + i, value, table)
        keep_ref[i] = clark
        keep_ref[3 + i] = similar
        clark = jnp.where(in_first, clark, pltpu.roll(clark, width // 2, 2))
        similar = jnp.where(in_first, pltpu.roll(similar, width // 2, 2), similar)
        send_ref[i] = jnp.where(first, clark, similar)
    sums_ref[...] = table


def finish_kernel(
    plane_cells, sums, keep, come, clark_model, similar_model, clark_corr, similar_corr
):
    _, layers, rows, width = keep.shape
    me_s = lax.axis_index("stream")
    table = sums[...] / plane_cells
    lane = lane_index((rows, width))
    useful = lane // (width // 2) == me_s
    corr = jnp.zeros((rows, width), jnp.float32)
    for i in range(3):
        cross_c, cross_s, power_e, power_c, power_s = (
            table[:, 3 * q + i : 3 * q + i + 1] for q in range(5)
        )
        packed = come[i]
        turned = pltpu.roll(packed, width // 2, 2)
        clark = jnp.where(useful[None], keep[i], jnp.where(me_s == 0, turned, packed))
        similar = jnp.where(useful[None], keep[3 + i], jnp.where(me_s == 0, packed, turned))
        clark_model[i] = clark / jnp.sqrt(power_c + small_eps)[None]
        similar_model[i] = similar / jnp.sqrt(power_s + small_eps)[None]
        value = cross_c / jnp.sqrt((power_e + small_eps) * (power_c + small_eps))
        corr = jnp.where(lane == i, value, corr)
        value = cross_s / jnp.sqrt((power_e + small_eps) * (power_s + small_eps))
        corr = jnp.where(lane == 8 + i, value, corr)
    square = jnp.concatenate([corr, jnp.zeros((width - rows, width), jnp.float32)], axis=0)
    turned = square.T
    clark_corr[...] = turned[:3, :rows]
    similar_corr[...] = turned[8:11, :rows]


def call(kernel, name, ins, outs, scratch=(), mib=4, hint=None):
    cost = hint and pl.CostEstimate(flops=hint, bytes_accessed=0, transcendentals=0)
    return pl.pallas_call(
        kernel,
        out_shape=tuple(jax.ShapeDtypeStruct(shape, jnp.float32) for shape in outs),
        in_specs=[pl.BlockSpec(memory_space=pltpu.VMEM)] * len(ins),
        out_specs=tuple(pl.BlockSpec(memory_space=pltpu.VMEM) for _ in outs),
        scratch_shapes=[pltpu.VMEM(shape, dtype) for shape, dtype in scratch],
        compiler_params=pltpu.CompilerParams(vmem_limit_bytes=mib * 1024 * 1024),
        cost_estimate=cost,
        name=name,
    )(*ins)


def shards(fields):
    _, layers, rows, width = fields.shape
    spans = lax.axis_size("span")
    walls = lax.axis_size("wall")
    streams = lax.axis_size("stream")
    both = streams * layers
    cells = both * rows

    def swap(value):
        return lax.ppermute(value, "stream", [(0, 1), (1, 0)])

    def pair_a(value):
        return lax.ppermute(value, "wall", [(w, w ^ 1) for w in range(walls)])

    def pair_b(value):
        return lax.ppermute(
            value, "wall", [(w, min(max(((w + 1) ^ 1) - 1, 0), walls - 1)) for w in range(walls)]
        )

    def place(p, s):
        return (p % spans) * streams + s

    to_other, to_same = [], []
    for p in range(spans):
        to_other += [(place(p, 0), place(p - 1, 1)), (place(p, 1), place(p + 1, 0))]
        to_same += [(place(p, 1), place(p - 1, 1)), (place(p, 0), place(p + 1, 0))]

    message, strip = (2 * layers + layers // 2, rows, width), (layers // 2, rows, width)
    to_partner, mine, first, second = call(
        pack_kernel, "pack", (fields,), (message, message, strip, strip)
    )
    part = swap(to_partner)
    part_strip = lax.ppermute(first, ("span", "stream"), to_other)
    own_strip = lax.ppermute(second, ("span", "stream"), to_same)
    mine_now, b_mine, a_mine = lax.optimization_barrier((mine, pair_b(mine), pair_a(mine)))
    (rest,) = call(
        rest_kernel,
        "rest",
        (part, own_strip, part_strip),
        ((message[0] + layers, rows, width),),
        hint=2**35,
    )
    a_rest, b_rest = pair_a(rest), pair_b(rest)

    matrices = jnp.asarray(plane_constants(both, rows))
    single_pass, split_pass = span_constants(width)
    both_passes = np.zeros((4 * width, 6 * width), ml_dtypes.bfloat16)
    both_passes[: 2 * width, : 2 * width] = single_pass
    both_passes[:, 2 * width :] = split_pass
    passes = jnp.asarray(both_passes)
    single, brief = jnp.float32, jnp.bfloat16
    block, quarter = (4, both, rows, width), (4, layers, rows, width)
    four, three, seven = (((3 * cells, n * width), brief) for n in (4, 3, 7))
    few = ((3 * both * reach, 3 * width), brief)
    upper, lower, products = call(
        centre_kernel,
        "centre",
        (mine_now, rest, matrices),
        ((cells, 4 * width), (cells, 4 * width), (cells, 3 * width)),
        [(block, single), four, three],
        mib=16,
        hint=2**31,
    )
    base, a_packed, a_slopes, a_second, products = call(
        mate_kernel,
        "mate",
        (a_mine, a_rest, upper, lower, products, matrices, passes),
        (
            (cells, 4 * width), quarter, (4, layers, reach, width), (cells, 7 * width),
            (cells, 3 * width),
        ),
        [(block, single), four, seven, (block, single), few],
        mib=16,
        hint=2**29,
    )
    keep, send, sums = call(
        functools.partial(flux_kernel, walls),
        "flux",
        (b_mine, b_rest, base, a_packed, a_slopes, a_second, products, matrices, passes),
        ((6, layers, rows, width), (3, layers, rows, width), (rows, width)),
        [
            (block, single),
            four,
            few,
            (block, single),
            seven,
            ((4, layers, 2 * rows, width), single),
            (quarter, single),
        ],
        mib=24,
    )

    come = swap(send)

    def from_span(value, step):
        return lax.ppermute(value, "span", [(p, p ^ step) for p in range(spans)])

    step = 1
    while step < spans:
        if 2 * step < spans:
            far = from_span(sums, 3 * step) + from_span(sums, 2 * step)
            sums = (sums + from_span(sums, step)) + far
        else:
            sums = sums + from_span(sums, step)
        step *= 4
    sums = sums + swap(sums)
    block, corr = (3, layers, rows, width), (3, rows)
    return call(
        functools.partial(finish_kernel, float(layers * width * spans * streams)),
        "finish",
        (sums, keep, come),
        (block, block, corr, corr),
    )


def solution(mesh):
    return jax.shard_map(
        shards,
        mesh=mesh,
        in_specs=(P(None, "stream", "wall", "span"),),
        out_specs=(
            P(None, "stream", "wall", "span"),
            P(None, "stream", "wall", "span"),
            P(None, "wall"),
            P(None, "wall"),
        ),
        check_vma=False,
    )
```

```python
import functools
import math

import jax
import jax.numpy as jnp
import ml_dtypes
import numpy as np
from jax import lax
from jax.experimental import pallas as pl
from jax.experimental.pallas import tpu as pltpu
from jax.sharding import PartitionSpec as P

raw_taps = [math.exp(-((k - 8) ** 2) / 18.0) for k in range(17)]
filter_taps = [value / sum(raw_taps) for value in raw_taps]
clark_coef = 9.0
small_eps = 1e-06

reach = 8
rim = 2 * reach


def split_constant(matrix):
    high = matrix.astype(ml_dtypes.bfloat16)
    low = (matrix - high.astype(np.float64)).astype(ml_dtypes.bfloat16)
    return high, low


def band(outs, ins, offset):
    matrix = np.zeros((outs, ins))
    for o in range(outs):
        for i in range(ins):
            k = i - o - offset + reach
            if 0 <= k <= 2 * reach:
                matrix[o, i] = filter_taps[k]
    return matrix


def plane_constants(layers, rows):
    stream = band(layers, layers, 0)
    wall = band(rows, 2 * rows, reach)
    ends = [0, reach, reach + rows, 2 * rows]
    thirds = [np.arange(ends[k], ends[k + 1]) for k in range(3)]
    parts = [np.arange(rows), np.arange(rows, 2 * rows), thirds[1], thirds[0], thirds[2]]
    blocks = [np.kron(stream, wall[:, part]) for part in parts]
    parts = [split_constant(block) for block in blocks]
    return np.concatenate([np.concatenate([high, low, high], axis=1) for high, low in parts], axis=1)


def span_constants(width):
    circle = np.zeros((width, width))
    for o in range(width):
        for k in range(2 * reach + 1):
            circle[(o + k - reach) % width, o] = filter_taps[k]
    half = width // 2

    def parts(matrix):
        high, low = split_constant(matrix)
        return np.block([[high, low], [high, np.zeros_like(low)]])

    packed = []
    for layers in range(2):
        row = []
        for s in range(2):
            matrix = np.zeros((width, width))
            matrix[:, layers * half : (layers + 1) * half] = circle[:, s * half : (s + 1) * half]
            row.append(parts(matrix))
        packed.append(np.concatenate(row, axis=1))
    return parts(circle), np.concatenate(packed, axis=0)


def halves(value):
    high = value.astype(jnp.bfloat16)
    return high, (value - high.astype(jnp.float32)).astype(jnp.bfloat16)


def dot(a, b):
    return lax.dot_general(a, b, (((1,), (0,)), ((), ())), preferred_element_type=jnp.float32)


def lane_index(shape):
    return lax.broadcasted_iota(jnp.int32, shape, len(shape) - 1)


def unit_index(shape):
    return lane_index(shape) // rim


def pack_halves(block, half):
    width = block.shape[-1]
    in_place = lane_index(block.shape[1:]) // (width // 2) == half
    for pair in range(2):
        moved = pltpu.roll(block[2 * pair + 1], width // 2, 2)
        yield pair, jnp.where(in_place, block[2 * pair], moved)


def pack_strip(block, unit):
    _, layers, rows, width = block.shape
    half = layers // 2
    units = unit_index((half, rows, width))
    total = jnp.zeros((half, rows, width), jnp.float32)
    for k in range(2):
        for f in range(4):
            step = 2 * f + k
            cells = block[f, k * half : (k + 1) * half]
            cells = pltpu.roll(cells, step * rim, 2) if step else cells
            total = jnp.where(units == lax.rem(unit + step, width // rim), cells, total)
    return total


def strip_tile(inner, outer, me_s):
    width = inner.shape[-1]
    is_outer = lax.rem(unit_index(inner.shape), 2) == 1 - me_s
    for k in range(2):
        shift = (width - k * rim) % width
        pieces = [pltpu.roll(strip, shift, 2) if k else strip for strip in (inner, outer)]
        yield k, jnp.where(is_outer, pieces[1], pieces[0])


def pack_kernel(own, to_partner, to_mine, to_other, to_same):
    _, layers, _, _ = own.shape
    me_s = lax.axis_index("stream")
    for message, half in ((to_partner, 1 - me_s), (to_mine, me_s)):
        for pair, tile in pack_halves(own, half):
            message[pair * layers : (pair + 1) * layers] = tile
        message[2 * layers :] = pack_strip(own, 4 - half)
    to_other[...] = pack_strip(own, 7 * me_s)
    to_same[...] = pack_strip(own, 7 * (1 - me_s))


def rest_kernel(part, own_strip, part_strip, rest):
    count, half = part.shape[0], own_strip.shape[0]
    rest[:count] = part[...]
    rest[count : count + half] = own_strip[...]
    rest[count + half :] = part_strip[...]


def unpack(mine, rest, me_s):
    count, rows, width = mine.shape
    layers = rest.shape[0] - count
    half = layers // 2
    unit = unit_index((half, rows, width))
    first = 4 * (1 - me_s)
    in_strip = (unit == first) | (unit == first + 3)
    for which, packed in enumerate((mine, rest)):
        far = rest[count + which * half : count + (which + 1) * half]
        for k, strip in strip_tile(packed[2 * layers : count], far, me_s):
            layer = (me_s if which == 0 else 1 - me_s) * layers + k * half
            for f in range(4):
                start = f // 2 * layers + k * half
                cells = packed[start : start + half]
                cells = pltpu.roll(cells, width // 2, 2) if f % 2 else cells
                moved = pltpu.roll(strip, width - 2 * f * rim, 2) if f else strip
                yield f, layer, jnp.where(in_strip, moved, cells)


def column(t, width=128):
    return slice(t * width, (t + 1) * width)


def put_parts(parts, down, across, value):
    third = parts.shape[0] // 3
    high, low = halves(value)
    for k, part in enumerate((high, high, low)):
        parts[pl.ds(k * third + down, value.shape[0]), across] = part


def planes_of(planes, part, parts):
    depth = parts.shape[0]
    start = part * depth if isinstance(part, int) else pl.multiple_of(part * depth, depth)
    return dot(planes[:, pl.ds(start, depth)], parts[...])


def add_products(planes, which, raw, base, parts):
    near = pl.ds(pl.multiple_of((1 - which) * reach, reach), reach)
    temperature = raw[3, :, near, :]
    for i in range(3):
        value = raw[i, :, near, :] * temperature
        put_parts(parts, 0, column(i), value.reshape(-1, value.shape[-1]))
    return base + planes_of(planes, 6 + which, parts)


def bring(mine, rest, raw, parts, keep=None):
    rows, width = mine.shape[1:]
    for f, layer, value in unpack(mine, rest, lax.axis_index("stream")):
        count = value.shape[0]
        value = value if keep is None else value * keep
        raw[f, pl.ds(layer, count)] = value
        down = pl.multiple_of(layer * rows, count * rows)
        put_parts(parts, down, column(f), value.reshape(-1, width))


def centre_kernel(
    mine, rest, planes, upper, lower, products, centre, parts, prod
):
    bring(mine, rest, centre, parts)
    for i in range(3):
        value = centre[i] * centre[3]
        put_parts(prod, 0, column(i), value.reshape(-1, value.shape[-1]))
    upper[...] = planes_of(planes, 1, parts)
    lower[...] = planes_of(planes, 0, parts)
    products[...] = planes_of(planes, 2, prod)


def span_pass(spans, planes, both):
    cells = planes.shape[0]
    rows = cells // both
    width = 128
    span_w = spans[: 2 * width, : 2 * width]
    high, low = halves(planes)
    tiles = planes.shape[1] // width
    parts = [jnp.concatenate([high[:, column(t)], low[:, column(t)]], axis=1) for t in range(tiles)]
    result = dot(jnp.concatenate(parts, axis=0), span_w)
    result = result[:, :width] + result[:, width:]
    return [result[t * cells : (t + 1) * cells].reshape(both, rows, width) for t in range(tiles)]


def second_input(means, parts):
    tiles = means + [means[i] * means[3] for i in range(3)]
    for t, value in enumerate(tiles):
        put_parts(parts, 0, column(t), value.reshape(-1, value.shape[-1]))


def packed_pass(spans, planes):
    cells = planes.shape[0]
    some, width = cells // 2, 128
    me_s = lax.axis_index("stream")
    along = pl.ds(pl.multiple_of((1 + me_s) * 2 * width, 2 * width), 2 * width)
    matrix = spans[:, along]
    high, low = halves(planes)
    tiles = planes.shape[1] // width
    parts = [
        jnp.concatenate(
            [high[:some, column(t)], low[:some, column(t)], high[some:, column(t)], low[some:, column(t)]],
            axis=1,
        )
        for t in range(tiles)
    ]
    result = dot(jnp.concatenate(parts, axis=0), matrix)
    result = result[:, :width] + result[:, width:]
    return [result[t * some : (t + 1) * some] for t in range(tiles)]


def pack_layers(own, other, me_s, shift=0):
    width = own.shape[-1]
    in_place = lane_index(own.shape) // (width // 2) == me_s
    own = pltpu.roll(own, shift % width, 2) if shift else own
    return jnp.where(in_place, own, pltpu.roll(other, (shift + width // 2) % width, 2))


def pack_means(mean, means, rows_near):
    for t, value in enumerate(means):
        mean[t] = value
    both = mean.shape[1]
    me_s = lax.axis_index("stream")
    own, other = pl.ds(me_s * (both // 2), both // 2), pl.ds((1 - me_s) * (both // 2), both // 2)
    for t in range(4):
        near = mean[t, own, rows_near, :], mean[t, other, rows_near, :]
        slope = (pack_layers(*near, me_s, -1) - pack_layers(*near, me_s, 1)) * 0.5
        yield t, pack_layers(mean[t, own], mean[t, other], me_s), slope


def mate_kernel(
    a_mine, a_rest, upper, lower, products, matrices, spans,
    base, packed, slopes, second, products_a, raw, parts, mid, mean, prod,
):
    both, rows = raw.shape[1:3]
    odd = lax.rem(lax.axis_index("wall"), 2)
    bring(a_mine, a_rest, raw, parts)
    planes = jnp.where(odd == 1, upper[...], lower[...])
    planes = planes + planes_of(matrices, 1 - odd, parts)
    means = span_pass(spans, planes, both)
    for t, value, slope in pack_means(mean, means, pl.ds(pl.multiple_of(odd * reach, reach), reach)):
        packed[t] = value
        slopes[t] = slope
    second_input(means, mid)
    second[...] = planes_of(matrices, 1 - odd, mid)
    base[...] = jnp.where(odd == 0, upper[...], lower[...])
    products_a[...] = add_products(matrices, 1 - odd, raw, products[...], prod)


def flux_kernel(
    walls, b_mine, b_rest, base, a_packed, a_slopes, a_second, products, matrices, spans,
    keep_ref, send_ref, sums_ref,
    raw, parts, prod, mean, mid, packed, slopes,
):
    _, layers, rows, width = keep_ref.shape
    both = 2 * layers
    cells = both * rows
    me_s = lax.axis_index("stream")
    me_w = lax.axis_index("wall")
    odd = lax.rem(me_w, 2)
    at_end = (me_w == 0) | (me_w == walls - 1)
    keep_b = jnp.where(at_end, 0.0, 1.0).astype(jnp.float32)

    bring(b_mine, b_rest, raw, parts, keep_b)

    planes = base[...] + planes_of(matrices, odd, parts)
    row = lax.rem(lax.broadcasted_iota(jnp.int32, planes.shape, 0), rows)
    inside = (row < reach) == (odd == 1)
    planes = jnp.where(jnp.logical_or(inside, jnp.logical_not(at_end)), planes, 0.0)
    means = span_pass(spans, planes, both)
    rows_b = pl.ds(pl.multiple_of(odd * rows, rows), rows)
    rows_a = pl.ds(pl.multiple_of((1 - odd) * rows, rows), rows)
    near_b = pl.ds(pl.multiple_of(odd * reach, reach), reach)
    near_a = pl.ds(pl.multiple_of((1 - odd) * reach, reach), reach)
    for t, value, slope in pack_means(mean, means, near_a):
        packed[t, :, rows_b, :] = value
        packed[t, :, rows_a, :] = a_packed[t]
        slopes[t, :, near_b, :] = slope
        slopes[t, :, near_a, :] = a_slopes[t]
    second_input(means, mid)
    second = packed_pass(spans, a_second[...] + planes_of(matrices, odd, mid))
    second = [value.reshape(layers, rows, width) for value in second]

    flux = packed_pass(spans, add_products(matrices, odd, raw, products[...], prod))
    flux = [value.reshape(layers, rows, width) for value in flux]

    mid_rows = slice(reach, reach + rows)
    first = lane_index((1, rows, width)) < width // 2
    centre, along_wall, along_stream = [], [], []
    for f in range(4):
        here = packed[f, :, mid_rows, :]
        centre.append(here)
        below = packed[f, :, reach + 1 : reach + rows + 1, :]
        above = packed[f, :, reach - 1 : reach + rows - 1, :]
        along_wall.append((below - above) * 0.5)
        after = jnp.where(first, pltpu.roll(here[:1], width // 2, 2), 0.0)
        before = jnp.where(first, 0.0, pltpu.roll(here[layers - 1 :], width // 2, 2))
        ahead = jnp.concatenate([here[1:], after], axis=0)
        behind = jnp.concatenate([before, here[: layers - 1]], axis=0)
        along_stream.append((ahead - behind) * 0.5)

    lane = lane_index((rows, width))
    table = jnp.zeros((rows, width), jnp.float32)
    first = lane_index((layers, rows, width)) < width // 2
    in_first = me_s == 1
    for i in range(3):
        exact = flux[i] - centre[i] * centre[3]
        similar = second[4 + i] - second[i] * second[3]
        total = slopes[i] * slopes[3] + along_wall[i] * along_wall[3]
        clark = clark_coef * (total + along_stream[i] * along_stream[3])
        terms = (exact * clark, exact * similar, exact * exact, clark * clark, similar * similar)
        for q, term in enumerate(terms):
            value = jnp.sum(jnp.sum(term, axis=0), axis=1, keepdims=True)
            table = jnp.where(lane == 3 * q + i, value, table)
        keep_ref[i] = clark
        keep_ref[3 + i] = similar
        clark = jnp.where(in_first, clark, pltpu.roll(clark, width // 2, 2))
        similar = jnp.where(in_first, pltpu.roll(similar, width // 2, 2), similar)
        send_ref[i] = jnp.where(first, clark, similar)
    sums_ref[...] = table


def finish_kernel(
    plane_cells, sums, keep, come, clark_model, similar_model, clark_corr, similar_corr,
    clark_done, similar_done, corr_done, sent,
):
    _, layers, rows, width = keep.shape
    me_s = lax.axis_index("stream")
    table = sums[...] / plane_cells
    lane = lane_index((rows, width))
    useful = lane // (width // 2) == me_s
    corr = jnp.zeros((rows, width), jnp.float32)
    copies = []

    def send(source, target):
        copies.append(pltpu.make_async_copy(source, target, sent.at[len(copies)]))
        copies[-1].start()

    for i in range(3):
        cross_c, cross_s, power_e, power_c, power_s = (
            table[:, 3 * q + i : 3 * q + i + 1] for q in range(5)
        )
        packed = come[i]
        turned = pltpu.roll(packed, width // 2, 2)
        clark = jnp.where(useful[None], keep[i], jnp.where(me_s == 0, turned, packed))
        clark_done[i] = clark / jnp.sqrt(power_c + small_eps)[None]
        send(clark_done.at[i], clark_model.at[i])
        similar = jnp.where(useful[None], keep[3 + i], jnp.where(me_s == 0, packed, turned))
        similar_done[i] = similar / jnp.sqrt(power_s + small_eps)[None]
        send(similar_done.at[i], similar_model.at[i])
        value = cross_c / jnp.sqrt((power_e + small_eps) * (power_c + small_eps))
        corr = jnp.where(lane == i, value, corr)
        value = cross_s / jnp.sqrt((power_e + small_eps) * (power_s + small_eps))
        corr = jnp.where(lane == 8 + i, value, corr)
    square = jnp.concatenate([corr, jnp.zeros((width - rows, width), jnp.float32)], axis=0)
    turned = square.T
    corr_done[0] = turned[:3, :rows]
    send(corr_done.at[0], clark_corr)
    corr_done[1] = turned[8:11, :rows]
    send(corr_done.at[1], similar_corr)
    for copy in copies:
        copy.wait()


def call(kernel, name, ins, outs, scratch=(), mib=4, hint=None, space=pltpu.VMEM):
    cost = hint and pl.CostEstimate(flops=hint, bytes_accessed=0, transcendentals=0)
    return pl.pallas_call(
        kernel,
        out_shape=tuple(jax.ShapeDtypeStruct(shape, jnp.float32) for shape in outs),
        in_specs=[pl.BlockSpec(memory_space=pltpu.VMEM)] * len(ins),
        out_specs=tuple(pl.BlockSpec(memory_space=space) for _ in outs),
        scratch_shapes=[
            pltpu.SemaphoreType.DMA(shape) if dtype is None else pltpu.VMEM(shape, dtype)
            for shape, dtype in scratch
        ],
        compiler_params=pltpu.CompilerParams(vmem_limit_bytes=mib * 1024 * 1024),
        cost_estimate=cost,
        name=name,
    )(*ins)


def shards(fields):
    _, layers, rows, width = fields.shape
    spans = lax.axis_size("span")
    walls = lax.axis_size("wall")
    streams = lax.axis_size("stream")
    both = streams * layers
    cells = both * rows

    def swap(value):
        return lax.ppermute(value, "stream", [(0, 1), (1, 0)])

    def pair_a(value):
        return lax.ppermute(value, "wall", [(w, w ^ 1) for w in range(walls)])

    def pair_b(value):
        return lax.ppermute(
            value, "wall", [(w, min(max(((w + 1) ^ 1) - 1, 0), walls - 1)) for w in range(walls)]
        )

    def place(p, s):
        return (p % spans) * streams + s

    to_other, to_same = [], []
    for p in range(spans):
        to_other += [(place(p, 0), place(p - 1, 1)), (place(p, 1), place(p + 1, 0))]
        to_same += [(place(p, 1), place(p - 1, 1)), (place(p, 0), place(p + 1, 0))]

    message, strip = (2 * layers + layers // 2, rows, width), (layers // 2, rows, width)
    to_partner, mine, first, second = call(
        pack_kernel, "pack", (fields,), (message, message, strip, strip)
    )
    part = swap(to_partner)
    part_strip = lax.ppermute(first, ("span", "stream"), to_other)
    own_strip = lax.ppermute(second, ("span", "stream"), to_same)
    mine_now, b_mine, a_mine = lax.optimization_barrier((mine, pair_b(mine), pair_a(mine)))
    (rest,) = call(
        rest_kernel,
        "rest",
        (part, own_strip, part_strip),
        ((message[0] + layers, rows, width),),
        hint=2**35,
    )
    a_rest, b_rest = pair_a(rest), pair_b(rest)

    matrices = jnp.asarray(plane_constants(both, rows))
    single_pass, split_pass = span_constants(width)
    both_passes = np.zeros((4 * width, 6 * width), ml_dtypes.bfloat16)
    both_passes[: 2 * width, : 2 * width] = single_pass
    both_passes[:, 2 * width :] = split_pass
    passes = jnp.asarray(both_passes)
    single, brief = jnp.float32, jnp.bfloat16
    block, quarter = (4, both, rows, width), (4, layers, rows, width)
    four, three, seven = (((3 * cells, n * width), brief) for n in (4, 3, 7))
    few = ((3 * both * reach, 3 * width), brief)
    upper, lower, products = call(
        centre_kernel,
        "centre",
        (mine_now, rest, matrices),
        ((cells, 4 * width), (cells, 4 * width), (cells, 3 * width)),
        [(block, single), four, three],
        mib=16,
        hint=2**31,
    )
    base, a_packed, a_slopes, a_second, products = call(
        mate_kernel,
        "mate",
        (a_mine, a_rest, upper, lower, products, matrices, passes),
        (
            (cells, 4 * width), quarter, (4, layers, reach, width), (cells, 7 * width),
            (cells, 3 * width),
        ),
        [(block, single), four, seven, (block, single), few],
        mib=16,
        hint=2**29,
    )
    keep, send, sums = call(
        functools.partial(flux_kernel, walls),
        "flux",
        (b_mine, b_rest, base, a_packed, a_slopes, a_second, products, matrices, passes),
        ((6, layers, rows, width), (3, layers, rows, width), (rows, width)),
        [
            (block, single),
            four,
            few,
            (block, single),
            seven,
            ((4, layers, 2 * rows, width), single),
            (quarter, single),
        ],
        mib=24,
    )

    come = swap(send)

    def from_span(value, step):
        return lax.ppermute(value, "span", [(p, p ^ step) for p in range(spans)])

    step = 1
    while step < spans:
        if 2 * step < spans:
            far = from_span(sums, 3 * step) + from_span(sums, 2 * step)
            sums = (sums + from_span(sums, step)) + far
        else:
            sums = sums + from_span(sums, step)
        step *= 4
    sums = sums + swap(sums)
    block, corr = (3, layers, rows, width), (3, rows)
    return call(
        functools.partial(finish_kernel, float(layers * width * spans * streams)),
        "finish",
        (sums, keep, come),
        (block, block, corr, corr),
        [(block, single), (block, single), ((2, *corr), single), ((8,), None)],
        space=pl.ANY,
    )


def solution(mesh):
    return jax.shard_map(
        shards,
        mesh=mesh,
        in_specs=(P(None, "stream", "wall", "span"),),
        out_specs=(
            P(None, "stream", "wall", "span"),
            P(None, "stream", "wall", "span"),
            P(None, "wall"),
            P(None, "wall"),
        ),
        check_vma=False,
    )
```

```python
import functools
import math

import jax
import jax.numpy as jnp
import ml_dtypes
import numpy as np
from jax import lax
from jax.experimental import pallas as pl
from jax.experimental.pallas import tpu as pltpu
from jax.sharding import PartitionSpec as P

raw_taps = [math.exp(-((k - 8) ** 2) / 18.0) for k in range(17)]
filter_taps = [value / sum(raw_taps) for value in raw_taps]
clark_coef = 9.0
small_eps = 1e-06

reach = 8
rim = 2 * reach


def split_constant(matrix):
    high = matrix.astype(ml_dtypes.bfloat16)
    low = (matrix - high.astype(np.float64)).astype(ml_dtypes.bfloat16)
    return high, low


def band(outs, ins, offset):
    matrix = np.zeros((outs, ins))
    for o in range(outs):
        for i in range(ins):
            k = i - o - offset + reach
            if 0 <= k <= 2 * reach:
                matrix[o, i] = filter_taps[k]
    return matrix


def plane_constants(layers, rows):
    stream = band(layers, layers, 0)
    wall = band(rows, 2 * rows, reach)
    ends = [0, reach, reach + rows, 2 * rows]
    thirds = [np.arange(ends[k], ends[k + 1]) for k in range(3)]
    parts = [np.arange(rows), np.arange(rows, 2 * rows), thirds[1], thirds[0], thirds[2]]
    blocks = [np.kron(stream, wall[:, part]) for part in parts]
    parts = [split_constant(block) for block in blocks]
    return np.concatenate([np.concatenate([high, low, high], axis=1) for high, low in parts], axis=1)


def span_constants(width):
    circle = np.zeros((width, width))
    for o in range(width):
        for k in range(2 * reach + 1):
            circle[(o + k - reach) % width, o] = filter_taps[k]
    half = width // 2

    def parts(matrix):
        high, low = split_constant(matrix)
        return np.block([[high, low], [high, np.zeros_like(low)]])

    packed = []
    for layers in range(2):
        row = []
        for s in range(2):
            matrix = np.zeros((width, width))
            matrix[:, layers * half : (layers + 1) * half] = circle[:, s * half : (s + 1) * half]
            row.append(parts(matrix))
        packed.append(np.concatenate(row, axis=1))
    return parts(circle), np.concatenate(packed, axis=0)


def halves(value):
    high = value.astype(jnp.bfloat16)
    return high, (value - high.astype(jnp.float32)).astype(jnp.bfloat16)


def dot(a, b):
    return lax.dot_general(a, b, (((1,), (0,)), ((), ())), preferred_element_type=jnp.float32)


def lane_index(shape):
    return lax.broadcasted_iota(jnp.int32, shape, len(shape) - 1)


def unit_index(shape):
    return lane_index(shape) // rim


def pack_halves(block, half):
    width = block.shape[-1]
    in_place = lane_index(block.shape[1:]) // (width // 2) == half
    for pair in range(2):
        moved = pltpu.roll(block[2 * pair + 1], width // 2, 2)
        yield pair, jnp.where(in_place, block[2 * pair], moved)


def pack_strip(block, unit):
    _, layers, rows, width = block.shape
    half = layers // 2
    units = unit_index((half, rows, width))
    total = jnp.zeros((half, rows, width), jnp.float32)
    for k in range(2):
        for f in range(4):
            step = 2 * f + k
            cells = block[f, k * half : (k + 1) * half]
            cells = pltpu.roll(cells, step * rim, 2) if step else cells
            total = jnp.where(units == lax.rem(unit + step, width // rim), cells, total)
    return total


def strip_tile(inner, outer, me_s):
    width = inner.shape[-1]
    is_outer = lax.rem(unit_index(inner.shape), 2) == 1 - me_s
    for k in range(2):
        shift = (width - k * rim) % width
        pieces = [pltpu.roll(strip, shift, 2) if k else strip for strip in (inner, outer)]
        yield k, jnp.where(is_outer, pieces[1], pieces[0])


def pack_kernel(own, to_partner, to_mine, to_other, to_same):
    _, layers, _, _ = own.shape
    me_s = lax.axis_index("stream")
    for message, half in ((to_partner, 1 - me_s), (to_mine, me_s)):
        for pair, tile in pack_halves(own, half):
            message[pair * layers : (pair + 1) * layers] = tile
        message[2 * layers :] = pack_strip(own, 4 - half)
    to_other[...] = pack_strip(own, 7 * me_s)
    to_same[...] = pack_strip(own, 7 * (1 - me_s))


def rest_kernel(part, own_strip, part_strip, rest):
    count, half = part.shape[0], own_strip.shape[0]
    rest[:count] = part[...]
    rest[count : count + half] = own_strip[...]
    rest[count + half :] = part_strip[...]


def unpack(mine, rest, me_s):
    count, rows, width = mine.shape
    layers = rest.shape[0] - count
    half = layers // 2
    unit = unit_index((half, rows, width))
    first = 4 * (1 - me_s)
    in_strip = (unit == first) | (unit == first + 3)
    for which, packed in enumerate((mine, rest)):
        far = rest[count + which * half : count + (which + 1) * half]
        for k, strip in strip_tile(packed[2 * layers : count], far, me_s):
            layer = (me_s if which == 0 else 1 - me_s) * layers + k * half
            for f in range(4):
                start = f // 2 * layers + k * half
                cells = packed[start : start + half]
                cells = pltpu.roll(cells, width // 2, 2) if f % 2 else cells
                moved = pltpu.roll(strip, width - 2 * f * rim, 2) if f else strip
                yield f, layer, jnp.where(in_strip, moved, cells)


def column(t, width=128):
    return slice(t * width, (t + 1) * width)


def put_parts(parts, down, across, value):
    third = parts.shape[0] // 3
    high, low = halves(value)
    for k, part in enumerate((high, high, low)):
        parts[pl.ds(k * third + down, value.shape[0]), across] = part


def planes_of(planes, part, parts):
    depth = parts.shape[0]
    start = part * depth if isinstance(part, int) else pl.multiple_of(part * depth, depth)
    return dot(planes[:, pl.ds(start, depth)], parts[...])


def add_products(planes, which, raw, base, parts):
    near = pl.ds(pl.multiple_of((1 - which) * reach, reach), reach)
    temperature = raw[3, :, near, :]
    for i in range(3):
        value = raw[i, :, near, :] * temperature
        put_parts(parts, 0, column(i), value.reshape(-1, value.shape[-1]))
    return base + planes_of(planes, 6 + which, parts)


def bring(mine, rest, raw, parts, keep=None):
    rows, width = mine.shape[1:]
    for f, layer, value in unpack(mine, rest, lax.axis_index("stream")):
        count = value.shape[0]
        value = value if keep is None else value * keep
        raw[f, pl.ds(layer, count)] = value
        down = pl.multiple_of(layer * rows, count * rows)
        put_parts(parts, down, column(f), value.reshape(-1, width))


def centre_kernel(
    mine, rest, planes, upper, lower, products, centre, parts, prod
):
    bring(mine, rest, centre, parts)
    for i in range(3):
        value = centre[i] * centre[3]
        put_parts(prod, 0, column(i), value.reshape(-1, value.shape[-1]))
    upper[...] = planes_of(planes, 1, parts)
    lower[...] = planes_of(planes, 0, parts)
    products[...] = planes_of(planes, 2, prod)


def span_pass(spans, planes, both):
    cells = planes.shape[0]
    rows = cells // both
    width = 128
    span_w = spans[: 2 * width, : 2 * width]
    high, low = halves(planes)
    tiles = planes.shape[1] // width
    parts = [jnp.concatenate([high[:, column(t)], low[:, column(t)]], axis=1) for t in range(tiles)]
    result = dot(jnp.concatenate(parts, axis=0), span_w)
    result = result[:, :width] + result[:, width:]
    return [result[t * cells : (t + 1) * cells].reshape(both, rows, width) for t in range(tiles)]


def second_input(means, parts):
    tiles = means + [means[i] * means[3] for i in range(3)]
    for t, value in enumerate(tiles):
        put_parts(parts, 0, column(t), value.reshape(-1, value.shape[-1]))


def packed_pass(spans, planes):
    cells = planes.shape[0]
    some, width = cells // 2, 128
    me_s = lax.axis_index("stream")
    along = pl.ds(pl.multiple_of((1 + me_s) * 2 * width, 2 * width), 2 * width)
    matrix = spans[:, along]
    high, low = halves(planes)
    tiles = planes.shape[1] // width
    parts = [
        jnp.concatenate(
            [high[:some, column(t)], low[:some, column(t)], high[some:, column(t)], low[some:, column(t)]],
            axis=1,
        )
        for t in range(tiles)
    ]
    result = dot(jnp.concatenate(parts, axis=0), matrix)
    result = result[:, :width] + result[:, width:]
    return [result[t * some : (t + 1) * some] for t in range(tiles)]


def pack_layers(own, other, me_s, shift=0):
    width = own.shape[-1]
    in_place = lane_index(own.shape) // (width // 2) == me_s
    own = pltpu.roll(own, shift % width, 2) if shift else own
    return jnp.where(in_place, own, pltpu.roll(other, (shift + width // 2) % width, 2))


def pack_means(mean, means, rows_near):
    for t, value in enumerate(means):
        mean[t] = value
    both = mean.shape[1]
    me_s = lax.axis_index("stream")
    own, other = pl.ds(me_s * (both // 2), both // 2), pl.ds((1 - me_s) * (both // 2), both // 2)
    for t in range(4):
        near = mean[t, own, rows_near, :], mean[t, other, rows_near, :]
        slope = (pack_layers(*near, me_s, -1) - pack_layers(*near, me_s, 1)) * 0.5
        yield t, pack_layers(mean[t, own], mean[t, other], me_s), slope


def mate_kernel(
    a_mine, a_rest, upper, lower, products, matrices, spans,
    base, packed, slopes, second, products_a, raw, parts, mid, mean, prod,
):
    both, rows = raw.shape[1:3]
    odd = lax.rem(lax.axis_index("wall"), 2)
    bring(a_mine, a_rest, raw, parts)
    planes = jnp.where(odd == 1, upper[...], lower[...])
    planes = planes + planes_of(matrices, 1 - odd, parts)
    means = span_pass(spans, planes, both)
    for t, value, slope in pack_means(mean, means, pl.ds(pl.multiple_of(odd * reach, reach), reach)):
        packed[t] = value
        slopes[t] = slope
    second_input(means, mid)
    second[...] = planes_of(matrices, 1 - odd, mid)
    base[...] = jnp.where(odd == 0, upper[...], lower[...])
    products_a[...] = add_products(matrices, 1 - odd, raw, products[...], prod)


def flux_kernel(
    walls, b_mine, b_rest, base, a_packed, a_slopes, a_second, products, matrices, spans,
    keep_ref, send_ref, sums_ref,
    raw, parts, prod, mean, mid, packed, slopes,
):
    _, layers, rows, width = keep_ref.shape
    both = 2 * layers
    cells = both * rows
    me_s = lax.axis_index("stream")
    me_w = lax.axis_index("wall")
    odd = lax.rem(me_w, 2)
    at_end = (me_w == 0) | (me_w == walls - 1)
    keep_b = jnp.where(at_end, 0.0, 1.0).astype(jnp.float32)

    bring(b_mine, b_rest, raw, parts, keep_b)

    planes = base[...] + planes_of(matrices, odd, parts)
    row = lax.rem(lax.broadcasted_iota(jnp.int32, planes.shape, 0), rows)
    inside = (row < reach) == (odd == 1)
    planes = jnp.where(jnp.logical_or(inside, jnp.logical_not(at_end)), planes, 0.0)
    means = span_pass(spans, planes, both)
    rows_b = pl.ds(pl.multiple_of(odd * rows, rows), rows)
    rows_a = pl.ds(pl.multiple_of((1 - odd) * rows, rows), rows)
    near_b = pl.ds(pl.multiple_of(odd * reach, reach), reach)
    near_a = pl.ds(pl.multiple_of((1 - odd) * reach, reach), reach)
    for t, value, slope in pack_means(mean, means, near_a):
        packed[t, :, rows_b, :] = value
        packed[t, :, rows_a, :] = a_packed[t]
        slopes[t, :, near_b, :] = slope
        slopes[t, :, near_a, :] = a_slopes[t]
    second_input(means, mid)
    second = packed_pass(spans, a_second[...] + planes_of(matrices, odd, mid))
    second = [value.reshape(layers, rows, width) for value in second]

    flux = packed_pass(spans, add_products(matrices, odd, raw, products[...], prod))
    flux = [value.reshape(layers, rows, width) for value in flux]

    mid_rows = slice(reach, reach + rows)
    first = lane_index((1, rows, width)) < width // 2
    centre, along_wall, along_stream = [], [], []
    for f in range(4):
        here = packed[f, :, mid_rows, :]
        centre.append(here)
        below = packed[f, :, reach + 1 : reach + rows + 1, :]
        above = packed[f, :, reach - 1 : reach + rows - 1, :]
        along_wall.append((below - above) * 0.5)
        after = jnp.where(first, pltpu.roll(here[:1], width // 2, 2), 0.0)
        before = jnp.where(first, 0.0, pltpu.roll(here[layers - 1 :], width // 2, 2))
        ahead = jnp.concatenate([here[1:], after], axis=0)
        behind = jnp.concatenate([before, here[: layers - 1]], axis=0)
        along_stream.append((ahead - behind) * 0.5)

    lane = lane_index((rows, width))
    table = jnp.zeros((rows, width), jnp.float32)
    first = lane_index((layers, rows, width)) < width // 2
    in_first = me_s == 1
    for i in range(3):
        exact = flux[i] - centre[i] * centre[3]
        similar = second[4 + i] - second[i] * second[3]
        total = slopes[i] * slopes[3] + along_wall[i] * along_wall[3]
        clark = clark_coef * (total + along_stream[i] * along_stream[3])
        terms = (exact * clark, exact * similar, exact * exact, clark * clark, similar * similar)
        for q, term in enumerate(terms):
            value = jnp.sum(jnp.sum(term, axis=0), axis=1, keepdims=True)
            table = jnp.where(lane == 3 * q + i, value, table)
        keep_ref[i] = clark
        keep_ref[3 + i] = similar
        clark = jnp.where(in_first, clark, pltpu.roll(clark, width // 2, 2))
        similar = jnp.where(in_first, pltpu.roll(similar, width // 2, 2), similar)
        send_ref[i] = jnp.where(first, clark, similar)
    sums_ref[...] = table


def finish_kernel(
    plane_cells, sums, keep, come, clark_model, similar_model, clark_corr, similar_corr
):
    _, layers, rows, width = keep.shape
    me_s = lax.axis_index("stream")
    table = sums[...] / plane_cells
    lane = lane_index((rows, width))
    useful = lane // (width // 2) == me_s
    corr = jnp.zeros((rows, width), jnp.float32)
    for i in range(3):
        cross_c, cross_s, power_e, power_c, power_s = (
            table[:, 3 * q + i : 3 * q + i + 1] for q in range(5)
        )
        packed = come[i]
        turned = pltpu.roll(packed, width // 2, 2)
        clark = jnp.where(useful[None], keep[i], jnp.where(me_s == 0, turned, packed))
        similar = jnp.where(useful[None], keep[3 + i], jnp.where(me_s == 0, packed, turned))
        clark_model[i] = clark / jnp.sqrt(power_c + small_eps)[None]
        similar_model[i] = similar / jnp.sqrt(power_s + small_eps)[None]
        value = cross_c / jnp.sqrt((power_e + small_eps) * (power_c + small_eps))
        corr = jnp.where(lane == i, value, corr)
        value = cross_s / jnp.sqrt((power_e + small_eps) * (power_s + small_eps))
        corr = jnp.where(lane == 8 + i, value, corr)
    square = jnp.concatenate([corr, jnp.zeros((width - rows, width), jnp.float32)], axis=0)
    turned = square.T
    clark_corr[...] = turned[:3, :rows]
    similar_corr[...] = turned[8:11, :rows]


def call(kernel, name, ins, outs, scratch=(), mib=4, hint=None):
    cost = hint and pl.CostEstimate(flops=hint, bytes_accessed=0, transcendentals=0)
    return pl.pallas_call(
        kernel,
        out_shape=tuple(jax.ShapeDtypeStruct(shape, jnp.float32) for shape in outs),
        in_specs=[pl.BlockSpec(memory_space=pltpu.VMEM)] * len(ins),
        out_specs=tuple(pl.BlockSpec(memory_space=pltpu.VMEM) for _ in outs),
        scratch_shapes=[pltpu.VMEM(shape, dtype) for shape, dtype in scratch],
        compiler_params=pltpu.CompilerParams(vmem_limit_bytes=mib * 1024 * 1024),
        cost_estimate=cost,
        name=name,
    )(*ins)


def shards(fields):
    _, layers, rows, width = fields.shape
    spans = lax.axis_size("span")
    walls = lax.axis_size("wall")
    streams = lax.axis_size("stream")
    both = streams * layers
    cells = both * rows

    def swap(value):
        return lax.ppermute(value, "stream", [(0, 1), (1, 0)])

    def pair_a(value):
        return lax.ppermute(value, "wall", [(w, w ^ 1) for w in range(walls)])

    def pass_on(value):
        ups = [(w, w + 2) for w in range(0, walls - 2, 2)]
        downs = [(w, w - 2) for w in range(3, walls, 2)]
        return lax.ppermute(value, "wall", ups + downs)

    def place(p, s):
        return (p % spans) * streams + s

    to_other, to_same = [], []
    for p in range(spans):
        to_other += [(place(p, 0), place(p - 1, 1)), (place(p, 1), place(p + 1, 0))]
        to_same += [(place(p, 1), place(p - 1, 1)), (place(p, 0), place(p + 1, 0))]

    message, strip = (2 * layers + layers // 2, rows, width), (layers // 2, rows, width)
    to_partner, mine, first, second = call(
        pack_kernel, "pack", (fields,), (message, message, strip, strip)
    )
    part = swap(to_partner)
    part_strip = lax.ppermute(first, ("span", "stream"), to_other)
    own_strip = lax.ppermute(second, ("span", "stream"), to_same)
    a_mine = pair_a(mine)
    own_strip, part_strip, a_mine = lax.optimization_barrier((own_strip, part_strip, a_mine))
    b_mine = pass_on(a_mine)
    (rest,) = call(
        rest_kernel,
        "rest",
        (part, own_strip, part_strip),
        ((message[0] + layers, rows, width),),
        hint=2**35,
    )
    a_rest = pair_a(rest)
    b_rest = pass_on(a_rest)

    matrices = jnp.asarray(plane_constants(both, rows))
    single_pass, split_pass = span_constants(width)
    both_passes = np.zeros((4 * width, 6 * width), ml_dtypes.bfloat16)
    both_passes[: 2 * width, : 2 * width] = single_pass
    both_passes[:, 2 * width :] = split_pass
    passes = jnp.asarray(both_passes)
    single, brief = jnp.float32, jnp.bfloat16
    block, quarter = (4, both, rows, width), (4, layers, rows, width)
    four, three, seven = (((3 * cells, n * width), brief) for n in (4, 3, 7))
    few = ((3 * both * reach, 3 * width), brief)
    upper, lower, products = call(
        centre_kernel,
        "centre",
        (mine, rest, matrices),
        ((cells, 4 * width), (cells, 4 * width), (cells, 3 * width)),
        [(block, single), four, three],
        mib=16,
        hint=2**31,
    )
    base, a_packed, a_slopes, a_second, products = call(
        mate_kernel,
        "mate",
        (a_mine, a_rest, upper, lower, products, matrices, passes),
        (
            (cells, 4 * width), quarter, (4, layers, reach, width), (cells, 7 * width),
            (cells, 3 * width),
        ),
        [(block, single), four, seven, (block, single), few],
        mib=16,
        hint=2**29,
    )
    keep, send, sums = call(
        functools.partial(flux_kernel, walls),
        "flux",
        (b_mine, b_rest, base, a_packed, a_slopes, a_second, products, matrices, passes),
        ((6, layers, rows, width), (3, layers, rows, width), (rows, width)),
        [
            (block, single),
            four,
            few,
            (block, single),
            seven,
            ((4, layers, 2 * rows, width), single),
            (quarter, single),
        ],
        mib=24,
    )

    come = swap(send)

    def from_span(value, step):
        return lax.ppermute(value, "span", [(p, p ^ step) for p in range(spans)])

    step = 1
    while step < spans:
        if 2 * step < spans:
            far = from_span(sums, 3 * step) + from_span(sums, 2 * step)
            sums = (sums + from_span(sums, step)) + far
        else:
            sums = sums + from_span(sums, step)
        step *= 4
    sums = sums + swap(sums)
    block, corr = (3, layers, rows, width), (3, rows)
    return call(
        functools.partial(finish_kernel, float(layers * width * spans * streams)),
        "finish",
        (sums, keep, come),
        (block, block, corr, corr),
    )


def solution(mesh):
    return jax.shard_map(
        shards,
        mesh=mesh,
        in_specs=(P(None, "stream", "wall", "span"),),
        out_specs=(
            P(None, "stream", "wall", "span"),
            P(None, "stream", "wall", "span"),
            P(None, "wall"),
            P(None, "wall"),
        ),
        check_vma=False,
    )
```

```python
import functools
import math

import jax
import jax.numpy as jnp
import ml_dtypes
import numpy as np
from jax import lax
from jax.experimental import pallas as pl
from jax.experimental.pallas import tpu as pltpu
from jax.sharding import PartitionSpec as P

raw_taps = [math.exp(-((k - 8) ** 2) / 18.0) for k in range(17)]
filter_taps = [value / sum(raw_taps) for value in raw_taps]
clark_coef = 9.0
small_eps = 1e-06

reach = 8
rim = 2 * reach


def split_constant(matrix):
    high = matrix.astype(ml_dtypes.bfloat16)
    low = (matrix - high.astype(np.float64)).astype(ml_dtypes.bfloat16)
    return high, low


def band(outs, ins, offset):
    matrix = np.zeros((outs, ins))
    for o in range(outs):
        for i in range(ins):
            k = i - o - offset + reach
            if 0 <= k <= 2 * reach:
                matrix[o, i] = filter_taps[k]
    return matrix


def plane_constants(layers, rows):
    stream = band(layers, layers, 0)
    wall = band(rows, 2 * rows, reach)
    ends = [0, reach, reach + rows, 2 * rows]
    thirds = [np.arange(ends[k], ends[k + 1]) for k in range(3)]
    parts = [np.arange(rows), np.arange(rows, 2 * rows), thirds[1], thirds[0], thirds[2]]
    blocks = [np.kron(stream, wall[:, part]) for part in parts]
    parts = [split_constant(block) for block in blocks]
    return np.concatenate([np.concatenate([high, low, high], axis=1) for high, low in parts], axis=1)


def span_constants(width):
    circle = np.zeros((width, width))
    for o in range(width):
        for k in range(2 * reach + 1):
            circle[(o + k - reach) % width, o] = filter_taps[k]
    half = width // 2

    def parts(matrix):
        high, low = split_constant(matrix)
        return np.block([[high, low], [high, np.zeros_like(low)]])

    packed = []
    for layers in range(2):
        row = []
        for s in range(2):
            matrix = np.zeros((width, width))
            matrix[:, layers * half : (layers + 1) * half] = circle[:, s * half : (s + 1) * half]
            row.append(parts(matrix))
        packed.append(np.concatenate(row, axis=1))
    return parts(circle), np.concatenate(packed, axis=0)


def halves(value):
    high = value.astype(jnp.bfloat16)
    return high, (value - high.astype(jnp.float32)).astype(jnp.bfloat16)


def dot(a, b):
    return lax.dot_general(a, b, (((1,), (0,)), ((), ())), preferred_element_type=jnp.float32)


def lane_index(shape):
    return lax.broadcasted_iota(jnp.int32, shape, len(shape) - 1)


def unit_index(shape):
    return lane_index(shape) // rim


def pack_halves(block, half):
    width = block.shape[-1]
    in_place = lane_index(block.shape[1:]) // (width // 2) == half
    for pair in range(2):
        moved = pltpu.roll(block[2 * pair + 1], width // 2, 2)
        yield pair, jnp.where(in_place, block[2 * pair], moved)


def pack_strip(block, unit):
    _, layers, rows, width = block.shape
    half = layers // 2
    units = unit_index((half, rows, width))
    total = jnp.zeros((half, rows, width), jnp.float32)
    for k in range(2):
        for f in range(4):
            step = 2 * f + k
            cells = block[f, k * half : (k + 1) * half]
            cells = pltpu.roll(cells, step * rim, 2) if step else cells
            total = jnp.where(units == lax.rem(unit + step, width // rim), cells, total)
    return total


def strip_tile(inner, outer, me_s):
    width = inner.shape[-1]
    is_outer = lax.rem(unit_index(inner.shape), 2) == 1 - me_s
    for k in range(2):
        shift = (width - k * rim) % width
        pieces = [pltpu.roll(strip, shift, 2) if k else strip for strip in (inner, outer)]
        yield k, jnp.where(is_outer, pieces[1], pieces[0])


def pack_kernel(own, to_partner, to_mine, to_other, to_same):
    _, layers, _, _ = own.shape
    me_s = lax.axis_index("stream")
    for message, half in ((to_partner, 1 - me_s), (to_mine, me_s)):
        for pair, tile in pack_halves(own, half):
            message[pair * layers : (pair + 1) * layers] = tile
        message[2 * layers :] = pack_strip(own, 4 - half)
    to_other[...] = pack_strip(own, 7 * me_s)
    to_same[...] = pack_strip(own, 7 * (1 - me_s))


def rest_kernel(part, own_strip, part_strip, rest):
    count, half = part.shape[0], own_strip.shape[0]
    rest[:count] = part[...]
    rest[count : count + half] = own_strip[...]
    rest[count + half :] = part_strip[...]


def unpack(mine, rest, me_s):
    count, rows, width = mine.shape
    layers = rest.shape[0] - count
    half = layers // 2
    unit = unit_index((half, rows, width))
    first = 4 * (1 - me_s)
    in_strip = (unit == first) | (unit == first + 3)
    for which, packed in enumerate((mine, rest)):
        far = rest[count + which * half : count + (which + 1) * half]
        for k, strip in strip_tile(packed[2 * layers : count], far, me_s):
            layer = (me_s if which == 0 else 1 - me_s) * layers + k * half
            for f in range(4):
                start = f // 2 * layers + k * half
                cells = packed[start : start + half]
                cells = pltpu.roll(cells, width // 2, 2) if f % 2 else cells
                moved = pltpu.roll(strip, width - 2 * f * rim, 2) if f else strip
                yield f, layer, jnp.where(in_strip, moved, cells)


def column(t, width=128):
    return slice(t * width, (t + 1) * width)


def put_parts(parts, down, across, value):
    third = parts.shape[0] // 3
    high, low = halves(value)
    for k, part in enumerate((high, high, low)):
        parts[pl.ds(k * third + down, value.shape[0]), across] = part


def planes_of(planes, part, parts):
    depth = parts.shape[0]
    start = part * depth if isinstance(part, int) else pl.multiple_of(part * depth, depth)
    return dot(planes[:, pl.ds(start, depth)], parts[...])


def add_products(planes, which, raw, base, parts):
    near = pl.ds(pl.multiple_of((1 - which) * reach, reach), reach)
    temperature = raw[3, :, near, :]
    for i in range(3):
        value = raw[i, :, near, :] * temperature
        put_parts(parts, 0, column(i), value.reshape(-1, value.shape[-1]))
    return base + planes_of(planes, 6 + which, parts)


def bring(mine, rest, raw, parts, keep=None):
    rows, width = mine.shape[1:]
    for f, layer, value in unpack(mine, rest, lax.axis_index("stream")):
        count = value.shape[0]
        value = value if keep is None else value * keep
        raw[f, pl.ds(layer, count)] = value
        down = pl.multiple_of(layer * rows, count * rows)
        put_parts(parts, down, column(f), value.reshape(-1, width))


def centre_kernel(
    mine, rest, planes, upper, lower, products, centre, parts, prod
):
    bring(mine, rest, centre, parts)
    for i in range(3):
        value = centre[i] * centre[3]
        put_parts(prod, 0, column(i), value.reshape(-1, value.shape[-1]))
    upper[...] = planes_of(planes, 1, parts)
    lower[...] = planes_of(planes, 0, parts)
    products[...] = planes_of(planes, 2, prod)


def span_pass(spans, planes, both):
    cells = planes.shape[0]
    rows = cells // both
    width = 128
    span_w = spans[: 2 * width, : 2 * width]
    high, low = halves(planes)
    tiles = planes.shape[1] // width
    parts = [jnp.concatenate([high[:, column(t)], low[:, column(t)]], axis=1) for t in range(tiles)]
    result = dot(jnp.concatenate(parts, axis=0), span_w)
    result = result[:, :width] + result[:, width:]
    return [result[t * cells : (t + 1) * cells].reshape(both, rows, width) for t in range(tiles)]


def second_input(means, parts):
    tiles = means + [means[i] * means[3] for i in range(3)]
    for t, value in enumerate(tiles):
        put_parts(parts, 0, column(t), value.reshape(-1, value.shape[-1]))


def packed_pass(spans, planes):
    cells = planes.shape[0]
    some, width = cells // 2, 128
    me_s = lax.axis_index("stream")
    along = pl.ds(pl.multiple_of((1 + me_s) * 2 * width, 2 * width), 2 * width)
    matrix = spans[:, along]
    high, low = halves(planes)
    tiles = planes.shape[1] // width
    parts = [
        jnp.concatenate(
            [high[:some, column(t)], low[:some, column(t)], high[some:, column(t)], low[some:, column(t)]],
            axis=1,
        )
        for t in range(tiles)
    ]
    result = dot(jnp.concatenate(parts, axis=0), matrix)
    result = result[:, :width] + result[:, width:]
    return [result[t * some : (t + 1) * some] for t in range(tiles)]


def pack_layers(own, other, me_s, shift=0):
    width = own.shape[-1]
    in_place = lane_index(own.shape) // (width // 2) == me_s
    own = pltpu.roll(own, shift % width, 2) if shift else own
    return jnp.where(in_place, own, pltpu.roll(other, (shift + width // 2) % width, 2))


def pack_means(mean, means, rows_near):
    for t, value in enumerate(means):
        mean[t] = value
    both = mean.shape[1]
    me_s = lax.axis_index("stream")
    own, other = pl.ds(me_s * (both // 2), both // 2), pl.ds((1 - me_s) * (both // 2), both // 2)
    for t in range(4):
        near = mean[t, own, rows_near, :], mean[t, other, rows_near, :]
        slope = (pack_layers(*near, me_s, -1) - pack_layers(*near, me_s, 1)) * 0.5
        yield t, pack_layers(mean[t, own], mean[t, other], me_s), slope


def mate_kernel(
    a_mine, a_rest, upper, lower, products, matrices, spans,
    base, packed, slopes, second, products_a, raw, parts, mid, mean, prod,
):
    both, rows = raw.shape[1:3]
    odd = lax.rem(lax.axis_index("wall"), 2)
    bring(a_mine, a_rest, raw, parts)
    planes = jnp.where(odd == 1, upper[...], lower[...])
    planes = planes + planes_of(matrices, 1 - odd, parts)
    means = span_pass(spans, planes, both)
    for t, value, slope in pack_means(mean, means, pl.ds(pl.multiple_of(odd * reach, reach), reach)):
        packed[t] = value
        slopes[t] = slope
    second_input(means, mid)
    second[...] = planes_of(matrices, 1 - odd, mid)
    base[...] = jnp.where(odd == 0, upper[...], lower[...])
    products_a[...] = add_products(matrices, 1 - odd, raw, products[...], prod)


def flux_kernel(
    walls, b_mine, b_rest, base, a_packed, a_slopes, a_second, products, matrices, spans,
    keep_ref, send_ref, sums_ref,
    raw, parts, prod, mean, mid, packed, slopes,
):
    _, layers, rows, width = keep_ref.shape
    both = 2 * layers
    cells = both * rows
    me_s = lax.axis_index("stream")
    me_w = lax.axis_index("wall")
    odd = lax.rem(me_w, 2)
    at_end = (me_w == 0) | (me_w == walls - 1)
    keep_b = jnp.where(at_end, 0.0, 1.0).astype(jnp.float32)

    bring(b_mine, b_rest, raw, parts, keep_b)

    planes = base[...] + planes_of(matrices, odd, parts)
    row = lax.rem(lax.broadcasted_iota(jnp.int32, planes.shape, 0), rows)
    inside = (row < reach) == (odd == 1)
    planes = jnp.where(jnp.logical_or(inside, jnp.logical_not(at_end)), planes, 0.0)
    means = span_pass(spans, planes, both)
    rows_b = pl.ds(pl.multiple_of(odd * rows, rows), rows)
    rows_a = pl.ds(pl.multiple_of((1 - odd) * rows, rows), rows)
    near_b = pl.ds(pl.multiple_of(odd * reach, reach), reach)
    near_a = pl.ds(pl.multiple_of((1 - odd) * reach, reach), reach)
    for t, value, slope in pack_means(mean, means, near_a):
        packed[t, :, rows_b, :] = value
        packed[t, :, rows_a, :] = a_packed[t]
        slopes[t, :, near_b, :] = slope
        slopes[t, :, near_a, :] = a_slopes[t]
    second_input(means, mid)
    second = packed_pass(spans, a_second[...] + planes_of(matrices, odd, mid))
    second = [value.reshape(layers, rows, width) for value in second]

    flux = packed_pass(spans, add_products(matrices, odd, raw, products[...], prod))
    flux = [value.reshape(layers, rows, width) for value in flux]

    mid_rows = slice(reach, reach + rows)
    first = lane_index((1, rows, width)) < width // 2
    centre, along_wall, along_stream = [], [], []
    for f in range(4):
        here = packed[f, :, mid_rows, :]
        centre.append(here)
        below = packed[f, :, reach + 1 : reach + rows + 1, :]
        above = packed[f, :, reach - 1 : reach + rows - 1, :]
        along_wall.append((below - above) * 0.5)
        after = jnp.where(first, pltpu.roll(here[:1], width // 2, 2), 0.0)
        before = jnp.where(first, 0.0, pltpu.roll(here[layers - 1 :], width // 2, 2))
        ahead = jnp.concatenate([here[1:], after], axis=0)
        behind = jnp.concatenate([before, here[: layers - 1]], axis=0)
        along_stream.append((ahead - behind) * 0.5)

    lane = lane_index((rows, width))
    table = jnp.zeros((rows, width), jnp.float32)
    first = lane_index((layers, rows, width)) < width // 2
    in_first = me_s == 1
    for i in range(3):
        exact = flux[i] - centre[i] * centre[3]
        similar = second[4 + i] - second[i] * second[3]
        total = slopes[i] * slopes[3] + along_wall[i] * along_wall[3]
        clark = clark_coef * (total + along_stream[i] * along_stream[3])
        terms = (exact * clark, exact * similar, exact * exact, clark * clark, similar * similar)
        for q, term in enumerate(terms):
            value = jnp.sum(jnp.sum(term, axis=0), axis=1, keepdims=True)
            table = jnp.where(lane == 3 * q + i, value, table)
        keep_ref[i] = clark
        keep_ref[3 + i] = similar
        clark = jnp.where(in_first, clark, pltpu.roll(clark, width // 2, 2))
        similar = jnp.where(in_first, pltpu.roll(similar, width // 2, 2), similar)
        send_ref[i] = jnp.where(first, clark, similar)
    sums_ref[...] = table


def finish_kernel(
    plane_cells, sums, keep, come, clark_model, similar_model, clark_corr, similar_corr
):
    _, layers, rows, width = keep.shape
    me_s = lax.axis_index("stream")
    table = sums[...] / plane_cells
    lane = lane_index((rows, width))
    useful = lane // (width // 2) == me_s
    corr = jnp.zeros((rows, width), jnp.float32)
    for i in range(3):
        cross_c, cross_s, power_e, power_c, power_s = (
            table[:, 3 * q + i : 3 * q + i + 1] for q in range(5)
        )
        packed = come[i]
        turned = pltpu.roll(packed, width // 2, 2)
        clark = jnp.where(useful[None], keep[i], jnp.where(me_s == 0, turned, packed))
        similar = jnp.where(useful[None], keep[3 + i], jnp.where(me_s == 0, packed, turned))
        clark_model[i] = clark / jnp.sqrt(power_c + small_eps)[None]
        similar_model[i] = similar / jnp.sqrt(power_s + small_eps)[None]
        value = cross_c / jnp.sqrt((power_e + small_eps) * (power_c + small_eps))
        corr = jnp.where(lane == i, value, corr)
        value = cross_s / jnp.sqrt((power_e + small_eps) * (power_s + small_eps))
        corr = jnp.where(lane == 8 + i, value, corr)
    square = jnp.concatenate([corr, jnp.zeros((width - rows, width), jnp.float32)], axis=0)
    turned = square.T
    clark_corr[...] = turned[:3, :rows]
    similar_corr[...] = turned[8:11, :rows]


def call(kernel, name, ins, outs, scratch=(), mib=4, hint=None):
    cost = hint and pl.CostEstimate(flops=hint, bytes_accessed=0, transcendentals=0)
    return pl.pallas_call(
        kernel,
        out_shape=tuple(jax.ShapeDtypeStruct(shape, jnp.float32) for shape in outs),
        in_specs=[pl.BlockSpec(memory_space=pltpu.VMEM)] * len(ins),
        out_specs=tuple(pl.BlockSpec(memory_space=pltpu.VMEM) for _ in outs),
        scratch_shapes=[pltpu.VMEM(shape, dtype) for shape, dtype in scratch],
        compiler_params=pltpu.CompilerParams(vmem_limit_bytes=mib * 1024 * 1024),
        cost_estimate=cost,
        name=name,
    )(*ins)


def shards(fields):
    _, layers, rows, width = fields.shape
    spans = lax.axis_size("span")
    walls = lax.axis_size("wall")
    streams = lax.axis_size("stream")
    both = streams * layers
    cells = both * rows

    def swap(value):
        return lax.ppermute(value, "stream", [(0, 1), (1, 0)])

    def pair_a(value):
        return lax.ppermute(value, "wall", [(w, w ^ 1) for w in range(walls)])

    def pass_on(value):
        ups = [(w, w + 2) for w in range(0, walls - 2, 2)]
        downs = [(w, w - 2) for w in range(3, walls, 2)]
        return lax.ppermute(value, "wall", ups + downs)

    def place(p, s):
        return (p % spans) * streams + s

    to_other, to_same = [], []
    for p in range(spans):
        to_other += [(place(p, 0), place(p - 1, 1)), (place(p, 1), place(p + 1, 0))]
        to_same += [(place(p, 1), place(p - 1, 1)), (place(p, 0), place(p + 1, 0))]

    message, strip = (2 * layers + layers // 2, rows, width), (layers // 2, rows, width)
    to_partner, mine, first, second = call(
        pack_kernel, "pack", (fields,), (message, message, strip, strip)
    )
    part = swap(to_partner)
    part_strip = lax.ppermute(first, ("span", "stream"), to_other)
    own_strip = lax.ppermute(second, ("span", "stream"), to_same)
    a_mine = pair_a(mine)
    mine_now, b_mine = lax.optimization_barrier((mine, pass_on(a_mine)))
    (rest,) = call(
        rest_kernel,
        "rest",
        (part, own_strip, part_strip),
        ((message[0] + layers, rows, width),),
        hint=2**35,
    )
    a_rest = pair_a(rest)

    matrices = jnp.asarray(plane_constants(both, rows))
    single_pass, split_pass = span_constants(width)
    both_passes = np.zeros((4 * width, 6 * width), ml_dtypes.bfloat16)
    both_passes[: 2 * width, : 2 * width] = single_pass
    both_passes[:, 2 * width :] = split_pass
    passes = jnp.asarray(both_passes)
    single, brief = jnp.float32, jnp.bfloat16
    block, quarter = (4, both, rows, width), (4, layers, rows, width)
    four, three, seven = (((3 * cells, n * width), brief) for n in (4, 3, 7))
    few = ((3 * both * reach, 3 * width), brief)
    upper, lower, products = call(
        centre_kernel,
        "centre",
        (mine_now, rest, matrices),
        ((cells, 4 * width), (cells, 4 * width), (cells, 3 * width)),
        [(block, single), four, three],
        mib=16,
        hint=2**31,
    )
    a_rest, upper = lax.optimization_barrier((a_rest, upper))
    b_rest = pass_on(a_rest)
    base, a_packed, a_slopes, a_second, products = call(
        mate_kernel,
        "mate",
        (a_mine, a_rest, upper, lower, products, matrices, passes),
        (
            (cells, 4 * width), quarter, (4, layers, reach, width), (cells, 7 * width),
            (cells, 3 * width),
        ),
        [(block, single), four, seven, (block, single), few],
        mib=16,
        hint=2**29,
    )
    keep, send, sums = call(
        functools.partial(flux_kernel, walls),
        "flux",
        (b_mine, b_rest, base, a_packed, a_slopes, a_second, products, matrices, passes),
        ((6, layers, rows, width), (3, layers, rows, width), (rows, width)),
        [
            (block, single),
            four,
            few,
            (block, single),
            seven,
            ((4, layers, 2 * rows, width), single),
            (quarter, single),
        ],
        mib=24,
    )

    come = swap(send)

    def from_span(value, step):
        return lax.ppermute(value, "span", [(p, p ^ step) for p in range(spans)])

    step = 1
    while step < spans:
        if 2 * step < spans:
            far = from_span(sums, 3 * step) + from_span(sums, 2 * step)
            sums = (sums + from_span(sums, step)) + far
        else:
            sums = sums + from_span(sums, step)
        step *= 4
    sums = sums + swap(sums)
    block, corr = (3, layers, rows, width), (3, rows)
    return call(
        functools.partial(finish_kernel, float(layers * width * spans * streams)),
        "finish",
        (sums, keep, come),
        (block, block, corr, corr),
    )


def solution(mesh):
    return jax.shard_map(
        shards,
        mesh=mesh,
        in_specs=(P(None, "stream", "wall", "span"),),
        out_specs=(
            P(None, "stream", "wall", "span"),
            P(None, "stream", "wall", "span"),
            P(None, "wall"),
            P(None, "wall"),
        ),
        check_vma=False,
    )
```

```python
import functools
import math

import jax
import jax.numpy as jnp
import ml_dtypes
import numpy as np
from jax import lax
from jax.experimental import pallas as pl
from jax.experimental.pallas import tpu as pltpu
from jax.sharding import PartitionSpec as P

raw_taps = [math.exp(-((k - 8) ** 2) / 18.0) for k in range(17)]
filter_taps = [value / sum(raw_taps) for value in raw_taps]
clark_coef = 9.0
small_eps = 1e-06

reach = 8
rim = 2 * reach


def split_constant(matrix):
    high = matrix.astype(ml_dtypes.bfloat16)
    low = (matrix - high.astype(np.float64)).astype(ml_dtypes.bfloat16)
    return high, low


def band(outs, ins, offset):
    matrix = np.zeros((outs, ins))
    for o in range(outs):
        for i in range(ins):
            k = i - o - offset + reach
            if 0 <= k <= 2 * reach:
                matrix[o, i] = filter_taps[k]
    return matrix


def plane_constants(layers, rows):
    stream = band(layers, layers, 0)
    wall = band(rows, 2 * rows, reach)
    ends = [0, reach, reach + rows, 2 * rows]
    thirds = [np.arange(ends[k], ends[k + 1]) for k in range(3)]
    parts = [np.arange(rows), np.arange(rows, 2 * rows), thirds[1], thirds[0], thirds[2]]
    blocks = [np.kron(stream, wall[:, part]) for part in parts]
    parts = [split_constant(block) for block in blocks]
    return np.concatenate([np.concatenate([high, low, high], axis=1) for high, low in parts], axis=1)


def span_constants(width):
    circle = np.zeros((width, width))
    for o in range(width):
        for k in range(2 * reach + 1):
            circle[(o + k - reach) % width, o] = filter_taps[k]
    half = width // 2

    def parts(matrix):
        high, low = split_constant(matrix)
        return np.block([[high, low], [high, np.zeros_like(low)]])

    packed = []
    for layers in range(2):
        row = []
        for s in range(2):
            matrix = np.zeros((width, width))
            matrix[:, layers * half : (layers + 1) * half] = circle[:, s * half : (s + 1) * half]
            row.append(parts(matrix))
        packed.append(np.concatenate(row, axis=1))
    return parts(circle), np.concatenate(packed, axis=0)


def halves(value):
    high = value.astype(jnp.bfloat16)
    return high, (value - high.astype(jnp.float32)).astype(jnp.bfloat16)


def dot(a, b):
    return lax.dot_general(a, b, (((1,), (0,)), ((), ())), preferred_element_type=jnp.float32)


def lane_index(shape):
    return lax.broadcasted_iota(jnp.int32, shape, len(shape) - 1)


def unit_index(shape):
    return lane_index(shape) // rim


def pack_halves(block, half):
    width = block.shape[-1]
    in_place = lane_index(block.shape[1:]) // (width // 2) == half
    for pair in range(2):
        moved = pltpu.roll(block[2 * pair + 1], width // 2, 2)
        yield pair, jnp.where(in_place, block[2 * pair], moved)


def pack_strip(block, unit):
    _, layers, rows, width = block.shape
    half = layers // 2
    units = unit_index((half, rows, width))
    total = jnp.zeros((half, rows, width), jnp.float32)
    for k in range(2):
        for f in range(4):
            step = 2 * f + k
            cells = block[f, k * half : (k + 1) * half]
            cells = pltpu.roll(cells, step * rim, 2) if step else cells
            total = jnp.where(units == lax.rem(unit + step, width // rim), cells, total)
    return total


def strip_tile(inner, outer, me_s):
    width = inner.shape[-1]
    is_outer = lax.rem(unit_index(inner.shape), 2) == 1 - me_s
    for k in range(2):
        shift = (width - k * rim) % width
        pieces = [pltpu.roll(strip, shift, 2) if k else strip for strip in (inner, outer)]
        yield k, jnp.where(is_outer, pieces[1], pieces[0])


def pack_kernel(own, to_partner, to_mine, to_other, to_same):
    _, layers, _, _ = own.shape
    me_s = lax.axis_index("stream")
    for message, half in ((to_partner, 1 - me_s), (to_mine, me_s)):
        for pair, tile in pack_halves(own, half):
            message[pair * layers : (pair + 1) * layers] = tile
        message[2 * layers :] = pack_strip(own, 4 - half)
    to_other[...] = pack_strip(own, 7 * me_s)
    to_same[...] = pack_strip(own, 7 * (1 - me_s))


def rest_kernel(part, own_strip, part_strip, rest):
    count, half = part.shape[0], own_strip.shape[0]
    rest[:count] = part[...]
    rest[count : count + half] = own_strip[...]
    rest[count + half :] = part_strip[...]


def unpack(mine, rest, me_s):
    count, rows, width = mine.shape
    layers = rest.shape[0] - count
    half = layers // 2
    unit = unit_index((half, rows, width))
    first = 4 * (1 - me_s)
    in_strip = (unit == first) | (unit == first + 3)
    for which, packed in enumerate((mine, rest)):
        far = rest[count + which * half : count + (which + 1) * half]
        for k, strip in strip_tile(packed[2 * layers : count], far, me_s):
            layer = (me_s if which == 0 else 1 - me_s) * layers + k * half
            for f in range(4):
                start = f // 2 * layers + k * half
                cells = packed[start : start + half]
                cells = pltpu.roll(cells, width // 2, 2) if f % 2 else cells
                moved = pltpu.roll(strip, width - 2 * f * rim, 2) if f else strip
                yield f, layer, jnp.where(in_strip, moved, cells)


def column(t, width=128):
    return slice(t * width, (t + 1) * width)


def put_parts(parts, down, across, value):
    third = parts.shape[0] // 3
    high, low = halves(value)
    for k, part in enumerate((high, high, low)):
        parts[pl.ds(k * third + down, value.shape[0]), across] = part


def planes_of(planes, part, parts):
    depth = parts.shape[0]
    start = part * depth if isinstance(part, int) else pl.multiple_of(part * depth, depth)
    return dot(planes[:, pl.ds(start, depth)], parts[...])


def add_products(planes, which, raw, base, parts):
    near = pl.ds(pl.multiple_of((1 - which) * reach, reach), reach)
    temperature = raw[3, :, near, :]
    for i in range(3):
        value = raw[i, :, near, :] * temperature
        put_parts(parts, 0, column(i), value.reshape(-1, value.shape[-1]))
    return base + planes_of(planes, 6 + which, parts)


def bring(mine, rest, raw, parts, keep=None):
    rows, width = mine.shape[1:]
    for f, layer, value in unpack(mine, rest, lax.axis_index("stream")):
        count = value.shape[0]
        value = value if keep is None else value * keep
        raw[f, pl.ds(layer, count)] = value
        down = pl.multiple_of(layer * rows, count * rows)
        put_parts(parts, down, column(f), value.reshape(-1, width))


def centre_kernel(
    mine, rest, planes, upper, lower, products, centre, parts, prod
):
    bring(mine, rest, centre, parts)
    for i in range(3):
        value = centre[i] * centre[3]
        put_parts(prod, 0, column(i), value.reshape(-1, value.shape[-1]))
    upper[...] = planes_of(planes, 1, parts)
    lower[...] = planes_of(planes, 0, parts)
    products[...] = planes_of(planes, 2, prod)


def span_pass(spans, planes, both):
    cells = planes.shape[0]
    rows = cells // both
    width = 128
    span_w = spans[: 2 * width, : 2 * width]
    high, low = halves(planes)
    tiles = planes.shape[1] // width
    parts = [jnp.concatenate([high[:, column(t)], low[:, column(t)]], axis=1) for t in range(tiles)]
    result = dot(jnp.concatenate(parts, axis=0), span_w)
    result = result[:, :width] + result[:, width:]
    return [result[t * cells : (t + 1) * cells].reshape(both, rows, width) for t in range(tiles)]


def second_input(means, parts):
    tiles = means + [means[i] * means[3] for i in range(3)]
    for t, value in enumerate(tiles):
        put_parts(parts, 0, column(t), value.reshape(-1, value.shape[-1]))


def packed_pass(spans, planes):
    cells = planes.shape[0]
    some, width = cells // 2, 128
    me_s = lax.axis_index("stream")
    along = pl.ds(pl.multiple_of((1 + me_s) * 2 * width, 2 * width), 2 * width)
    matrix = spans[:, along]
    high, low = halves(planes)
    tiles = planes.shape[1] // width
    parts = [
        jnp.concatenate(
            [high[:some, column(t)], low[:some, column(t)], high[some:, column(t)], low[some:, column(t)]],
            axis=1,
        )
        for t in range(tiles)
    ]
    result = dot(jnp.concatenate(parts, axis=0), matrix)
    result = result[:, :width] + result[:, width:]
    return [result[t * some : (t + 1) * some] for t in range(tiles)]


def pack_layers(own, other, me_s, shift=0):
    width = own.shape[-1]
    in_place = lane_index(own.shape) // (width // 2) == me_s
    own = pltpu.roll(own, shift % width, 2) if shift else own
    return jnp.where(in_place, own, pltpu.roll(other, (shift + width // 2) % width, 2))


def pack_means(mean, means, rows_near):
    for t, value in enumerate(means):
        mean[t] = value
    both = mean.shape[1]
    me_s = lax.axis_index("stream")
    own, other = pl.ds(me_s * (both // 2), both // 2), pl.ds((1 - me_s) * (both // 2), both // 2)
    for t in range(4):
        near = mean[t, own, rows_near, :], mean[t, other, rows_near, :]
        slope = (pack_layers(*near, me_s, -1) - pack_layers(*near, me_s, 1)) * 0.5
        yield t, pack_layers(mean[t, own], mean[t, other], me_s), slope


def mate_kernel(
    a_mine, a_rest, upper, lower, products, matrices, spans,
    base, packed, slopes, second, products_a, raw, parts, mid, mean, prod,
):
    both, rows = raw.shape[1:3]
    odd = lax.rem(lax.axis_index("wall"), 2)
    bring(a_mine, a_rest, raw, parts)
    planes = jnp.where(odd == 1, upper[...], lower[...])
    planes = planes + planes_of(matrices, 1 - odd, parts)
    means = span_pass(spans, planes, both)
    for t, value, slope in pack_means(mean, means, pl.ds(pl.multiple_of(odd * reach, reach), reach)):
        packed[t] = value
        slopes[t] = slope
    second_input(means, mid)
    second[...] = planes_of(matrices, 1 - odd, mid)
    base[...] = jnp.where(odd == 0, upper[...], lower[...])
    products_a[...] = add_products(matrices, 1 - odd, raw, products[...], prod)


def flux_kernel(
    walls, b_mine, b_rest, base, a_packed, a_slopes, a_second, products, matrices, spans,
    keep_ref, send_ref, sums_ref,
    raw, parts, prod, mean, mid, packed, slopes,
):
    _, layers, rows, width = keep_ref.shape
    both = 2 * layers
    cells = both * rows
    me_s = lax.axis_index("stream")
    me_w = lax.axis_index("wall")
    odd = lax.rem(me_w, 2)
    at_end = (me_w == 0) | (me_w == walls - 1)
    keep_b = jnp.where(at_end, 0.0, 1.0).astype(jnp.float32)

    bring(b_mine, b_rest, raw, parts, keep_b)

    planes = base[...] + planes_of(matrices, odd, parts)
    row = lax.rem(lax.broadcasted_iota(jnp.int32, planes.shape, 0), rows)
    inside = (row < reach) == (odd == 1)
    planes = jnp.where(jnp.logical_or(inside, jnp.logical_not(at_end)), planes, 0.0)
    means = span_pass(spans, planes, both)
    rows_b = pl.ds(pl.multiple_of(odd * rows, rows), rows)
    rows_a = pl.ds(pl.multiple_of((1 - odd) * rows, rows), rows)
    near_b = pl.ds(pl.multiple_of(odd * reach, reach), reach)
    near_a = pl.ds(pl.multiple_of((1 - odd) * reach, reach), reach)
    for t, value, slope in pack_means(mean, means, near_a):
        packed[t, :, rows_b, :] = value
        packed[t, :, rows_a, :] = a_packed[t]
        slopes[t, :, near_b, :] = slope
        slopes[t, :, near_a, :] = a_slopes[t]
    second_input(means, mid)
    second = packed_pass(spans, a_second[...] + planes_of(matrices, odd, mid))
    second = [value.reshape(layers, rows, width) for value in second]

    flux = packed_pass(spans, add_products(matrices, odd, raw, products[...], prod))
    flux = [value.reshape(layers, rows, width) for value in flux]

    mid_rows = slice(reach, reach + rows)
    first = lane_index((1, rows, width)) < width // 2
    centre, along_wall, along_stream = [], [], []
    for f in range(4):
        here = packed[f, :, mid_rows, :]
        centre.append(here)
        below = packed[f, :, reach + 1 : reach + rows + 1, :]
        above = packed[f, :, reach - 1 : reach + rows - 1, :]
        along_wall.append((below - above) * 0.5)
        after = jnp.where(first, pltpu.roll(here[:1], width // 2, 2), 0.0)
        before = jnp.where(first, 0.0, pltpu.roll(here[layers - 1 :], width // 2, 2))
        ahead = jnp.concatenate([here[1:], after], axis=0)
        behind = jnp.concatenate([before, here[: layers - 1]], axis=0)
        along_stream.append((ahead - behind) * 0.5)

    lane = lane_index((rows, width))
    table = jnp.zeros((rows, width), jnp.float32)
    first = lane_index((layers, rows, width)) < width // 2
    in_first = me_s == 1
    for i in range(3):
        exact = flux[i] - centre[i] * centre[3]
        similar = second[4 + i] - second[i] * second[3]
        total = slopes[i] * slopes[3] + along_wall[i] * along_wall[3]
        clark = clark_coef * (total + along_stream[i] * along_stream[3])
        terms = (exact * clark, exact * similar, exact * exact, clark * clark, similar * similar)
        for q, term in enumerate(terms):
            value = jnp.sum(jnp.sum(term, axis=0), axis=1, keepdims=True)
            table = jnp.where(lane == 3 * q + i, value, table)
        keep_ref[i] = clark
        keep_ref[3 + i] = similar
        clark = jnp.where(in_first, clark, pltpu.roll(clark, width // 2, 2))
        similar = jnp.where(in_first, pltpu.roll(similar, width // 2, 2), similar)
        send_ref[i] = jnp.where(first, clark, similar)
    sums_ref[...] = table


def finish_kernel(
    plane_cells, sums, keep, come, clark_model, similar_model, clark_corr, similar_corr
):
    _, layers, rows, width = keep.shape
    me_s = lax.axis_index("stream")
    table = sums[...] / plane_cells
    lane = lane_index((rows, width))
    useful = lane // (width // 2) == me_s
    corr = jnp.zeros((rows, width), jnp.float32)
    for i in range(3):
        cross_c, cross_s, power_e, power_c, power_s = (
            table[:, 3 * q + i : 3 * q + i + 1] for q in range(5)
        )
        packed = come[i]
        turned = pltpu.roll(packed, width // 2, 2)
        clark = jnp.where(useful[None], keep[i], jnp.where(me_s == 0, turned, packed))
        similar = jnp.where(useful[None], keep[3 + i], jnp.where(me_s == 0, packed, turned))
        clark_model[i] = clark / jnp.sqrt(power_c + small_eps)[None]
        similar_model[i] = similar / jnp.sqrt(power_s + small_eps)[None]
        value = cross_c / jnp.sqrt((power_e + small_eps) * (power_c + small_eps))
        corr = jnp.where(lane == i, value, corr)
        value = cross_s / jnp.sqrt((power_e + small_eps) * (power_s + small_eps))
        corr = jnp.where(lane == 8 + i, value, corr)
    square = jnp.concatenate([corr, jnp.zeros((width - rows, width), jnp.float32)], axis=0)
    turned = square.T
    clark_corr[...] = turned[:3, :rows]
    similar_corr[...] = turned[8:11, :rows]


def call(kernel, name, ins, outs, scratch=(), mib=4, hint=None):
    cost = hint and pl.CostEstimate(flops=hint, bytes_accessed=0, transcendentals=0)
    return pl.pallas_call(
        kernel,
        out_shape=tuple(jax.ShapeDtypeStruct(shape, jnp.float32) for shape in outs),
        in_specs=[pl.BlockSpec(memory_space=pltpu.VMEM)] * len(ins),
        out_specs=tuple(pl.BlockSpec(memory_space=pltpu.VMEM) for _ in outs),
        scratch_shapes=[pltpu.VMEM(shape, dtype) for shape, dtype in scratch],
        compiler_params=pltpu.CompilerParams(vmem_limit_bytes=mib * 1024 * 1024),
        cost_estimate=cost,
        name=name,
    )(*ins)


def shards(fields):
    _, layers, rows, width = fields.shape
    spans = lax.axis_size("span")
    walls = lax.axis_size("wall")
    streams = lax.axis_size("stream")
    both = streams * layers
    cells = both * rows

    def swap(value):
        return lax.ppermute(value, "stream", [(0, 1), (1, 0)])

    def pair_a(value):
        return lax.ppermute(value, "wall", [(w, w ^ 1) for w in range(walls)])

    def pair_b(value):
        return lax.ppermute(
            value, "wall", [(w, min(max(((w + 1) ^ 1) - 1, 0), walls - 1)) for w in range(walls)]
        )

    def place(p, s):
        return (p % spans) * streams + s

    to_other, to_same = [], []
    for p in range(spans):
        to_other += [(place(p, 0), place(p - 1, 1)), (place(p, 1), place(p + 1, 0))]
        to_same += [(place(p, 1), place(p - 1, 1)), (place(p, 0), place(p + 1, 0))]

    message, strip = (2 * layers + layers // 2, rows, width), (layers // 2, rows, width)
    to_partner, mine, first, second = call(
        pack_kernel, "pack", (fields,), (message, message, strip, strip)
    )
    part = swap(to_partner)
    part_strip = lax.ppermute(first, ("span", "stream"), to_other)
    own_strip = lax.ppermute(second, ("span", "stream"), to_same)
    own_strip, part_strip, a_mine = lax.optimization_barrier((own_strip, part_strip, pair_a(mine)))
    mine_now, b_mine = lax.optimization_barrier((mine, pair_b(mine)))
    (rest,) = call(
        rest_kernel,
        "rest",
        (part, own_strip, part_strip),
        ((message[0] + layers, rows, width),),
        hint=2**35,
    )
    a_rest, b_rest = pair_a(rest), pair_b(rest)

    matrices = jnp.asarray(plane_constants(both, rows))
    single_pass, split_pass = span_constants(width)
    both_passes = np.zeros((4 * width, 6 * width), ml_dtypes.bfloat16)
    both_passes[: 2 * width, : 2 * width] = single_pass
    both_passes[:, 2 * width :] = split_pass
    passes = jnp.asarray(both_passes)
    single, brief = jnp.float32, jnp.bfloat16
    block, quarter = (4, both, rows, width), (4, layers, rows, width)
    four, three, seven = (((3 * cells, n * width), brief) for n in (4, 3, 7))
    few = ((3 * both * reach, 3 * width), brief)
    upper, lower, products = call(
        centre_kernel,
        "centre",
        (mine_now, rest, matrices),
        ((cells, 4 * width), (cells, 4 * width), (cells, 3 * width)),
        [(block, single), four, three],
        mib=16,
        hint=2**31,
    )
    base, a_packed, a_slopes, a_second, products = call(
        mate_kernel,
        "mate",
        (a_mine, a_rest, upper, lower, products, matrices, passes),
        (
            (cells, 4 * width), quarter, (4, layers, reach, width), (cells, 7 * width),
            (cells, 3 * width),
        ),
        [(block, single), four, seven, (block, single), few],
        mib=16,
        hint=2**29,
    )
    keep, send, sums = call(
        functools.partial(flux_kernel, walls),
        "flux",
        (b_mine, b_rest, base, a_packed, a_slopes, a_second, products, matrices, passes),
        ((6, layers, rows, width), (3, layers, rows, width), (rows, width)),
        [
            (block, single),
            four,
            few,
            (block, single),
            seven,
            ((4, layers, 2 * rows, width), single),
            (quarter, single),
        ],
        mib=24,
    )

    come = swap(send)

    def from_span(value, step):
        return lax.ppermute(value, "span", [(p, p ^ step) for p in range(spans)])

    step = 1
    while step < spans:
        if 2 * step < spans:
            far = from_span(sums, 3 * step) + from_span(sums, 2 * step)
            sums = (sums + from_span(sums, step)) + far
        else:
            sums = sums + from_span(sums, step)
        step *= 4
    sums = sums + swap(sums)
    block, corr = (3, layers, rows, width), (3, rows)
    return call(
        functools.partial(finish_kernel, float(layers * width * spans * streams)),
        "finish",
        (sums, keep, come),
        (block, block, corr, corr),
    )


def solution(mesh):
    return jax.shard_map(
        shards,
        mesh=mesh,
        in_specs=(P(None, "stream", "wall", "span"),),
        out_specs=(
            P(None, "stream", "wall", "span"),
            P(None, "stream", "wall", "span"),
            P(None, "wall"),
            P(None, "wall"),
        ),
        check_vma=False,
    )
```

```python
import functools
import math

import jax
import jax.numpy as jnp
import ml_dtypes
import numpy as np
from jax import lax
from jax.experimental import pallas as pl
from jax.experimental.pallas import tpu as pltpu
from jax.sharding import PartitionSpec as P

raw_taps = [math.exp(-((k - 8) ** 2) / 18.0) for k in range(17)]
filter_taps = [value / sum(raw_taps) for value in raw_taps]
clark_coef = 9.0
small_eps = 1e-06

reach = 8
rim = 2 * reach


def split_constant(matrix):
    high = matrix.astype(ml_dtypes.bfloat16)
    low = (matrix - high.astype(np.float64)).astype(ml_dtypes.bfloat16)
    return high, low


def band(outs, ins, offset):
    matrix = np.zeros((outs, ins))
    for o in range(outs):
        for i in range(ins):
            k = i - o - offset + reach
            if 0 <= k <= 2 * reach:
                matrix[o, i] = filter_taps[k]
    return matrix


def plane_constants(layers, rows):
    stream = band(layers, layers, 0)
    wall = band(rows, 2 * rows, reach)
    ends = [0, reach, reach + rows, 2 * rows]
    thirds = [np.arange(ends[k], ends[k + 1]) for k in range(3)]
    parts = [np.arange(rows), np.arange(rows, 2 * rows), thirds[1], thirds[0], thirds[2]]
    blocks = [np.kron(stream, wall[:, part]) for part in parts]
    parts = [split_constant(block) for block in blocks]
    return np.concatenate([np.concatenate([high, low, high], axis=1) for high, low in parts], axis=1)


def span_constants(width):
    circle = np.zeros((width, width))
    for o in range(width):
        for k in range(2 * reach + 1):
            circle[(o + k - reach) % width, o] = filter_taps[k]
    half = width // 2

    def parts(matrix):
        high, low = split_constant(matrix)
        return np.block([[high, low], [high, np.zeros_like(low)]])

    packed = []
    for layers in range(2):
        row = []
        for s in range(2):
            matrix = np.zeros((width, width))
            matrix[:, layers * half : (layers + 1) * half] = circle[:, s * half : (s + 1) * half]
            row.append(parts(matrix))
        packed.append(np.concatenate(row, axis=1))
    return parts(circle), np.concatenate(packed, axis=0)


def halves(value):
    high = value.astype(jnp.bfloat16)
    return high, (value - high.astype(jnp.float32)).astype(jnp.bfloat16)


def dot(a, b):
    return lax.dot_general(a, b, (((1,), (0,)), ((), ())), preferred_element_type=jnp.float32)


def lane_index(shape):
    return lax.broadcasted_iota(jnp.int32, shape, len(shape) - 1)


def unit_index(shape):
    return lane_index(shape) // rim


def pack_halves(block, half):
    width = block.shape[-1]
    in_place = lane_index(block.shape[1:]) // (width // 2) == half
    for pair in range(2):
        moved = pltpu.roll(block[2 * pair + 1], width // 2, 2)
        yield pair, jnp.where(in_place, block[2 * pair], moved)


def pack_strip(block, unit):
    _, layers, rows, width = block.shape
    half = layers // 2
    units = unit_index((half, rows, width))
    total = jnp.zeros((half, rows, width), jnp.float32)
    for k in range(2):
        for f in range(4):
            step = 2 * f + k
            cells = block[f, k * half : (k + 1) * half]
            cells = pltpu.roll(cells, step * rim, 2) if step else cells
            total = jnp.where(units == lax.rem(unit + step, width // rim), cells, total)
    return total


def strip_tile(inner, outer, me_s):
    width = inner.shape[-1]
    is_outer = lax.rem(unit_index(inner.shape), 2) == 1 - me_s
    for k in range(2):
        shift = (width - k * rim) % width
        pieces = [pltpu.roll(strip, shift, 2) if k else strip for strip in (inner, outer)]
        yield k, jnp.where(is_outer, pieces[1], pieces[0])


def pack_kernel(own, to_partner, to_mine, to_other, to_same):
    _, layers, _, _ = own.shape
    me_s = lax.axis_index("stream")
    for message, half in ((to_partner, 1 - me_s), (to_mine, me_s)):
        for pair, tile in pack_halves(own, half):
            message[pair * layers : (pair + 1) * layers] = tile
        message[2 * layers :] = pack_strip(own, 4 - half)
    to_other[...] = pack_strip(own, 7 * me_s)
    to_same[...] = pack_strip(own, 7 * (1 - me_s))


def rest_kernel(part, strips, rest):
    count = part.shape[0]
    rest[:count] = part[...]
    rest[count:] = strips[...]


def unpack(mine, rest, me_s):
    count, rows, width = mine.shape
    layers = rest.shape[0] - count
    half = layers // 2
    unit = unit_index((half, rows, width))
    first = 4 * (1 - me_s)
    in_strip = (unit == first) | (unit == first + 3)
    for which, packed in enumerate((mine, rest)):
        far = rest[count + which * half : count + (which + 1) * half]
        for k, strip in strip_tile(packed[2 * layers : count], far, me_s):
            layer = (me_s if which == 0 else 1 - me_s) * layers + k * half
            for f in range(4):
                start = f // 2 * layers + k * half
                cells = packed[start : start + half]
                cells = pltpu.roll(cells, width // 2, 2) if f % 2 else cells
                moved = pltpu.roll(strip, width - 2 * f * rim, 2) if f else strip
                yield f, layer, jnp.where(in_strip, moved, cells)


def column(t, width=128):
    return slice(t * width, (t + 1) * width)


def put_parts(parts, down, across, value):
    third = parts.shape[0] // 3
    high, low = halves(value)
    for k, part in enumerate((high, high, low)):
        parts[pl.ds(k * third + down, value.shape[0]), across] = part


def planes_of(planes, part, parts):
    depth = parts.shape[0]
    start = part * depth if isinstance(part, int) else pl.multiple_of(part * depth, depth)
    return dot(planes[:, pl.ds(start, depth)], parts[...])


def add_products(planes, which, raw, base, parts):
    near = pl.ds(pl.multiple_of((1 - which) * reach, reach), reach)
    temperature = raw[3, :, near, :]
    for i in range(3):
        value = raw[i, :, near, :] * temperature
        put_parts(parts, 0, column(i), value.reshape(-1, value.shape[-1]))
    return base + planes_of(planes, 6 + which, parts)


def bring(mine, rest, raw, parts, keep=None):
    rows, width = mine.shape[1:]
    for f, layer, value in unpack(mine, rest, lax.axis_index("stream")):
        count = value.shape[0]
        value = value if keep is None else value * keep
        raw[f, pl.ds(layer, count)] = value
        down = pl.multiple_of(layer * rows, count * rows)
        put_parts(parts, down, column(f), value.reshape(-1, width))


def centre_kernel(
    mine, rest, planes, upper, lower, products, centre, parts, prod
):
    bring(mine, rest, centre, parts)
    for i in range(3):
        value = centre[i] * centre[3]
        put_parts(prod, 0, column(i), value.reshape(-1, value.shape[-1]))
    upper[...] = planes_of(planes, 1, parts)
    lower[...] = planes_of(planes, 0, parts)
    products[...] = planes_of(planes, 2, prod)


def span_pass(spans, planes, both):
    cells = planes.shape[0]
    rows = cells // both
    width = 128
    span_w = spans[: 2 * width, : 2 * width]
    high, low = halves(planes)
    tiles = planes.shape[1] // width
    parts = [jnp.concatenate([high[:, column(t)], low[:, column(t)]], axis=1) for t in range(tiles)]
    result = dot(jnp.concatenate(parts, axis=0), span_w)
    result = result[:, :width] + result[:, width:]
    return [result[t * cells : (t + 1) * cells].reshape(both, rows, width) for t in range(tiles)]


def second_input(means, parts):
    tiles = means + [means[i] * means[3] for i in range(3)]
    for t, value in enumerate(tiles):
        put_parts(parts, 0, column(t), value.reshape(-1, value.shape[-1]))


def packed_pass(spans, planes):
    cells = planes.shape[0]
    some, width = cells // 2, 128
    me_s = lax.axis_index("stream")
    along = pl.ds(pl.multiple_of((1 + me_s) * 2 * width, 2 * width), 2 * width)
    matrix = spans[:, along]
    high, low = halves(planes)
    tiles = planes.shape[1] // width
    parts = [
        jnp.concatenate(
            [high[:some, column(t)], low[:some, column(t)], high[some:, column(t)], low[some:, column(t)]],
            axis=1,
        )
        for t in range(tiles)
    ]
    result = dot(jnp.concatenate(parts, axis=0), matrix)
    result = result[:, :width] + result[:, width:]
    return [result[t * some : (t + 1) * some] for t in range(tiles)]


def pack_layers(own, other, me_s, shift=0):
    width = own.shape[-1]
    in_place = lane_index(own.shape) // (width // 2) == me_s
    own = pltpu.roll(own, shift % width, 2) if shift else own
    return jnp.where(in_place, own, pltpu.roll(other, (shift + width // 2) % width, 2))


def pack_means(mean, means, rows_near):
    for t, value in enumerate(means):
        mean[t] = value
    both = mean.shape[1]
    me_s = lax.axis_index("stream")
    own, other = pl.ds(me_s * (both // 2), both // 2), pl.ds((1 - me_s) * (both // 2), both // 2)
    for t in range(4):
        near = mean[t, own, rows_near, :], mean[t, other, rows_near, :]
        slope = (pack_layers(*near, me_s, -1) - pack_layers(*near, me_s, 1)) * 0.5
        yield t, pack_layers(mean[t, own], mean[t, other], me_s), slope


def mate_kernel(
    a_mine, a_rest, upper, lower, products, matrices, spans,
    base, packed, slopes, second, products_a, raw, parts, mid, mean, prod,
):
    both, rows = raw.shape[1:3]
    odd = lax.rem(lax.axis_index("wall"), 2)
    bring(a_mine, a_rest, raw, parts)
    planes = jnp.where(odd == 1, upper[...], lower[...])
    planes = planes + planes_of(matrices, 1 - odd, parts)
    means = span_pass(spans, planes, both)
    for t, value, slope in pack_means(mean, means, pl.ds(pl.multiple_of(odd * reach, reach), reach)):
        packed[t] = value
        slopes[t] = slope
    second_input(means, mid)
    second[...] = planes_of(matrices, 1 - odd, mid)
    base[...] = jnp.where(odd == 0, upper[...], lower[...])
    products_a[...] = add_products(matrices, 1 - odd, raw, products[...], prod)


def flux_kernel(
    walls, b_mine, b_rest, base, a_packed, a_slopes, a_second, products, matrices, spans,
    keep_ref, send_ref, sums_ref,
    raw, parts, prod, mean, mid, packed, slopes,
):
    _, layers, rows, width = keep_ref.shape
    both = 2 * layers
    cells = both * rows
    me_s = lax.axis_index("stream")
    me_w = lax.axis_index("wall")
    odd = lax.rem(me_w, 2)
    at_end = (me_w == 0) | (me_w == walls - 1)
    keep_b = jnp.where(at_end, 0.0, 1.0).astype(jnp.float32)

    bring(b_mine, b_rest, raw, parts, keep_b)

    planes = base[...] + planes_of(matrices, odd, parts)
    row = lax.rem(lax.broadcasted_iota(jnp.int32, planes.shape, 0), rows)
    inside = (row < reach) == (odd == 1)
    planes = jnp.where(jnp.logical_or(inside, jnp.logical_not(at_end)), planes, 0.0)
    means = span_pass(spans, planes, both)
    rows_b = pl.ds(pl.multiple_of(odd * rows, rows), rows)
    rows_a = pl.ds(pl.multiple_of((1 - odd) * rows, rows), rows)
    near_b = pl.ds(pl.multiple_of(odd * reach, reach), reach)
    near_a = pl.ds(pl.multiple_of((1 - odd) * reach, reach), reach)
    for t, value, slope in pack_means(mean, means, near_a):
        packed[t, :, rows_b, :] = value
        packed[t, :, rows_a, :] = a_packed[t]
        slopes[t, :, near_b, :] = slope
        slopes[t, :, near_a, :] = a_slopes[t]
    second_input(means, mid)
    second = packed_pass(spans, a_second[...] + planes_of(matrices, odd, mid))
    second = [value.reshape(layers, rows, width) for value in second]

    flux = packed_pass(spans, add_products(matrices, odd, raw, products[...], prod))
    flux = [value.reshape(layers, rows, width) for value in flux]

    mid_rows = slice(reach, reach + rows)
    first = lane_index((1, rows, width)) < width // 2
    centre, along_wall, along_stream = [], [], []
    for f in range(4):
        here = packed[f, :, mid_rows, :]
        centre.append(here)
        below = packed[f, :, reach + 1 : reach + rows + 1, :]
        above = packed[f, :, reach - 1 : reach + rows - 1, :]
        along_wall.append((below - above) * 0.5)
        after = jnp.where(first, pltpu.roll(here[:1], width // 2, 2), 0.0)
        before = jnp.where(first, 0.0, pltpu.roll(here[layers - 1 :], width // 2, 2))
        ahead = jnp.concatenate([here[1:], after], axis=0)
        behind = jnp.concatenate([before, here[: layers - 1]], axis=0)
        along_stream.append((ahead - behind) * 0.5)

    lane = lane_index((rows, width))
    table = jnp.zeros((rows, width), jnp.float32)
    first = lane_index((layers, rows, width)) < width // 2
    in_first = me_s == 1
    for i in range(3):
        exact = flux[i] - centre[i] * centre[3]
        similar = second[4 + i] - second[i] * second[3]
        total = slopes[i] * slopes[3] + along_wall[i] * along_wall[3]
        clark = clark_coef * (total + along_stream[i] * along_stream[3])
        terms = (exact * clark, exact * similar, exact * exact, clark * clark, similar * similar)
        for q, term in enumerate(terms):
            value = jnp.sum(jnp.sum(term, axis=0), axis=1, keepdims=True)
            table = jnp.where(lane == 3 * q + i, value, table)
        keep_ref[i] = clark
        keep_ref[3 + i] = similar
        clark = jnp.where(in_first, clark, pltpu.roll(clark, width // 2, 2))
        similar = jnp.where(in_first, pltpu.roll(similar, width // 2, 2), similar)
        send_ref[i] = jnp.where(first, clark, similar)
    sums_ref[...] = table


def finish_kernel(
    plane_cells, sums, keep, come, clark_model, similar_model, clark_corr, similar_corr
):
    _, layers, rows, width = keep.shape
    me_s = lax.axis_index("stream")
    table = sums[...] / plane_cells
    lane = lane_index((rows, width))
    useful = lane // (width // 2) == me_s
    corr = jnp.zeros((rows, width), jnp.float32)
    for i in range(3):
        cross_c, cross_s, power_e, power_c, power_s = (
            table[:, 3 * q + i : 3 * q + i + 1] for q in range(5)
        )
        packed = come[i]
        turned = pltpu.roll(packed, width // 2, 2)
        clark = jnp.where(useful[None], keep[i], jnp.where(me_s == 0, turned, packed))
        similar = jnp.where(useful[None], keep[3 + i], jnp.where(me_s == 0, packed, turned))
        clark_model[i] = clark / jnp.sqrt(power_c + small_eps)[None]
        similar_model[i] = similar / jnp.sqrt(power_s + small_eps)[None]
        value = cross_c / jnp.sqrt((power_e + small_eps) * (power_c + small_eps))
        corr = jnp.where(lane == i, value, corr)
        value = cross_s / jnp.sqrt((power_e + small_eps) * (power_s + small_eps))
        corr = jnp.where(lane == 8 + i, value, corr)
    square = jnp.concatenate([corr, jnp.zeros((width - rows, width), jnp.float32)], axis=0)
    turned = square.T
    clark_corr[...] = turned[:3, :rows]
    similar_corr[...] = turned[8:11, :rows]


def call(kernel, name, ins, outs, scratch=(), mib=4, hint=None):
    cost = hint and pl.CostEstimate(flops=hint, bytes_accessed=0, transcendentals=0)
    return pl.pallas_call(
        kernel,
        out_shape=tuple(jax.ShapeDtypeStruct(shape, jnp.float32) for shape in outs),
        in_specs=[pl.BlockSpec(memory_space=pltpu.VMEM)] * len(ins),
        out_specs=tuple(pl.BlockSpec(memory_space=pltpu.VMEM) for _ in outs),
        scratch_shapes=[pltpu.VMEM(shape, dtype) for shape, dtype in scratch],
        compiler_params=pltpu.CompilerParams(vmem_limit_bytes=mib * 1024 * 1024),
        cost_estimate=cost,
        name=name,
    )(*ins)


def shards(fields):
    _, layers, rows, width = fields.shape
    spans = lax.axis_size("span")
    walls = lax.axis_size("wall")
    streams = lax.axis_size("stream")
    both = streams * layers
    cells = both * rows

    def swap(value):
        return lax.ppermute(value, "stream", [(0, 1), (1, 0)])

    def pair_a(value):
        return lax.ppermute(value, "wall", [(w, w ^ 1) for w in range(walls)])

    def pair_b(value):
        return lax.ppermute(
            value, "wall", [(w, min(max(((w + 1) ^ 1) - 1, 0), walls - 1)) for w in range(walls)]
        )

    def place(p, s):
        return (p % spans) * streams + s

    to_same = []
    for p in range(spans):
        to_same += [(place(p, 1), place(p - 1, 1)), (place(p, 0), place(p + 1, 0))]

    message, strip = (2 * layers + layers // 2, rows, width), (layers // 2, rows, width)
    to_partner, mine, first, second = call(
        pack_kernel, "pack", (fields,), (message, message, strip, strip)
    )
    part = swap(to_partner)
    strips = lax.ppermute(jnp.concatenate([second, swap(first)]), ("span", "stream"), to_same)
    mine_now, b_mine, a_mine = lax.optimization_barrier((mine, pair_b(mine), pair_a(mine)))
    (rest,) = call(
        rest_kernel,
        "rest",
        (part, strips),
        ((message[0] + layers, rows, width),),
        hint=2**35,
    )
    a_rest, b_rest = pair_a(rest), pair_b(rest)

    matrices = jnp.asarray(plane_constants(both, rows))
    single_pass, split_pass = span_constants(width)
    both_passes = np.zeros((4 * width, 6 * width), ml_dtypes.bfloat16)
    both_passes[: 2 * width, : 2 * width] = single_pass
    both_passes[:, 2 * width :] = split_pass
    passes = jnp.asarray(both_passes)
    single, brief = jnp.float32, jnp.bfloat16
    block, quarter = (4, both, rows, width), (4, layers, rows, width)
    four, three, seven = (((3 * cells, n * width), brief) for n in (4, 3, 7))
    few = ((3 * both * reach, 3 * width), brief)
    upper, lower, products = call(
        centre_kernel,
        "centre",
        (mine_now, rest, matrices),
        ((cells, 4 * width), (cells, 4 * width), (cells, 3 * width)),
        [(block, single), four, three],
        mib=16,
        hint=2**31,
    )
    base, a_packed, a_slopes, a_second, products = call(
        mate_kernel,
        "mate",
        (a_mine, a_rest, upper, lower, products, matrices, passes),
        (
            (cells, 4 * width), quarter, (4, layers, reach, width), (cells, 7 * width),
            (cells, 3 * width),
        ),
        [(block, single), four, seven, (block, single), few],
        mib=16,
        hint=2**29,
    )
    keep, send, sums = call(
        functools.partial(flux_kernel, walls),
        "flux",
        (b_mine, b_rest, base, a_packed, a_slopes, a_second, products, matrices, passes),
        ((6, layers, rows, width), (3, layers, rows, width), (rows, width)),
        [
            (block, single),
            four,
            few,
            (block, single),
            seven,
            ((4, layers, 2 * rows, width), single),
            (quarter, single),
        ],
        mib=24,
    )

    come = swap(send)

    def from_span(value, step):
        return lax.ppermute(value, "span", [(p, p ^ step) for p in range(spans)])

    step = 1
    while step < spans:
        if 2 * step < spans:
            far = from_span(sums, 3 * step) + from_span(sums, 2 * step)
            sums = (sums + from_span(sums, step)) + far
        else:
            sums = sums + from_span(sums, step)
        step *= 4
    sums = sums + swap(sums)
    block, corr = (3, layers, rows, width), (3, rows)
    return call(
        functools.partial(finish_kernel, float(layers * width * spans * streams)),
        "finish",
        (sums, keep, come),
        (block, block, corr, corr),
    )


def solution(mesh):
    return jax.shard_map(
        shards,
        mesh=mesh,
        in_specs=(P(None, "stream", "wall", "span"),),
        out_specs=(
            P(None, "stream", "wall", "span"),
            P(None, "stream", "wall", "span"),
            P(None, "wall"),
            P(None, "wall"),
        ),
        check_vma=False,
    )
```

```python
import functools
import math

import jax
import jax.numpy as jnp
import ml_dtypes
import numpy as np
from jax import lax
from jax.experimental import pallas as pl
from jax.experimental.pallas import tpu as pltpu
from jax.sharding import PartitionSpec as P

raw_taps = [math.exp(-((k - 8) ** 2) / 18.0) for k in range(17)]
filter_taps = [value / sum(raw_taps) for value in raw_taps]
clark_coef = 9.0
small_eps = 1e-06

reach = 8
rim = 2 * reach


def split_constant(matrix):
    high = matrix.astype(ml_dtypes.bfloat16)
    low = (matrix - high.astype(np.float64)).astype(ml_dtypes.bfloat16)
    return high, low


def band(outs, ins, offset):
    matrix = np.zeros((outs, ins))
    for o in range(outs):
        for i in range(ins):
            k = i - o - offset + reach
            if 0 <= k <= 2 * reach:
                matrix[o, i] = filter_taps[k]
    return matrix


def plane_constants(layers, rows):
    stream = band(layers, layers, 0)
    wall = band(rows, 2 * rows, reach)
    ends = [0, reach, reach + rows, 2 * rows]
    thirds = [np.arange(ends[k], ends[k + 1]) for k in range(3)]
    parts = [np.arange(rows), np.arange(rows, 2 * rows), thirds[1], thirds[0], thirds[2]]
    blocks = [np.kron(stream, wall[:, part]) for part in parts]
    parts = [split_constant(block) for block in blocks]
    return np.concatenate([np.concatenate([high, low, high], axis=1) for high, low in parts], axis=1)


def span_constants(width):
    circle = np.zeros((width, width))
    for o in range(width):
        for k in range(2 * reach + 1):
            circle[(o + k - reach) % width, o] = filter_taps[k]
    half = width // 2

    def parts(matrix):
        high, low = split_constant(matrix)
        return np.block([[high, low], [high, np.zeros_like(low)]])

    packed = []
    for layers in range(2):
        row = []
        for s in range(2):
            matrix = np.zeros((width, width))
            matrix[:, layers * half : (layers + 1) * half] = circle[:, s * half : (s + 1) * half]
            row.append(parts(matrix))
        packed.append(np.concatenate(row, axis=1))
    return parts(circle), np.concatenate(packed, axis=0)


def halves(value):
    high = value.astype(jnp.bfloat16)
    return high, (value - high.astype(jnp.float32)).astype(jnp.bfloat16)


def dot(a, b):
    return lax.dot_general(a, b, (((1,), (0,)), ((), ())), preferred_element_type=jnp.float32)


def lane_index(shape):
    return lax.broadcasted_iota(jnp.int32, shape, len(shape) - 1)


def unit_index(shape):
    return lane_index(shape) // rim


def pack_halves(block, half):
    width = block.shape[-1]
    in_place = lane_index(block.shape[1:]) // (width // 2) == half
    for pair in range(2):
        moved = pltpu.roll(block[2 * pair + 1], width // 2, 2)
        yield pair, jnp.where(in_place, block[2 * pair], moved)


def pack_strip(block, unit):
    _, layers, rows, width = block.shape
    half = layers // 2
    units = unit_index((half, rows, width))
    total = jnp.zeros((half, rows, width), jnp.float32)
    for k in range(2):
        for f in range(4):
            step = 2 * f + k
            cells = block[f, k * half : (k + 1) * half]
            cells = pltpu.roll(cells, step * rim, 2) if step else cells
            total = jnp.where(units == lax.rem(unit + step, width // rim), cells, total)
    return total


def strip_tile(inner, outer, me_s):
    width = inner.shape[-1]
    is_outer = lax.rem(unit_index(inner.shape), 2) == 1 - me_s
    for k in range(2):
        shift = (width - k * rim) % width
        pieces = [pltpu.roll(strip, shift, 2) if k else strip for strip in (inner, outer)]
        yield k, jnp.where(is_outer, pieces[1], pieces[0])


def pack_kernel(own, to_partner, to_mine, to_other, to_same):
    _, layers, _, _ = own.shape
    me_s = lax.axis_index("stream")
    for message, half in ((to_partner, 1 - me_s), (to_mine, me_s)):
        for pair, tile in pack_halves(own, half):
            message[pair * layers : (pair + 1) * layers] = tile
        message[2 * layers :] = pack_strip(own, 4 - half)
    to_other[...] = pack_strip(own, 7 * me_s)
    to_same[...] = pack_strip(own, 7 * (1 - me_s))


def rest_kernel(part, own_strip, part_strip, rest):
    count, half = part.shape[0], own_strip.shape[0]
    rest[:count] = part[...]
    rest[count : count + half] = own_strip[...]
    rest[count + half :] = part_strip[...]


def unpack(mine, rest, me_s):
    count, rows, width = mine.shape
    layers = rest.shape[0] - count
    half = layers // 2
    unit = unit_index((half, rows, width))
    first = 4 * (1 - me_s)
    in_strip = (unit == first) | (unit == first + 3)
    for which, packed in enumerate((mine, rest)):
        far = rest[count + which * half : count + (which + 1) * half]
        for k, strip in strip_tile(packed[2 * layers : count], far, me_s):
            layer = (me_s if which == 0 else 1 - me_s) * layers + k * half
            for f in range(4):
                start = f // 2 * layers + k * half
                cells = packed[start : start + half]
                cells = pltpu.roll(cells, width // 2, 2) if f % 2 else cells
                moved = pltpu.roll(strip, width - 2 * f * rim, 2) if f else strip
                yield f, layer, jnp.where(in_strip, moved, cells)


def column(t, width=128):
    return slice(t * width, (t + 1) * width)


def put_parts(parts, down, across, value):
    third = parts.shape[0] // 3
    high, low = halves(value)
    for k, part in enumerate((high, high, low)):
        parts[pl.ds(k * third + down, value.shape[0]), across] = part


def planes_of(planes, part, parts):
    depth = parts.shape[0]
    start = part * depth if isinstance(part, int) else pl.multiple_of(part * depth, depth)
    return dot(planes[:, pl.ds(start, depth)], parts[...])


def add_products(planes, which, raw, base, parts):
    temperature = raw[3]
    for i in range(3):
        value = raw[i] * temperature
        put_parts(parts, 0, column(i), value.reshape(-1, value.shape[-1]))
    return base + planes_of(planes, 6 + which, parts)


def bring(mine, rest, raw, parts, keep=None, which=None):
    rows, width = mine.shape[1:]
    for f, layer, value in unpack(mine, rest, lax.axis_index("stream")):
        count = value.shape[0]
        value = value if keep is None else value * keep
        near = value if which is None else jnp.where(which == 0, value[:, rows - reach :], value[:, :reach])
        raw[f, pl.ds(layer, count)] = near
        down = pl.multiple_of(layer * rows, count * rows)
        put_parts(parts, down, column(f), value.reshape(-1, width))


def centre_kernel(
    mine, rest, planes, upper, lower, products, centre, parts, prod
):
    bring(mine, rest, centre, parts)
    for i in range(3):
        value = centre[i] * centre[3]
        put_parts(prod, 0, column(i), value.reshape(-1, value.shape[-1]))
    upper[...] = planes_of(planes, 1, parts)
    lower[...] = planes_of(planes, 0, parts)
    products[...] = planes_of(planes, 2, prod)


def span_pass(spans, planes, both):
    cells = planes.shape[0]
    rows = cells // both
    width = 128
    span_w = spans[: 2 * width, : 2 * width]
    high, low = halves(planes)
    tiles = planes.shape[1] // width
    parts = [jnp.concatenate([high[:, column(t)], low[:, column(t)]], axis=1) for t in range(tiles)]
    result = dot(jnp.concatenate(parts, axis=0), span_w)
    result = result[:, :width] + result[:, width:]
    return [result[t * cells : (t + 1) * cells].reshape(both, rows, width) for t in range(tiles)]


def second_input(means, parts):
    tiles = means + [means[i] * means[3] for i in range(3)]
    for t, value in enumerate(tiles):
        put_parts(parts, 0, column(t), value.reshape(-1, value.shape[-1]))


def packed_pass(spans, planes):
    cells = planes.shape[0]
    some, width = cells // 2, 128
    me_s = lax.axis_index("stream")
    along = pl.ds(pl.multiple_of((1 + me_s) * 2 * width, 2 * width), 2 * width)
    matrix = spans[:, along]
    high, low = halves(planes)
    tiles = planes.shape[1] // width
    parts = [
        jnp.concatenate(
            [high[:some, column(t)], low[:some, column(t)], high[some:, column(t)], low[some:, column(t)]],
            axis=1,
        )
        for t in range(tiles)
    ]
    result = dot(jnp.concatenate(parts, axis=0), matrix)
    result = result[:, :width] + result[:, width:]
    return [result[t * some : (t + 1) * some] for t in range(tiles)]


def pack_layers(own, other, me_s, shift=0):
    width = own.shape[-1]
    in_place = lane_index(own.shape) // (width // 2) == me_s
    own = pltpu.roll(own, shift % width, 2) if shift else own
    return jnp.where(in_place, own, pltpu.roll(other, (shift + width // 2) % width, 2))


def pack_means(mean, means, rows_near):
    for t, value in enumerate(means):
        mean[t] = value
    both = mean.shape[1]
    me_s = lax.axis_index("stream")
    own, other = pl.ds(me_s * (both // 2), both // 2), pl.ds((1 - me_s) * (both // 2), both // 2)
    for t in range(4):
        near = mean[t, own, rows_near, :], mean[t, other, rows_near, :]
        slope = (pack_layers(*near, me_s, -1) - pack_layers(*near, me_s, 1)) * 0.5
        yield t, pack_layers(mean[t, own], mean[t, other], me_s), slope


def mate_kernel(
    a_mine, a_rest, upper, lower, products, matrices, spans,
    base, packed, slopes, second, products_a, raw, parts, mid, mean, prod,
):
    both, rows = raw.shape[1:3]
    odd = lax.rem(lax.axis_index("wall"), 2)
    bring(a_mine, a_rest, raw, parts, which=1 - odd)
    planes = jnp.where(odd == 1, upper[...], lower[...])
    planes = planes + planes_of(matrices, 1 - odd, parts)
    means = span_pass(spans, planes, both)
    for t, value, slope in pack_means(mean, means, pl.ds(pl.multiple_of(odd * reach, reach), reach)):
        packed[t] = value
        slopes[t] = slope
    second_input(means, mid)
    second[...] = planes_of(matrices, 1 - odd, mid)
    base[...] = jnp.where(odd == 0, upper[...], lower[...])
    products_a[...] = add_products(matrices, 1 - odd, raw, products[...], prod)


def flux_kernel(
    walls, b_mine, b_rest, base, a_packed, a_slopes, a_second, products, matrices, spans,
    keep_ref, send_ref, sums_ref,
    raw, parts, prod, mean, mid, packed, slopes,
):
    _, layers, rows, width = keep_ref.shape
    both = 2 * layers
    cells = both * rows
    me_s = lax.axis_index("stream")
    me_w = lax.axis_index("wall")
    odd = lax.rem(me_w, 2)
    at_end = (me_w == 0) | (me_w == walls - 1)
    keep_b = jnp.where(at_end, 0.0, 1.0).astype(jnp.float32)

    bring(b_mine, b_rest, raw, parts, keep_b, odd)

    planes = base[...] + planes_of(matrices, odd, parts)
    row = lax.rem(lax.broadcasted_iota(jnp.int32, planes.shape, 0), rows)
    inside = (row < reach) == (odd == 1)
    planes = jnp.where(jnp.logical_or(inside, jnp.logical_not(at_end)), planes, 0.0)
    means = span_pass(spans, planes, both)
    rows_b = pl.ds(pl.multiple_of(odd * rows, rows), rows)
    rows_a = pl.ds(pl.multiple_of((1 - odd) * rows, rows), rows)
    near_b = pl.ds(pl.multiple_of(odd * reach, reach), reach)
    near_a = pl.ds(pl.multiple_of((1 - odd) * reach, reach), reach)
    for t, value, slope in pack_means(mean, means, near_a):
        packed[t, :, rows_b, :] = value
        packed[t, :, rows_a, :] = a_packed[t]
        slopes[t, :, near_b, :] = slope
        slopes[t, :, near_a, :] = a_slopes[t]
    second_input(means, mid)
    second = packed_pass(spans, a_second[...] + planes_of(matrices, odd, mid))
    second = [value.reshape(layers, rows, width) for value in second]

    flux = packed_pass(spans, add_products(matrices, odd, raw, products[...], prod))
    flux = [value.reshape(layers, rows, width) for value in flux]

    mid_rows = slice(reach, reach + rows)
    first = lane_index((1, rows, width)) < width // 2
    centre, along_wall, along_stream = [], [], []
    for f in range(4):
        here = packed[f, :, mid_rows, :]
        centre.append(here)
        below = packed[f, :, reach + 1 : reach + rows + 1, :]
        above = packed[f, :, reach - 1 : reach + rows - 1, :]
        along_wall.append((below - above) * 0.5)
        after = jnp.where(first, pltpu.roll(here[:1], width // 2, 2), 0.0)
        before = jnp.where(first, 0.0, pltpu.roll(here[layers - 1 :], width // 2, 2))
        ahead = jnp.concatenate([here[1:], after], axis=0)
        behind = jnp.concatenate([before, here[: layers - 1]], axis=0)
        along_stream.append((ahead - behind) * 0.5)

    lane = lane_index((rows, width))
    table = jnp.zeros((rows, width), jnp.float32)
    first = lane_index((layers, rows, width)) < width // 2
    in_first = me_s == 1
    for i in range(3):
        exact = flux[i] - centre[i] * centre[3]
        similar = second[4 + i] - second[i] * second[3]
        total = slopes[i] * slopes[3] + along_wall[i] * along_wall[3]
        clark = clark_coef * (total + along_stream[i] * along_stream[3])
        terms = (exact * clark, exact * similar, exact * exact, clark * clark, similar * similar)
        for q, term in enumerate(terms):
            value = jnp.sum(jnp.sum(term, axis=0), axis=1, keepdims=True)
            table = jnp.where(lane == 3 * q + i, value, table)
        keep_ref[i] = clark
        keep_ref[3 + i] = similar
        clark = jnp.where(in_first, clark, pltpu.roll(clark, width // 2, 2))
        similar = jnp.where(in_first, pltpu.roll(similar, width // 2, 2), similar)
        send_ref[i] = jnp.where(first, clark, similar)
    sums_ref[...] = table


def finish_kernel(
    plane_cells, sums, keep, come, clark_model, similar_model, clark_corr, similar_corr
):
    _, layers, rows, width = keep.shape
    me_s = lax.axis_index("stream")
    table = sums[...] / plane_cells
    lane = lane_index((rows, width))
    useful = lane // (width // 2) == me_s
    corr = jnp.zeros((rows, width), jnp.float32)
    for i in range(3):
        cross_c, cross_s, power_e, power_c, power_s = (
            table[:, 3 * q + i : 3 * q + i + 1] for q in range(5)
        )
        packed = come[i]
        turned = pltpu.roll(packed, width // 2, 2)
        clark = jnp.where(useful[None], keep[i], jnp.where(me_s == 0, turned, packed))
        similar = jnp.where(useful[None], keep[3 + i], jnp.where(me_s == 0, packed, turned))
        clark_model[i] = clark / jnp.sqrt(power_c + small_eps)[None]
        similar_model[i] = similar / jnp.sqrt(power_s + small_eps)[None]
        value = cross_c / jnp.sqrt((power_e + small_eps) * (power_c + small_eps))
        corr = jnp.where(lane == i, value, corr)
        value = cross_s / jnp.sqrt((power_e + small_eps) * (power_s + small_eps))
        corr = jnp.where(lane == 8 + i, value, corr)
    square = jnp.concatenate([corr, jnp.zeros((width - rows, width), jnp.float32)], axis=0)
    turned = square.T
    clark_corr[...] = turned[:3, :rows]
    similar_corr[...] = turned[8:11, :rows]


def call(kernel, name, ins, outs, scratch=(), mib=4, hint=None):
    cost = hint and pl.CostEstimate(flops=hint, bytes_accessed=0, transcendentals=0)
    return pl.pallas_call(
        kernel,
        out_shape=tuple(jax.ShapeDtypeStruct(shape, jnp.float32) for shape in outs),
        in_specs=[pl.BlockSpec(memory_space=pltpu.VMEM)] * len(ins),
        out_specs=tuple(pl.BlockSpec(memory_space=pltpu.VMEM) for _ in outs),
        scratch_shapes=[pltpu.VMEM(shape, dtype) for shape, dtype in scratch],
        compiler_params=pltpu.CompilerParams(vmem_limit_bytes=mib * 1024 * 1024),
        cost_estimate=cost,
        name=name,
    )(*ins)


def shards(fields):
    _, layers, rows, width = fields.shape
    spans = lax.axis_size("span")
    walls = lax.axis_size("wall")
    streams = lax.axis_size("stream")
    both = streams * layers
    cells = both * rows

    def swap(value):
        return lax.ppermute(value, "stream", [(0, 1), (1, 0)])

    def pair_a(value):
        return lax.ppermute(value, "wall", [(w, w ^ 1) for w in range(walls)])

    def pair_b(value):
        return lax.ppermute(
            value, "wall", [(w, min(max(((w + 1) ^ 1) - 1, 0), walls - 1)) for w in range(walls)]
        )

    def place(p, s):
        return (p % spans) * streams + s

    to_other, to_same = [], []
    for p in range(spans):
        to_other += [(place(p, 0), place(p - 1, 1)), (place(p, 1), place(p + 1, 0))]
        to_same += [(place(p, 1), place(p - 1, 1)), (place(p, 0), place(p + 1, 0))]

    message, strip = (2 * layers + layers // 2, rows, width), (layers // 2, rows, width)
    to_partner, mine, first, second = call(
        pack_kernel, "pack", (fields,), (message, message, strip, strip)
    )
    part = swap(to_partner)
    part_strip = lax.ppermute(first, ("span", "stream"), to_other)
    own_strip = lax.ppermute(second, ("span", "stream"), to_same)
    mine_now, b_mine, a_mine = lax.optimization_barrier((mine, pair_b(mine), pair_a(mine)))
    (rest,) = call(
        rest_kernel,
        "rest",
        (part, own_strip, part_strip),
        ((message[0] + layers, rows, width),),
        hint=2**35,
    )
    a_rest, b_rest = pair_a(rest), pair_b(rest)

    matrices = jnp.asarray(plane_constants(both, rows))
    single_pass, split_pass = span_constants(width)
    both_passes = np.zeros((4 * width, 6 * width), ml_dtypes.bfloat16)
    both_passes[: 2 * width, : 2 * width] = single_pass
    both_passes[:, 2 * width :] = split_pass
    passes = jnp.asarray(both_passes)
    single, brief = jnp.float32, jnp.bfloat16
    block, quarter = (4, both, rows, width), (4, layers, rows, width)
    four, three, seven = (((3 * cells, n * width), brief) for n in (4, 3, 7))
    few, near = ((3 * both * reach, 3 * width), brief), ((4, both, reach, width), single)
    upper, lower, products = call(
        centre_kernel,
        "centre",
        (mine_now, rest, matrices),
        ((cells, 4 * width), (cells, 4 * width), (cells, 3 * width)),
        [(block, single), four, three],
        mib=16,
        hint=2**31,
    )
    base, a_packed, a_slopes, a_second, products = call(
        mate_kernel,
        "mate",
        (a_mine, a_rest, upper, lower, products, matrices, passes),
        (
            (cells, 4 * width), quarter, (4, layers, reach, width), (cells, 7 * width),
            (cells, 3 * width),
        ),
        [near, four, seven, (block, single), few],
        mib=16,
        hint=2**29,
    )
    keep, send, sums = call(
        functools.partial(flux_kernel, walls),
        "flux",
        (b_mine, b_rest, base, a_packed, a_slopes, a_second, products, matrices, passes),
        ((6, layers, rows, width), (3, layers, rows, width), (rows, width)),
        [
            near,
            four,
            few,
            (block, single),
            seven,
            ((4, layers, 2 * rows, width), single),
            (quarter, single),
        ],
        mib=24,
    )

    come = swap(send)

    def from_span(value, step):
        return lax.ppermute(value, "span", [(p, p ^ step) for p in range(spans)])

    step = 1
    while step < spans:
        if 2 * step < spans:
            far = from_span(sums, 3 * step) + from_span(sums, 2 * step)
            sums = (sums + from_span(sums, step)) + far
        else:
            sums = sums + from_span(sums, step)
        step *= 4
    sums = sums + swap(sums)
    block, corr = (3, layers, rows, width), (3, rows)
    return call(
        functools.partial(finish_kernel, float(layers * width * spans * streams)),
        "finish",
        (sums, keep, come),
        (block, block, corr, corr),
    )


def solution(mesh):
    return jax.shard_map(
        shards,
        mesh=mesh,
        in_specs=(P(None, "stream", "wall", "span"),),
        out_specs=(
            P(None, "stream", "wall", "span"),
            P(None, "stream", "wall", "span"),
            P(None, "wall"),
            P(None, "wall"),
        ),
        check_vma=False,
    )
```
